32 devices in a mesh: grp: 8 (over y, x, core), psg: 4 (over z).
Axes of the slice: x: 2, y: 2, z: 4, core: 2. Of those that a mesh axis runs over, the one named last changes fastest.
Arguments:
- passages: bfloat16 [32768, 512], P(('grp', 'psg')), may hold values from -6 to 6
- queries: bfloat16 [4096, 512], P(('grp', 'psg')), may hold values from -6 to 6
- lengths: int32 [32, 16], P(('grp', 'psg')), may hold values from 1 to 512, 1024 in all within a row
- positives: int32 [128], P('grp'), may hold values from 0 to 63
- query_weight: bfloat16 [512, 512], replicated, may hold values from -0.25 to 0.25
- query_bias: float32 [512], replicated, may hold values from -3 to 3
- key_weight: bfloat16 [512, 512], replicated, may hold values from -0.25 to 0.25
- value_weight: bfloat16 [512, 512], replicated, may hold values from -0.25 to 0.25
- value_bias: float32 [512], replicated, may hold values from -3 to 3
- output_weight: bfloat16 [512, 512], replicated, may hold values from -0.75 to 0.75
- output_bias: float32 [512], replicated, may hold values from -3 to 3
- first_gain: float32 [512], replicated, may hold values from 0.5 to 1.5
- first_shift: float32 [512], replicated, may hold values from -2 to 2
- inner_weight: bfloat16 [512, 2048], replicated, may hold values from -0.25 to 0.25
- inner_bias: float32 [2048], replicated, may hold values from -3 to 3
- outer_weight: bfloat16 [2048, 512], replicated, may hold values from -0.125 to 0.125
- outer_bias: float32 [512], replicated, may hold values from -2 to 2
- second_gain: float32 [512], replicated, may hold values from 0.5 to 1.5
- second_shift: float32 [512], replicated, may hold values from -2 to 2
- project_weight: bfloat16 [512, 128], replicated, may hold values from -0.25 to 0.25
Outputs:
- passage_embeddings: bfloat16 [32768, 128], P(('grp', 'psg'))
- query_embeddings: bfloat16 [4096, 128], P(('grp', 'psg'))
- losses: float32 [128], P('grp')
- passage_grad: bfloat16 [32768, 512], P(('grp', 'psg'))
- query_grad: bfloat16 [4096, 512], P(('grp', 'psg'))
- query_weight_grad: float32 [512, 512], replicated
- query_bias_grad: float32 [512], replicated
- key_weight_grad: float32 [512, 512], replicated
- value_weight_grad: float32 [512, 512], replicated
- value_bias_grad: float32 [512], replicated
- output_weight_grad: float32 [512, 512], replicated
- output_bias_grad: float32 [512], replicated
- first_gain_grad: float32 [512], replicated
- first_shift_grad: float32 [512], replicated
- inner_weight_grad: float32 [512, 2048], replicated
- inner_bias_grad: float32 [2048], replicated
- outer_weight_grad: float32 [2048, 512], replicated
- outer_bias_grad: float32 [512], replicated
- second_gain_grad: float32 [512], replicated
- second_shift_grad: float32 [512], replicated
- project_weight_grad: float32 [512, 128], replicated
The draws below stay inside these ranges and needn't reach their ends.
Inputs may be any that keep to these rules, and one draw needn't show every extreme that they name: Each device's 16 lengths sum to 1024, and one of them is exactly 512.
All inputs are finite; a program needn't handle non-finite values.
Results may differ from the reference program's by a relative error of at most 0.017.
Values may be sent and summed in bfloat16 or wider, within the bound.
No kernel may reach another device: no remote copies, remote signals or barrier semaphores. Data moves between devices by JAX's collectives and lax.ppermute only.
A program may use at most 256 MiB of HBM per device.

```python
import math
import jax
import jax.numpy as jnp
import numpy as np
from jax import lax

D = 512
HEADS = 8
HEAD = 64
FF = 2048
DIM = 128
QLEN = 32
LONGEST = 512
P_DEV = 16
PTOK = 1024
QPG = 16
PG = 64
QUERIES = 128
N_GRP = 8
N_PSG = 4
DEVICES = 32


def plant(result, own_key, low, high):
    longest = result.shape.index(max(result.shape))
    spots = []
    for shift in (0, 1):
        where = [jax.random.randint(jax.random.fold_in(own_key, axis), (), 0, length) for axis, length in enumerate(result.shape)]
        where[longest] = (where[longest] + shift) % result.shape[longest]
        spots.append(tuple(where))
    return result.at[spots[0]].set(low).at[spots[1]].set(high)


def shard_levels(own_key, shape, shards, low, largest):
    def one(position, blocks):
        draws = jax.random.uniform(jax.random.fold_in(jax.random.fold_in(own_key, 6), position), (blocks,), jnp.float32, low / len(shards), largest / len(shards))
        return jnp.repeat(jnp.exp(draws), shape[position] // blocks).reshape((-1,) + (1,) * (len(shape) - position - 1))

    gain = one(*shards[0])
    for cut in shards[1:]:
        gain = gain * one(*cut)
    return gain


def split_up(amount, total, bound, lean):
    loads = [(1 << 20) // math.isqrt(standing ** lean) + 1 for standing in range(2, amount + 1)]
    rest, counts = total - bound - (amount - 1), [1] * (amount - 1)
    while rest > 0:
        candidates = [i for i in range(amount - 1) if counts[i] < bound]
        pool, budget = sum([loads[i] for i in candidates]), rest
        for i in candidates:
            extra = min(bound - counts[i], max(1, budget * loads[i] // pool), rest)
            counts[i] = counts[i] + extra
            rest = rest - extra
    return np.array([bound] + counts)


def uneven(rng, amount, total, bound, skew):
    if amount == 2:
        one = jax.random.randint(rng, (), max(1, total - bound), min(bound, total - 1) + 1)
        return jnp.stack([one, total - one])
    tallies = jnp.asarray(split_up(amount, total, bound, skew), jnp.int32)
    pairs = (amount - 1) // 2
    giver, taker = tallies[1:1 + 2 * pairs:2], tallies[2:2 + 2 * pairs:2]
    room = jnp.minimum(giver - 1, bound - taker)
    shifted = jax.random.randint(jax.random.fold_in(rng, 1), (pairs,), 0, 1 << 20) % (room + 1)
    tallies = tallies.at[1:1 + 2 * pairs:2].set(giver - shifted).at[2:2 + 2 * pairs:2].set(taker + shifted)
    return tallies[jax.random.permutation(jax.random.fold_in(rng, 2), amount)]


def noise(key, extent, deviation, most, cuts=(), held_as=jnp.bfloat16):
    factor_of = shard_levels(key, extent, cuts, -0.22, 0.18) if cuts else 1.0
    drawn = jax.random.normal(key, extent, jnp.float32) * deviation * factor_of
    return jnp.minimum(jnp.maximum(drawn, -most), most).astype(held_as)


def setup_inputs(seed: int = 0) -> dict:
    key_of = jax.random.split(jax.random.key(seed), 21)
    passages = noise(key_of[0], (DEVICES * PTOK, D), 1.0, 6.0, ((0, 32),))
    queries = noise(key_of[1], (QUERIES * QLEN, D), 1.0, 6.0, ((0, 32),))
    lengths = jax.vmap(lambda own: uneven(own, P_DEV, PTOK, LONGEST, 2))(jax.random.split(key_of[2], DEVICES)).reshape((DEVICES, P_DEV)).astype(jnp.int32)
    positives = plant(jax.random.randint(key_of[3], (QUERIES,), 0, PG), jax.random.fold_in(key_of[3], 1), 0, PG - 1).astype(jnp.int32)
    query_weight = noise(key_of[4], (D, D), D ** -0.5, 0.25)
    query_bias = noise(key_of[5], (D,), 0.5, 3.0, (), jnp.float32)
    key_weight = noise(key_of[6], (D, D), D ** -0.5, 0.25)
    value_weight = noise(key_of[7], (D, D), D ** -0.5, 0.25)
    value_bias = noise(key_of[8], (D,), 0.5, 3.0, (), jnp.float32)
    output_weight = noise(key_of[9], (D, D), (D // 8) ** -0.5, 0.75)
    output_bias = noise(key_of[10], (D,), 0.5, 3.0, (), jnp.float32)
    first_gain = jnp.clip(1.0 + 0.1 * jax.random.normal(key_of[11], (D,), jnp.float32), 0.5, 1.5)
    first_shift = noise(key_of[12], (D,), 0.3, 2.0, (), jnp.float32)
    inner_weight = noise(key_of[13], (D, FF), D ** -0.5, 0.25)
    inner_bias = noise(key_of[14], (FF,), 0.5, 3.0, (), jnp.float32)
    outer_weight = noise(key_of[15], (FF, D), FF ** -0.5, 0.125)
    outer_bias = noise(key_of[16], (D,), 0.3, 2.0, (), jnp.float32)
    second_gain = jnp.clip(1.0 + 0.1 * jax.random.normal(key_of[17], (D,), jnp.float32), 0.5, 1.5)
    second_shift = noise(key_of[18], (D,), 0.3, 2.0, (), jnp.float32)
    project_weight = noise(key_of[19], (D, DIM), D ** -0.5, 0.25)
    return dict(passages=passages, queries=queries, lengths=lengths, positives=positives, query_weight=query_weight, query_bias=query_bias, key_weight=key_weight, value_weight=value_weight, value_bias=value_bias, output_weight=output_weight, output_bias=output_bias, first_gain=first_gain, first_shift=first_shift, inner_weight=inner_weight, inner_bias=inner_bias, outer_weight=outer_weight, outer_bias=outer_bias, second_gain=second_gain, second_shift=second_shift, project_weight=project_weight)


@jax.custom_vjp
def low(v):
    return lax.optimization_barrier(v.astype(jnp.bfloat16)).astype(jnp.float32)

@jax.custom_vjp
def low_back(v):
    return v

def low_keep(v):
    return (low(v), None)

def low_pass(kept, grad):
    return (grad,)

def back_keep(v):
    return (v, None)

def back_low(kept, grad):
    return (low(grad),)
low.defvjp(low_keep, low_pass)
low_back.defvjp(back_keep, back_low)
SHARPNESS = 10.0
SCORE_SCALE = 0.25
NORM_EPS = 1e-06
EMBED_EPS = 1e-06
NEG_FILL = -1e+30
PRECISE = lax.Precision.HIGHEST

def product(left_side, right_side):
    return jnp.dot(left_side, right_side, precision=PRECISE, preferred_element_type=jnp.float32)

def layer_norm(norm_input, norm_gain, norm_shift):
    center = norm_input - lax.optimization_barrier(jnp.mean(norm_input, axis=-1, keepdims=True))
    spread = lax.optimization_barrier(jnp.mean(center * center, axis=-1, keepdims=True))
    return center * lax.rsqrt(spread + NORM_EPS) * norm_gain + norm_shift

def encode(inputs, segment, params):
    query_weight, query_bias, key_weight, value_weight, value_bias, output_weight, output_bias, first_gain, first_shift, inner_weight, inner_bias, outer_weight, outer_bias, second_gain, second_shift, project_weight = params
    row_count = inputs.shape[0]
    query_full = low(low_back(product(inputs, query_weight) + query_bias))
    key_full = low(low_back(product(inputs, key_weight)))
    value_full = low(low_back(product(inputs, value_weight) + value_bias))
    query_heads = query_full.reshape(row_count, HEADS, HEAD)
    key_heads = key_full.reshape(row_count, HEADS, HEAD)
    value_heads = value_full.reshape(row_count, HEADS, HEAD)
    logits = jnp.einsum('qhd,khd->hqk', query_heads, key_heads, precision=PRECISE) * HEAD ** (-0.5)
    logits = low_back(logits)
    same_seg = segment[:, None] == segment[None, :]
    logits = jnp.where(same_seg[None], logits, NEG_FILL)
    probability = low(jax.nn.softmax(logits, axis=-1))
    mixed_heads = jnp.einsum('hqk,khd->qhd', probability, value_heads, precision=PRECISE)
    attended = low(low_back(mixed_heads.reshape(row_count, HEADS * HEAD)))
    branch = low_back(product(attended, output_weight) + output_bias)
    hidden_one = layer_norm(inputs + branch, first_gain, first_shift)
    inner_pre = low_back(product(low(hidden_one), inner_weight) + inner_bias)
    active = low(jax.nn.gelu(inner_pre, approximate=False))
    outer_out = low_back(product(active, outer_weight) + outer_bias)
    hidden_two = layer_norm(hidden_one + outer_out, second_gain, second_shift)
    projected = low_back(product(low(hidden_two), project_weight))
    scaled = projected * lax.rsqrt(lax.optimization_barrier(jnp.sum(projected * projected, axis=-1, keepdims=True)) + EMBED_EPS)
    return low(scaled)

def group_loss(query_embed, pass_embed, group_seg, chosen_index):
    passage_ids = jnp.arange(PG, dtype=jnp.int32)
    member = (group_seg[:, None] == passage_ids[None, :]).astype(jnp.float32)
    similar = low_back(product(query_embed, pass_embed.T))
    exponent = jnp.exp(SHARPNESS * (similar - 1.0))
    pooled = product(exponent, member)
    smooth = 1.0 + jnp.log(pooled) / SHARPNESS
    scores = SCORE_SCALE * lax.optimization_barrier(jnp.sum(smooth.reshape(QPG, QLEN, PG), axis=1))
    chosen = (chosen_index[:, None] == passage_ids[None, :]).astype(jnp.float32)
    picked = lax.optimization_barrier(jnp.sum(scores * chosen, axis=1))
    return jax.nn.logsumexp(scores, axis=1) - picked

def total_forward(params, passages_full, queries_full, pass_seg, group_seg, positives):

    def encode_passages(items):
        return encode(items[0], items[1], params)

    def encode_queries(block_in):
        query_seg = jnp.arange(QPG * QLEN, dtype=jnp.int32) // QLEN
        return encode(block_in, query_seg, params)

    def score_group(items):
        return group_loss(items[0], items[1], items[2], items[3])
    pass_embed = lax.map(jax.checkpoint(encode_passages), (passages_full.reshape(DEVICES, PTOK, D), pass_seg))
    query_embed = lax.map(jax.checkpoint(encode_queries), queries_full.reshape(N_GRP, QPG * QLEN, D))
    losses = lax.map(jax.checkpoint(score_group), (query_embed, pass_embed.reshape(N_GRP, N_PSG * PTOK, DIM), group_seg, positives.reshape(N_GRP, QPG)))
    return (losses.reshape(QUERIES), (pass_embed.reshape(DEVICES * PTOK, DIM), query_embed.reshape(QUERIES * QLEN, DIM)))

def reference(passages, queries, lengths, positives, query_weight, query_bias, key_weight, value_weight, value_bias, output_weight, output_bias, first_gain, first_shift, inner_weight, inner_bias, outer_weight, outer_bias, second_gain, second_shift, project_weight):
    params = tuple((weight_in.astype(jnp.float32) for weight_in in (query_weight, query_bias, key_weight, value_weight, value_bias, output_weight, output_bias, first_gain, first_shift, inner_weight, inner_bias, outer_weight, outer_bias, second_gain, second_shift, project_weight)))
    length_ends = jnp.cumsum(lengths, axis=1).astype(jnp.int32)
    token_index = jnp.arange(PTOK, dtype=jnp.int32)
    pass_seg = lax.optimization_barrier(jnp.sum((token_index[None, :, None] >= length_ends[:, None, :]).astype(jnp.int32), axis=2)).astype(jnp.int32)
    device_ids = jnp.arange(DEVICES, dtype=jnp.int32)
    group_seg = (pass_seg + (device_ids % N_PSG)[:, None] * P_DEV).astype(jnp.int32).reshape(N_GRP, N_PSG * PTOK)

    def forward(params_f, passages_f, queries_f):
        return total_forward(params_f, passages_f, queries_f, pass_seg, group_seg, positives)
    losses, pull_back, embeds = jax.vjp(forward, params, passages.astype(jnp.float32), queries.astype(jnp.float32), has_aux=True)
    grad_params, grad_pass, grad_query = pull_back(jnp.ones_like(losses))
    return (embeds[0].astype(jnp.bfloat16), embeds[1].astype(jnp.bfloat16), losses, grad_pass.astype(jnp.bfloat16), grad_query.astype(jnp.bfloat16), grad_params[0], grad_params[1], grad_params[2], grad_params[3], grad_params[4], grad_params[5], grad_params[6], grad_params[7], grad_params[8], grad_params[9], grad_params[10], grad_params[11], grad_params[12], grad_params[13], grad_params[14], grad_params[15])
```

```python
import functools

import jax
import jax.numpy as jnp
from jax import lax
from jax.experimental import pallas as pl
from jax.experimental.pallas import tpu as pltpu
from jax.sharding import PartitionSpec as P

HEADS = 8
HEAD = 64
QLEN = 32

SHARPNESS = 10.0
SCORE_SCALE = 0.25
NORM_EPS = 1e-06
EMBED_EPS = 1e-06
NEG_FILL = -1e30

F32 = jnp.float32
BF16 = jnp.bfloat16

TAIL_RATE = 0.31
TAIL = (
    7.983606475521152e-07,
    0.1236395104756606,
    0.1242090884595448,
    0.10710904223979588,
    0.11180972726115022,
    -0.017506651471085752,
    0.15741012515832603,
    -0.14274382211708148,
    0.036072242976455976,
)
INV_SQRT_2PI = 0.3989422804014327

QUAD = 4
QLANES = QUAD * HEAD
RB = 256
CB = 256
LANES = 128
FCHUNK = 512
VMEM_LIMIT = 56 * 1024 * 1024


def dot(left, right):
    return jnp.dot(left, right, preferred_element_type=F32)


def dot_t(left, right):
    return lax.dot_general(left, right, (((1,), (1,)), ((), ())), preferred_element_type=F32)


def t_dot(left, right):
    return lax.dot_general(left, right, (((0,), (0,)), ((), ())), preferred_element_type=F32)


def two_part_dot(left, right_low):
    high = left.astype(BF16)
    rest = (left - high.astype(F32)).astype(BF16)
    return dot(high, right_low) + dot(rest, right_low)


def norm_stats(x):
    center = x - jnp.mean(x, axis=-1, keepdims=True)
    rate = lax.rsqrt(jnp.mean(center * center, axis=-1, keepdims=True) + NORM_EPS)
    return center * rate, rate


def norm_backward(grad, x, gain):
    scaled, rate = norm_stats(x)
    inner = grad * gain
    mean_in = jnp.mean(inner, axis=-1, keepdims=True)
    mean_dot = jnp.mean(inner * scaled, axis=-1, keepdims=True)
    grad_x = rate * (inner - mean_in - scaled * mean_dot)
    return grad_x, jnp.sum(grad * scaled, axis=0, keepdims=True), jnp.sum(grad, axis=0, keepdims=True), scaled


def unit_backward(grad, projected):
    rate = lax.rsqrt(jnp.sum(projected * projected, axis=-1, keepdims=True) + EMBED_EPS)
    unit = projected * rate
    return rate * (grad - unit * jnp.sum(grad * unit, axis=-1, keepdims=True))


def gelu_pair(f):
    u = jnp.abs(f)
    t = 1.0 / (1.0 + TAIL_RATE * u)
    e = jnp.exp(-0.5 * (f * f))
    poly = TAIL[-1]
    for coefficient in TAIL[-2::-1]:
        poly = poly * t + coefficient
    tail = e * poly
    phi = jnp.where(f < 0.0, tail, 1.0 - tail)
    return f * phi, phi + f * (e * INV_SQRT_2PI)


def segment_ends(lengths_ref):
    count = lengths_ref.shape[1]
    ends = []
    total = jnp.int32(0)
    for s in range(count):
        total = total + lengths_ref[0, s]
        ends.append(total)
    return ends


def fill_bias(bias_ref, lengths_ref, ptok, rows):
    ends = segment_ends(lengths_ref)
    count = len(ends)

    def segments(token):
        seg = jnp.zeros_like(token)
        for end in ends:
            seg = seg + jnp.where(token >= end, 1, 0)
        return jnp.where(token >= ptok, count + (token - ptok) // QLEN, seg)

    row_seg = segments(lax.broadcasted_iota(jnp.int32, (8, rows), 1))[:1]

    def fill(b, carry):
        r0 = pl.multiple_of(b * LANES, LANES)
        col = segments(lax.broadcasted_iota(jnp.int32, (LANES, LANES), 0) + r0)
        for c in range(rows // LANES):
            part = row_seg[:, c * LANES : (c + 1) * LANES]
            bias_ref[pl.ds(r0, LANES), c * LANES : (c + 1) * LANES] = jnp.where(col == part, 0.0, NEG_FILL)
        return carry

    lax.fori_loop(0, rows // LANES, fill, 0)


def windows(lengths_ref, ptok):
    ends = segment_ends(lengths_ref)
    found = []
    for b in range(ptok // RB):
        first = b * RB
        last = first + RB - 1
        low = jnp.int32(0)
        high = jnp.int32(ptok)
        for end in ends:
            low = jnp.where(end <= first, jnp.maximum(low, end), low)
            high = jnp.where(end > last, jnp.minimum(high, end), high)
        start = (low // LANES) * LANES
        found.append((start, (high - start + CB - 1) // CB))
    return found


def head_masks(rows, lanes):
    lane = lax.broadcasted_iota(jnp.int32, (rows, lanes), 1) // HEAD
    return [lane == h for h in range(lanes // HEAD)]


def attention_forward_kernel(
    ptok,
    lengths_ref,
    xp_ref,
    xq_ref,
    wq_ref,
    bq_ref,
    wk_ref,
    wv_ref,
    bv_ref,
    wo_ref,
    bo_ref,
    q_ref,
    k_ref,
    v_ref,
    o_ref,
    lse_ref,
    r1_ref,
    x_scr,
    bias_scr,
    s_scr,
    mx_scr,
    l_scr,
    acc_scr,
    qm_scr,
):
    step = pl.program_id(0)
    rows = x_scr.shape[0]
    qtok = rows - ptok

    @pl.when(step == 0)
    def _():
        x_scr[:ptok] = xp_ref[...]
        x_scr[ptok:] = xq_ref[...]
        r1_ref[...] = x_scr[...].astype(F32) + bo_ref[...]
        fill_bias(bias_scr, lengths_ref, ptok, rows)

    x = x_scr[...]
    q_ref[...] = (dot(x, wq_ref[...]) + bq_ref[...]).astype(BF16) * BF16(HEAD**-0.5)
    k_ref[...] = dot(x, wk_ref[...]).astype(BF16)
    v_ref[...] = (dot(x, wv_ref[...]) + bv_ref[...]).astype(BF16)
    lse_ref[...] = jnp.zeros_like(lse_ref)

    def block(r0, size, first_key, chunks, width):
        masks = head_masks(size, QLANES)
        q = q_ref[pl.ds(r0, size), :]
        for h in range(QUAD):
            qm_scr[h, :size] = jnp.where(masks[h], q, BF16(0))
        mx_scr[:, :size] = jnp.full((QUAD, size, LANES), -jnp.inf, F32)
        l_scr[:, :size] = jnp.zeros((QUAD, size, LANES), F32)
        acc_scr[:, :size] = jnp.zeros((QUAD, size, LANES), F32)

        def score(c, carry):
            k0 = pl.multiple_of(first_key + c * width, LANES)
            keys = k_ref[pl.ds(k0, width), :]
            bias = bias_scr[pl.ds(r0, size), pl.ds(k0, width)]
            for h in range(QUAD):
                s = dot_t(qm_scr[h, :size], keys) + bias
                s_scr[h, c, :size, :width] = s
                peak = mx_scr[h, :size]
                for part in range(width // LANES):
                    peak = jnp.maximum(peak, s[:, part * LANES : (part + 1) * LANES])
                mx_scr[h, :size] = peak
            return carry

        if isinstance(chunks, int):
            for c in range(chunks):
                score(c, 0)
        else:
            lax.fori_loop(0, chunks, score, 0)
        for h in range(QUAD):
            peak = jnp.max(mx_scr[h, :size], axis=-1, keepdims=True)
            mx_scr[h, :size] = jnp.broadcast_to(peak, (size, LANES))

        def mix(c, carry):
            k0 = pl.multiple_of(first_key + c * width, LANES)
            for h in range(QUAD):
                peak = mx_scr[h, :size]
                s = s_scr[h, c, :size, :width]
                parts = [
                    jnp.exp(s[:, part * LANES : (part + 1) * LANES] - peak) for part in range(width // LANES)
                ]
                total = l_scr[h, :size]
                for part in parts:
                    total = total + part
                l_scr[h, :size] = total
                lanes = (h // 2) * LANES
                e = jnp.concatenate([part.astype(BF16) for part in parts], axis=1)
                acc_scr[h, :size] += dot(e, v_ref[pl.ds(k0, width), lanes : lanes + LANES])
            return carry

        if isinstance(chunks, int):
            for c in range(chunks):
                mix(c, 0)
        else:
            lax.fori_loop(0, chunks, mix, 0)
        lane = lax.broadcasted_iota(jnp.int32, (size, LANES), 1)
        logs = jnp.zeros((size, LANES), F32)
        mixed = []
        for h in range(QUAD):
            total = jnp.sum(l_scr[h, :size], axis=-1, keepdims=True)
            mixed.append(acc_scr[h, :size] * (1.0 / total))
            logs = jnp.where(lane == h, mx_scr[h, :size] + jnp.log(total), logs)
        for pair in range(QUAD // 2):
            both = jnp.where(lane < HEAD, mixed[2 * pair], mixed[2 * pair + 1])
            o_ref[pl.ds(r0, size), pair * LANES : (pair + 1) * LANES] = both.astype(BF16)
        lse_ref[0, :, pl.ds(r0, size)] = jnp.transpose(logs)[:8]

    for b, (first_key, chunks) in enumerate(windows(lengths_ref, ptok)):
        block(b * RB, RB, first_key, chunks, CB)
    block(ptok, qtok, ptok, 1, qtok)
    r1_ref[...] += dot(o_ref[...], wo_ref[...])


def spec(shape, index):
    return pl.BlockSpec(shape, index)


def whole(array):
    nd = len(array.shape)
    return pl.BlockSpec(array.shape, lambda *_: (0,) * nd)


def smem():
    return pl.BlockSpec(memory_space=pltpu.SMEM)


def shaped(shape, dtype):
    return jax.ShapeDtypeStruct(shape, dtype)


def params(grid_rank):
    return pltpu.CompilerParams(
        dimension_semantics=("arbitrary",) * grid_rank, vmem_limit_bytes=VMEM_LIMIT
    )


def attention_forward(lengths, xp, xq, wq, bq, wk, wv, bv, wo, bo):
    ptok, width = xp.shape
    qtok = xq.shape[0]
    rows = ptok + qtok
    quads = HEADS // QUAD
    cols = lambda size: spec((size, QLANES), lambda g: (0, g))
    deepest = ptok // CB + 1
    return pl.pallas_call(
        functools.partial(attention_forward_kernel, ptok),
        grid=(quads,),
        in_specs=[
            smem(),
            whole(xp),
            whole(xq),
            cols(width),
            cols(1),
            cols(width),
            cols(width),
            cols(1),
            spec((QLANES, width), lambda g: (g, 0)),
            whole(bo),
        ],
        out_specs=[
            cols(rows),
            cols(rows),
            cols(rows),
            cols(rows),
            spec((1, 8, rows), lambda g: (g, 0, 0)),
            spec((rows, width), lambda g: (0, 0)),
        ],
        out_shape=[shaped((rows, width), BF16)] * 4
        + [shaped((quads, 8, rows), F32), shaped((rows, width), F32)],
        scratch_shapes=[
            pltpu.VMEM((rows, width), BF16),
            pltpu.VMEM((rows, rows), F32),
            pltpu.VMEM((QUAD, deepest, RB, CB), F32),
            pltpu.VMEM((QUAD, RB, LANES), F32),
            pltpu.VMEM((QUAD, RB, LANES), F32),
            pltpu.VMEM((QUAD, RB, LANES), F32),
            pltpu.VMEM((QUAD, RB, QLANES), BF16),
        ],
        compiler_params=params(1),
        name="attention_forward",
    )(lengths, xp, xq, wq, bq, wk, wv, bv, wo, bo)


def ffn_forward_kernel(
    aliased,
    rb,
    r1_ref,
    g1_ref,
    s1_ref,
    wi_ref,
    bi_ref,
    wo_ref,
    bo_ref,
    g2_ref,
    s2_ref,
    wp_ref,
    *rest,
):
    rest = rest[aliased:]
    u_ref, d_ref, r2_ref, e_ref, emb_ref, h1_scr = rest
    step = pl.program_id(0)
    rows = r1_ref.shape[0]

    @pl.when(step == 0)
    def _():
        scaled, rate = norm_stats(r1_ref[...])
        h1 = scaled * g1_ref[...] + s1_ref[...]
        h1_scr[...] = h1.astype(BF16)
        r2_ref[...] = h1 + bo_ref[...]

    for r in range(0, rows, rb):
        f = dot(h1_scr[r : r + rb], wi_ref[...]) + bi_ref[...]
        u, d = gelu_pair(f)
        low = u.astype(BF16)
        u_ref[r : r + rb] = low
        d_ref[r : r + rb] = d.astype(BF16)
        r2_ref[r : r + rb] += dot(low, wo_ref[...])

    @pl.when(step == pl.num_programs(0) - 1)
    def _():
        scaled, rate = norm_stats(r2_ref[...])
        h2 = (scaled * g2_ref[...] + s2_ref[...]).astype(BF16)
        e = dot(h2, wp_ref[...])
        e_ref[...] = e
        size = jnp.sum(e * e, axis=-1, keepdims=True)
        emb_ref[...] = (e * lax.rsqrt(size + EMBED_EPS)).astype(BF16)


def ffn_forward(count, offset, total, r1, g1, s1, wi, bi, wo, bo, g2, s2, wp, previous):
    width = r1.shape[1]
    ff = wi.shape[1]
    dim = wp.shape[1]
    at = offset // count
    first = 10
    held = list(previous)
    return pl.pallas_call(
        functools.partial(ffn_forward_kernel, len(held), min(RB, count)),
        grid=(ff // FCHUNK,),
        in_specs=[
            spec((count, width), lambda c: (at, 0)),
            whole(g1),
            whole(s1),
            spec((width, FCHUNK), lambda c: (0, c)),
            spec((1, FCHUNK), lambda c: (0, c)),
            spec((FCHUNK, width), lambda c: (c, 0)),
            whole(bo),
            whole(g2),
            whole(s2),
            whole(wp),
        ]
        + [pl.BlockSpec(memory_space=pl.ANY)] * len(held),
        out_specs=[
            spec((count, FCHUNK), lambda c: (at, c)),
            spec((count, FCHUNK), lambda c: (at, c)),
            spec((count, width), lambda c: (at, 0)),
            spec((count, dim), lambda c: (at, 0)),
            spec((count, dim), lambda c: (0, 0)),
        ],
        out_shape=[
            shaped((total, ff), BF16),
            shaped((total, ff), BF16),
            shaped((total, width), F32),
            shaped((total, dim), F32),
            shaped((count, dim), BF16),
        ],
        scratch_shapes=[pltpu.VMEM((count, width), BF16)],
        input_output_aliases={first + i: i for i in range(len(held))},
        compiler_params=params(1),
        name="ffn_forward",
    )(r1, g1, s1, wi, bi, wo, bo, g2, s2, wp, *held)


def passage_member(lengths_ref, rows):
    ends = segment_ends(lengths_ref)
    lane = lax.broadcasted_iota(jnp.int32, (8, LANES), 1)
    low = jnp.full((8, LANES), rows, jnp.int32)
    high = jnp.zeros((8, LANES), jnp.int32)
    start = jnp.int32(0)
    for s, end in enumerate(ends):
        low = jnp.where(lane == s, start, low)
        high = jnp.where(lane == s, end, high)
        start = end
    token = lax.broadcasted_iota(jnp.int32, (rows, LANES), 0)
    inside = (token >= low[:1]) & (token < high[:1])
    return jnp.where(inside, 1.0, 0.0).astype(BF16)


def soft_match(group, pass_embed):
    return jnp.exp(SHARPNESS * dot_t(group, pass_embed) - SHARPNESS)


def score_kernel(psg, count, lengths_ref, emb_ref, *rest):
    group_refs = rest[:psg]
    score_ref, pooled_ref = rest[psg:]
    member = passage_member(lengths_ref, emb_ref.shape[0])
    group = jnp.concatenate([ref[...] for ref in group_refs], axis=0)
    matched = soft_match(group, emb_ref[...])
    pooled = two_part_dot(matched, member)
    lane = lax.broadcasted_iota(jnp.int32, pooled.shape, 1)
    pooled = jnp.where(lane < count, pooled, 1.0)
    pooled_ref[...] = pooled
    smooth = 1.0 + jnp.log(pooled) * (1.0 / SHARPNESS)
    queries = pooled.shape[0] // QLEN
    score_ref[...] = SCORE_SCALE * jnp.sum(smooth.reshape(queries, QLEN, LANES), axis=1)


def score(lengths, emb, groups):
    psg = len(groups)
    tokens = sum(g.shape[0] for g in groups)
    return pl.pallas_call(
        functools.partial(score_kernel, psg, lengths.shape[1]),
        in_specs=[smem()] + [pl.BlockSpec(memory_space=pltpu.VMEM)] * (1 + psg),
        out_shape=[shaped((tokens // QLEN, LANES), F32), shaped((tokens, LANES), F32)],
        compiler_params=pltpu.CompilerParams(vmem_limit_bytes=VMEM_LIMIT),
        name="score",
    )(lengths, emb, *groups)


def loss_kernel(psg, count, where_ref, lengths_ref, positives_ref, pooled_ref, emb_ref, *rest):
    group_refs = rest[:psg]
    score_refs = rest[psg : 2 * psg]
    loss_ref, own_ref = rest[2 * psg : 2 * psg + 2]
    away_refs = rest[2 * psg + 2 : 3 * psg + 1]
    grad_ref = rest[3 * psg + 1]
    position = where_ref[0]
    queries = score_refs[0].shape[0]
    each = queries // psg
    lane = lax.broadcasted_iota(jnp.int32, (queries, LANES), 1)
    row = lax.broadcasted_iota(jnp.int32, (queries, LANES), 0)
    valid = lane < count
    blocks = []
    for e in range(psg):
        found = score_refs[e][...]
        found = jnp.concatenate(
            [found[((d - e) % psg) * each : ((d - e) % psg + 1) * each] for d in range(psg)], axis=0
        )
        blocks.append(jnp.where(valid, found, -jnp.inf))
    target = jnp.zeros((queries, LANES), jnp.int32)
    for d in range(psg):
        for j in range(each):
            chosen = positives_ref[lax.rem(position + d, psg) * each + j]
            target = jnp.where(row == d * each + j, chosen, target)
    peak = blocks[0]
    for found in blocks[1:]:
        peak = jnp.maximum(peak, found)
    peak = jnp.max(peak, axis=-1, keepdims=True)
    total = jnp.zeros((queries, 1), F32)
    picked = jnp.zeros((queries, 1), F32)
    for e in range(psg):
        owner = lax.rem(position + e, psg)
        hit = (target == owner * count + lane) & valid
        total = total + jnp.sum(jnp.exp(blocks[e] - peak), axis=-1, keepdims=True)
        picked = picked + jnp.sum(jnp.where(hit, blocks[e], 0.0), axis=-1, keepdims=True)
        if e == 0:
            own_hit = jnp.where(hit, 1.0, 0.0)
    log_total = peak + jnp.log(total)
    losses = jnp.broadcast_to(log_total - picked, (queries, LANES))
    for d in range(psg):
        owner = lax.rem(position + d, psg)
        for j in range(each):
            loss_ref[pl.ds(owner * each + j, 1), :] = losses[d * each + j : d * each + j + 1]
    grad = jnp.where(valid, jnp.exp(blocks[0] - log_total) - own_hit, 0.0) * SCORE_SCALE
    tokens = queries * QLEN
    grad = jnp.broadcast_to(grad[:, None, :], (queries, QLEN, LANES)).reshape(tokens, LANES)
    grad = grad / pooled_ref[...]
    member = passage_member(lengths_ref, emb_ref.shape[0])
    high = grad.astype(BF16)
    rest_low = (grad - high.astype(F32)).astype(BF16)
    spread = dot_t(high, member) + dot_t(rest_low, member)
    group = jnp.concatenate([ref[...] for ref in group_refs], axis=0)
    low = (soft_match(group, emb_ref[...]) * spread).astype(BF16)
    group_grad = dot(low, emb_ref[...])
    each_tokens = tokens // psg
    own_ref[...] = group_grad[:each_tokens]
    for d in range(1, psg):
        away_refs[d - 1][...] = group_grad[d * each_tokens : (d + 1) * each_tokens].astype(BF16)
    grad_ref[...] = t_dot(low, group)


def loss_and_grads(position, lengths, positives, pooled, emb, groups, scores):
    psg = len(groups)
    queries = scores[0].shape[0]
    tokens, dim = groups[0].shape
    vmem = pl.BlockSpec(memory_space=pltpu.VMEM)
    return pl.pallas_call(
        functools.partial(loss_kernel, psg, lengths.shape[1]),
        in_specs=[smem(), smem(), smem()] + [vmem] * (2 + 2 * psg),
        out_shape=[shaped((queries, LANES), F32), shaped((tokens, dim), F32)]
        + [shaped((tokens, dim), BF16)] * (psg - 1)
        + [shaped(emb.shape, F32)],
        compiler_params=pltpu.CompilerParams(vmem_limit_bytes=VMEM_LIMIT),
        name="loss_and_grads",
    )(position, lengths, positives, pooled, emb, *groups, *scores)


def head_backward(grad_embed, e, r2, wp, g2, s2):
    low = unit_backward(grad_embed, e).astype(BF16)
    grad_h2 = dot_t(low, wp)
    grad_r2, gain_term, shift_term, scaled = norm_backward(grad_h2, r2, g2)
    h2 = (scaled * g2 + s2).astype(BF16)
    return grad_r2, gain_term, shift_term, t_dot(h2, low)


def passage_head_kernel(grad_ref, e_ref, r2_ref, wp_ref, g2_ref, s2_ref, gr2_ref, vec_ref, proj_ref):
    grad_r2, gain_term, shift_term, proj = head_backward(
        grad_ref[...], e_ref[...], r2_ref[...], wp_ref[...], g2_ref[...], s2_ref[...]
    )
    gr2_ref[...] = grad_r2
    vec_ref[...] = jnp.zeros_like(vec_ref)
    vec_ref[0:1] = gain_term
    vec_ref[1:2] = shift_term
    proj_ref[...] = proj


def passage_head(grad, e, r2, wp, g2, s2):
    ptok, dim = grad.shape
    width = r2.shape[1]
    return pl.pallas_call(
        passage_head_kernel,
        grid=(1,),
        in_specs=[
            whole(grad),
            spec((ptok, dim), lambda i: (0, 0)),
            spec((ptok, width), lambda i: (0, 0)),
            whole(wp),
            whole(g2),
            whole(s2),
        ],
        out_specs=[
            spec((ptok, width), lambda i: (0, 0)),
            spec((8, width), lambda i: (0, 0)),
            spec((width, dim), lambda i: (0, 0)),
        ],
        out_shape=[shaped((ptok, width), F32), shaped((8, width), F32), shaped((width, dim), F32)],
        compiler_params=params(1),
        name="passage_head",
    )(grad, e, r2, wp, g2, s2)


def ffn_backward_kernel(
    psg,
    gr2p_ref,
    vec_ref,
    proj_ref,
    own_ref,
    *rest,
):
    away_refs = rest[: psg - 1]
    (
        e_ref,
        r2_ref,
        wp_ref,
        g2_ref,
        s2_ref,
        r1_ref,
        g1_ref,
        s1_ref,
        wi_ref,
        wo_ref,
        u_ref,
        d_ref,
        dproj_ref,
        dvec_ref,
        dbi_ref,
        dwo_ref,
        dwi_ref,
        gh1_ref,
        gz_scr,
        h1_scr,
    ) = rest[psg - 1 :]
    step = pl.program_id(0)
    ptok = gr2p_ref.shape[0]
    rows = gz_scr.shape[0]

    @pl.when(step == 0)
    def _():
        grad = own_ref[...]
        for ref in away_refs:
            grad = grad + ref[...].astype(F32)
        grad_r2, gain_term, shift_term, proj = head_backward(
            grad, e_ref[...], r2_ref[...], wp_ref[...], g2_ref[...], s2_ref[...]
        )
        dproj_ref[...] = (proj_ref[...] + proj).astype(BF16)
        gr2p = gr2p_ref[...]
        gh1_ref[:ptok] = gr2p
        gh1_ref[ptok:] = grad_r2
        low_p = gr2p.astype(BF16)
        low_q = grad_r2.astype(BF16)
        gz_scr[:ptok] = low_p
        gz_scr[ptok:] = low_q
        dvec_ref[...] = jnp.zeros_like(dvec_ref)
        dvec_ref[0:1] = vec_ref[0:1] + gain_term
        dvec_ref[1:2] = vec_ref[1:2] + shift_term
        dvec_ref[2:3] = jnp.sum(low_p.astype(F32), axis=0, keepdims=True) + jnp.sum(
            low_q.astype(F32), axis=0, keepdims=True
        )
        scaled, rate = norm_stats(r1_ref[...])
        h1_scr[...] = (scaled * g1_ref[...] + s1_ref[...]).astype(BF16)

    gz = gz_scr[...]
    grad_active = dot_t(gz, wo_ref[...])
    grad_inner = (grad_active * d_ref[...].astype(F32)).astype(BF16)
    dbi_ref[...] = jnp.sum(grad_inner.astype(F32), axis=0, keepdims=True)
    gh1_ref[...] += dot_t(grad_inner, wi_ref[...])
    dwo_ref[...] = t_dot(u_ref[...], gz).astype(BF16)
    dwi_ref[...] = t_dot(h1_scr[...], grad_inner).astype(BF16)


def ffn_backward(gr2p, vec, proj, own, aways, e, r2, wp, g2, s2, r1, g1, s1, wi, wo, u, d):
    ptok, width = gr2p.shape
    rows = r1.shape[0]
    qtok = rows - ptok
    dim = wp.shape[1]
    ff = wi.shape[1]
    at = ptok // qtok
    return pl.pallas_call(
        functools.partial(ffn_backward_kernel, 1 + len(aways)),
        grid=(ff // FCHUNK,),
        in_specs=[whole(gr2p), whole(vec), whole(proj), whole(own)]
        + [whole(a) for a in aways]
        + [
            spec((qtok, dim), lambda c: (at, 0)),
            spec((qtok, width), lambda c: (at, 0)),
            whole(wp),
            whole(g2),
            whole(s2),
            whole(r1),
            whole(g1),
            whole(s1),
            spec((width, FCHUNK), lambda c: (0, c)),
            spec((FCHUNK, width), lambda c: (c, 0)),
            spec((rows, FCHUNK), lambda c: (0, c)),
            spec((rows, FCHUNK), lambda c: (0, c)),
        ],
        out_specs=[
            spec((width, dim), lambda c: (0, 0)),
            spec((8, width), lambda c: (0, 0)),
            spec((1, FCHUNK), lambda c: (0, c)),
            spec((FCHUNK, width), lambda c: (c, 0)),
            spec((width, FCHUNK), lambda c: (0, c)),
            spec((rows, width), lambda c: (0, 0)),
        ],
        out_shape=[
            shaped((width, dim), BF16),
            shaped((8, width), F32),
            shaped((1, ff), F32),
            shaped((ff, width), BF16),
            shaped((width, ff), BF16),
            shaped((rows, width), F32),
        ],
        scratch_shapes=[pltpu.VMEM((rows, width), BF16), pltpu.VMEM((rows, width), BF16)],
        compiler_params=params(1),
        name="ffn_backward",
    )(gr2p, vec, proj, own, *aways, e, r2, wp, g2, s2, r1, g1, s1, wi, wo, u, d)


def attention_backward_kernel(
    ptok,
    lengths_ref,
    gh1_ref,
    r1_ref,
    g1_ref,
    wo_ref,
    oall_ref,
    xp_ref,
    xq_ref,
    q_ref,
    k_ref,
    v_ref,
    o_ref,
    lse_ref,
    wq_ref,
    wk_ref,
    wv_ref,
    dvec_ref,
    dout_ref,
    dwq_ref,
    dwk_ref,
    dwv_ref,
    dbq_ref,
    dbv_ref,
    gp_ref,
    gq_ref,
    x_scr,
    bias_scr,
    go_scr,
    gin_scr,
    dd_scr,
    gq_scr,
    gk_scr,
    gv_scr,
    qm_scr,
    gm_scr,
):
    step = pl.program_id(0)
    rows = x_scr.shape[0]
    qtok = rows - ptok
    quads = HEADS // QUAD

    @pl.when(step == 0)
    def _():
        x_scr[:ptok] = xp_ref[...]
        x_scr[ptok:] = xq_ref[...]
        fill_bias(bias_scr, lengths_ref, ptok, rows)
        grad_r1, gain_term, shift_term, scaled = norm_backward(gh1_ref[...], r1_ref[...], g1_ref[...])
        gin_scr[...] = grad_r1
        low = grad_r1.astype(BF16)
        dvec_ref[...] = jnp.zeros_like(dvec_ref)
        dvec_ref[0:1] = gain_term
        dvec_ref[1:2] = shift_term
        dvec_ref[2:3] = jnp.sum(low.astype(F32), axis=0, keepdims=True)
        dout_ref[...] = t_dot(oall_ref[...], low).astype(BF16)
        go = dot_t(low, wo_ref[...]).astype(BF16)
        for g in range(quads):
            go_scr[g] = go[:, g * QLANES : (g + 1) * QLANES]

    for b in range(0, rows, LANES):
        both = go_scr[step, b : b + LANES].astype(F32) * o_ref[b : b + LANES].astype(F32)
        turned = jnp.transpose(both)
        for h in range(QUAD):
            dd_scr[h : h + 1, b : b + LANES] = jnp.sum(
                turned[h * HEAD : (h + 1) * HEAD], axis=0, keepdims=True
            )
    gk_scr[...] = jnp.zeros_like(gk_scr)
    gv_scr[...] = jnp.zeros_like(gv_scr)

    def block(r0, size, first_key, chunks, width):
        masks = head_masks(size, QLANES)
        q = q_ref[pl.ds(r0, size), :]
        go = go_scr[step, pl.ds(r0, size), :]
        for h in range(QUAD):
            qm_scr[h * size : (h + 1) * size] = jnp.where(masks[h], q, BF16(0))
            gm_scr[h * size : (h + 1) * size] = jnp.where(masks[h], go, BF16(0))
        key_masks = head_masks(width, QLANES)
        gq_scr[pl.ds(r0, size), :] = jnp.zeros((size, QLANES), F32)

        def chunk(c, carry):
            k0 = pl.multiple_of(first_key + c * width, LANES)
            keys = k_ref[pl.ds(k0, width), :]
            values = v_ref[pl.ds(k0, width), :]
            bias = bias_scr[pl.ds(k0, width), pl.ds(r0, size)]
            probs = []
            grads = []
            masked = []
            for h in range(QUAD):
                s = dot_t(keys, qm_scr[h * size : (h + 1) * size]) + bias
                p = jnp.exp(s - lse_ref[0, h : h + 1, pl.ds(r0, size)])
                gp = dot_t(values, gm_scr[h * size : (h + 1) * size])
                gs = p * (gp - dd_scr[h : h + 1, pl.ds(r0, size)])
                probs.append(p.astype(BF16))
                grads.append(gs.astype(BF16))
                masked.append(jnp.where(key_masks[h], keys, BF16(0)))
            prob = jnp.concatenate(probs, axis=1)
            grad = jnp.concatenate(grads, axis=1)
            gv_scr[pl.ds(k0, width), :] += dot(prob, gm_scr[: QUAD * size])
            gk_scr[pl.ds(k0, width), :] += dot(grad, qm_scr[: QUAD * size])
            gq_scr[pl.ds(r0, size), :] += t_dot(
                jnp.concatenate(grads, axis=0), jnp.concatenate(masked, axis=0)
            )
            return carry

        if isinstance(chunks, int):
            for c in range(chunks):
                chunk(c, 0)
        else:
            lax.fori_loop(0, chunks, chunk, 0)

    for b, (first_key, chunks) in enumerate(windows(lengths_ref, ptok)):
        block(b * RB, RB, first_key, chunks, CB)
    block(ptok, qtok, ptok, 1, qtok)

    x = x_scr[...]
    grad_q = (gq_scr[...] * (HEAD**-0.5)).astype(BF16)
    grad_k = gk_scr[...].astype(BF16)
    grad_v = gv_scr[...].astype(BF16)
    dbq_ref[...] = jnp.sum(grad_q.astype(F32), axis=0, keepdims=True)
    dbv_ref[...] = jnp.sum(grad_v.astype(F32), axis=0, keepdims=True)
    dwq_ref[...] = t_dot(x, grad_q).astype(BF16)
    dwk_ref[...] = t_dot(x, grad_k).astype(BF16)
    dwv_ref[...] = t_dot(x, grad_v).astype(BF16)
    gin_scr[...] += dot_t(grad_q, wq_ref[...]) + dot_t(grad_k, wk_ref[...]) + dot_t(grad_v, wv_ref[...])

    @pl.when(step == pl.num_programs(0) - 1)
    def _():
        gp_ref[...] = gin_scr[:ptok].astype(BF16)
        gq_ref[...] = gin_scr[ptok:].astype(BF16)


def attention_backward(lengths, gh1, r1, g1, wo, o, xp, xq, q, k, v, lse, wq, wk, wv):
    ptok, width = xp.shape
    qtok = xq.shape[0]
    rows = ptok + qtok
    quads = HEADS // QUAD
    cols = lambda size: spec((size, QLANES), lambda g: (0, g))
    fixed = lambda shape: spec(shape, lambda g: (0,) * len(shape))
    return pl.pallas_call(
        functools.partial(attention_backward_kernel, ptok),
        grid=(quads,),
        in_specs=[
            smem(),
            whole(gh1),
            whole(r1),
            whole(g1),
            whole(wo),
            whole(o),
            whole(xp),
            whole(xq),
            cols(rows),
            cols(rows),
            cols(rows),
            cols(rows),
            spec((1, 8, rows), lambda g: (g, 0, 0)),
            cols(width),
            cols(width),
            cols(width),
        ],
        out_specs=[
            fixed((8, width)),
            fixed((width, width)),
            cols(width),
            cols(width),
            cols(width),
            cols(1),
            cols(1),
            fixed((ptok, width)),
            fixed((qtok, width)),
        ],
        out_shape=[
            shaped((8, width), F32),
            shaped((width, width), BF16),
            shaped((width, width), BF16),
            shaped((width, width), BF16),
            shaped((width, width), BF16),
            shaped((1, width), F32),
            shaped((1, width), F32),
            shaped((ptok, width), BF16),
            shaped((qtok, width), BF16),
        ],
        scratch_shapes=[
            pltpu.VMEM((rows, width), BF16),
            pltpu.VMEM((rows, rows), F32),
            pltpu.VMEM((quads, rows, QLANES), BF16),
            pltpu.VMEM((rows, width), F32),
            pltpu.VMEM((8, rows), F32),
            pltpu.VMEM((rows, QLANES), F32),
            pltpu.VMEM((rows, QLANES), F32),
            pltpu.VMEM((rows, QLANES), F32),
            pltpu.VMEM((QUAD * RB, QLANES), BF16),
            pltpu.VMEM((QUAD * RB, QLANES), BF16),
        ],
        compiler_params=params(1),
        name="attention_backward",
    )(lengths, gh1, r1, g1, wo, o, xp, xq, q, k, v, o, lse, wq, wk, wv)


def shift_gather(block, axis_name, axis_size):
    found = [block]
    for distance in range(1, axis_size):
        ring = [(i, (i - distance) % axis_size) for i in range(axis_size)]
        found.append(lax.ppermute(block, axis_name, ring))
    return found


def halve(total, axis_name, size, bit):
    side = (lax.axis_index(axis_name) // bit) % 2
    half = total.shape[0] // 2
    swap = [(i, i ^ bit) for i in range(size)]
    away = lax.dynamic_slice_in_dim(total, (1 - side) * half, half, 0).astype(BF16)
    kept = lax.dynamic_slice_in_dim(total, side * half, half, 0)
    return kept.astype(F32) + lax.ppermute(away, axis_name, swap).astype(F32)


def double(piece, axis_name, size, bit):
    side = (lax.axis_index(axis_name) // bit) % 2
    swap = [(i, i ^ bit) for i in range(size)]
    other = lax.ppermute(piece, axis_name, swap)
    return jnp.where(side == 0, jnp.concatenate([piece, other]), jnp.concatenate([other, piece]))


def sum_over(total, steps):
    scattered = []
    for axis_name, size, bit in steps:
        if total.shape[0] % 2:
            swap = [(i, i ^ bit) for i in range(size)]
            total = total + lax.ppermute(total, axis_name, swap)
        else:
            total = halve(total, axis_name, size, bit)
            scattered.append((axis_name, size, bit))
    piece = total.astype(BF16)
    for axis_name, size, bit in reversed(scattered):
        piece = double(piece, axis_name, size, bit)
    return piece.astype(F32)


def bits_of(axis_name, size):
    steps = []
    bit = 1
    while bit < size:
        steps.append((axis_name, size, bit))
        bit *= 2
    return steps


def all_sum(total, grp_size, psg_size):
    inner = bits_of("grp", grp_size)
    outer = bits_of("psg", psg_size)
    half = total.shape[0] // 2
    first = sum_over(total[:half], inner + outer)
    second = sum_over(total[half:], inner[:1] + inner[:0:-1] + outer)
    return jnp.concatenate([first, second])


def local(
    grp_size,
    psg_size,
    passages,
    queries,
    lengths,
    positives,
    query_weight,
    query_bias,
    key_weight,
    value_weight,
    value_bias,
    output_weight,
    output_bias,
    first_gain,
    first_shift,
    inner_weight,
    inner_bias,
    outer_weight,
    outer_bias,
    second_gain,
    second_shift,
    project_weight,
):
    ptok, width = passages.shape
    qtok = queries.shape[0]
    rows = ptok + qtok
    row = lambda vector: vector.reshape(1, -1)
    g1, s1, g2, s2 = row(first_gain), row(first_shift), row(second_gain), row(second_shift)
    q, k, v, o, lse, r1 = attention_forward(
        lengths,
        passages,
        queries,
        query_weight,
        row(query_bias),
        key_weight,
        value_weight,
        row(value_bias),
        output_weight,
        row(output_bias),
    )
    layer = (r1, g1, s1, inner_weight, row(inner_bias), outer_weight, row(outer_bias), g2, s2, project_weight)
    *held, query_embed = ffn_forward(qtok, ptok, rows, *layer, ())
    groups = shift_gather(query_embed, "psg", psg_size)
    u, d, r2, e, pass_embed = ffn_forward(ptok, 0, rows, *layer, held)
    own_scores, pooled = score(lengths, pass_embed, groups)
    scores = shift_gather(own_scores, "psg", psg_size)
    position = lax.axis_index("psg").astype(jnp.int32).reshape(1)
    loss_rows, own, *rest = loss_and_grads(
        position, lengths, positives, pooled, pass_embed, groups, scores
    )
    aways = []
    for distance, part in enumerate(rest[:-1], 1):
        ring = [(i, (i + distance) % psg_size) for i in range(psg_size)]
        aways.append(lax.ppermute(part, "psg", ring))
    gr2p, vec, proj = passage_head(rest[-1], e, r2, project_weight, g2, s2)
    dproj, vec2, dbi, dwo, dwi, gh1 = ffn_backward(
        gr2p, vec, proj, own, aways, e, r2, project_weight, g2, s2, r1, g1, s1, inner_weight, outer_weight, u, d
    )
    vec1, dout, dwq, dwk, dwv, dbq, dbv, grad_p, grad_q = attention_backward(
        lengths, gh1, r1, g1, output_weight, o, passages, queries, q, k, v, lse, query_weight, key_weight, value_weight
    )
    big = jnp.concatenate([dwo, dwi.reshape(-1, width), dproj.reshape(-1, width)])
    vectors = jnp.concatenate([dbq, dbv, vec1[2:3], vec1[:2], vec2, dbi.reshape(-1, width)]).astype(BF16)
    pad = (-vectors.shape[0]) % 64
    vectors = jnp.concatenate([vectors, jnp.zeros((pad, width), BF16)])
    small = jnp.concatenate([dwq, dwk, dwv, dout, vectors])
    big_total = all_sum(big, grp_size, psg_size)
    small_total = all_sum(small, grp_size, psg_size)
    ff = inner_weight.shape[1]
    dwq, dwk, dwv, dout = [small_total[i * width : (i + 1) * width] for i in range(4)]
    lines = small_total[4 * width :]
    return (
        pass_embed,
        query_embed,
        loss_rows[:, 0],
        grad_p,
        grad_q,
        dwq,
        lines[0],
        dwk,
        dwv,
        lines[1],
        dout,
        lines[2],
        lines[3],
        lines[4],
        big_total[ff : 2 * ff].reshape(width, ff),
        lines[13 : 13 + ff // width].reshape(-1),
        big_total[:ff],
        lines[7],
        lines[5],
        lines[6],
        big_total[2 * ff :].reshape(project_weight.shape),
    )


def solution(mesh):
    split = P(("grp", "psg"), None)
    in_specs = (split, split, split, P("grp")) + (P(),) * 16
    out_specs = (split, split, P("grp"), split, split) + (P(),) * 16
    body = functools.partial(local, mesh.shape["grp"], mesh.shape["psg"])
    return jax.shard_map(body, mesh=mesh, in_specs=in_specs, out_specs=out_specs, check_vma=False)
```

```python
import functools

import jax
import jax.numpy as jnp
from jax import lax
from jax.experimental import pallas as pl
from jax.experimental.pallas import tpu as pltpu
from jax.sharding import PartitionSpec as P

HEADS = 8
HEAD = 64
QLEN = 32

SHARPNESS = 10.0
SCORE_SCALE = 0.25
NORM_EPS = 1e-06
EMBED_EPS = 1e-06
NEG_FILL = -1e30

F32 = jnp.float32
BF16 = jnp.bfloat16

TAIL_RATE = 0.31
TAIL = (
    7.983606475521152e-07,
    0.1236395104756606,
    0.1242090884595448,
    0.10710904223979588,
    0.11180972726115022,
    -0.017506651471085752,
    0.15741012515832603,
    -0.14274382211708148,
    0.036072242976455976,
)
INV_SQRT_2PI = 0.3989422804014327

QUAD = 4
QLANES = QUAD * HEAD
RB = 256
CB = 256
LANES = 128
FCHUNK = 512
SLICE = 16
ASLICE = 32
PIECE = 16
VMEM_LIMIT = 56 * 1024 * 1024


def dot(left, right):
    return jnp.dot(left, right, preferred_element_type=F32)


def dot_t(left, right):
    return lax.dot_general(left, right, (((1,), (1,)), ((), ())), preferred_element_type=F32)


def t_dot(left, right):
    return lax.dot_general(left, right, (((0,), (0,)), ((), ())), preferred_element_type=F32)


def two_part_dot(left, right_low):
    high = left.astype(BF16)
    rest = (left - high.astype(F32)).astype(BF16)
    return dot(high, right_low) + dot(rest, right_low)


def norm_stats(x):
    center = x - jnp.mean(x, axis=-1, keepdims=True)
    rate = lax.rsqrt(jnp.mean(center * center, axis=-1, keepdims=True) + NORM_EPS)
    return center * rate, rate


def norm_backward(grad, scaled, rate, gain):
    inner = grad * gain
    mean_in = jnp.mean(inner, axis=-1, keepdims=True)
    mean_dot = jnp.mean(inner * scaled, axis=-1, keepdims=True)
    grad_x = rate * (inner - mean_in - scaled * mean_dot)
    return grad_x, jnp.sum(grad * scaled, axis=0, keepdims=True), jnp.sum(grad, axis=0, keepdims=True)


def unit_backward(grad, projected):
    rate = lax.rsqrt(jnp.sum(projected * projected, axis=-1, keepdims=True) + EMBED_EPS)
    unit = projected * rate
    return rate * (grad - unit * jnp.sum(grad * unit, axis=-1, keepdims=True))


def gelu_pair(f):
    u = jnp.abs(f)
    t = 1.0 / (1.0 + TAIL_RATE * u)
    e = jnp.exp(-0.5 * (f * f))
    poly = TAIL[-1]
    for coefficient in TAIL[-2::-1]:
        poly = poly * t + coefficient
    tail = e * poly
    phi = jnp.where(f < 0.0, tail, 1.0 - tail)
    return f * phi, phi + f * (e * INV_SQRT_2PI)


def segment_ends(lengths_ref):
    count = lengths_ref.shape[1]
    ends = []
    total = jnp.int32(0)
    for s in range(count):
        total = total + lengths_ref[0, s]
        ends.append(total)
    return ends


def fill_bias(bias_ref, lengths_ref, ptok, rows):
    ends = segment_ends(lengths_ref)
    count = len(ends)

    def segments(token):
        seg = jnp.zeros_like(token)
        for end in ends:
            seg = seg + jnp.where(token >= end, 1, 0)
        return jnp.where(token >= ptok, count + (token - ptok) // QLEN, seg)

    row_seg = segments(lax.broadcasted_iota(jnp.int32, (8, rows), 1))[:1]

    def fill(b, carry):
        r0 = pl.multiple_of(b * LANES, LANES)
        col = segments(lax.broadcasted_iota(jnp.int32, (LANES, LANES), 0) + r0)
        for c in range(rows // LANES):
            part = row_seg[:, c * LANES : (c + 1) * LANES]
            bias_ref[pl.ds(r0, LANES), c * LANES : (c + 1) * LANES] = jnp.where(col == part, 0.0, NEG_FILL)
        return carry

    lax.fori_loop(0, rows // LANES, fill, 0)


def windows(lengths_ref, ptok):
    ends = segment_ends(lengths_ref)
    found = []
    for b in range(ptok // RB):
        first = b * RB
        last = first + RB - 1
        low = jnp.int32(0)
        high = jnp.int32(ptok)
        for end in ends:
            low = jnp.where(end <= first, jnp.maximum(low, end), low)
            high = jnp.where(end > last, jnp.minimum(high, end), high)
        start = (low // LANES) * LANES
        found.append((start, (high - start + CB - 1) // CB))
    return found


def head_masks(rows, lanes):
    lane = lax.broadcasted_iota(jnp.int32, (rows, lanes), 1) // HEAD
    return [lane == h for h in range(lanes // HEAD)]


def attention_forward_kernel(
    ptok,
    lengths_ref,
    xp_ref,
    xq_ref,
    wq_ref,
    bq_ref,
    wk_ref,
    wv_ref,
    bv_ref,
    wo_ref,
    bo_ref,
    q_ref,
    k_ref,
    v_ref,
    o_ref,
    lse_ref,
    x1_ref,
    rate1_ref,
    xt_ref,
    r1_ref,
    x_scr,
    bias_scr,
    s_scr,
    mx_scr,
    l_scr,
    acc_scr,
    qm_scr,
    e_scr,
):
    step = pl.program_id(0)
    rows = x_scr.shape[0]
    qtok = rows - ptok

    @pl.when(step == 0)
    def _():
        x_scr[:ptok] = xp_ref[...]
        x_scr[ptok:] = xq_ref[...]
        r1_ref[...] = x_scr[...].astype(F32) + bo_ref[...]
        fill_bias(bias_scr, lengths_ref, ptok, rows)

    x = x_scr[...]
    q_ref[...] = (dot(x, wq_ref[...]) + bq_ref[...]).astype(BF16) * BF16(HEAD**-0.5)
    k_ref[...] = dot(x, wk_ref[...]).astype(BF16)
    v_ref[...] = (dot(x, wv_ref[...]) + bv_ref[...]).astype(BF16)
    lse_ref[...] = jnp.zeros_like(lse_ref)

    def block(r0, size, first_key, chunks, width):
        masks = head_masks(size, QLANES)
        q = q_ref[pl.ds(r0, size), :]
        for h in range(QUAD):
            qm_scr[h, :size] = jnp.where(masks[h], q, BF16(0))
        mx_scr[:, :size] = jnp.full((QUAD, size, LANES), -jnp.inf, F32)
        l_scr[:, :size] = jnp.zeros((QUAD, size, LANES), F32)
        acc_scr[:, :size] = jnp.zeros((QUAD, size, LANES), F32)

        def score(c, carry):
            k0 = pl.multiple_of(first_key + c * width, LANES)
            keys = k_ref[pl.ds(k0, width), :]
            for h in range(QUAD):
                product = dot_t(qm_scr[h, :size], keys)
                for i in range(0, size, ASLICE):
                    s = product[i : i + ASLICE] + bias_scr[pl.ds(r0 + i, ASLICE), pl.ds(k0, width)]
                    s_scr[h, c, i : i + ASLICE, :width] = s
                    peak = mx_scr[h, i : i + ASLICE]
                    for part in range(width // LANES):
                        peak = jnp.maximum(peak, s[:, part * LANES : (part + 1) * LANES])
                    mx_scr[h, i : i + ASLICE] = peak
            return carry

        if isinstance(chunks, int):
            for c in range(chunks):
                score(c, 0)
        else:
            lax.fori_loop(0, chunks, score, 0)
        for h in range(QUAD):
            peak = jnp.max(mx_scr[h, :size], axis=-1, keepdims=True)
            mx_scr[h, :size] = jnp.broadcast_to(peak, (size, LANES))

        def mix(c, carry):
            k0 = pl.multiple_of(first_key + c * width, LANES)
            for h in range(QUAD):
                for i in range(0, size, ASLICE):
                    peak = mx_scr[h, i : i + ASLICE]
                    total = l_scr[h, i : i + ASLICE]
                    for part in range(0, width, LANES):
                        e = jnp.exp(s_scr[h, c, i : i + ASLICE, part : part + LANES] - peak)
                        total = total + e
                        e_scr[h, i : i + ASLICE, part : part + LANES] = e.astype(BF16)
                    l_scr[h, i : i + ASLICE] = total
                lanes = (h // 2) * LANES
                acc_scr[h, :size] += dot(
                    e_scr[h, :size, :width], v_ref[pl.ds(k0, width), lanes : lanes + LANES]
                )
            return carry

        if isinstance(chunks, int):
            for c in range(chunks):
                mix(c, 0)
        else:
            lax.fori_loop(0, chunks, mix, 0)
        lane = lax.broadcasted_iota(jnp.int32, (size, LANES), 1)
        logs = jnp.zeros((size, LANES), F32)
        mixed = []
        for h in range(QUAD):
            total = jnp.sum(l_scr[h, :size], axis=-1, keepdims=True)
            mixed.append(acc_scr[h, :size] * (1.0 / total))
            logs = jnp.where(lane == h, mx_scr[h, :size] + jnp.log(total), logs)
        for pair in range(QUAD // 2):
            both = jnp.where(lane < HEAD, mixed[2 * pair], mixed[2 * pair + 1])
            o_ref[pl.ds(r0, size), pair * LANES : (pair + 1) * LANES] = both.astype(BF16)
        lse_ref[0, :, pl.ds(r0, size)] = jnp.transpose(logs)[:8]

    for b, (first_key, chunks) in enumerate(windows(lengths_ref, ptok)):
        block(b * RB, RB, first_key, chunks, CB)
    block(ptok, qtok, ptok, 1, qtok)
    r1_ref[...] += dot(o_ref[...], wo_ref[...])

    @pl.when(step == pl.num_programs(0) - 1)
    def _():
        scaled, rate = norm_stats(r1_ref[...])
        x1_ref[...] = scaled
        rate1_ref[...] = jnp.broadcast_to(rate, rate1_ref.shape)
        xt_ref[...] = jnp.transpose(x_scr[...])


def pieces(me_ref, half, q):
    core, x, y, z = me_ref[0] ^ half, me_ref[1], me_ref[2], me_ref[3] ^ (q & 3)
    first, second = (q >> 3) & 1, (q >> 2) & 1
    left = (((y ^ second) * 2 + (x ^ first)) * 2 + core) * 4 + z
    right = (((y ^ first) * 2 + (x ^ second)) * 2 + core) * 4 + z
    return pl.multiple_of(left * PIECE, PIECE), pl.multiple_of(right * PIECE, PIECE)


def pack(me_ref, wave_ref, keep_ref, send_ref):
    middle = wave_ref.shape[1] // 2
    for half, ref in ((0, keep_ref), (1, send_ref)):
        for q in range(16):
            left, right = pieces(me_ref, half, q)
            rows = slice(q * PIECE, (q + 1) * PIECE)
            ref[rows, :middle] = wave_ref[pl.ds(left, PIECE), :middle]
            ref[rows, middle:] = wave_ref[pl.ds(right, PIECE), middle:]


def unpack(me_ref, kept_ref, other_ref, wave_ref):
    middle = wave_ref.shape[1] // 2
    for half, ref in ((0, kept_ref), (1, other_ref)):
        for q in range(16):
            left, right = pieces(me_ref, half, q)
            rows = slice(q * PIECE, (q + 1) * PIECE)
            wave_ref[pl.ds(left, PIECE), :middle] = ref[rows, :middle]
            wave_ref[pl.ds(right, PIECE), middle:] = ref[rows, middle:]


def spec(shape, index):
    return pl.BlockSpec(shape, index)


def whole(array):
    nd = len(array.shape)
    return pl.BlockSpec(array.shape, lambda *_: (0,) * nd)


def smem():
    return pl.BlockSpec(memory_space=pltpu.SMEM)


def cost(micros):
    return pl.CostEstimate(flops=int(micros * 1e9), bytes_accessed=int(micros * 1e6), transcendentals=0)


def shaped(shape, dtype):
    return jax.ShapeDtypeStruct(shape, dtype)


def params(grid_rank):
    return pltpu.CompilerParams(
        dimension_semantics=("arbitrary",) * grid_rank, vmem_limit_bytes=VMEM_LIMIT
    )


def attention_forward(lengths, xp, xq, wq, bq, wk, wv, bv, wo, bo):
    ptok, width = xp.shape
    qtok = xq.shape[0]
    rows = ptok + qtok
    quads = HEADS // QUAD
    cols = lambda size: spec((size, QLANES), lambda g: (0, g))
    deepest = ptok // CB + 1
    return pl.pallas_call(
        functools.partial(attention_forward_kernel, ptok),
        grid=(quads,),
        in_specs=[
            smem(),
            whole(xp),
            whole(xq),
            cols(width),
            cols(1),
            cols(width),
            cols(width),
            cols(1),
            spec((QLANES, width), lambda g: (g, 0)),
            whole(bo),
        ],
        out_specs=[
            cols(rows),
            cols(rows),
            cols(rows),
            cols(rows),
            spec((1, 8, rows), lambda g: (g, 0, 0)),
            spec((rows, width), lambda g: (0, 0)),
            spec((rows, LANES), lambda g: (0, 0)),
            spec((width, rows), lambda g: (0, 0)),
        ],
        out_shape=[shaped((rows, width), BF16)] * 4
        + [
            shaped((quads, 8, rows), F32),
            shaped((rows, width), F32),
            shaped((rows, LANES), F32),
            shaped((width, rows), BF16),
        ],
        scratch_shapes=[
            pltpu.VMEM((rows, width), F32),
            pltpu.VMEM((rows, width), BF16),
            pltpu.VMEM((rows, rows), F32),
            pltpu.VMEM((QUAD, deepest, RB, CB), F32),
            pltpu.VMEM((QUAD, RB, LANES), F32),
            pltpu.VMEM((QUAD, RB, LANES), F32),
            pltpu.VMEM((QUAD, RB, LANES), F32),
            pltpu.VMEM((QUAD, RB, QLANES), BF16),
            pltpu.VMEM((QUAD, RB, CB), BF16),
        ],
        compiler_params=params(1),
        cost_estimate=cost(20),
        name="attention_forward",
    )(lengths, xp, xq, wq, bq, wk, wv, bv, wo, bo)


def ffn_forward_kernel(
    aliased,
    rb,
    x1_ref,
    g1_ref,
    s1_ref,
    wi_ref,
    bi_ref,
    wo_ref,
    bo_ref,
    g2_ref,
    s2_ref,
    wp_ref,
    *rest,
):
    rest = rest[aliased:]
    ut_ref, d_ref, x2_ref, rate2_ref, e_ref, emb_ref, h1_scr, r2_scr, u_scr = rest
    step = pl.program_id(0)
    rows = x1_ref.shape[0]

    @pl.when(step == 0)
    def _():
        h1 = x1_ref[...] * g1_ref[...] + s1_ref[...]
        h1_scr[...] = h1.astype(BF16)
        r2_scr[...] = h1 + bo_ref[...]

    for r in range(0, rows, rb):
        f = dot(h1_scr[r : r + rb], wi_ref[...])
        bias = bi_ref[...]
        for i in range(0, rb, SLICE):
            u, d = gelu_pair(f[i : i + SLICE] + bias)
            u_scr[r + i : r + i + SLICE] = u.astype(BF16)
            d_ref[r + i : r + i + SLICE] = d.astype(BF16)
        ut_ref[:, r : r + rb] = jnp.transpose(u_scr[r : r + rb])
        r2_scr[r : r + rb] += dot(u_scr[r : r + rb], wo_ref[...])

    @pl.when(step == pl.num_programs(0) - 1)
    def _():
        scaled, rate = norm_stats(r2_scr[...])
        x2_ref[...] = scaled
        rate2_ref[...] = jnp.broadcast_to(rate, rate2_ref.shape)
        h2 = (scaled * g2_ref[...] + s2_ref[...]).astype(BF16)
        e = dot(h2, wp_ref[...])
        e_ref[...] = e
        size = jnp.sum(e * e, axis=-1, keepdims=True)
        emb_ref[...] = (e * lax.rsqrt(size + EMBED_EPS)).astype(BF16)


def ffn_forward(count, offset, total, x1, g1, s1, wi, bi, wo, bo, g2, s2, wp, previous):
    width = x1.shape[1]
    ff = wi.shape[1]
    dim = wp.shape[1]
    at = offset // count
    first = 10
    held = list(previous)
    return pl.pallas_call(
        functools.partial(ffn_forward_kernel, len(held), min(RB, count)),
        grid=(ff // FCHUNK,),
        in_specs=[
            spec((count, width), lambda c: (at, 0)),
            whole(g1),
            whole(s1),
            spec((width, FCHUNK), lambda c: (0, c)),
            spec((1, FCHUNK), lambda c: (0, c)),
            spec((FCHUNK, width), lambda c: (c, 0)),
            whole(bo),
            whole(g2),
            whole(s2),
            whole(wp),
        ]
        + [pl.BlockSpec(memory_space=pl.ANY)] * len(held),
        out_specs=[
            spec((FCHUNK, count), lambda c: (c, at)),
            spec((count, FCHUNK), lambda c: (at, c)),
            spec((count, width), lambda c: (at, 0)),
            spec((count, LANES), lambda c: (at, 0)),
            spec((count, dim), lambda c: (at, 0)),
            spec((count, dim), lambda c: (0, 0)),
        ],
        out_shape=[
            shaped((ff, total), BF16),
            shaped((total, ff), BF16),
            shaped((total, width), F32),
            shaped((total, LANES), F32),
            shaped((total, dim), F32),
            shaped((count, dim), BF16),
        ],
        scratch_shapes=[
            pltpu.VMEM((count, width), BF16),
            pltpu.VMEM((count, width), F32),
            pltpu.VMEM((count, FCHUNK), BF16),
        ],
        input_output_aliases={first + i: i for i in range(len(held))},
        compiler_params=params(1),
        cost_estimate=cost(12 if count > 256 else 4),
        name="ffn_forward",
    )(x1, g1, s1, wi, bi, wo, bo, g2, s2, wp, *held)


def passage_member(lengths_ref, rows):
    ends = segment_ends(lengths_ref)
    lane = lax.broadcasted_iota(jnp.int32, (8, LANES), 1)
    low = jnp.full((8, LANES), rows, jnp.int32)
    high = jnp.zeros((8, LANES), jnp.int32)
    start = jnp.int32(0)
    for s, end in enumerate(ends):
        low = jnp.where(lane == s, start, low)
        high = jnp.where(lane == s, end, high)
        start = end
    token = lax.broadcasted_iota(jnp.int32, (rows, LANES), 0)
    inside = (token >= low[:1]) & (token < high[:1])
    return jnp.where(inside, 1.0, 0.0).astype(BF16)


def soft_match(group, pass_embed):
    return jnp.exp(SHARPNESS * dot_t(group, pass_embed) - SHARPNESS)


def score_kernel(psg, count, lengths_ref, emb_ref, *rest):
    group_refs = rest[:psg]
    score_ref, pooled_ref = rest[psg:]
    member = passage_member(lengths_ref, emb_ref.shape[0])
    group = jnp.concatenate([ref[...] for ref in group_refs], axis=0)
    matched = soft_match(group, emb_ref[...])
    pooled = two_part_dot(matched, member)
    lane = lax.broadcasted_iota(jnp.int32, pooled.shape, 1)
    pooled = jnp.where(lane < count, pooled, 1.0)
    pooled_ref[...] = pooled
    smooth = 1.0 + jnp.log(pooled) * (1.0 / SHARPNESS)
    queries = pooled.shape[0] // QLEN
    score_ref[...] = SCORE_SCALE * jnp.sum(smooth.reshape(queries, QLEN, LANES), axis=1)


def score(lengths, emb, groups):
    psg = len(groups)
    tokens = sum(g.shape[0] for g in groups)
    return pl.pallas_call(
        functools.partial(score_kernel, psg, lengths.shape[1]),
        in_specs=[smem()] + [pl.BlockSpec(memory_space=pltpu.VMEM)] * (1 + psg),
        out_shape=[shaped((tokens // QLEN, LANES), F32), shaped((tokens, LANES), F32)],
        compiler_params=pltpu.CompilerParams(vmem_limit_bytes=VMEM_LIMIT),
        cost_estimate=cost(3),
        name="score",
    )(lengths, emb, *groups)


def loss_kernel(psg, count, where_ref, lengths_ref, positives_ref, pooled_ref, emb_ref, *rest):
    group_refs = rest[:psg]
    score_refs = rest[psg : 2 * psg]
    loss_ref, own_ref = rest[2 * psg : 2 * psg + 2]
    away_refs = rest[2 * psg + 2 : 3 * psg + 1]
    grad_ref = rest[3 * psg + 1]
    position = where_ref[0]
    queries = score_refs[0].shape[0]
    each = queries // psg
    lane = lax.broadcasted_iota(jnp.int32, (queries, LANES), 1)
    row = lax.broadcasted_iota(jnp.int32, (queries, LANES), 0)
    valid = lane < count
    blocks = []
    for e in range(psg):
        found = score_refs[e][...]
        found = jnp.concatenate(
            [found[((d - e) % psg) * each : ((d - e) % psg + 1) * each] for d in range(psg)], axis=0
        )
        blocks.append(jnp.where(valid, found, -jnp.inf))
    target = jnp.zeros((queries, LANES), jnp.int32)
    for d in range(psg):
        for j in range(each):
            chosen = positives_ref[lax.rem(position + d, psg) * each + j]
            target = jnp.where(row == d * each + j, chosen, target)
    peak = blocks[0]
    for found in blocks[1:]:
        peak = jnp.maximum(peak, found)
    peak = jnp.max(peak, axis=-1, keepdims=True)
    total = jnp.zeros((queries, 1), F32)
    picked = jnp.zeros((queries, 1), F32)
    for e in range(psg):
        owner = lax.rem(position + e, psg)
        hit = (target == owner * count + lane) & valid
        total = total + jnp.sum(jnp.exp(blocks[e] - peak), axis=-1, keepdims=True)
        picked = picked + jnp.sum(jnp.where(hit, blocks[e], 0.0), axis=-1, keepdims=True)
        if e == 0:
            own_hit = jnp.where(hit, 1.0, 0.0)
    log_total = peak + jnp.log(total)
    losses = jnp.broadcast_to(log_total - picked, (queries, LANES))
    place = lax.rem(position + row // each, psg) * each + row % each
    losses = jnp.sum(jnp.where(lane == place, losses, 0.0), axis=0, keepdims=True)
    loss_ref[...] = losses[:, :queries]
    grad = jnp.where(valid, jnp.exp(blocks[0] - log_total) - own_hit, 0.0) * SCORE_SCALE
    tokens = queries * QLEN
    grad = jnp.broadcast_to(grad[:, None, :], (queries, QLEN, LANES)).reshape(tokens, LANES)
    grad = grad / pooled_ref[...]
    member = passage_member(lengths_ref, emb_ref.shape[0])
    high = grad.astype(BF16)
    rest_low = (grad - high.astype(F32)).astype(BF16)
    spread = dot_t(high, member) + dot_t(rest_low, member)
    group = jnp.concatenate([ref[...] for ref in group_refs], axis=0)
    low = (soft_match(group, emb_ref[...]) * spread).astype(BF16)
    group_grad = dot(low, emb_ref[...])
    each_tokens = tokens // psg
    own_ref[...] = group_grad[:each_tokens]
    for d in range(1, psg):
        away_refs[d - 1][...] = group_grad[d * each_tokens : (d + 1) * each_tokens].astype(BF16)
    grad_ref[...] = jnp.transpose(dot(jnp.transpose(group), low))


def loss_and_grads(position, lengths, positives, pooled, emb, groups, scores):
    psg = len(groups)
    queries = scores[0].shape[0]
    tokens, dim = groups[0].shape
    vmem = pl.BlockSpec(memory_space=pltpu.VMEM)
    return pl.pallas_call(
        functools.partial(loss_kernel, psg, lengths.shape[1]),
        in_specs=[smem(), smem(), smem()] + [vmem] * (2 + 2 * psg),
        out_shape=[shaped((1, queries), F32), shaped((tokens, dim), F32)]
        + [shaped((tokens, dim), BF16)] * (psg - 1)
        + [shaped(emb.shape, F32)],
        compiler_params=pltpu.CompilerParams(vmem_limit_bytes=VMEM_LIMIT),
        cost_estimate=cost(3),
        name="loss_and_grads",
    )(position, lengths, positives, pooled, emb, *groups, *scores)


def head_backward(grad_embed, e, x2, rate2, wp, g2, s2):
    low = unit_backward(grad_embed, e).astype(BF16)
    grad_h2 = dot_t(low, wp)
    grad_r2, gain_term, shift_term = norm_backward(grad_h2, x2, rate2[:, :1], g2)
    h2 = (x2 * g2 + s2).astype(BF16)
    return grad_r2, gain_term, shift_term, dot(jnp.transpose(low), h2)


def passage_head_kernel(
    grad_ref, e_ref, x2_ref, rate2_ref, wp_ref, g2_ref, s2_ref, gr2_ref, vec_ref, proj_ref
):
    grad_r2, gain_term, shift_term, proj = head_backward(
        grad_ref[...], e_ref[...], x2_ref[...], rate2_ref[...], wp_ref[...], g2_ref[...], s2_ref[...]
    )
    gr2_ref[...] = grad_r2
    vec_ref[...] = jnp.zeros_like(vec_ref)
    vec_ref[0:1] = gain_term
    vec_ref[1:2] = shift_term
    proj_ref[...] = proj


def passage_head(grad, e, x2, rate2, wp, g2, s2):
    ptok, dim = grad.shape
    width = x2.shape[1]
    at = lambda shape: spec(shape, lambda i: (0, 0))
    return pl.pallas_call(
        passage_head_kernel,
        grid=(1,),
        in_specs=[
            whole(grad),
            at((ptok, dim)),
            at((ptok, width)),
            at((ptok, LANES)),
            whole(wp),
            whole(g2),
            whole(s2),
        ],
        out_specs=[at((ptok, width)), at((8, width)), at((dim, width))],
        out_shape=[shaped((ptok, width), F32), shaped((8, width), F32), shaped((dim, width), F32)],
        compiler_params=params(1),
        cost_estimate=cost(4),
        name="passage_head",
    )(grad, e, x2, rate2, wp, g2, s2)


def ffn_chunk(wi_ref, wo_ref, ut_ref, d_ref, gz, h1t, dbi_ref, gh1_ref, wave_ref, step):
    grad_active = dot_t(gz, wo_ref[...])
    grad_inner = (grad_active * d_ref[...].astype(F32)).astype(BF16)
    dbi_ref[...] = jnp.sum(grad_inner.astype(F32), axis=0, keepdims=True)
    gh1_ref[...] += dot_t(grad_inner, wi_ref[...])
    wave_ref[:, pl.ds(pl.multiple_of(step * FCHUNK, FCHUNK), FCHUNK)] = dot(h1t, grad_inner).astype(BF16)
    right = wave_ref.shape[1] // 2
    wave_ref[:, pl.ds(pl.multiple_of(right + step * FCHUNK, FCHUNK), FCHUNK)] = dot(ut_ref[...], gz).astype(BF16)


def ffn_backward_first_kernel(
    psg,
    me_ref,
    gr2p_ref,
    vec_ref,
    proj_ref,
    own_ref,
    *rest,
):
    away_refs = rest[: psg - 1]
    (
        e_ref,
        x2_ref,
        rate2_ref,
        wp_ref,
        g2_ref,
        s2_ref,
        x1_ref,
        g1_ref,
        s1_ref,
        wi_ref,
        wo_ref,
        ut_ref,
        d_ref,
        dproj_ref,
        dvec_ref,
        dbi_ref,
        gh1_ref,
        gz_ref,
        h1t_ref,
        keep_ref,
        send_ref,
        wave_scr,
    ) = rest[psg - 1 :]
    step = pl.program_id(0)
    ptok = gr2p_ref.shape[0]

    @pl.when(step == 0)
    def _():
        grad = own_ref[...]
        for ref in away_refs:
            grad = grad + ref[...].astype(F32)
        grad_r2, gain_term, shift_term, proj = head_backward(
            grad, e_ref[...], x2_ref[...], rate2_ref[...], wp_ref[...], g2_ref[...], s2_ref[...]
        )
        dproj_ref[...] = jnp.transpose(proj_ref[...] + proj).astype(BF16)
        gr2p = gr2p_ref[...]
        gh1_ref[:ptok] = gr2p
        gh1_ref[ptok:] = grad_r2
        low_p = gr2p.astype(BF16)
        low_q = grad_r2.astype(BF16)
        gz_ref[:ptok] = low_p
        gz_ref[ptok:] = low_q
        dvec_ref[...] = jnp.zeros_like(dvec_ref)
        dvec_ref[0:1] = vec_ref[0:1] + gain_term
        dvec_ref[1:2] = vec_ref[1:2] + shift_term
        dvec_ref[2:3] = jnp.sum(low_p.astype(F32), axis=0, keepdims=True) + jnp.sum(
            low_q.astype(F32), axis=0, keepdims=True
        )
        h1t_ref[...] = jnp.transpose((x1_ref[...] * g1_ref[...] + s1_ref[...]).astype(BF16))

    ffn_chunk(wi_ref, wo_ref, ut_ref, d_ref, gz_ref[...], h1t_ref[...], dbi_ref, gh1_ref, wave_scr, step)

    @pl.when(step == pl.num_programs(0) - 1)
    def _():
        pack(me_ref, wave_scr, keep_ref, send_ref)


def ffn_backward_second_kernel(
    me_ref, gz_ref, h1t_ref, held_ref, wi_ref, wo_ref, ut_ref, d_ref, dbi_ref, gh1_ref, keep_ref, send_ref, wave_scr
):
    step = pl.program_id(0)

    @pl.when(step == 0)
    def _():
        gh1_ref[...] = held_ref[...]

    ffn_chunk(wi_ref, wo_ref, ut_ref, d_ref, gz_ref[...], h1t_ref[...], dbi_ref, gh1_ref, wave_scr, step)

    @pl.when(step == pl.num_programs(0) - 1)
    def _():
        pack(me_ref, wave_scr, keep_ref, send_ref)


def ffn_specs(width, rows, offset):
    return [
        spec((width, FCHUNK), lambda c: (0, c + offset)),
        spec((FCHUNK, width), lambda c: (c + offset, 0)),
        spec((FCHUNK, rows), lambda c: (c + offset, 0)),
        spec((rows, FCHUNK), lambda c: (0, c + offset)),
    ]


def fixed(shape):
    return spec(shape, lambda *_: (0,) * len(shape))


def ffn_backward_first(me, gr2p, vec, proj, own, aways, e, x2, rate2, wp, g2, s2, x1, g1, s1, wi, wo, ut, d):
    ptok, width = gr2p.shape
    rows = x1.shape[0]
    qtok = rows - ptok
    dim = wp.shape[1]
    ff = wi.shape[1]
    at = ptok // qtok
    return pl.pallas_call(
        functools.partial(ffn_backward_first_kernel, 1 + len(aways)),
        grid=(ff // FCHUNK // 2,),
        in_specs=[smem(), whole(gr2p), whole(vec), whole(proj), whole(own)]
        + [whole(a) for a in aways]
        + [
            spec((qtok, dim), lambda c: (at, 0)),
            spec((qtok, width), lambda c: (at, 0)),
            spec((qtok, LANES), lambda c: (at, 0)),
            whole(wp),
            whole(g2),
            whole(s2),
            whole(x1),
            whole(g1),
            whole(s1),
        ]
        + ffn_specs(width, rows, 0),
        out_specs=[
            fixed((width, dim)),
            fixed((8, width)),
            spec((1, FCHUNK), lambda c: (0, c)),
            fixed((rows, width)),
            fixed((rows, width)),
            fixed((width, rows)),
            fixed((width // 2, ff)),
            fixed((width // 2, ff)),
        ],
        out_shape=[
            shaped((width, dim), BF16),
            shaped((8, width), F32),
            shaped((1, ff // 2), F32),
            shaped((rows, width), F32),
            shaped((rows, width), BF16),
            shaped((width, rows), BF16),
            shaped((width // 2, ff), BF16),
            shaped((width // 2, ff), BF16),
        ],
        scratch_shapes=[pltpu.VMEM((width, ff), BF16)],
        compiler_params=params(1),
        cost_estimate=cost(9),
        name="ffn_backward_first",
    )(me, gr2p, vec, proj, own, *aways, e, x2, rate2, wp, g2, s2, x1, g1, s1, wi, wo, ut, d)


def ffn_backward_second(me, gz, h1t, held, wi, wo, ut, d):
    rows, width = gz.shape
    ff = wi.shape[1]
    return pl.pallas_call(
        ffn_backward_second_kernel,
        grid=(ff // FCHUNK // 2,),
        in_specs=[smem(), whole(gz), whole(h1t), whole(held)] + ffn_specs(width, rows, ff // FCHUNK // 2),
        out_specs=[
            spec((1, FCHUNK), lambda c: (0, c)),
            fixed((rows, width)),
            fixed((width // 2, ff)),
            fixed((width // 2, ff)),
        ],
        out_shape=[
            shaped((1, ff // 2), F32),
            shaped((rows, width), F32),
            shaped((width // 2, ff), BF16),
            shaped((width // 2, ff), BF16),
        ],
        scratch_shapes=[pltpu.VMEM((width, ff), BF16)],
        compiler_params=params(1),
        cost_estimate=cost(8),
        name="ffn_backward_second",
    )(me, gz, h1t, held, wi, wo, ut, d)


def first_norm_kernel(gh1_ref, x1_ref, rate1_ref, g1_ref, wo_ref, o_ref, gr1_ref, go_ref, dout_ref, dvec_ref):
    grad_r1, gain_term, shift_term = norm_backward(gh1_ref[...], x1_ref[...], rate1_ref[:, :1], g1_ref[...])
    gr1_ref[...] = grad_r1
    low = grad_r1.astype(BF16)
    dvec_ref[...] = jnp.zeros_like(dvec_ref)
    dvec_ref[0:1] = gain_term
    dvec_ref[1:2] = shift_term
    dvec_ref[2:3] = jnp.sum(low.astype(F32), axis=0, keepdims=True)
    dout_ref[...] = t_dot(o_ref[...], low).astype(BF16)
    go_ref[...] = dot_t(low, wo_ref[...]).astype(BF16)


def first_norm(gh1, x1, rate1, g1, wo, o):
    rows, width = x1.shape
    return pl.pallas_call(
        first_norm_kernel,
        out_shape=[
            shaped((rows, width), F32),
            shaped((rows, width), BF16),
            shaped((width, width), BF16),
            shaped((8, width), F32),
        ],
        compiler_params=pltpu.CompilerParams(vmem_limit_bytes=VMEM_LIMIT),
        cost_estimate=cost(4),
        name="first_norm",
    )(gh1, x1, rate1, g1, wo, o)


def heads_backward_kernel(
    ptok,
    lengths_ref,
    go_ref,
    q_ref,
    k_ref,
    v_ref,
    o_ref,
    lse_ref,
    grads_ref,
    bias_scr,
    dd_scr,
    gqt_scr,
    gk_scr,
    gv_scr,
    qm_scr,
    gm_scr,
    p_scr,
    gs_scr,
    kt_scr,
):
    rows = q_ref.shape[0]
    qtok = rows - ptok
    fill_bias(bias_scr, lengths_ref, ptok, rows)

    for b in range(0, rows, LANES):
        both = go_ref[b : b + LANES].astype(F32) * o_ref[b : b + LANES].astype(F32)
        turned = jnp.transpose(both)
        for h in range(QUAD):
            dd_scr[h : h + 1, b : b + LANES] = jnp.sum(
                turned[h * HEAD : (h + 1) * HEAD], axis=0, keepdims=True
            )
    kt_scr[...] = jnp.transpose(k_ref[...])
    gk_scr[...] = jnp.zeros_like(gk_scr)
    gv_scr[...] = jnp.zeros_like(gv_scr)
    gqt_scr[...] = jnp.zeros_like(gqt_scr)

    def block(r0, size, first_key, chunks, width):
        masks = head_masks(size, QLANES)
        q = q_ref[pl.ds(r0, size), :]
        go = go_ref[pl.ds(r0, size), :]
        for h in range(QUAD):
            qm_scr[h * size : (h + 1) * size] = jnp.where(masks[h], q, BF16(0))
            gm_scr[h * size : (h + 1) * size] = jnp.where(masks[h], go, BF16(0))

        def chunk(c, carry):
            k0 = pl.multiple_of(first_key + c * width, LANES)
            keys = k_ref[pl.ds(k0, width), :]
            values = v_ref[pl.ds(k0, width), :]
            for h in range(QUAD):
                product = dot_t(keys, qm_scr[h * size : (h + 1) * size])
                grad_prob = dot_t(values, gm_scr[h * size : (h + 1) * size])
                lse = lse_ref[0, h : h + 1, pl.ds(r0, size)]
                dd = dd_scr[h : h + 1, pl.ds(r0, size)]
                for i in range(0, width, ASLICE):
                    s = product[i : i + ASLICE] + bias_scr[pl.ds(k0 + i, ASLICE), pl.ds(r0, size)]
                    p = jnp.exp(s - lse)
                    gs = p * (grad_prob[i : i + ASLICE] - dd)
                    p_scr[i : i + ASLICE, h * size : (h + 1) * size] = p.astype(BF16)
                    gs_scr[i : i + ASLICE, h * size : (h + 1) * size] = gs.astype(BF16)
            gv_scr[pl.ds(k0, width), :] += dot(p_scr[:width, : QUAD * size], gm_scr[: QUAD * size])
            gk_scr[pl.ds(k0, width), :] += dot(gs_scr[:width, : QUAD * size], qm_scr[: QUAD * size])
            for h in range(QUAD):
                gqt_scr[h * HEAD : (h + 1) * HEAD, pl.ds(r0, size)] += dot(
                    kt_scr[h * HEAD : (h + 1) * HEAD, pl.ds(k0, width)],
                    gs_scr[:width, h * size : (h + 1) * size],
                )
            return carry

        if isinstance(chunks, int):
            for c in range(chunks):
                chunk(c, 0)
        else:
            lax.fori_loop(0, chunks, chunk, 0)

    for b, (first_key, chunks) in enumerate(windows(lengths_ref, ptok)):
        block(b * RB, RB, first_key, chunks, CB)
    block(ptok, qtok, ptok, 1, qtok)
    grads_ref[:, :QLANES] = (jnp.transpose(gqt_scr[...]) * (HEAD**-0.5)).astype(BF16)
    grads_ref[:, QLANES : 2 * QLANES] = gk_scr[...].astype(BF16)
    grads_ref[:, 2 * QLANES :] = gv_scr[...].astype(BF16)


def heads_backward(quad, lengths, go, q, k, v, o, lse, ptok):
    rows, width = q.shape
    cols = lambda size: spec((size, QLANES), lambda i: (0, quad))
    return pl.pallas_call(
        functools.partial(heads_backward_kernel, ptok),
        grid=(1,),
        in_specs=[smem()]
        + [cols(rows)] * 5
        + [spec((1, 8, rows), lambda i: (quad, 0, 0))],
        out_specs=fixed((rows, 3 * QLANES)),
        out_shape=shaped((rows, 3 * QLANES), BF16),
        scratch_shapes=[
            pltpu.VMEM((rows, rows), F32),
            pltpu.VMEM((8, rows), F32),
            pltpu.VMEM((QLANES, rows), F32),
            pltpu.VMEM((rows, QLANES), F32),
            pltpu.VMEM((rows, QLANES), F32),
            pltpu.VMEM((QUAD * RB, QLANES), BF16),
            pltpu.VMEM((QUAD * RB, QLANES), BF16),
            pltpu.VMEM((CB, QUAD * RB), BF16),
            pltpu.VMEM((CB, QUAD * RB), BF16),
            pltpu.VMEM((QLANES, rows), BF16),
        ],
        compiler_params=params(1),
        cost_estimate=cost(14),
        name="heads_backward",
    )(lengths, go, q, k, v, o, lse)


def put_vector(wave_ref, row, column, vector):
    for i in range(vector.shape[1] // LANES):
        wave_ref[row + i : row + i + 1, column : column + LANES] = vector[
            :, i * LANES : (i + 1) * LANES
        ].astype(BF16)
    return row + vector.shape[1] // LANES


def take_vector(wave_ref, row, column, out_ref, start, size):
    for i in range(size // LANES):
        out_ref[:, start + i * LANES : start + (i + 1) * LANES] = wave_ref[
            row + i : row + i + 1, column : column + LANES
        ].astype(F32)
    return row + size // LANES


def weights_common(xt_ref, grads_ref, wq_ref, wk_ref, wv_ref, wave_scr):
    grads = grads_ref[...]
    wave_scr[:, : 3 * QLANES] = dot(xt_ref[...], grads).astype(BF16)
    total = dot_t(grads[:, :QLANES], wq_ref[...])
    total = total + dot_t(grads[:, QLANES : 2 * QLANES], wk_ref[...])
    total = total + dot_t(grads[:, 2 * QLANES :], wv_ref[...])
    bias_q = jnp.sum(grads[:, :QLANES].astype(F32), axis=0, keepdims=True)
    bias_v = jnp.sum(grads[:, 2 * QLANES :].astype(F32), axis=0, keepdims=True)
    return total, bias_q, bias_v


def weights_first_kernel(
    me_ref,
    xt_ref,
    grads_ref,
    wq_ref,
    wk_ref,
    wv_ref,
    gr1_ref,
    dout_ref,
    dproj_ref,
    vec1_ref,
    vec2_ref,
    dbi1_ref,
    dbi2_ref,
    gin_ref,
    keep_ref,
    send_ref,
    wave_scr,
):
    total, bias_q, bias_v = weights_common(xt_ref, grads_ref, wq_ref, wk_ref, wv_ref, wave_scr)
    gin_ref[...] = gr1_ref[...] + total
    column = 3 * QLANES
    for ref in (dout_ref, dproj_ref):
        wave_scr[:, column : column + ref.shape[1]] = ref[...]
        column += ref.shape[1]
    wave_scr[:, column:] = jnp.zeros((wave_scr.shape[0], LANES), BF16)
    row = 0
    for vector in (
        vec2_ref[0:1],
        vec2_ref[1:2],
        vec2_ref[2:3],
        vec1_ref[0:1],
        vec1_ref[1:2],
        vec1_ref[2:3],
        dbi1_ref[...],
        dbi2_ref[...],
        bias_q,
        bias_v,
    ):
        row = put_vector(wave_scr, row, column, vector)
    pack(me_ref, wave_scr, keep_ref, send_ref)


def weights_second_kernel(
    me_ref, xt_ref, grads_ref, wq_ref, wk_ref, wv_ref, held_ref, gp_ref, gq_ref, keep_ref, send_ref, wave_scr
):
    total, bias_q, bias_v = weights_common(xt_ref, grads_ref, wq_ref, wk_ref, wv_ref, wave_scr)
    ptok = gp_ref.shape[0]
    gp_ref[...] = (held_ref[:ptok] + total[:ptok]).astype(BF16)
    gq_ref[...] = (held_ref[ptok:] + total[ptok:]).astype(BF16)
    column = 3 * QLANES
    wave_scr[:, column:] = jnp.zeros((wave_scr.shape[0], LANES), BF16)
    row = put_vector(wave_scr, 0, column, bias_q)
    put_vector(wave_scr, row, column, bias_v)
    pack(me_ref, wave_scr, keep_ref, send_ref)


def weights_first(me, xt, grads, wq, wk, wv, gr1, dout, dproj, vec1, vec2, dbi1, dbi2):
    width, rows = xt.shape
    lanes = 3 * QLANES + dout.shape[1] + dproj.shape[1] + LANES
    cols = spec((width, QLANES), lambda i: (0, 0))
    return pl.pallas_call(
        weights_first_kernel,
        grid=(1,),
        in_specs=[smem(), whole(xt), whole(grads), cols, cols, cols]
        + [whole(a) for a in (gr1, dout, dproj, vec1, vec2, dbi1, dbi2)],
        out_specs=[fixed((rows, width)), fixed((width // 2, lanes)), fixed((width // 2, lanes))],
        out_shape=[
            shaped((rows, width), F32),
            shaped((width // 2, lanes), BF16),
            shaped((width // 2, lanes), BF16),
        ],
        scratch_shapes=[pltpu.VMEM((width, lanes), BF16)],
        compiler_params=params(1),
        cost_estimate=cost(4),
        name="weights_first",
    )(me, xt, grads, wq, wk, wv, gr1, dout, dproj, vec1, vec2, dbi1, dbi2)


def weights_second(me, xt, grads, wq, wk, wv, held, ptok):
    width, rows = xt.shape
    lanes = 3 * QLANES + LANES
    cols = spec((width, QLANES), lambda i: (0, 1))
    return pl.pallas_call(
        weights_second_kernel,
        grid=(1,),
        in_specs=[smem(), whole(xt), whole(grads), cols, cols, cols, whole(held)],
        out_specs=[
            fixed((ptok, width)),
            fixed((rows - ptok, width)),
            fixed((width // 2, lanes)),
            fixed((width // 2, lanes)),
        ],
        out_shape=[
            shaped((ptok, width), BF16),
            shaped((rows - ptok, width), BF16),
            shaped((width // 2, lanes), BF16),
            shaped((width // 2, lanes), BF16),
        ],
        scratch_shapes=[pltpu.VMEM((width, lanes), BF16)],
        compiler_params=params(1),
        cost_estimate=cost(4),
        name="weights_second",
    )(me, xt, grads, wq, wk, wv, held)


def local_call(kernel, name, out_shape, *arrays, micros=1):
    return pl.pallas_call(
        kernel,
        out_shape=out_shape,
        compiler_params=pltpu.CompilerParams(vmem_limit_bytes=VMEM_LIMIT),
        cost_estimate=cost(micros),
        name=name,
    )(*arrays)


def add_core_kernel(keep_ref, found_ref, keep_out, left_out, right_out):
    half = keep_out.shape[0]
    middle = left_out.shape[1]
    keep_out[...] = (keep_ref[:half].astype(F32) + found_ref[:half].astype(F32)).astype(BF16)
    left_out[...] = (keep_ref[half:, :middle].astype(F32) + found_ref[half:, :middle].astype(F32)).astype(BF16)
    right_out[...] = (keep_ref[half:, middle:].astype(F32) + found_ref[half:, middle:].astype(F32)).astype(BF16)


def add_plane_kernel(keep_ref, left_ref, right_ref, *outs):
    middle = left_ref.shape[1]
    for part, found, lanes in (
        (keep_ref[:, :middle], left_ref, slice(0, middle)),
        (keep_ref[:, middle:], right_ref, slice(middle, 2 * middle)),
    ):
        total = (part.astype(F32) + found[...].astype(F32)).astype(BF16)
        start = 0
        for out in outs:
            size = out.shape[0]
            if out.shape[1] == middle:
                if (out is outs[1]) == (lanes.start == 0):
                    out[...] = total[start : start + size]
                if out is outs[1]:
                    continue
            else:
                out[:, lanes] = total[start : start + size]
            start += size


def add_line_kernel(*refs):
    *parts, out = refs
    total = parts[0][...].astype(F32)
    for part in parts[1:]:
        total = total + part[...].astype(F32)
    out[...] = total.astype(BF16)


def join_line_kernel(*refs):
    *parts, left_out, right_out = refs
    middle = left_out.shape[1]
    size = parts[0].shape[0]
    for i, part in enumerate(parts):
        left_out[i * size : (i + 1) * size] = part[:, :middle]
        right_out[i * size : (i + 1) * size] = part[:, middle:]


def join_plane_kernel(left_ref, right_ref, left_found, right_found, left_out, right_out):
    half = left_ref.shape[0]
    left_out[:half] = left_ref[...]
    left_out[half:] = left_found[...]
    right_out[:half] = right_ref[...]
    right_out[half:] = right_found[...]


def join_lanes_kernel(left_ref, right_ref, left_found, right_found, out):
    half, middle = left_ref.shape
    out[:half, :middle] = left_ref[...]
    out[half:, :middle] = left_found[...]
    out[:half, middle:] = right_ref[...]
    out[half:, middle:] = right_found[...]


def swap(block, axis_name, size, bit):
    return lax.ppermute(block, axis_name, [(i, i ^ bit) for i in range(size)])


def gradient_sum(keep, send, grp_size, psg_size):
    half, lanes = keep.shape
    low = lambda rows, columns: shaped((rows, columns), BF16)
    found = swap(send, "grp", grp_size, 1)
    yield (found,)
    keep, left, right = local_call(
        add_core_kernel,
        "add_core",
        [low(half // 2, lanes), low(half // 2, lanes // 2), low(half // 2, lanes // 2)],
        keep,
        found,
    )
    left, right = swap(left, "grp", grp_size, 2), swap(right, "grp", grp_size, 4)
    yield (left, right)
    keep, send_left, send_right = local_call(
        add_plane_kernel,
        "add_plane",
        [low(half // 4, lanes), low(half // 4, lanes // 2), low(half // 4, lanes // 2)],
        keep,
        left,
        right,
    )
    left, right = swap(send_left, "grp", grp_size, 4), swap(send_right, "grp", grp_size, 2)
    yield (left, right)
    size = half // 4 // psg_size
    keep, *sends = local_call(
        add_plane_kernel, "add_plane_last", [low(size, lanes)] * psg_size, keep, left, right
    )
    founds = [swap(part, "psg", psg_size, d) for d, part in enumerate(sends, 1)]
    yield tuple(founds)
    piece = local_call(add_line_kernel, "add_line", low(size, lanes), keep, *founds)
    bit = 8
    while bit < grp_size:
        piece = local_call(add_line_kernel, "add_line", low(size, lanes), piece, swap(piece, "grp", grp_size, bit))
        bit *= 2
    founds = [swap(piece, "psg", psg_size, d) for d in range(1, psg_size)]
    yield tuple(founds)
    left, right = local_call(
        join_line_kernel, "join_line", [low(half // 4, lanes // 2)] * 2, piece, *founds
    )
    left_found, right_found = swap(left, "grp", grp_size, 4), swap(right, "grp", grp_size, 2)
    yield (left_found, right_found)
    left, right = local_call(
        join_plane_kernel, "join_plane", [low(half // 2, lanes // 2)] * 2, left, right, left_found, right_found
    )
    left_found, right_found = swap(left, "grp", grp_size, 2), swap(right, "grp", grp_size, 4)
    yield (left_found, right_found)
    kept = local_call(
        join_lanes_kernel, "join_lanes", low(half, lanes), left, right, left_found, right_found
    )
    other = swap(kept, "grp", grp_size, 1)
    yield (kept, other)


def unpack_ffn_kernel(aliased, me_ref, kept_ref, other_ref, *rest):
    dwi_ref, dwo_ref, wave_scr = rest[aliased:]
    step = pl.program_id(0)

    @pl.when(step == 0)
    def _():
        unpack(me_ref, kept_ref, other_ref, wave_scr)

    right = wave_scr.shape[1] // 2
    dwi_ref[...] = wave_scr[:, pl.ds(pl.multiple_of(step * FCHUNK, FCHUNK), FCHUNK)].astype(F32)
    dwo_ref[...] = wave_scr[:, pl.ds(pl.multiple_of(right + step * FCHUNK, FCHUNK), FCHUNK)].astype(F32)


def unpack_ffn(me, kept, other, previous, offset):
    half, lanes = kept.shape
    width, ff = 2 * half, lanes
    held = list(previous)
    return pl.pallas_call(
        functools.partial(unpack_ffn_kernel, len(held)),
        grid=(ff // FCHUNK // 2,),
        in_specs=[smem(), whole(kept), whole(other)] + [pl.BlockSpec(memory_space=pl.ANY)] * len(held),
        out_specs=[
            spec((width, FCHUNK), lambda c: (0, c + offset)),
            spec((FCHUNK, width), lambda c: (c + offset, 0)),
        ],
        out_shape=[shaped((width, ff), F32), shaped((ff, width), F32)],
        scratch_shapes=[pltpu.VMEM((width, lanes), BF16)],
        input_output_aliases={3 + i: i for i in range(len(held))},
        compiler_params=params(1),
        cost_estimate=cost(3),
        name="unpack_ffn",
    )(me, kept, other, *held)


def unpack_attention_kernel(
    me_ref,
    kept1_ref,
    other1_ref,
    kept2_ref,
    other2_ref,
    dwq_ref,
    dwk_ref,
    dwv_ref,
    dout_ref,
    dproj_ref,
    g2_ref,
    s2_ref,
    bo_ref,
    g1_ref,
    s1_ref,
    bout_ref,
    bi_ref,
    bq_ref,
    bv_ref,
    first_scr,
    second_scr,
):
    unpack(me_ref, kept1_ref, other1_ref, first_scr)
    unpack(me_ref, kept2_ref, other2_ref, second_scr)
    for quad, scr in enumerate((first_scr, second_scr)):
        for i, ref in enumerate((dwq_ref, dwk_ref, dwv_ref)):
            ref[:, quad * QLANES : (quad + 1) * QLANES] = scr[:, i * QLANES : (i + 1) * QLANES].astype(F32)
    column = 3 * QLANES
    for ref in (dout_ref, dproj_ref):
        ref[...] = first_scr[:, column : column + ref.shape[1]].astype(F32)
        column += ref.shape[1]
    row = 0
    for ref in (g2_ref, s2_ref, bo_ref, g1_ref, s1_ref, bout_ref, bi_ref):
        row = take_vector(first_scr, row, column, ref, 0, ref.shape[1])
    row = take_vector(first_scr, row, column, bq_ref, 0, QLANES)
    take_vector(first_scr, row, column, bv_ref, 0, QLANES)
    column = 3 * QLANES
    row = take_vector(second_scr, 0, column, bq_ref, QLANES, QLANES)
    take_vector(second_scr, row, column, bv_ref, QLANES, QLANES)


def unpack_attention(me, kept1, other1, kept2, other2, width, dim, ff):
    vmem = pl.BlockSpec(memory_space=pltpu.VMEM)
    return pl.pallas_call(
        unpack_attention_kernel,
        in_specs=[smem()] + [vmem] * 4,
        out_shape=[shaped((width, width), F32)] * 4
        + [shaped((width, dim), F32)]
        + [shaped((1, width), F32)] * 6
        + [shaped((1, ff), F32)]
        + [shaped((1, width), F32)] * 2,
        scratch_shapes=[
            pltpu.VMEM((width, kept1.shape[1]), BF16),
            pltpu.VMEM((width, kept2.shape[1]), BF16),
        ],
        compiler_params=pltpu.CompilerParams(vmem_limit_bytes=VMEM_LIMIT),
        cost_estimate=cost(3),
        name="unpack_attention",
    )(me, kept1, other1, kept2, other2)


def after(array, *arrived):
    return lax.optimization_barrier((array,) + arrived)[0]


def shift_gather(block, axis_name, axis_size):
    found = [block]
    for distance in range(1, axis_size):
        ring = [(i, (i - distance) % axis_size) for i in range(axis_size)]
        found.append(lax.ppermute(block, axis_name, ring))
    return found


def local(
    grp_size,
    psg_size,
    passages,
    queries,
    lengths,
    positives,
    query_weight,
    query_bias,
    key_weight,
    value_weight,
    value_bias,
    output_weight,
    output_bias,
    first_gain,
    first_shift,
    inner_weight,
    inner_bias,
    outer_weight,
    outer_bias,
    second_gain,
    second_shift,
    project_weight,
):
    ptok, width = passages.shape
    qtok = queries.shape[0]
    rows = ptok + qtok
    row = lambda vector: vector.reshape(1, -1)
    g1, s1, g2, s2 = row(first_gain), row(first_shift), row(second_gain), row(second_shift)
    psg_index = lax.axis_index("psg").astype(jnp.int32)
    grp_index = lax.axis_index("grp").astype(jnp.int32)
    me = jnp.stack([grp_index & 1, (grp_index >> 1) & 1, (grp_index >> 2) & 1, psg_index])
    position = psg_index.reshape(1)
    q, k, v, o, lse, x1, rate1, xt = attention_forward(
        lengths,
        passages,
        queries,
        query_weight,
        row(query_bias),
        key_weight,
        value_weight,
        row(value_bias),
        output_weight,
        row(output_bias),
    )
    layer = (x1, g1, s1, inner_weight, row(inner_bias), outer_weight, row(outer_bias), g2, s2, project_weight)
    *held, query_embed = ffn_forward(qtok, ptok, rows, *layer, ())
    groups = shift_gather(query_embed, "psg", psg_size)
    ut, d, x2, rate2, e, pass_embed = ffn_forward(ptok, 0, rows, *layer, held)
    own_scores, pooled = score(lengths, pass_embed, groups)
    scores = shift_gather(own_scores, "psg", psg_size)
    losses, own, *rest = loss_and_grads(position, lengths, positives, pooled, pass_embed, groups, scores)
    aways = []
    for distance, part in enumerate(rest[:-1], 1):
        ring = [(i, (i + distance) % psg_size) for i in range(psg_size)]
        aways.append(lax.ppermute(part, "psg", ring))
    gr2p, vec, proj = passage_head(rest[-1], e, x2, rate2, project_weight, g2, s2)
    dproj, vec2, dbi1, gh1, gz, h1t, keep, send = ffn_backward_first(
        me,
        gr2p,
        vec,
        proj,
        own,
        aways,
        e,
        x2,
        rate2,
        project_weight,
        g2,
        s2,
        x1,
        g1,
        s1,
        inner_weight,
        outer_weight,
        ut,
        d,
    )
    sum_a = gradient_sum(keep, send, grp_size, psg_size)
    arrived = next(sum_a)
    dbi2, gh1, keep, send = ffn_backward_second(me, gz, h1t, gh1, inner_weight, outer_weight, ut, d)
    sum_b = gradient_sum(keep, send, grp_size, psg_size)
    arrived_b = next(sum_b)
    gh1 = after(gh1, *arrived)
    arrived = next(sum_a)
    gr1, go, dout, vec1 = first_norm(gh1, x1, rate1, g1, output_weight, o)
    go = after(go, *arrived, *arrived_b)
    arrived = next(sum_a)
    arrived_b = next(sum_b)
    grads = heads_backward(0, lengths, go, q, k, v, o, lse, ptok)
    grads = after(grads, *arrived, *arrived_b)
    arrived = next(sum_a)
    arrived_b = next(sum_b)
    gin, keep, send = weights_first(
        me, xt, grads, query_weight, key_weight, value_weight, gr1, dout, dproj, vec1, vec2, dbi1, dbi2
    )
    sum_c = gradient_sum(keep, send, grp_size, psg_size)
    arrived_c = next(sum_c)
    go = after(go, *arrived, *arrived_b)
    arrived = next(sum_a)
    arrived_b = next(sum_b)
    grads = heads_backward(1, lengths, go, q, k, v, o, lse, ptok)
    grads = after(grads, *arrived, *arrived_b, *arrived_c)
    arrived = next(sum_a)
    arrived_b = next(sum_b)
    arrived_c = next(sum_c)
    grad_p, grad_q, keep, send = weights_second(
        me, xt, grads, query_weight, key_weight, value_weight, gin, ptok
    )
    sum_d = gradient_sum(keep, send, grp_size, psg_size)
    *_, (kept_a, other_a) = sum_a
    *_, (kept_b, other_b) = sum_b
    *_, (kept_c, other_c) = sum_c
    *_, (kept_d, other_d) = sum_d
    held = unpack_ffn(me, kept_a, other_a, (), 0)
    dwi, dwo = unpack_ffn(me, kept_b, other_b, held, inner_weight.shape[1] // FCHUNK // 2)
    dwq, dwk, dwv, dout, dproj, g2, s2, bo, g1, s1, bout, bi, bq, bv = unpack_attention(
        me, kept_c, other_c, kept_d, other_d, width, project_weight.shape[1], inner_weight.shape[1]
    )
    flat = lambda vector: vector.reshape(-1)
    return (
        pass_embed,
        query_embed,
        flat(losses),
        grad_p,
        grad_q,
        dwq,
        flat(bq),
        dwk,
        dwv,
        flat(bv),
        dout,
        flat(bout),
        flat(g1),
        flat(s1),
        dwi,
        flat(bi),
        dwo,
        flat(bo),
        flat(g2),
        flat(s2),
        dproj,
    )


def solution(mesh):
    split = P(("grp", "psg"), None)
    in_specs = (split, split, split, P("grp")) + (P(),) * 16
    out_specs = (split, split, P("grp"), split, split) + (P(),) * 16
    body = functools.partial(local, mesh.shape["grp"], mesh.shape["psg"])
    return jax.shard_map(body, mesh=mesh, in_specs=in_specs, out_specs=out_specs, check_vma=False)
```

```python
import functools

import jax
import jax.numpy as jnp
from jax import lax
from jax.experimental import pallas as pl
from jax.experimental.pallas import tpu as pltpu
from jax.sharding import PartitionSpec as P

HEADS = 8
HEAD = 64
QLEN = 32

SHARPNESS = 10.0
SCORE_SCALE = 0.25
NORM_EPS = 1e-06
EMBED_EPS = 1e-06
NEG_FILL = -1e30

F32 = jnp.float32
BF16 = jnp.bfloat16

INV_SQRT_2PI = 0.3989422804014327

INV_SQRT_2 = 0.7071067811865476

QUAD = 4
QLANES = QUAD * HEAD
RB = 256
LANES = 128
FCHUNK = 512
SLICE = 16
ASLICE = 32
PIECE = 16
VMEM_LIMIT = 32 * 1024 * 1024


def dot(left, right):
    return jnp.dot(left, right, preferred_element_type=F32)


def dot_t(left, right):
    return lax.dot_general(left, right, (((1,), (1,)), ((), ())), preferred_element_type=F32)


def t_dot(left, right):
    return lax.dot_general(left, right, (((0,), (0,)), ((), ())), preferred_element_type=F32)


def two_part_dot(left, right_low):
    high = left.astype(BF16)
    rest = (left - high.astype(F32)).astype(BF16)
    return dot(high, right_low) + dot(rest, right_low)


def norm_stats(x):
    center = x - jnp.mean(x, axis=-1, keepdims=True)
    rate = lax.rsqrt(jnp.mean(center * center, axis=-1, keepdims=True) + NORM_EPS)
    return center * rate, rate


def norm_backward(grad, scaled, rate, gain):
    inner = grad * gain
    mean_in = jnp.mean(inner, axis=-1, keepdims=True)
    mean_dot = jnp.mean(inner * scaled, axis=-1, keepdims=True)
    grad_x = rate * (inner - mean_in - scaled * mean_dot)
    return grad_x, jnp.sum(grad * scaled, axis=0, keepdims=True), jnp.sum(grad, axis=0, keepdims=True)


def unit_backward(grad, projected):
    rate = lax.rsqrt(jnp.sum(projected * projected, axis=-1, keepdims=True) + EMBED_EPS)
    unit = projected * rate
    return rate * (grad - unit * jnp.sum(grad * unit, axis=-1, keepdims=True))


def gelu_pair(f):
    phi = 0.5 + 0.5 * lax.erf(f * INV_SQRT_2)
    density = jnp.exp(-0.5 * (f * f)) * INV_SQRT_2PI
    return f * phi, phi + f * density


def segment_ends(lengths_ref):
    count = lengths_ref.shape[1]
    ends = []
    total = jnp.int32(0)
    for s in range(count):
        total = total + lengths_ref[0, s]
        ends.append(total)
    return ends


def longest_start(lengths_ref, longest):
    found = jnp.int32(0)
    start = jnp.int32(0)
    for s in range(lengths_ref.shape[1]):
        found = jnp.where(lengths_ref[0, s] == longest, start, found)
        start = start + lengths_ref[0, s]
    return found


def fill_bias(bias_ref, lengths_ref, ptok, qtok):
    half = ptok // 2
    ends = segment_ends(lengths_ref)
    first = longest_start(lengths_ref, half)

    def segments(place):
        token = place + half + first
        token = jnp.where(token >= ptok, token - ptok, token)
        seg = jnp.zeros_like(token)
        for end in ends:
            seg = seg + jnp.where(token >= end, 1, 0)
        return seg

    row_seg = segments(lax.broadcasted_iota(jnp.int32, (8, half), 1))[:1]
    for r0 in range(0, half, LANES):
        col = segments(lax.broadcasted_iota(jnp.int32, (LANES, LANES), 0) + r0)
        for c in range(0, half, LANES):
            bias_ref[r0 : r0 + LANES, c : c + LANES] = jnp.where(col == row_seg[:, c : c + LANES], 0.0, NEG_FILL)
    for c in range(0, qtok, LANES):
        for r0 in range(0, qtok, LANES):
            row = (lax.broadcasted_iota(jnp.int32, (LANES, LANES), 0) + r0) // QLEN
            col = (lax.broadcasted_iota(jnp.int32, (LANES, LANES), 1) + c) // QLEN
            bias_ref[half + r0 : half + r0 + LANES, c : c + LANES] = jnp.where(row == col, 0.0, NEG_FILL)


def spans(ptok, qtok):
    half = ptok // 2
    return ((0, half, None), (half, half, 0), (ptok, qtok, half))


def owner_place(me_ref, r, turned=False):
    first, second = (r >> 3) & 1, (r >> 2) & 1
    if turned:
        first, second = second, first
    core, x, y, z = me_ref[0] ^ (r >> 4), me_ref[1] ^ first, me_ref[2] ^ second, me_ref[3] ^ (r & 3)
    return pl.multiple_of((((y * 2 + x) * 2 + core) * 4 + z) * PIECE, PIECE)


def to_relative(me_ref, plain_ref, out_ref, turned=False):
    for r in range(32):
        out_ref[r * PIECE : (r + 1) * PIECE] = plain_ref[pl.ds(owner_place(me_ref, r, turned), PIECE), :]


def attention_forward_kernel(
    ptok,
    lengths_hbm,
    xp_hbm,
    xq_hbm,
    wq_hbm,
    wk_hbm,
    wv_hbm,
    wo_hbm,
    bq_hbm,
    bv_hbm,
    bo_hbm,
    q_ref,
    k_ref,
    v_ref,
    o_ref,
    lse_ref,
    x1_ref,
    rate1_ref,
    xt_ref,
    x_scr,
    r1_scr,
    bias_scr,
    logs_scr,
    lengths_ref,
    xp_ref,
    wq_ref,
    wk_ref,
    wv_ref,
    wo_ref,
    bq_ref,
    bv_ref,
    bo_ref,
    sems,
):
    step = pl.program_id(0)
    rows = x_scr.shape[0]
    qtok = rows - ptok

    @pl.when(step == 0)
    def _():
        pairs = (
            (lengths_hbm, lengths_ref),
            (xp_hbm, xp_ref),
            (xq_hbm, x_scr.at[pl.ds(ptok, qtok)]),
            (bo_hbm, bo_ref),
            (wq_hbm, wq_ref),
            (bq_hbm, bq_ref),
            (wk_hbm, wk_ref),
            (wv_hbm, wv_ref),
            (bv_hbm, bv_ref),
            (wo_hbm, wo_ref),
        )
        copies = [pltpu.make_async_copy(held, ref, sems.at[i]) for i, (held, ref) in enumerate(pairs)]
        for copy in copies:
            copy.start()
        for copy in copies:
            copy.wait()
        first = longest_start(lengths_ref, ptok // 2)
        source = xp_ref[...]
        for r0 in range(0, ptok, LANES):
            token = lax.broadcasted_iota(jnp.int32, (LANES, ptok), 0) + (r0 + first)
            token = jnp.where(token >= ptok, token - ptok, token)
            pick = jnp.where(lax.broadcasted_iota(jnp.int32, (LANES, ptok), 1) == token, 1.0, 0.0).astype(BF16)
            x_scr[r0 : r0 + LANES] = dot(pick, source).astype(BF16)
        x = x_scr[...]
        xt_ref[...] = jnp.transpose(x)
        r1_scr[...] = x.astype(F32) + bo_ref[...]
        fill_bias(bias_scr, lengths_ref, ptok, qtok)

    x = x_scr[...]
    quad = pl.ds(pl.multiple_of(step * QLANES, QLANES), QLANES)
    q_ref[...] = (dot(x, wq_ref[:, quad]) + bq_ref[:, quad]).astype(BF16) * BF16(HEAD**-0.5)
    k_ref[...] = dot(x, wk_ref[:, quad]).astype(BF16)
    v_ref[...] = (dot(x, wv_ref[:, quad]) + bv_ref[:, quad]).astype(BF16)
    logs_scr[...] = jnp.zeros_like(logs_scr)

    for pair in range(QUAD // 2):
        lanes = slice(pair * LANES, (pair + 1) * LANES)
        for base, size, bias_row in spans(ptok, qtok):
            block = min(RB, size)
            for r0 in range(base, base + size, block):
                lane = lax.broadcasted_iota(jnp.int32, (block, LANES), 1)
                q = q_ref[r0 : r0 + block, lanes]
                keys = k_ref[base : base + size, lanes]
                values = v_ref[base : base + size, lanes]
                mixed = []
                for side in range(2):
                    inside = (lane < HEAD) if side == 0 else (lane >= HEAD)
                    s = dot_t(jnp.where(inside, q, BF16(0)), keys)
                    parts = []
                    totals = []
                    peaks = []
                    for i in range(0, block, ASLICE):
                        part = s[i : i + ASLICE]
                        if bias_row is not None:
                            at = bias_row + r0 - base + i
                            part = part + bias_scr[at : at + ASLICE, :size]
                        peak = jnp.max(part, axis=-1, keepdims=True)
                        e = jnp.exp(part - peak)
                        totals.append(jnp.sum(e, axis=-1, keepdims=True))
                        peaks.append(peak)
                        parts.append(e.astype(BF16))
                    total = jnp.concatenate(totals, axis=0)
                    mixed.append(dot(jnp.concatenate(parts, axis=0), values) * (1.0 / total))
                    log = jnp.concatenate(peaks, axis=0) + jnp.log(total)
                    logs_scr[r0 : r0 + block] = jnp.where(
                        lane == 2 * pair + side, log, logs_scr[r0 : r0 + block]
                    )
                o_ref[r0 : r0 + block, lanes] = jnp.where(lane < HEAD, mixed[0], mixed[1]).astype(BF16)
    lse_ref[0] = jnp.transpose(logs_scr[...])[:8]
    r1_scr[...] += dot(o_ref[...], wo_ref[quad, :])

    @pl.when(step == pl.num_programs(0) - 1)
    def _():
        scaled, rate = norm_stats(r1_scr[...])
        x1_ref[...] = scaled
        rate1_ref[...] = jnp.broadcast_to(rate, rate1_ref.shape)


def spec(shape, index):
    return pl.BlockSpec(shape, index)


def whole(array):
    return pl.BlockSpec(memory_space=pltpu.VMEM)


def const(array):
    nd = len(array.shape)
    return pl.BlockSpec(array.shape, lambda *_: (0,) * nd)


def smem():
    return pl.BlockSpec(memory_space=pltpu.SMEM)


def cost(micros):
    return pl.CostEstimate(flops=int(micros * 1e9), bytes_accessed=int(micros * 1e6), transcendentals=0)


def shaped(shape, dtype):
    return jax.ShapeDtypeStruct(shape, dtype)


def params(grid_rank):
    return pltpu.CompilerParams(
        dimension_semantics=("arbitrary",) * grid_rank, vmem_limit_bytes=VMEM_LIMIT
    )


def attention_forward(lengths, xp, xq, wq, bq, wk, wv, bv, wo, bo):
    ptok, width = xp.shape
    qtok = xq.shape[0]
    rows = ptok + qtok
    quads = HEADS // QUAD
    cols = lambda size: spec((size, QLANES), lambda g: (0, g))
    half = ptok // 2
    return pl.pallas_call(
        functools.partial(attention_forward_kernel, ptok),
        grid=(quads,),
        in_specs=[pl.BlockSpec(memory_space=pltpu.HBM)] * 10,
        out_specs=[
            cols(rows),
            cols(rows),
            cols(rows),
            cols(rows),
            spec((1, 8, rows), lambda g: (g, 0, 0)),
            whole(None),
            whole(None),
            whole(None),
        ],
        out_shape=[shaped((rows, width), BF16)] * 4
        + [
            shaped((quads, 8, rows), F32),
            shaped((rows, width), F32),
            shaped((rows, LANES), F32),
            shaped((width, rows), BF16),
        ],
        scratch_shapes=[
            pltpu.VMEM((rows, width), BF16),
            pltpu.VMEM((rows, width), F32),
            pltpu.VMEM((half + qtok, half), F32),
            pltpu.VMEM((rows, LANES), F32),
            pltpu.SMEM(lengths.shape, jnp.int32),
            pltpu.VMEM(xp.shape, BF16),
        ]
        + [pltpu.VMEM((width, width), BF16)] * 4
        + [pltpu.VMEM((1, width), F32)] * 3
        + [pltpu.SemaphoreType.DMA((10,))],
        compiler_params=params(1),
        cost_estimate=cost(20),
        name="attention_forward",
    )(lengths, xp, xq, wq, wk, wv, wo, bq, bv, bo)


def ffn_forward_kernel(
    aliased,
    rb,
    x1_ref,
    g1_ref,
    s1_ref,
    wi_ref,
    bi_ref,
    wo_ref,
    bo_ref,
    g2_ref,
    s2_ref,
    wp_ref,
    *rest,
):
    rest = rest[aliased:]
    u_ref, d_ref, x2_ref, rate2_ref, e_ref, emb_ref, h1_scr, r2_scr = rest
    step = pl.program_id(0)
    rows = x1_ref.shape[0]

    @pl.when(step == 0)
    def _():
        h1 = x1_ref[...] * g1_ref[...] + s1_ref[...]
        h1_scr[...] = h1.astype(BF16)
        r2_scr[...] = h1 + bo_ref[...]

    for r in range(0, rows, rb):
        f = dot(h1_scr[r : r + rb], wi_ref[...])
        bias = bi_ref[...]
        for i in range(0, rb, SLICE):
            u, d = gelu_pair(f[i : i + SLICE] + bias)
            u_ref[r + i : r + i + SLICE] = u.astype(BF16)
            d_ref[r + i : r + i + SLICE] = d.astype(BF16)
        r2_scr[r : r + rb] += dot(u_ref[r : r + rb], wo_ref[...])

    @pl.when(step == pl.num_programs(0) - 1)
    def _():
        scaled, rate = norm_stats(r2_scr[...])
        x2_ref[...] = scaled
        rate2_ref[...] = jnp.broadcast_to(rate, rate2_ref.shape)
        h2 = (scaled * g2_ref[...] + s2_ref[...]).astype(BF16)
        e = dot(h2, wp_ref[...])
        e_ref[...] = e
        size = jnp.sum(e * e, axis=-1, keepdims=True)
        emb_ref[...] = (e * lax.rsqrt(size + EMBED_EPS)).astype(BF16)


def ffn_forward(count, offset, total, x1, g1, s1, wi, bi, wo, bo, g2, s2, wp, previous):
    width = x1.shape[1]
    ff = wi.shape[1]
    dim = wp.shape[1]
    at = offset // count
    first = 10
    held = list(previous)
    return pl.pallas_call(
        functools.partial(ffn_forward_kernel, len(held), min(RB, count)),
        grid=(ff // FCHUNK,),
        in_specs=[
            spec((count, width), lambda c: (at, 0)),
            const(g1),
            const(s1),
            spec((width, FCHUNK), lambda c: (0, c)),
            spec((1, FCHUNK), lambda c: (0, c)),
            spec((FCHUNK, width), lambda c: (c, 0)),
            const(bo),
            const(g2),
            const(s2),
            const(wp),
        ]
        + [pl.BlockSpec(memory_space=pl.ANY)] * len(held),
        out_specs=[
            spec((count, FCHUNK), lambda c: (at, c)),
            spec((count, FCHUNK), lambda c: (at, c)),
            spec((count, width), lambda c: (at, 0)),
            spec((count, LANES), lambda c: (at, 0)),
            spec((count, dim), lambda c: (at, 0)),
            spec((count, dim), lambda c: (0, 0)),
        ],
        out_shape=[
            shaped((total, ff), BF16),
            shaped((total, ff), BF16),
            shaped((total, width), F32),
            shaped((total, LANES), F32),
            shaped((total, dim), F32),
            shaped((count, dim), BF16),
        ],
        scratch_shapes=[
            pltpu.VMEM((count, width), BF16),
            pltpu.VMEM((count, width), F32),
        ],
        input_output_aliases={first + i: i for i in range(len(held))},
        compiler_params=params(1),
        cost_estimate=cost(12 if count > 256 else 4),
        name="ffn_forward",
    )(x1, g1, s1, wi, bi, wo, bo, g2, s2, wp, *held)


def passage_member(lengths_ref, rows):
    ends = segment_ends(lengths_ref)
    lane = lax.broadcasted_iota(jnp.int32, (8, LANES), 1)
    low = jnp.full((8, LANES), rows, jnp.int32)
    high = jnp.zeros((8, LANES), jnp.int32)
    start = jnp.int32(0)
    for s, end in enumerate(ends):
        low = jnp.where(lane == s, start, low)
        high = jnp.where(lane == s, end, high)
        start = end
    token = lax.broadcasted_iota(jnp.int32, (rows, LANES), 0) + longest_start(lengths_ref, rows // 2)
    token = jnp.where(token >= rows, token - rows, token)
    inside = (token >= low[:1]) & (token < high[:1])
    return jnp.where(inside, 1.0, 0.0).astype(BF16)


def soft_match(group, pass_embed):
    return jnp.exp(SHARPNESS * dot_t(group, pass_embed) - SHARPNESS)


def score_kernel(psg, count, lengths_ref, emb_ref, *rest):
    group_refs = rest[:psg]
    score_ref, pooled_ref = rest[psg:]
    member = passage_member(lengths_ref, emb_ref.shape[0])
    group = jnp.concatenate([ref[...] for ref in group_refs], axis=0)
    matched = soft_match(group, emb_ref[...])
    pooled = two_part_dot(matched, member)
    lane = lax.broadcasted_iota(jnp.int32, pooled.shape, 1)
    pooled = jnp.where(lane < count, pooled, 1.0)
    pooled_ref[...] = pooled
    smooth = 1.0 + jnp.log(pooled) * (1.0 / SHARPNESS)
    queries = pooled.shape[0] // QLEN
    score_ref[...] = SCORE_SCALE * jnp.sum(smooth.reshape(queries, QLEN, LANES), axis=1)


def score(lengths, emb, groups):
    psg = len(groups)
    tokens = sum(g.shape[0] for g in groups)
    return pl.pallas_call(
        functools.partial(score_kernel, psg, lengths.shape[1]),
        in_specs=[smem()] + [pl.BlockSpec(memory_space=pltpu.VMEM)] * (1 + psg),
        out_shape=[shaped((tokens // QLEN, LANES), F32), shaped((tokens, LANES), F32)],
        compiler_params=pltpu.CompilerParams(vmem_limit_bytes=VMEM_LIMIT),
        cost_estimate=cost(3),
        name="score",
    )(lengths, emb, *groups)


def loss_kernel(psg, count, where_ref, lengths_ref, positives_ref, pooled_ref, emb_ref, *rest):
    group_refs = rest[:psg]
    score_refs = rest[psg : 2 * psg]
    loss_ref, own_ref = rest[2 * psg : 2 * psg + 2]
    away_refs = rest[2 * psg + 2 : 3 * psg + 1]
    grad_ref = rest[3 * psg + 1]
    position = where_ref[0]
    queries = score_refs[0].shape[0]
    each = queries // psg
    lane = lax.broadcasted_iota(jnp.int32, (queries, LANES), 1)
    row = lax.broadcasted_iota(jnp.int32, (queries, LANES), 0)
    valid = lane < count
    blocks = []
    for e in range(psg):
        found = score_refs[e][...]
        found = jnp.concatenate(
            [found[((d - e) % psg) * each : ((d - e) % psg + 1) * each] for d in range(psg)], axis=0
        )
        blocks.append(jnp.where(valid, found, -jnp.inf))
    target = jnp.zeros((queries, LANES), jnp.int32)
    for d in range(psg):
        for j in range(each):
            chosen = positives_ref[lax.rem(position + d, psg) * each + j]
            target = jnp.where(row == d * each + j, chosen, target)
    peak = blocks[0]
    for found in blocks[1:]:
        peak = jnp.maximum(peak, found)
    peak = jnp.max(peak, axis=-1, keepdims=True)
    total = jnp.zeros((queries, 1), F32)
    picked = jnp.zeros((queries, 1), F32)
    for e in range(psg):
        owner = lax.rem(position + e, psg)
        hit = (target == owner * count + lane) & valid
        total = total + jnp.sum(jnp.exp(blocks[e] - peak), axis=-1, keepdims=True)
        picked = picked + jnp.sum(jnp.where(hit, blocks[e], 0.0), axis=-1, keepdims=True)
        if e == 0:
            own_hit = jnp.where(hit, 1.0, 0.0)
    log_total = peak + jnp.log(total)
    losses = jnp.broadcast_to(log_total - picked, (queries, LANES))
    place = lax.rem(position + row // each, psg) * each + row % each
    losses = jnp.sum(jnp.where(lane == place, losses, 0.0), axis=0, keepdims=True)
    loss_ref[...] = losses[:, :queries]
    grad = jnp.where(valid, jnp.exp(blocks[0] - log_total) - own_hit, 0.0) * SCORE_SCALE
    tokens = queries * QLEN
    grad = jnp.broadcast_to(grad[:, None, :], (queries, QLEN, LANES)).reshape(tokens, LANES)
    grad = grad / pooled_ref[...]
    member = passage_member(lengths_ref, emb_ref.shape[0])
    high = grad.astype(BF16)
    rest_low = (grad - high.astype(F32)).astype(BF16)
    spread = dot_t(high, member) + dot_t(rest_low, member)
    group = jnp.concatenate([ref[...] for ref in group_refs], axis=0)
    low = (soft_match(group, emb_ref[...]) * spread).astype(BF16)
    group_grad = dot(low, emb_ref[...])
    each_tokens = tokens // psg
    own_ref[...] = group_grad[:each_tokens]
    for d in range(1, psg):
        away_refs[d - 1][...] = group_grad[d * each_tokens : (d + 1) * each_tokens].astype(BF16)
    grad_ref[...] = jnp.transpose(dot(jnp.transpose(group), low))


def loss_and_grads(position, lengths, positives, pooled, emb, groups, scores):
    psg = len(groups)
    queries = scores[0].shape[0]
    tokens, dim = groups[0].shape
    vmem = pl.BlockSpec(memory_space=pltpu.VMEM)
    return pl.pallas_call(
        functools.partial(loss_kernel, psg, lengths.shape[1]),
        in_specs=[smem(), smem(), smem()] + [vmem] * (2 + 2 * psg),
        out_shape=[shaped((1, queries), F32), shaped((tokens, dim), F32)]
        + [shaped((tokens, dim), BF16)] * (psg - 1)
        + [shaped(emb.shape, F32)],
        compiler_params=pltpu.CompilerParams(vmem_limit_bytes=VMEM_LIMIT),
        cost_estimate=cost(3),
        name="loss_and_grads",
    )(position, lengths, positives, pooled, emb, *groups, *scores)


def head_backward(grad_embed, e, x2, rate2, wp, g2, s2):
    low = unit_backward(grad_embed, e).astype(BF16)
    grad_h2 = dot_t(low, wp)
    grad_r2, gain_term, shift_term = norm_backward(grad_h2, x2, rate2[:, :1], g2)
    h2 = (x2 * g2 + s2).astype(BF16)
    return grad_r2, gain_term, shift_term, dot(jnp.transpose(low), h2)


def passage_head_kernel(
    grad_ref, e_ref, x2_ref, rate2_ref, wp_ref, g2_ref, s2_ref, gr2_ref, vec_ref, proj_ref
):
    grad_r2, gain_term, shift_term, proj = head_backward(
        grad_ref[...], e_ref[...], x2_ref[...], rate2_ref[...], wp_ref[...], g2_ref[...], s2_ref[...]
    )
    gr2_ref[...] = grad_r2
    vec_ref[...] = jnp.zeros_like(vec_ref)
    vec_ref[0:1] = gain_term
    vec_ref[1:2] = shift_term
    proj_ref[...] = proj


def passage_head(grad, e, x2, rate2, wp, g2, s2):
    ptok, dim = grad.shape
    width = x2.shape[1]
    at = lambda shape: spec(shape, lambda i: (0, 0))
    return pl.pallas_call(
        passage_head_kernel,
        grid=(1,),
        in_specs=[
            whole(grad),
            at((ptok, dim)),
            at((ptok, width)),
            at((ptok, LANES)),
            const(wp),
            const(g2),
            const(s2),
        ],
        out_specs=[at((ptok, width)), at((8, width)), at((dim, width))],
        out_shape=[shaped((ptok, width), F32), shaped((8, width), F32), shaped((dim, width), F32)],
        compiler_params=params(1),
        cost_estimate=cost(4),
        name="passage_head",
    )(grad, e, x2, rate2, wp, g2, s2)


def fixed(shape):
    return pl.BlockSpec(memory_space=pltpu.VMEM)


def ffn_backward_kernel(
    psg,
    me_ref,
    gr2p_ref,
    vec_ref,
    proj_ref,
    own_ref,
    *rest,
):
    away_refs = rest[: psg - 1]
    (
        e_ref,
        x2_ref,
        rate2_ref,
        wp_ref,
        g2_ref,
        s2_ref,
        x1_ref,
        g1_ref,
        s1_ref,
        wi_ref,
        wo_ref,
        u_ref,
        d_ref,
        dproj_ref,
        dvec_ref,
        dbi_ref,
        gh1_ref,
        keep_i_ref,
        send_i_ref,
        keep_o_ref,
        send_o_ref,
        gz_scr,
        turn_scr,
        gzt_scr,
        h1t_scr,
    ) = rest[psg - 1 :]
    step = pl.program_id(0)
    ptok = gr2p_ref.shape[0]

    @pl.when(step == 0)
    def _():
        grad = own_ref[...]
        for ref in away_refs:
            grad = grad + ref[...].astype(F32)
        grad_r2, gain_term, shift_term, proj = head_backward(
            grad, e_ref[...], x2_ref[...], rate2_ref[...], wp_ref[...], g2_ref[...], s2_ref[...]
        )
        dproj_ref[...] = jnp.transpose(proj_ref[...] + proj).astype(BF16)
        gr2p = gr2p_ref[...]
        gh1_ref[:ptok] = gr2p
        gh1_ref[ptok:] = grad_r2
        low_p = gr2p.astype(BF16)
        low_q = grad_r2.astype(BF16)
        gz_scr[:ptok] = low_p
        gz_scr[ptok:] = low_q
        dvec_ref[...] = jnp.zeros_like(dvec_ref)
        dvec_ref[0:1] = vec_ref[0:1] + gain_term
        dvec_ref[1:2] = vec_ref[1:2] + shift_term
        dvec_ref[2:3] = jnp.sum(low_p.astype(F32), axis=0, keepdims=True) + jnp.sum(
            low_q.astype(F32), axis=0, keepdims=True
        )
        turn_scr[...] = jnp.transpose((x1_ref[...] * g1_ref[...] + s1_ref[...]).astype(BF16))
        to_relative(me_ref, turn_scr, h1t_scr)
        turn_scr[...] = jnp.transpose(gz_scr[...])
        to_relative(me_ref, turn_scr, gzt_scr, turned=True)

    gz = gz_scr[...]
    grad_active = dot_t(gz, wo_ref[...])
    grad_inner = (grad_active * d_ref[...].astype(F32)).astype(BF16)
    dbi_ref[...] = jnp.sum(grad_inner.astype(F32), axis=0, keepdims=True)
    gh1_ref[...] += dot_t(grad_inner, wi_ref[...])
    half = keep_i_ref.shape[0]
    for ref, start in ((keep_i_ref, 0), (send_i_ref, half)):
        ref[...] = dot(h1t_scr[start : start + half], grad_inner).astype(BF16)
    for ref, start in ((keep_o_ref, 0), (send_o_ref, half)):
        ref[...] = dot(gzt_scr[start : start + half], u_ref[...]).astype(BF16)


def ffn_backward(me, gr2p, vec, proj, own, aways, e, x2, rate2, wp, g2, s2, x1, g1, s1, wi, wo, u, d):
    ptok, width = gr2p.shape
    rows = x1.shape[0]
    qtok = rows - ptok
    dim = wp.shape[1]
    ff = wi.shape[1]
    at = ptok // qtok
    return pl.pallas_call(
        functools.partial(ffn_backward_kernel, 1 + len(aways)),
        grid=(ff // FCHUNK,),
        in_specs=[smem(), whole(gr2p), whole(vec), whole(proj), whole(own)]
        + [whole(a) for a in aways]
        + [
            spec((qtok, dim), lambda c: (at, 0)),
            spec((qtok, width), lambda c: (at, 0)),
            spec((qtok, LANES), lambda c: (at, 0)),
            const(wp),
            const(g2),
            const(s2),
            whole(x1),
            const(g1),
            const(s1),
            spec((width, FCHUNK), lambda c: (0, c)),
            spec((FCHUNK, width), lambda c: (c, 0)),
            spec((rows, FCHUNK), lambda c: (0, c)),
            spec((rows, FCHUNK), lambda c: (0, c)),
        ],
        out_specs=[
            fixed((width, dim)),
            fixed((8, width)),
            spec((1, FCHUNK), lambda c: (0, c)),
            fixed((rows, width)),
        ]
        + [spec((width // 2, FCHUNK), lambda c: (0, c))] * 4,
        out_shape=[
            shaped((width, dim), BF16),
            shaped((8, width), F32),
            shaped((1, ff), F32),
            shaped((rows, width), F32),
        ]
        + [shaped((width // 2, ff), BF16)] * 4,
        scratch_shapes=[
            pltpu.VMEM((rows, width), BF16),
            pltpu.VMEM((width, rows), BF16),
            pltpu.VMEM((width, rows), BF16),
            pltpu.VMEM((width, rows), BF16),
        ],
        compiler_params=params(1),
        cost_estimate=cost(15),
        name="ffn_backward",
    )(me, gr2p, vec, proj, own, *aways, e, x2, rate2, wp, g2, s2, x1, g1, s1, wi, wo, u, d)


def put_vector(wave_ref, row, vector):
    for i in range(vector.shape[1] // LANES):
        wave_ref[row + i : row + i + 1] = vector[:, i * LANES : (i + 1) * LANES]
    return row + vector.shape[1] // LANES


def take_vector(wave_ref, row, column, out_ref):
    size = out_ref.shape[1]
    for i in range(size // LANES):
        out_ref[:, i * LANES : (i + 1) * LANES] = wave_ref[row + i : row + i + 1, column : column + LANES].astype(
            F32
        )
    return row + size // LANES


def units(pair, ptok, qtok):
    for index, (base, size, bias_row) in enumerate(spans(ptok, qtok)):
        block = min(RB, size)
        place = 0
        for r0 in range(base, base + size, block):
            for side in range(2):
                yield index, base, size, bias_row, r0, block, side, place
                place += block


def one_head(block, side, rows):
    lane = lax.broadcasted_iota(jnp.int32, (block, LANES), 1)
    return jnp.where((lane < HEAD) if side == 0 else (lane >= HEAD), rows, BF16(0))


def probabilities_kernel(ptok, lengths_ref, q_ref, k_ref, lse_ref, p_ref, pq_ref, bias_scr):
    qtok = q_ref.shape[0] - ptok

    @pl.when(pl.program_id(0) == 0)
    def _():
        fill_bias(bias_scr, lengths_ref, ptok, qtok)

    step = pl.program_id(0)
    for pair in range(QUAD // 2):
        lanes = slice(pair * LANES, (pair + 1) * LANES)
        for index, base, size, bias_row, r0, block, side, place in units(pair, ptok, qtok):
            h = 2 * pair + side
            s = dot_t(k_ref[base : base + size, lanes], one_head(block, side, q_ref[r0 : r0 + block, lanes]))
            lse = lse_ref[0, h : h + 1, r0 : r0 + block]
            for i in range(0, size, ASLICE):
                part = s[i : i + ASLICE]
                if bias_row is not None:
                    part = part + bias_scr[bias_row + i : bias_row + i + ASLICE, r0 - base : r0 - base + block]
                p = jnp.exp(part - lse).astype(BF16)
                if index < 2:
                    p_ref[step, 2 * pair + index, i : i + ASLICE, place : place + block] = p
                else:
                    pq_ref[step, pair, i : i + ASLICE, place : place + block] = p


def probabilities(lengths, q, k, lse, ptok):
    rows, width = q.shape
    quads = HEADS // QUAD
    half, qtok = ptok // 2, rows - ptok
    cols = spec((rows, QLANES), lambda g: (0, g))
    return pl.pallas_call(
        functools.partial(probabilities_kernel, ptok),
        grid=(quads,),
        in_specs=[smem(), cols, cols, spec((1, 8, rows), lambda g: (g, 0, 0))],
        out_specs=[whole(None), whole(None)],
        out_shape=[
            shaped((quads, QUAD, half, 2 * half), BF16),
            shaped((quads, QUAD // 2, qtok, 2 * qtok), BF16),
        ],
        scratch_shapes=[pltpu.VMEM((half + qtok, half), F32)],
        compiler_params=params(1),
        cost_estimate=cost(8),
        name="probabilities",
    )(lengths, q, k, lse)


def first_norm_kernel(gh1_ref, x1_ref, rate1_ref, g1_ref, wo_ref, gr1_ref, go_ref, vec_ref):
    grad_r1, gain_term, shift_term = norm_backward(gh1_ref[...], x1_ref[...], rate1_ref[:, :1], g1_ref[...])
    gr1_ref[...] = grad_r1
    low = grad_r1.astype(BF16)
    vec_ref[...] = jnp.zeros_like(vec_ref)
    vec_ref[0:1] = gain_term
    vec_ref[1:2] = shift_term
    vec_ref[2:3] = jnp.sum(low.astype(F32), axis=0, keepdims=True)
    go_ref[...] = dot_t(low, wo_ref[...]).astype(BF16)


def first_norm(gh1, x1, rate1, g1, wo):
    rows, width = x1.shape
    return pl.pallas_call(
        first_norm_kernel,
        grid=(1,),
        in_specs=[whole(gh1), whole(x1), whole(rate1), const(g1), const(wo)],
        out_specs=[whole(None)] * 3,
        out_shape=[shaped((rows, width), F32), shaped((rows, width), BF16), shaped((8, width), F32)],
        compiler_params=params(1),
        cost_estimate=cost(4),
        name="first_norm",
    )(gh1, x1, rate1, g1, wo)


def heads_backward_kernel(
    quad,
    ptok,
    p_ref,
    pq_ref,
    q_ref,
    k_ref,
    v_ref,
    o_ref,
    go_ref,
    gq_ref,
    gk_ref,
    gv_ref,
    dd_scr,
    gqt_scr,
    qm_scr,
    gm_scr,
    gs_scr,
    kt_scr,
):
    qtok = q_ref.shape[0] - ptok

    product = go_ref[...].astype(F32) * o_ref[...].astype(F32)
    ones = jnp.where(
        lax.broadcasted_iota(jnp.int32, (16, QLANES), 1) // HEAD
        == lax.broadcasted_iota(jnp.int32, (16, QLANES), 0),
        1.0,
        0.0,
    ).astype(BF16)
    high = product.astype(BF16)
    dd_scr[...] = dot_t(ones, high) + dot_t(ones, (product - high.astype(F32)).astype(BF16))
    kt_scr[...] = jnp.transpose(k_ref[...])
    for pair in range(QUAD // 2):
        lanes = slice(pair * LANES, (pair + 1) * LANES)
        last = None
        for index, base, size, bias_row, r0, block, side, place in units(pair, ptok, qtok):
            buffer = (3 * pair + index) % 2
            h = 2 * pair + side
            qm_scr[buffer, place : place + block] = one_head(block, side, q_ref[r0 : r0 + block, lanes])
            gm = one_head(block, side, go_ref[r0 : r0 + block, lanes])
            gm_scr[buffer, place : place + block] = gm
            grad_prob = dot_t(v_ref[base : base + size, lanes], gm)
            dd = dd_scr[h : h + 1, r0 : r0 + block]
            p_at = p_ref.at[quad, 2 * pair + index] if index < 2 else pq_ref.at[quad, pair]
            for i in range(0, size, ASLICE):
                p = p_at[i : i + ASLICE, place : place + block].astype(F32)
                gs = p * (grad_prob[i : i + ASLICE] - dd)
                gs_scr[buffer, i : i + ASLICE, place : place + block] = gs.astype(BF16)
            gqt_scr[h * HEAD : (h + 1) * HEAD, r0 : r0 + block] = dot(
                kt_scr[h * HEAD : (h + 1) * HEAD, base : base + size],
                gs_scr[buffer, :size, place : place + block],
            )
            end = place + block
            if end == 2 * size:
                gv_ref[base : base + size, lanes] = dot(p_at[...], gm_scr[buffer, :end]).astype(BF16)
                gk_ref[base : base + size, lanes] = dot(gs_scr[buffer, :size, :end], qm_scr[buffer, :end]).astype(
                    BF16
                )
    gq_ref[...] = (jnp.transpose(gqt_scr[...]) * (HEAD**-0.5)).astype(BF16)


def heads_backward(quad, p, pq, q, k, v, o, go, ptok):
    rows, width = q.shape
    half = ptok // 2
    cols = spec((rows, QLANES), lambda i: (0, quad))
    low = lambda *shape: pltpu.VMEM(shape, BF16)
    return pl.pallas_call(
        functools.partial(heads_backward_kernel, quad, ptok),
        grid=(1,),
        in_specs=[whole(p), whole(pq)] + [cols] * 5,
        out_specs=[whole(None)] * 3,
        out_shape=[shaped((rows, QLANES), BF16)] * 3,
        scratch_shapes=[
            pltpu.VMEM((16, rows), F32),
            pltpu.VMEM((QLANES, rows), F32),
            low(2, 4 * RB, LANES),
            low(2, 4 * RB, LANES),
            low(2, half, 4 * RB),
            low(QLANES, rows),
        ],
        compiler_params=params(1),
        cost_estimate=cost(10),
        name="heads_backward",
    )(p, pq, q, k, v, o, go)


def weights_kernel(
    ptok,
    me_ref,
    gr1_ref,
    o_ref,
    xt_ref,
    gq0_ref,
    gk0_ref,
    gv0_ref,
    gq1_ref,
    gk1_ref,
    gv1_ref,
    dproj_ref,
    vec1_ref,
    vec2_ref,
    dbi_ref,
    wq_ref,
    wk_ref,
    wv_ref,
    keep_ref,
    send_ref,
    gp_ref,
    gq_ref,
    turn_scr,
    xt_scr,
    ot_scr,
    lines_scr,
    tail_scr,
):
    half_rows = keep_ref.shape[0]
    width = gr1_ref.shape[1]
    gr1 = gr1_ref[...]
    to_relative(me_ref, xt_ref, xt_scr)
    turn_scr[...] = jnp.transpose(o_ref[...])
    to_relative(me_ref, turn_scr, ot_scr)
    joined = [
        jnp.concatenate([left[...], right[...]], axis=1)
        for left, right in ((gq0_ref, gq1_ref), (gk0_ref, gk1_ref), (gv0_ref, gv1_ref))
    ]
    low = gr1.astype(BF16)
    for ref, start in ((keep_ref, 0), (send_ref, half_rows)):
        for i, grad in enumerate(joined):
            ref[:, i * width : (i + 1) * width] = dot(xt_scr[start : start + half_rows], grad).astype(BF16)
        ref[:, 3 * width : 4 * width] = dot(ot_scr[start : start + half_rows], low).astype(BF16)
    gin = gr1 + dot_t(joined[0], wq_ref[...]) + dot_t(joined[1], wk_ref[...]) + dot_t(joined[2], wv_ref[...])
    gp_ref[...] = gin[:ptok].astype(BF16)
    gq_ref[...] = gin[ptok:].astype(BF16)
    row = 0
    for vector in (
        vec2_ref[0:1],
        vec2_ref[1:2],
        vec2_ref[2:3],
        vec1_ref[0:1],
        vec1_ref[1:2],
        vec1_ref[2:3],
        dbi_ref[...],
        jnp.sum(joined[0].astype(F32), axis=0, keepdims=True),
        jnp.sum(joined[2].astype(F32), axis=0, keepdims=True),
    ):
        row = put_vector(lines_scr, row, vector)
    lines_scr[row:] = jnp.zeros((lines_scr.shape[0] - row, LANES), F32)
    dim = dproj_ref.shape[1]
    tail_scr[:, :dim] = dproj_ref[...]
    tail_scr[:, dim:] = lines_scr[...].astype(BF16)
    for r in range(32):
        ref = keep_ref if r < 16 else send_ref
        at = (r % 16) * PIECE
        ref[at : at + PIECE, 4 * width :] = tail_scr[pl.ds(owner_place(me_ref, r), PIECE), :]


def weights(me, gr1, o, xt, first, second, dproj, vec1, vec2, dbi, wq, wk, wv, ptok):
    rows, width = gr1.shape
    lanes = 4 * width + dproj.shape[1] + LANES
    low = lambda *shape: pltpu.VMEM(shape, BF16)
    return pl.pallas_call(
        functools.partial(weights_kernel, ptok),
        grid=(1,),
        in_specs=[smem()] + [whole(None)] * 13 + [const(wq), const(wk), const(wv)],
        out_specs=[whole(None)] * 4,
        out_shape=[
            shaped((width // 2, lanes), BF16),
            shaped((width // 2, lanes), BF16),
            shaped((ptok, width), BF16),
            shaped((rows - ptok, width), BF16),
        ],
        scratch_shapes=[
            low(width, rows),
            low(width, rows),
            low(width, rows),
            pltpu.VMEM((width, LANES), F32),
            low(width, dproj.shape[1] + LANES),
        ],
        compiler_params=params(1),
        cost_estimate=cost(6),
        name="weights",
    )(me, gr1, o, xt, *first, *second, dproj, vec1, vec2, dbi, wq, wk, wv)


def from_relative(me_ref, kept_ref, other_ref, wave_ref, turned=False):
    for r in range(32):
        ref = kept_ref if r < 16 else other_ref
        at = (r % 16) * PIECE
        wave_ref[pl.ds(owner_place(me_ref, r, turned), PIECE), :] = ref[at : at + PIECE]


def unpack_ffn_kernel(
    me_ref, kept_i_ref, other_i_ref, kept_o_ref, other_o_ref, dwi_ref, dwo_ref, wave_i_scr, wave_o_scr
):
    from_relative(me_ref, kept_i_ref, other_i_ref, wave_i_scr)
    from_relative(me_ref, kept_o_ref, other_o_ref, wave_o_scr, turned=True)
    dwi_ref[...] = wave_i_scr[...].astype(F32)
    dwo_ref[...] = jnp.transpose(wave_o_scr[...].astype(F32))


def unpack_ffn(me, *halves):
    half, ff = halves[0].shape
    width = 2 * half
    return pl.pallas_call(
        unpack_ffn_kernel,
        grid=(ff // FCHUNK,),
        in_specs=[smem()] + [spec((half, FCHUNK), lambda c: (0, c))] * 4,
        out_specs=[
            spec((width, FCHUNK), lambda c: (0, c)),
            spec((FCHUNK, width), lambda c: (c, 0)),
        ],
        out_shape=[shaped((width, ff), F32), shaped((ff, width), F32)],
        scratch_shapes=[pltpu.VMEM((width, FCHUNK), BF16)] * 2,
        compiler_params=params(1),
        cost_estimate=cost(6),
        name="unpack_ffn",
    )(me, *halves)


def unpack_attention_kernel(
    me_ref,
    kept_ref,
    other_ref,
    dwq_ref,
    dwk_ref,
    dwv_ref,
    dout_ref,
    dproj_ref,
    g2_ref,
    s2_ref,
    bo_ref,
    g1_ref,
    s1_ref,
    bout_ref,
    bi_ref,
    bq_ref,
    bv_ref,
    wave_scr,
):
    from_relative(me_ref, kept_ref, other_ref, wave_scr)
    column = 0
    for ref in (dwq_ref, dwk_ref, dwv_ref, dout_ref, dproj_ref):
        ref[...] = wave_scr[:, column : column + ref.shape[1]].astype(F32)
        column += ref.shape[1]
    row = 0
    for ref in (g2_ref, s2_ref, bo_ref, g1_ref, s1_ref, bout_ref, bi_ref, bq_ref, bv_ref):
        row = take_vector(wave_scr, row, column, ref)


def unpack_attention(me, kept, other, width, dim, ff):
    vmem = pl.BlockSpec(memory_space=pltpu.VMEM)
    return pl.pallas_call(
        unpack_attention_kernel,
        in_specs=[smem()] + [vmem] * 2,
        out_shape=[shaped((width, width), F32)] * 4
        + [shaped((width, dim), F32)]
        + [shaped((1, width), F32)] * 6
        + [shaped((1, ff), F32)]
        + [shaped((1, width), F32)] * 2,
        scratch_shapes=[pltpu.VMEM((width, kept.shape[1]), BF16)],
        compiler_params=pltpu.CompilerParams(vmem_limit_bytes=VMEM_LIMIT),
        cost_estimate=cost(3),
        name="unpack_attention",
    )(me, kept, other)


def swap(block, axis_name, size, bit):
    return lax.ppermute(block, axis_name, [(i, i ^ bit) for i in range(size)])


def total(*parts):
    found = parts[0].astype(F32)
    for part in parts[1:]:
        found = found + part.astype(F32)
    return found.astype(BF16)


def core_parts(keep, found):
    size = keep.shape[0] // 4
    return [total(keep[i * size : (i + 1) * size], found[i * size : (i + 1) * size]) for i in range(4)]


def halves(block):
    size = block.shape[0] // 2
    return block[:size], block[size:]


def plane_send(blocks, grp_size):
    return tuple(swap(block, "grp", grp_size, bits) for block, bits in zip(blocks, (4, 2, 6)))


def line_parts(parts, psg_size):
    size = parts[0].shape[0] // psg_size
    return [total(*[part[i * size : (i + 1) * size] for part in parts]) for i in range(psg_size)]


def line_send(blocks, psg_size):
    return tuple(swap(block, "psg", psg_size, d) for d, block in enumerate(blocks, 1))


def line_total(own, founds, grp_size):
    piece = total(own, *founds)
    bit = 8
    while bit < grp_size:
        piece = total(piece, swap(piece, "grp", grp_size, bit))
        bit *= 2
    return piece


def tie(values, *others):
    return lax.optimization_barrier((tuple(values), others))[0]


def unroll(rolled, start):
    count = rolled.shape[0]
    return lax.dynamic_slice_in_dim(jnp.concatenate([rolled, rolled]), count - start, count, 0)


def shift_gather(block, axis_name, axis_size):
    found = [block]
    for distance in range(1, axis_size):
        ring = [(i, (i - distance) % axis_size) for i in range(axis_size)]
        found.append(lax.ppermute(block, axis_name, ring))
    return found


def local(
    grp_size,
    psg_size,
    passages,
    queries,
    lengths,
    positives,
    query_weight,
    query_bias,
    key_weight,
    value_weight,
    value_bias,
    output_weight,
    output_bias,
    first_gain,
    first_shift,
    inner_weight,
    inner_bias,
    outer_weight,
    outer_bias,
    second_gain,
    second_shift,
    project_weight,
):
    ptok, width = passages.shape
    qtok = queries.shape[0]
    rows = ptok + qtok
    row = lambda vector: vector.reshape(1, -1)
    g1, s1, g2, s2 = row(first_gain), row(first_shift), row(second_gain), row(second_shift)
    psg_index = lax.axis_index("psg").astype(jnp.int32)
    grp_index = lax.axis_index("grp").astype(jnp.int32)
    me = jnp.stack([grp_index & 1, (grp_index >> 1) & 1, (grp_index >> 2) & 1, psg_index])
    position = psg_index.reshape(1)
    starts = jnp.cumsum(lengths[0]) - lengths[0]
    start = jnp.sum(jnp.where(lengths[0] == ptok // 2, starts, 0))
    q, k, v, o, lse, x1, rate1, xt = attention_forward(
        lengths,
        passages,
        queries,
        query_weight,
        row(query_bias),
        key_weight,
        value_weight,
        row(value_bias),
        output_weight,
        row(output_bias),
    )
    layer = (x1, g1, s1, inner_weight, row(inner_bias), outer_weight, row(outer_bias), g2, s2, project_weight)
    *held, query_embed = ffn_forward(qtok, ptok, rows, *layer, ())
    groups = shift_gather(query_embed, "psg", psg_size)
    u, d, x2, rate2, e, pass_embed = ffn_forward(ptok, 0, rows, *layer, held)
    own_scores, pooled = score(lengths, pass_embed, groups)
    scores = shift_gather(own_scores, "psg", psg_size)
    (late_lse,) = tie((lse,), own_scores)
    p, pq = probabilities(lengths, q, k, late_lse, ptok)
    scores[1:] = tie(scores[1:], p, pq)
    losses, own, *rest = loss_and_grads(position, lengths, positives, pooled, pass_embed, groups, scores)
    aways = []
    for distance, part in enumerate(rest[:-1], 1):
        ring = [(i, (i + distance) % psg_size) for i in range(psg_size)]
        aways.append(lax.ppermute(part, "psg", ring))
    gr2p, vec, proj = passage_head(rest[-1], e, x2, rate2, project_weight, g2, s2)
    dproj, vec2, dbi, gh1, keep_i, send_i, keep_o, send_o = ffn_backward(
        me,
        gr2p,
        vec,
        proj,
        own,
        aways,
        e,
        x2,
        rate2,
        project_weight,
        g2,
        s2,
        x1,
        g1,
        s1,
        inner_weight,
        outer_weight,
        u,
        d,
    )
    core_a = (swap(send_i, "grp", grp_size, 1), swap(send_o, "grp", grp_size, 1))
    gr1, go, vec1 = first_norm(gh1, x1, rate1, g1, output_weight)
    *core_a, go = tie((*core_a, go))
    next_i, away_i = [total(part, found) for part, found in zip(halves(keep_i), halves(core_a[0]))]
    next_o, away_o = [total(part, found) for part, found in zip(halves(keep_o), halves(core_a[1]))]
    plane_a = (swap(away_i, "grp", grp_size, 2), swap(away_o, "grp", grp_size, 4))
    first = heads_backward(0, p, pq, q, k, v, o, go, ptok)
    plane_a = tie(plane_a, *first)
    (go,) = tie((go,), *plane_a)
    next_i, away_i = [total(part, found) for part, found in zip(halves(next_i), halves(plane_a[0]))]
    next_o, away_o = [total(part, found) for part, found in zip(halves(next_o), halves(plane_a[1]))]
    plane_a = (swap(away_i, "grp", grp_size, 4), swap(away_o, "grp", grp_size, 2))
    second = heads_backward(1, p, pq, q, k, v, o, go, ptok)
    plane_a = tie(plane_a, *second)
    (gr1,) = tie((gr1,), *plane_a)
    both = lambda left, right: jnp.concatenate([left, right], axis=1)
    quarter = next_i.shape[0] // psg_size
    lines_a = [
        both(
            total(next_i[i * quarter : (i + 1) * quarter], plane_a[0][i * quarter : (i + 1) * quarter]),
            total(next_o[i * quarter : (i + 1) * quarter], plane_a[1][i * quarter : (i + 1) * quarter]),
        )
        for i in range(psg_size)
    ]
    line_a = line_send(lines_a[1:], psg_size)
    keep_b, send_b, grad_p, grad_q = weights(
        me,
        gr1,
        o,
        xt,
        first,
        second,
        dproj,
        vec1,
        vec2,
        dbi,
        query_weight,
        key_weight,
        value_weight,
        ptok,
    )
    core_b = swap(send_b, "grp", grp_size, 1)
    line_a = tie(line_a, grad_q)
    piece_a = line_total(lines_a[0], line_a, grp_size)
    spread_a = line_send([piece_a] * (psg_size - 1), psg_size)
    parts_b = core_parts(keep_b, core_b)
    plane_b = plane_send(parts_b[1:], grp_size)
    out_embed = unroll(pass_embed, start)
    out_grad = unroll(grad_p, start)
    plane_b = tie(plane_b, out_embed, out_grad, *spread_a)
    lines_b = line_parts((parts_b[0], *plane_b), psg_size)
    line_b = line_send(lines_b[1:], psg_size)
    spread_a = tie(spread_a, *plane_b)
    ff = inner_weight.shape[1]
    held_i = jnp.concatenate([part[:, :ff] for part in (piece_a, *spread_a)])
    held_o = jnp.concatenate([part[:, ff:] for part in (piece_a, *spread_a)])
    found_a = (swap(held_i, "grp", grp_size, 4), swap(held_o, "grp", grp_size, 2))
    line_b = tie(line_b, *found_a)
    piece_b = line_total(lines_b[0], line_b, grp_size)
    spread_b = line_send([piece_b] * (psg_size - 1), psg_size)
    found_a = tie(found_a, *line_b)
    held_i = jnp.concatenate([held_i, found_a[0]])
    held_o = jnp.concatenate([held_o, found_a[1]])
    found_a = (swap(held_i, "grp", grp_size, 2), swap(held_o, "grp", grp_size, 4))
    found_a = tie(found_a, *spread_b)
    joined_b = jnp.concatenate([piece_b, *spread_b])
    gathered_b = plane_send([joined_b] * 3, grp_size)
    held_i = jnp.concatenate([held_i, found_a[0]])
    held_o = jnp.concatenate([held_o, found_a[1]])
    other_i, other_o = swap(held_i, "grp", grp_size, 1), swap(held_o, "grp", grp_size, 1)
    dwi, dwo = unpack_ffn(me, held_i, other_i, held_o, other_o)
    gathered_b = tie(gathered_b, dwi, dwo)
    kept_b = jnp.concatenate([joined_b, *gathered_b])
    other_b = swap(kept_b, "grp", grp_size, 1)
    dwq, dwk, dwv, dout, dproj, g2, s2, bo, g1, s1, bout, bi, bq, bv = unpack_attention(
        me, kept_b, other_b, width, project_weight.shape[1], inner_weight.shape[1]
    )
    flat = lambda vector: vector.reshape(-1)
    return (
        out_embed,
        query_embed,
        flat(losses),
        out_grad,
        grad_q,
        dwq,
        flat(bq),
        dwk,
        dwv,
        flat(bv),
        dout,
        flat(bout),
        flat(g1),
        flat(s1),
        dwi,
        flat(bi),
        dwo,
        flat(bo),
        flat(g2),
        flat(s2),
        dproj,
    )


def solution(mesh):
    split = P(("grp", "psg"), None)
    in_specs = (split, split, split, P("grp")) + (P(),) * 16
    out_specs = (split, split, P("grp"), split, split) + (P(),) * 16
    body = functools.partial(local, mesh.shape["grp"], mesh.shape["psg"])
    return jax.shard_map(body, mesh=mesh, in_specs=in_specs, out_specs=out_specs, check_vma=False)
```

```python
import functools

import jax
import jax.numpy as jnp
from jax import lax
from jax.experimental import pallas as pl
from jax.experimental.pallas import tpu as pltpu
from jax.sharding import PartitionSpec as P

HEADS = 8
HEAD = 64
QLEN = 32

SHARPNESS = 10.0
SCORE_SCALE = 0.25
NORM_EPS = 1e-06
EMBED_EPS = 1e-06
NEG_FILL = -1e30

F32 = jnp.float32
BF16 = jnp.bfloat16

INV_SQRT_2PI = 0.3989422804014327

INV_SQRT_2 = 0.7071067811865476

QUAD = 4
QLANES = QUAD * HEAD
RB = 256
LANES = 128
FCHUNK = 512
SLICE = 16
ASLICE = 32
PIECE = 16


def dot(left, right):
    return jnp.dot(left, right, preferred_element_type=F32)


def dot_t(left, right):
    return lax.dot_general(left, right, (((1,), (1,)), ((), ())), preferred_element_type=F32)


def t_dot(left, right):
    return lax.dot_general(left, right, (((0,), (0,)), ((), ())), preferred_element_type=F32)


def two_part_dot(left, right_low):
    high = left.astype(BF16)
    rest = (left - high.astype(F32)).astype(BF16)
    return dot(high, right_low) + dot(rest, right_low)


def norm_stats(x):
    center = x - jnp.mean(x, axis=-1, keepdims=True)
    rate = lax.rsqrt(jnp.mean(center * center, axis=-1, keepdims=True) + NORM_EPS)
    return center * rate, rate


def norm_backward(grad, scaled, rate, gain):
    inner = grad * gain
    mean_in = jnp.mean(inner, axis=-1, keepdims=True)
    mean_dot = jnp.mean(inner * scaled, axis=-1, keepdims=True)
    grad_x = rate * (inner - mean_in - scaled * mean_dot)
    return grad_x, jnp.sum(grad * scaled, axis=0, keepdims=True), jnp.sum(grad, axis=0, keepdims=True)


def unit_backward(grad, projected):
    rate = lax.rsqrt(jnp.sum(projected * projected, axis=-1, keepdims=True) + EMBED_EPS)
    unit = projected * rate
    return rate * (grad - unit * jnp.sum(grad * unit, axis=-1, keepdims=True))


def gelu_pair(f):
    phi = 0.5 + 0.5 * lax.erf(f * INV_SQRT_2)
    density = jnp.exp(-0.5 * (f * f)) * INV_SQRT_2PI
    return f * phi, phi + f * density


def segment_ends(lengths_ref):
    count = lengths_ref.shape[1]
    ends = []
    total = jnp.int32(0)
    for s in range(count):
        total = total + lengths_ref[0, s]
        ends.append(total)
    return ends


def longest_start(lengths_ref, longest):
    found = jnp.int32(0)
    start = jnp.int32(0)
    for s in range(lengths_ref.shape[1]):
        found = jnp.where(lengths_ref[0, s] == longest, start, found)
        start = start + lengths_ref[0, s]
    return found


def fill_bias(bias_ref, lengths_ref, ptok, qtok):
    half = ptok // 2
    ends = segment_ends(lengths_ref)
    first = longest_start(lengths_ref, half)

    def segments(place):
        token = place + half + first
        token = jnp.where(token >= ptok, token - ptok, token)
        seg = jnp.zeros_like(token)
        for end in ends:
            seg = seg + jnp.where(token >= end, 1, 0)
        return seg

    row_seg = segments(lax.broadcasted_iota(jnp.int32, (8, half), 1))[:1]
    for r0 in range(0, half, LANES):
        col = segments(lax.broadcasted_iota(jnp.int32, (LANES, LANES), 0) + r0)
        for c in range(0, half, LANES):
            bias_ref[r0 : r0 + LANES, c : c + LANES] = jnp.where(col == row_seg[:, c : c + LANES], 0.0, NEG_FILL)
    for c in range(0, qtok, LANES):
        for r0 in range(0, qtok, LANES):
            row = (lax.broadcasted_iota(jnp.int32, (LANES, LANES), 0) + r0) // QLEN
            col = (lax.broadcasted_iota(jnp.int32, (LANES, LANES), 1) + c) // QLEN
            bias_ref[half + r0 : half + r0 + LANES, c : c + LANES] = jnp.where(row == col, 0.0, NEG_FILL)


def spans(ptok, qtok):
    half = ptok // 2
    return ((0, half, None), (half, half, 0), (ptok, qtok, half))


def owner_place(me_ref, r, turned=False):
    first, second = (r >> 3) & 1, (r >> 2) & 1
    if turned:
        first, second = second, first
    core, x, y, z = me_ref[0] ^ (r >> 4), me_ref[1] ^ first, me_ref[2] ^ second, me_ref[3] ^ (r & 3)
    return pl.multiple_of((((y * 2 + x) * 2 + core) * 4 + z) * PIECE, PIECE)


def to_relative(me_ref, plain_ref, out_ref, turned=False):
    for r in range(32):
        out_ref[r * PIECE : (r + 1) * PIECE] = plain_ref[pl.ds(owner_place(me_ref, r, turned), PIECE), :]


def attention_forward_kernel(
    ptok,
    lengths_hbm,
    xp_hbm,
    xq_hbm,
    wq_hbm,
    wk_hbm,
    wv_hbm,
    wo_hbm,
    bq_hbm,
    bv_hbm,
    bo_hbm,
    q_ref,
    k_ref,
    v_ref,
    o_ref,
    lse_ref,
    x1_ref,
    rate1_ref,
    xt_ref,
    me_ref,
    x_scr,
    r1_scr,
    bias_scr,
    logs_scr,
    lengths_ref,
    xp_ref,
    wq_ref,
    wk_ref,
    wv_ref,
    wo_ref,
    bq_ref,
    bv_ref,
    bo_ref,
    sems,
):
    step = pl.program_id(0)
    rows = x_scr.shape[0]
    qtok = rows - ptok

    @pl.when(step == 0)
    def _():
        pairs = (
            (lengths_hbm, lengths_ref),
            (xp_hbm, xp_ref),
            (xq_hbm, x_scr.at[pl.ds(ptok, qtok)]),
            (bo_hbm, bo_ref),
            (wq_hbm, wq_ref),
            (bq_hbm, bq_ref),
            (wk_hbm, wk_ref),
            (wv_hbm, wv_ref),
            (bv_hbm, bv_ref),
            (wo_hbm, wo_ref),
        )
        copies = [pltpu.make_async_copy(held, ref, sems.at[i]) for i, (held, ref) in enumerate(pairs)]
        for copy in copies:
            copy.start()
        grp = lax.axis_index("grp")
        me_ref[0] = grp & 1
        me_ref[1] = (grp >> 1) & 1
        me_ref[2] = (grp >> 2) & 1
        me_ref[3] = lax.axis_index("psg")
        for copy in copies:
            copy.wait()
        first = longest_start(lengths_ref, ptok // 2)
        source = xp_ref[...]
        for r0 in range(0, ptok, LANES):
            token = lax.broadcasted_iota(jnp.int32, (LANES, ptok), 0) + (r0 + first)
            token = jnp.where(token >= ptok, token - ptok, token)
            pick = jnp.where(lax.broadcasted_iota(jnp.int32, (LANES, ptok), 1) == token, 1.0, 0.0).astype(BF16)
            x_scr[r0 : r0 + LANES] = dot(pick, source).astype(BF16)
        x = x_scr[...]
        xt_ref[...] = jnp.transpose(x)
        r1_scr[...] = x.astype(F32) + bo_ref[...]
        fill_bias(bias_scr, lengths_ref, ptok, qtok)

    x = x_scr[...]
    quad = pl.ds(pl.multiple_of(step * QLANES, QLANES), QLANES)
    q_ref[:, quad] = (dot(x, wq_ref[:, quad]) + bq_ref[:, quad]).astype(BF16) * BF16(HEAD**-0.5)
    k_ref[:, quad] = dot(x, wk_ref[:, quad]).astype(BF16)
    v_ref[:, quad] = (dot(x, wv_ref[:, quad]) + bv_ref[:, quad]).astype(BF16)
    logs_scr[...] = jnp.zeros_like(logs_scr)

    for pair in range(QUAD // 2):
        lanes = pl.ds(pl.multiple_of(step * QLANES + pair * LANES, LANES), LANES)
        for base, size, bias_row in spans(ptok, qtok):
            block = min(RB, size)
            for r0 in range(base, base + size, block):
                lane = lax.broadcasted_iota(jnp.int32, (block, LANES), 1)
                q = q_ref[r0 : r0 + block, lanes]
                keys = k_ref[base : base + size, lanes]
                values = v_ref[base : base + size, lanes]
                mixed = []
                for side in range(2):
                    inside = (lane < HEAD) if side == 0 else (lane >= HEAD)
                    s = dot_t(jnp.where(inside, q, BF16(0)), keys)
                    parts = []
                    totals = []
                    peaks = []
                    for i in range(0, block, ASLICE):
                        part = s[i : i + ASLICE]
                        if bias_row is not None:
                            at = bias_row + r0 - base + i
                            part = part + bias_scr[at : at + ASLICE, :size]
                        peak = jnp.max(part, axis=-1, keepdims=True)
                        e = jnp.exp(part - peak)
                        totals.append(jnp.sum(e, axis=-1, keepdims=True))
                        peaks.append(peak)
                        parts.append(e.astype(BF16))
                    total = jnp.concatenate(totals, axis=0)
                    mixed.append(dot(jnp.concatenate(parts, axis=0), values) * (1.0 / total))
                    log = jnp.concatenate(peaks, axis=0) + jnp.log(total)
                    logs_scr[r0 : r0 + block] = jnp.where(
                        lane == 2 * pair + side, log, logs_scr[r0 : r0 + block]
                    )
                o_ref[r0 : r0 + block, lanes] = jnp.where(lane < HEAD, mixed[0], mixed[1]).astype(BF16)
    lse_ref[step] = jnp.transpose(logs_scr[...])[:8]
    r1_scr[...] += dot(o_ref[:, quad], wo_ref[quad, :])

    @pl.when(step == pl.num_programs(0) - 1)
    def _():
        scaled, rate = norm_stats(r1_scr[...])
        x1_ref[...] = scaled
        rate1_ref[...] = jnp.broadcast_to(rate, rate1_ref.shape)


def spec(shape, index):
    return pl.BlockSpec(shape, index)


def whole(array):
    return pl.BlockSpec(memory_space=pltpu.VMEM)


def in_hbm(array):
    return pltpu.with_memory_space_constraint(array, pltpu.HBM)


def const(array):
    nd = len(array.shape)
    return pl.BlockSpec(array.shape, lambda *_: (0,) * nd)


def smem():
    return pl.BlockSpec(memory_space=pltpu.SMEM)


def cost(micros):
    return pl.CostEstimate(flops=int(micros * 1e9), bytes_accessed=int(micros * 1e6), transcendentals=0)


def shaped(shape, dtype):
    return jax.ShapeDtypeStruct(shape, dtype)


def params(grid_rank, mebibytes):
    return pltpu.CompilerParams(
        dimension_semantics=("arbitrary",) * grid_rank, vmem_limit_bytes=int(mebibytes * 1024 * 1024)
    )


def attention_forward(lengths, xp, xq, wq, bq, wk, wv, bv, wo, bo):
    ptok, width = xp.shape
    qtok = xq.shape[0]
    rows = ptok + qtok
    quads = HEADS // QUAD
    half = ptok // 2
    return pl.pallas_call(
        functools.partial(attention_forward_kernel, ptok),
        grid=(quads,),
        in_specs=[pl.BlockSpec(memory_space=pltpu.HBM)] * 10,
        out_specs=[whole(None)] * 8 + [smem()],
        out_shape=[shaped((rows, width), BF16)] * 4
        + [
            shaped((quads, 8, rows), F32),
            shaped((rows, width), F32),
            shaped((rows, LANES), F32),
            shaped((width, rows), BF16),
            shaped((4,), jnp.int32),
        ],
        scratch_shapes=[
            pltpu.VMEM((rows, width), BF16),
            pltpu.VMEM((rows, width), F32),
            pltpu.VMEM((half + qtok, half), F32),
            pltpu.VMEM((rows, LANES), F32),
            pltpu.SMEM(lengths.shape, jnp.int32),
            pltpu.VMEM(xp.shape, BF16),
        ]
        + [pltpu.VMEM((width, width), BF16)] * 4
        + [pltpu.VMEM((1, width), F32)] * 3
        + [pltpu.SemaphoreType.DMA((10,))],
        compiler_params=params(1, 26),
        cost_estimate=cost(20),
        name="attention_forward",
    )(*[in_hbm(a) for a in (lengths, xp, xq, wq, wk, wv, wo, bq, bv, bo)])


def ffn_forward_kernel(
    aliased,
    rb,
    offset,
    x1_ref,
    g1_ref,
    s1_ref,
    wi_ref,
    bi_ref,
    wo_ref,
    bo_ref,
    g2_ref,
    s2_ref,
    wp_ref,
    *rest,
):
    rest = rest[aliased:]
    u_ref, d_ref, x2_ref, rate2_ref, e_ref, emb_ref, h1_scr, r2_scr = rest
    step = pl.program_id(0)
    rows = h1_scr.shape[0]
    own = slice(offset, offset + rows)
    chunk = pl.ds(pl.multiple_of(step * FCHUNK, FCHUNK), FCHUNK)

    @pl.when(step == 0)
    def _():
        h1 = x1_ref[own] * g1_ref[...] + s1_ref[...]
        h1_scr[...] = h1.astype(BF16)
        r2_scr[...] = h1 + bo_ref[...]

    for r in range(0, rows, rb):
        f = dot(h1_scr[r : r + rb], wi_ref[...])
        bias = bi_ref[...]
        for i in range(0, rb, SLICE):
            u, d = gelu_pair(f[i : i + SLICE] + bias)
            at = offset + r + i
            u_ref[at : at + SLICE, chunk] = u.astype(BF16)
            d_ref[at : at + SLICE, chunk] = d.astype(BF16)
        r2_scr[r : r + rb] += dot(u_ref[offset + r : offset + r + rb, chunk], wo_ref[...])

    @pl.when(step == pl.num_programs(0) - 1)
    def _():
        scaled, rate = norm_stats(r2_scr[...])
        x2_ref[own] = scaled
        rate2_ref[own] = jnp.broadcast_to(rate, (rows, LANES))
        h2 = (scaled * g2_ref[...] + s2_ref[...]).astype(BF16)
        e = dot(h2, wp_ref[...])
        e_ref[own] = e
        size = jnp.sum(e * e, axis=-1, keepdims=True)
        emb_ref[...] = (e * lax.rsqrt(size + EMBED_EPS)).astype(BF16)


def ffn_forward(count, offset, total, x1, g1, s1, wi, bi, wo, bo, g2, s2, wp, previous):
    width = x1.shape[1]
    ff = wi.shape[1]
    dim = wp.shape[1]
    first = 10
    held = list(previous)
    return pl.pallas_call(
        functools.partial(ffn_forward_kernel, len(held), min(RB, count), offset),
        grid=(ff // FCHUNK,),
        in_specs=[
            whole(x1),
            const(g1),
            const(s1),
            spec((width, FCHUNK), lambda c: (0, c)),
            spec((1, FCHUNK), lambda c: (0, c)),
            spec((FCHUNK, width), lambda c: (c, 0)),
            const(bo),
            const(g2),
            const(s2),
            const(wp),
        ]
        + [whole(None)] * len(held),
        out_specs=[whole(None)] * 6,
        out_shape=[
            shaped((total, ff), BF16),
            shaped((total, ff), BF16),
            shaped((total, width), F32),
            shaped((total, LANES), F32),
            shaped((total, dim), F32),
            shaped((count, dim), BF16),
        ],
        scratch_shapes=[
            pltpu.VMEM((count, width), BF16),
            pltpu.VMEM((count, width), F32),
        ],
        input_output_aliases={first + i: i for i in range(len(held))},
        compiler_params=params(1, 16),
        cost_estimate=cost(12 if count > 256 else 4),
        name="ffn_forward",
    )(x1, g1, s1, in_hbm(wi), bi, in_hbm(wo), bo, g2, s2, wp, *held)


def passage_member(lengths_ref, rows):
    ends = segment_ends(lengths_ref)
    lane = lax.broadcasted_iota(jnp.int32, (8, LANES), 1)
    low = jnp.full((8, LANES), rows, jnp.int32)
    high = jnp.zeros((8, LANES), jnp.int32)
    start = jnp.int32(0)
    for s, end in enumerate(ends):
        low = jnp.where(lane == s, start, low)
        high = jnp.where(lane == s, end, high)
        start = end
    token = lax.broadcasted_iota(jnp.int32, (rows, LANES), 0) + longest_start(lengths_ref, rows // 2)
    token = jnp.where(token >= rows, token - rows, token)
    inside = (token >= low[:1]) & (token < high[:1])
    return jnp.where(inside, 1.0, 0.0).astype(BF16)


def soft_match(group, pass_embed):
    return jnp.exp(SHARPNESS * dot_t(group, pass_embed) - SHARPNESS)


def score_kernel(psg, count, lengths_ref, emb_ref, *rest):
    group_refs = rest[:psg]
    score_ref, pooled_ref = rest[psg:]
    member = passage_member(lengths_ref, emb_ref.shape[0])
    group = jnp.concatenate([ref[...] for ref in group_refs], axis=0)
    matched = soft_match(group, emb_ref[...])
    pooled = two_part_dot(matched, member)
    lane = lax.broadcasted_iota(jnp.int32, pooled.shape, 1)
    pooled = jnp.where(lane < count, pooled, 1.0)
    pooled_ref[...] = pooled
    smooth = 1.0 + jnp.log(pooled) * (1.0 / SHARPNESS)
    queries = pooled.shape[0] // QLEN
    score_ref[...] = SCORE_SCALE * jnp.sum(smooth.reshape(queries, QLEN, LANES), axis=1)


def score(lengths, emb, groups):
    psg = len(groups)
    tokens = sum(g.shape[0] for g in groups)
    return pl.pallas_call(
        functools.partial(score_kernel, psg, lengths.shape[1]),
        in_specs=[smem()] + [pl.BlockSpec(memory_space=pltpu.VMEM)] * (1 + psg),
        out_shape=[shaped((tokens // QLEN, LANES), F32), shaped((tokens, LANES), F32)],
        compiler_params=params(0, 8),
        cost_estimate=cost(3),
        name="score",
    )(lengths, emb, *groups)


def loss_kernel(psg, count, where_ref, lengths_ref, positives_ref, pooled_ref, emb_ref, *rest):
    group_refs = rest[:psg]
    score_refs = rest[psg : 2 * psg]
    loss_ref, own_ref = rest[2 * psg : 2 * psg + 2]
    away_refs = rest[2 * psg + 2 : 3 * psg + 1]
    grad_ref = rest[3 * psg + 1]
    position = where_ref[3]
    queries = score_refs[0].shape[0]
    each = queries // psg
    lane = lax.broadcasted_iota(jnp.int32, (queries, LANES), 1)
    row = lax.broadcasted_iota(jnp.int32, (queries, LANES), 0)
    valid = lane < count
    blocks = []
    for e in range(psg):
        found = score_refs[e][...]
        found = jnp.concatenate(
            [found[((d - e) % psg) * each : ((d - e) % psg + 1) * each] for d in range(psg)], axis=0
        )
        blocks.append(jnp.where(valid, found, -jnp.inf))
    target = jnp.zeros((queries, LANES), jnp.int32)
    for d in range(psg):
        for j in range(each):
            chosen = positives_ref[lax.rem(position + d, psg) * each + j]
            target = jnp.where(row == d * each + j, chosen, target)
    peak = blocks[0]
    for found in blocks[1:]:
        peak = jnp.maximum(peak, found)
    peak = jnp.max(peak, axis=-1, keepdims=True)
    total = jnp.zeros((queries, 1), F32)
    picked = jnp.zeros((queries, 1), F32)
    for e in range(psg):
        owner = lax.rem(position + e, psg)
        hit = (target == owner * count + lane) & valid
        total = total + jnp.sum(jnp.exp(blocks[e] - peak), axis=-1, keepdims=True)
        picked = picked + jnp.sum(jnp.where(hit, blocks[e], 0.0), axis=-1, keepdims=True)
        if e == 0:
            own_hit = jnp.where(hit, 1.0, 0.0)
    log_total = peak + jnp.log(total)
    losses = jnp.broadcast_to(log_total - picked, (queries, LANES))
    place = lax.rem(position + row // each, psg) * each + row % each
    losses = jnp.sum(jnp.where(lane == place, losses, 0.0), axis=0, keepdims=True)
    loss_ref[...] = losses[:, :queries]
    grad = jnp.where(valid, jnp.exp(blocks[0] - log_total) - own_hit, 0.0) * SCORE_SCALE
    tokens = queries * QLEN
    grad = jnp.broadcast_to(grad[:, None, :], (queries, QLEN, LANES)).reshape(tokens, LANES)
    grad = grad / pooled_ref[...]
    member = passage_member(lengths_ref, emb_ref.shape[0])
    high = grad.astype(BF16)
    rest_low = (grad - high.astype(F32)).astype(BF16)
    spread = dot_t(high, member) + dot_t(rest_low, member)
    group = jnp.concatenate([ref[...] for ref in group_refs], axis=0)
    low = (soft_match(group, emb_ref[...]) * spread).astype(BF16)
    group_grad = dot(low, emb_ref[...])
    each_tokens = tokens // psg
    own_ref[...] = group_grad[:each_tokens]
    for d in range(1, psg):
        away_refs[d - 1][...] = group_grad[d * each_tokens : (d + 1) * each_tokens].astype(BF16)
    grad_ref[...] = jnp.transpose(dot(jnp.transpose(group), low))


def loss_and_grads(position, lengths, positives, pooled, emb, groups, scores):
    psg = len(groups)
    queries = scores[0].shape[0]
    tokens, dim = groups[0].shape
    vmem = pl.BlockSpec(memory_space=pltpu.VMEM)
    return pl.pallas_call(
        functools.partial(loss_kernel, psg, lengths.shape[1]),
        in_specs=[smem(), smem(), smem()] + [vmem] * (2 + 2 * psg),
        out_shape=[shaped((1, queries), F32), shaped((tokens, dim), F32)]
        + [shaped((tokens, dim), BF16)] * (psg - 1)
        + [shaped(emb.shape, F32)],
        compiler_params=params(0, 8),
        cost_estimate=cost(3),
        name="loss_and_grads",
    )(position, lengths, positives, pooled, emb, *groups, *scores)


def head_backward(grad_embed, e, x2, rate2, wp, g2, s2):
    low = unit_backward(grad_embed, e).astype(BF16)
    grad_h2 = dot_t(low, wp)
    grad_r2, gain_term, shift_term = norm_backward(grad_h2, x2, rate2[:, :1], g2)
    h2 = (x2 * g2 + s2).astype(BF16)
    return grad_r2, gain_term, shift_term, dot(jnp.transpose(low), h2)


def passage_head_kernel(
    grad_ref, e_ref, x2_ref, rate2_ref, wp_ref, g2_ref, s2_ref, gr2_ref, vec_ref, proj_ref
):
    ptok = grad_ref.shape[0]
    grad_r2, gain_term, shift_term, proj = head_backward(
        grad_ref[...], e_ref[:ptok], x2_ref[:ptok], rate2_ref[:ptok], wp_ref[...], g2_ref[...], s2_ref[...]
    )
    gr2_ref[...] = grad_r2
    vec_ref[...] = jnp.zeros_like(vec_ref)
    vec_ref[0:1] = gain_term
    vec_ref[1:2] = shift_term
    proj_ref[...] = proj


def passage_head(grad, e, x2, rate2, wp, g2, s2):
    ptok, dim = grad.shape
    width = x2.shape[1]
    return pl.pallas_call(
        passage_head_kernel,
        grid=(1,),
        in_specs=[
            whole(grad),
            whole(e),
            whole(x2),
            whole(rate2),
            const(wp),
            const(g2),
            const(s2),
        ],
        out_specs=[whole(None)] * 3,
        out_shape=[shaped((ptok, width), F32), shaped((8, width), F32), shaped((dim, width), F32)],
        compiler_params=params(1, 10),
        cost_estimate=cost(4),
        name="passage_head",
    )(grad, e, x2, rate2, wp, g2, s2)


def fixed(shape):
    return pl.BlockSpec(memory_space=pltpu.VMEM)


def ffn_backward_kernel(
    psg,
    me_ref,
    gr2p_ref,
    vec_ref,
    proj_ref,
    own_ref,
    *rest,
):
    away_refs = rest[: psg - 1]
    (
        e_ref,
        x2_ref,
        rate2_ref,
        wp_ref,
        g2_ref,
        s2_ref,
        x1_ref,
        g1_ref,
        s1_ref,
        wi_ref,
        wo_ref,
        u_ref,
        d_ref,
        dproj_ref,
        dvec_ref,
        dbi_ref,
        gh1_ref,
        keep_i_ref,
        send_i_ref,
        keep_o_ref,
        send_o_ref,
        gz_scr,
        turn_scr,
        gzt_scr,
        h1t_scr,
    ) = rest[psg - 1 :]
    step = pl.program_id(0)
    ptok = gr2p_ref.shape[0]

    @pl.when(step == 0)
    def _():
        grad = own_ref[...]
        for ref in away_refs:
            grad = grad + ref[...].astype(F32)
        grad_r2, gain_term, shift_term, proj = head_backward(
            grad, e_ref[ptok:], x2_ref[ptok:], rate2_ref[ptok:], wp_ref[...], g2_ref[...], s2_ref[...]
        )
        dproj_ref[...] = jnp.transpose(proj_ref[...] + proj).astype(BF16)
        gr2p = gr2p_ref[...]
        gh1_ref[:ptok] = gr2p
        gh1_ref[ptok:] = grad_r2
        low_p = gr2p.astype(BF16)
        low_q = grad_r2.astype(BF16)
        gz_scr[:ptok] = low_p
        gz_scr[ptok:] = low_q
        dvec_ref[...] = jnp.zeros_like(dvec_ref)
        dvec_ref[0:1] = vec_ref[0:1] + gain_term
        dvec_ref[1:2] = vec_ref[1:2] + shift_term
        dvec_ref[2:3] = jnp.sum(low_p.astype(F32), axis=0, keepdims=True) + jnp.sum(
            low_q.astype(F32), axis=0, keepdims=True
        )
        turn_scr[...] = jnp.transpose((x1_ref[...] * g1_ref[...] + s1_ref[...]).astype(BF16))
        to_relative(me_ref, turn_scr, h1t_scr)
        turn_scr[...] = jnp.transpose(gz_scr[...])
        to_relative(me_ref, turn_scr, gzt_scr, turned=True)

    chunk = pl.ds(pl.multiple_of(step * FCHUNK, FCHUNK), FCHUNK)
    gz = gz_scr[...]
    grad_active = dot_t(gz, wo_ref[...])
    grad_inner = (grad_active * d_ref[:, chunk].astype(F32)).astype(BF16)
    dbi_ref[:, chunk] = jnp.sum(grad_inner.astype(F32), axis=0, keepdims=True)
    gh1_ref[...] += dot_t(grad_inner, wi_ref[...])
    half = keep_i_ref.shape[0]
    for ref, start in ((keep_i_ref, 0), (send_i_ref, half)):
        ref[:, chunk] = dot(h1t_scr[start : start + half], grad_inner).astype(BF16)
    for ref, start in ((keep_o_ref, 0), (send_o_ref, half)):
        ref[:, chunk] = dot(gzt_scr[start : start + half], u_ref[:, chunk]).astype(BF16)


def ffn_backward(me, gr2p, vec, proj, own, aways, e, x2, rate2, wp, g2, s2, x1, g1, s1, wi, wo, u, d):
    ptok, width = gr2p.shape
    rows = x1.shape[0]
    dim = wp.shape[1]
    ff = wi.shape[1]
    return pl.pallas_call(
        functools.partial(ffn_backward_kernel, 1 + len(aways)),
        grid=(ff // FCHUNK,),
        in_specs=[smem(), whole(gr2p), whole(vec), whole(proj), whole(own)]
        + [whole(a) for a in aways]
        + [
            whole(e),
            whole(x2),
            whole(rate2),
            const(wp),
            const(g2),
            const(s2),
            whole(x1),
            const(g1),
            const(s1),
            spec((width, FCHUNK), lambda c: (0, c)),
            spec((FCHUNK, width), lambda c: (c, 0)),
            whole(u),
            whole(d),
        ],
        out_specs=[
            fixed((width, dim)),
            fixed((8, width)),
            fixed((1, ff)),
            fixed((rows, width)),
        ]
        + [whole(None)] * 4,
        out_shape=[
            shaped((width, dim), BF16),
            shaped((8, width), F32),
            shaped((1, ff), F32),
            shaped((rows, width), F32),
        ]
        + [shaped((width // 2, ff), BF16)] * 4,
        scratch_shapes=[
            pltpu.VMEM((rows, width), BF16),
            pltpu.VMEM((width, rows), BF16),
            pltpu.VMEM((width, rows), BF16),
            pltpu.VMEM((width, rows), BF16),
        ],
        compiler_params=params(1, 20),
        cost_estimate=cost(15),
        name="ffn_backward",
    )(me, gr2p, vec, proj, own, *aways, e, x2, rate2, wp, g2, s2, x1, g1, s1, in_hbm(wi), in_hbm(wo), u, d)


def put_vector(wave_ref, row, vector):
    for i in range(vector.shape[1] // LANES):
        wave_ref[row + i : row + i + 1] = vector[:, i * LANES : (i + 1) * LANES]
    return row + vector.shape[1] // LANES


def take_vector(wave_ref, row, column, out_ref):
    size = out_ref.shape[1]
    for i in range(size // LANES):
        out_ref[:, i * LANES : (i + 1) * LANES] = wave_ref[row + i : row + i + 1, column : column + LANES].astype(
            F32
        )
    return row + size // LANES


def units(pair, ptok, qtok):
    for index, (base, size, bias_row) in enumerate(spans(ptok, qtok)):
        block = min(RB, size)
        place = 0
        for r0 in range(base, base + size, block):
            for side in range(2):
                yield index, base, size, bias_row, r0, block, side, place
                place += block


def one_head(block, side, rows):
    lane = lax.broadcasted_iota(jnp.int32, (block, LANES), 1)
    return jnp.where((lane < HEAD) if side == 0 else (lane >= HEAD), rows, BF16(0))


def probabilities_kernel(ptok, lengths_ref, q_ref, k_ref, lse_ref, p_ref, pq_ref, bias_scr):
    qtok = q_ref.shape[0] - ptok

    @pl.when(pl.program_id(0) == 0)
    def _():
        fill_bias(bias_scr, lengths_ref, ptok, qtok)

    step = pl.program_id(0)
    for pair in range(QUAD // 2):
        lanes = pl.ds(pl.multiple_of(step * QLANES + pair * LANES, LANES), LANES)
        for index, base, size, bias_row, r0, block, side, place in units(pair, ptok, qtok):
            h = 2 * pair + side
            s = dot_t(k_ref[base : base + size, lanes], one_head(block, side, q_ref[r0 : r0 + block, lanes]))
            lse = lse_ref[step, h : h + 1, r0 : r0 + block]
            for i in range(0, size, ASLICE):
                part = s[i : i + ASLICE]
                if bias_row is not None:
                    part = part + bias_scr[bias_row + i : bias_row + i + ASLICE, r0 - base : r0 - base + block]
                p = jnp.exp(part - lse).astype(BF16)
                if index < 2:
                    p_ref[step, 2 * pair + index, i : i + ASLICE, place : place + block] = p
                else:
                    pq_ref[step, pair, i : i + ASLICE, place : place + block] = p


def probabilities(lengths, q, k, lse, ptok):
    rows, width = q.shape
    quads = HEADS // QUAD
    half, qtok = ptok // 2, rows - ptok
    return pl.pallas_call(
        functools.partial(probabilities_kernel, ptok),
        grid=(quads,),
        in_specs=[smem(), whole(q), whole(k), whole(lse)],
        out_specs=[whole(None), whole(None)],
        out_shape=[
            shaped((quads, QUAD, half, 2 * half), BF16),
            shaped((quads, QUAD // 2, qtok, 2 * qtok), BF16),
        ],
        scratch_shapes=[pltpu.VMEM((half + qtok, half), F32)],
        compiler_params=params(1, 10),
        cost_estimate=cost(8),
        name="probabilities",
    )(lengths, q, k, lse)


def first_norm_kernel(gh1_ref, x1_ref, rate1_ref, g1_ref, wo_ref, gr1_ref, go_ref, vec_ref):
    grad_r1, gain_term, shift_term = norm_backward(gh1_ref[...], x1_ref[...], rate1_ref[:, :1], g1_ref[...])
    gr1_ref[...] = grad_r1
    low = grad_r1.astype(BF16)
    vec_ref[...] = jnp.zeros_like(vec_ref)
    vec_ref[0:1] = gain_term
    vec_ref[1:2] = shift_term
    vec_ref[2:3] = jnp.sum(low.astype(F32), axis=0, keepdims=True)
    go_ref[...] = dot_t(low, wo_ref[...]).astype(BF16)


def first_norm(gh1, x1, rate1, g1, wo):
    rows, width = x1.shape
    return pl.pallas_call(
        first_norm_kernel,
        grid=(1,),
        in_specs=[whole(gh1), whole(x1), whole(rate1), const(g1), const(wo)],
        out_specs=[whole(None)] * 3,
        out_shape=[shaped((rows, width), F32), shaped((rows, width), BF16), shaped((8, width), F32)],
        compiler_params=params(1, 9),
        cost_estimate=cost(4),
        name="first_norm",
    )(gh1, x1, rate1, g1, wo)


def heads_backward_kernel(
    quad,
    ptok,
    p_ref,
    pq_ref,
    q_ref,
    k_ref,
    v_ref,
    o_ref,
    go_ref,
    gq_ref,
    gk_ref,
    gv_ref,
    dd_scr,
    gqt_scr,
    qm_scr,
    gm_scr,
    gs_scr,
    kt_scr,
):
    qtok = q_ref.shape[0] - ptok

    own = slice(quad * QLANES, (quad + 1) * QLANES)
    product = go_ref[:, own].astype(F32) * o_ref[:, own].astype(F32)
    ones = jnp.where(
        lax.broadcasted_iota(jnp.int32, (16, QLANES), 1) // HEAD
        == lax.broadcasted_iota(jnp.int32, (16, QLANES), 0),
        1.0,
        0.0,
    ).astype(BF16)
    high = product.astype(BF16)
    dd_scr[...] = dot_t(ones, high) + dot_t(ones, (product - high.astype(F32)).astype(BF16))
    kt_scr[...] = jnp.transpose(k_ref[:, own])
    for pair in range(QUAD // 2):
        inner = slice(pair * LANES, (pair + 1) * LANES)
        lanes = slice(quad * QLANES + pair * LANES, quad * QLANES + (pair + 1) * LANES)
        last = None
        for index, base, size, bias_row, r0, block, side, place in units(pair, ptok, qtok):
            buffer = (3 * pair + index) % 2
            h = 2 * pair + side
            qm_scr[buffer, place : place + block] = one_head(block, side, q_ref[r0 : r0 + block, lanes])
            gm = one_head(block, side, go_ref[r0 : r0 + block, lanes])
            gm_scr[buffer, place : place + block] = gm
            grad_prob = dot_t(v_ref[base : base + size, lanes], gm)
            dd = dd_scr[h : h + 1, r0 : r0 + block]
            p_at = p_ref.at[quad, 2 * pair + index] if index < 2 else pq_ref.at[quad, pair]
            for i in range(0, size, ASLICE):
                p = p_at[i : i + ASLICE, place : place + block].astype(F32)
                gs = p * (grad_prob[i : i + ASLICE] - dd)
                gs_scr[buffer, i : i + ASLICE, place : place + block] = gs.astype(BF16)
            gqt_scr[h * HEAD : (h + 1) * HEAD, r0 : r0 + block] = dot(
                kt_scr[h * HEAD : (h + 1) * HEAD, base : base + size],
                gs_scr[buffer, :size, place : place + block],
            )
            end = place + block
            if end == 2 * size:
                gv_ref[base : base + size, inner] = dot(p_at[...], gm_scr[buffer, :end]).astype(BF16)
                gk_ref[base : base + size, inner] = dot(gs_scr[buffer, :size, :end], qm_scr[buffer, :end]).astype(
                    BF16
                )
    gq_ref[...] = (jnp.transpose(gqt_scr[...]) * (HEAD**-0.5)).astype(BF16)


def heads_backward(quad, p, pq, q, k, v, o, go, ptok):
    rows, width = q.shape
    half = ptok // 2
    low = lambda *shape: pltpu.VMEM(shape, BF16)
    return pl.pallas_call(
        functools.partial(heads_backward_kernel, quad, ptok),
        grid=(1,),
        in_specs=[whole(None)] * 7,
        out_specs=[whole(None)] * 3,
        out_shape=[shaped((rows, QLANES), BF16)] * 3,
        scratch_shapes=[
            pltpu.VMEM((16, rows), F32),
            pltpu.VMEM((QLANES, rows), F32),
            low(2, 4 * RB, LANES),
            low(2, 4 * RB, LANES),
            low(2, half, 4 * RB),
            low(QLANES, rows),
        ],
        compiler_params=params(1, 16),
        cost_estimate=cost(10),
        name="heads_backward",
    )(p, pq, q, k, v, o, go)


def weights_kernel(
    ptok,
    me_ref,
    gr1_ref,
    o_ref,
    xt_ref,
    gq0_ref,
    gk0_ref,
    gv0_ref,
    gq1_ref,
    gk1_ref,
    gv1_ref,
    dproj_ref,
    vec1_ref,
    vec2_ref,
    dbi_ref,
    wq_ref,
    wk_ref,
    wv_ref,
    keep_ref,
    send_ref,
    gp_ref,
    gq_ref,
    turn_scr,
    xt_scr,
    ot_scr,
    lines_scr,
    tail_scr,
):
    half_rows = keep_ref.shape[0]
    width = gr1_ref.shape[1]
    gr1 = gr1_ref[...]
    to_relative(me_ref, xt_ref, xt_scr)
    turn_scr[...] = jnp.transpose(o_ref[...])
    to_relative(me_ref, turn_scr, ot_scr)
    joined = [
        jnp.concatenate([left[...], right[...]], axis=1)
        for left, right in ((gq0_ref, gq1_ref), (gk0_ref, gk1_ref), (gv0_ref, gv1_ref))
    ]
    low = gr1.astype(BF16)
    for ref, start in ((keep_ref, 0), (send_ref, half_rows)):
        for i, grad in enumerate(joined):
            ref[:, i * width : (i + 1) * width] = dot(xt_scr[start : start + half_rows], grad).astype(BF16)
        ref[:, 3 * width : 4 * width] = dot(ot_scr[start : start + half_rows], low).astype(BF16)
    gin = gr1 + dot_t(joined[0], wq_ref[...]) + dot_t(joined[1], wk_ref[...]) + dot_t(joined[2], wv_ref[...])
    gp_ref[...] = gin[:ptok].astype(BF16)
    gq_ref[...] = gin[ptok:].astype(BF16)
    row = 0
    for vector in (
        vec2_ref[0:1],
        vec2_ref[1:2],
        vec2_ref[2:3],
        vec1_ref[0:1],
        vec1_ref[1:2],
        vec1_ref[2:3],
        dbi_ref[...],
        jnp.sum(joined[0].astype(F32), axis=0, keepdims=True),
        jnp.sum(joined[2].astype(F32), axis=0, keepdims=True),
    ):
        row = put_vector(lines_scr, row, vector)
    lines_scr[row:] = jnp.zeros((lines_scr.shape[0] - row, LANES), F32)
    dim = dproj_ref.shape[1]
    tail_scr[:, :dim] = dproj_ref[...]
    tail_scr[:, dim:] = lines_scr[...].astype(BF16)
    for r in range(32):
        ref = keep_ref if r < 16 else send_ref
        at = (r % 16) * PIECE
        ref[at : at + PIECE, 4 * width :] = tail_scr[pl.ds(owner_place(me_ref, r), PIECE), :]


def weights(me, gr1, o, xt, first, second, dproj, vec1, vec2, dbi, wq, wk, wv, ptok):
    rows, width = gr1.shape
    lanes = 4 * width + dproj.shape[1] + LANES
    low = lambda *shape: pltpu.VMEM(shape, BF16)
    return pl.pallas_call(
        functools.partial(weights_kernel, ptok),
        grid=(1,),
        in_specs=[smem()] + [whole(None)] * 16,
        out_specs=[whole(None)] * 4,
        out_shape=[
            shaped((width // 2, lanes), BF16),
            shaped((width // 2, lanes), BF16),
            shaped((ptok, width), BF16),
            shaped((rows - ptok, width), BF16),
        ],
        scratch_shapes=[
            low(width, rows),
            low(width, rows),
            low(width, rows),
            pltpu.VMEM((width, LANES), F32),
            low(width, dproj.shape[1] + LANES),
        ],
        compiler_params=params(1, 16),
        cost_estimate=cost(6),
        name="weights",
    )(me, gr1, o, xt, *first, *second, dproj, vec1, vec2, dbi, wq, wk, wv)


def from_relative(me_ref, kept_ref, other_ref, wave_ref, turned=False):
    for r in range(32):
        ref = kept_ref if r < 16 else other_ref
        at = (r % 16) * PIECE
        wave_ref[pl.ds(owner_place(me_ref, r, turned), PIECE), :] = ref[at : at + PIECE]


def unpack_ffn_kernel(
    me_ref, kept_i_ref, other_i_ref, kept_o_ref, other_o_ref, dwi_ref, dwo_ref, wave_i_scr, wave_o_scr
):
    from_relative(me_ref, kept_i_ref, other_i_ref, wave_i_scr)
    from_relative(me_ref, kept_o_ref, other_o_ref, wave_o_scr, turned=True)
    dwi_ref[...] = wave_i_scr[...].astype(F32)
    dwo_ref[...] = jnp.transpose(wave_o_scr[...].astype(F32))


def unpack_ffn(me, *halves):
    half, ff = halves[0].shape
    width = 2 * half
    return pl.pallas_call(
        unpack_ffn_kernel,
        grid=(ff // FCHUNK,),
        in_specs=[smem()] + [spec((half, FCHUNK), lambda c: (0, c))] * 4,
        out_specs=[
            spec((width, FCHUNK), lambda c: (0, c)),
            spec((FCHUNK, width), lambda c: (c, 0)),
        ],
        out_shape=[shaped((width, ff), F32), shaped((ff, width), F32)],
        scratch_shapes=[pltpu.VMEM((width, FCHUNK), BF16)] * 2,
        compiler_params=params(1, 16),
        cost_estimate=cost(6),
        name="unpack_ffn",
    )(me, *halves)


def unpack_attention_kernel(
    me_ref,
    kept_ref,
    other_ref,
    dwq_ref,
    dwk_ref,
    dwv_ref,
    dout_ref,
    dproj_ref,
    g2_ref,
    s2_ref,
    bo_ref,
    g1_ref,
    s1_ref,
    bout_ref,
    bi_ref,
    bq_ref,
    bv_ref,
    wave_scr,
):
    from_relative(me_ref, kept_ref, other_ref, wave_scr)
    column = 0
    for ref in (dwq_ref, dwk_ref, dwv_ref, dout_ref, dproj_ref):
        ref[...] = wave_scr[:, column : column + ref.shape[1]].astype(F32)
        column += ref.shape[1]
    row = 0
    for ref in (g2_ref, s2_ref, bo_ref, g1_ref, s1_ref, bout_ref, bi_ref, bq_ref, bv_ref):
        row = take_vector(wave_scr, row, column, ref)


def unpack_attention(me, kept, other, width, dim, ff):
    vmem = pl.BlockSpec(memory_space=pltpu.VMEM)
    return pl.pallas_call(
        unpack_attention_kernel,
        in_specs=[smem()] + [vmem] * 2,
        out_shape=[shaped((width, width), F32)] * 4
        + [shaped((width, dim), F32)]
        + [shaped((1, width), F32)] * 6
        + [shaped((1, ff), F32)]
        + [shaped((1, width), F32)] * 2,
        scratch_shapes=[pltpu.VMEM((width, kept.shape[1]), BF16)],
        compiler_params=params(0, 16),
        cost_estimate=cost(3),
        name="unpack_attention",
    )(me, kept, other)


def swap(block, axis_name, size, bit):
    return lax.ppermute(block, axis_name, [(i, i ^ bit) for i in range(size)])


def total(*parts):
    found = parts[0].astype(F32)
    for part in parts[1:]:
        found = found + part.astype(F32)
    return found.astype(BF16)


def core_parts(keep, found):
    size = keep.shape[0] // 4
    return [total(keep[i * size : (i + 1) * size], found[i * size : (i + 1) * size]) for i in range(4)]


def halves(block):
    size = block.shape[0] // 2
    return block[:size], block[size:]


def plane_send(blocks, grp_size):
    return tuple(swap(block, "grp", grp_size, bits) for block, bits in zip(blocks, (4, 2, 6)))


def line_parts(parts, psg_size):
    size = parts[0].shape[0] // psg_size
    return [total(*[part[i * size : (i + 1) * size] for part in parts]) for i in range(psg_size)]


def line_send(blocks, psg_size):
    return tuple(swap(block, "psg", psg_size, d) for d, block in enumerate(blocks, 1))


def line_total(own, founds, grp_size):
    piece = total(own, *founds)
    bit = 8
    while bit < grp_size:
        piece = total(piece, swap(piece, "grp", grp_size, bit))
        bit *= 2
    return piece


def tie(values, *others):
    return lax.optimization_barrier((tuple(values), others))[0]


def roll_back_kernel(lengths_ref, embed_ref, grad_ref, embed_out, grad_out):
    count = embed_ref.shape[0]
    first = longest_start(lengths_ref, count // 2)
    for r0 in range(0, count, LANES):
        token = lax.broadcasted_iota(jnp.int32, (LANES, count), 0) + (r0 - first)
        token = jnp.where(token < 0, token + count, token)
        pick = jnp.where(lax.broadcasted_iota(jnp.int32, (LANES, count), 1) == token, 1.0, 0.0).astype(BF16)
        embed_out[r0 : r0 + LANES] = dot(pick, embed_ref[...]).astype(BF16)
        grad_out[r0 : r0 + LANES] = dot(pick, grad_ref[...]).astype(BF16)


def roll_back(lengths, embed, grad):
    return pl.pallas_call(
        roll_back_kernel,
        grid=(1,),
        in_specs=[smem(), whole(embed), whole(grad)],
        out_specs=[whole(None)] * 2,
        out_shape=[shaped(embed.shape, BF16), shaped(grad.shape, BF16)],
        compiler_params=params(1, 8),
        cost_estimate=cost(4),
        name="roll_back",
    )(lengths, embed, grad)


def shift_gather(block, axis_name, axis_size):
    found = [block]
    for distance in range(1, axis_size):
        ring = [(i, (i - distance) % axis_size) for i in range(axis_size)]
        found.append(lax.ppermute(block, axis_name, ring))
    return found


def local(
    grp_size,
    psg_size,
    passages,
    queries,
    lengths,
    positives,
    query_weight,
    query_bias,
    key_weight,
    value_weight,
    value_bias,
    output_weight,
    output_bias,
    first_gain,
    first_shift,
    inner_weight,
    inner_bias,
    outer_weight,
    outer_bias,
    second_gain,
    second_shift,
    project_weight,
):
    ptok, width = passages.shape
    qtok = queries.shape[0]
    rows = ptok + qtok
    row = lambda vector: vector.reshape(1, -1)
    g1, s1, g2, s2 = row(first_gain), row(first_shift), row(second_gain), row(second_shift)
    q, k, v, o, lse, x1, rate1, xt, me = attention_forward(
        lengths,
        passages,
        queries,
        query_weight,
        row(query_bias),
        key_weight,
        value_weight,
        row(value_bias),
        output_weight,
        row(output_bias),
    )
    layer = (x1, g1, s1, inner_weight, row(inner_bias), outer_weight, row(outer_bias), g2, s2, project_weight)
    *held, query_embed = ffn_forward(qtok, ptok, rows, *layer, ())
    groups = shift_gather(query_embed, "psg", psg_size)
    u, d, x2, rate2, e, pass_embed = ffn_forward(ptok, 0, rows, *layer, held)
    own_scores, pooled = score(lengths, pass_embed, groups)
    scores = shift_gather(own_scores, "psg", psg_size)
    (late_lse,) = tie((lse,), own_scores)
    p, pq = probabilities(lengths, q, k, late_lse, ptok)
    scores[1:] = tie(scores[1:], p, pq)
    losses, own, *rest = loss_and_grads(me, lengths, positives, pooled, pass_embed, groups, scores)
    aways = []
    for distance, part in enumerate(rest[:-1], 1):
        ring = [(i, (i + distance) % psg_size) for i in range(psg_size)]
        aways.append(lax.ppermute(part, "psg", ring))
    gr2p, vec, proj = passage_head(rest[-1], e, x2, rate2, project_weight, g2, s2)
    dproj, vec2, dbi, gh1, keep_i, send_i, keep_o, send_o = ffn_backward(
        me,
        gr2p,
        vec,
        proj,
        own,
        aways,
        e,
        x2,
        rate2,
        project_weight,
        g2,
        s2,
        x1,
        g1,
        s1,
        inner_weight,
        outer_weight,
        u,
        d,
    )
    core_a = (swap(send_i, "grp", grp_size, 1), swap(send_o, "grp", grp_size, 1))
    gr1, go, vec1 = first_norm(gh1, x1, rate1, g1, output_weight)
    *core_a, go = tie((*core_a, go))
    next_i, away_i = [total(part, found) for part, found in zip(halves(keep_i), halves(core_a[0]))]
    next_o, away_o = [total(part, found) for part, found in zip(halves(keep_o), halves(core_a[1]))]
    plane_a = (swap(away_i, "grp", grp_size, 2), swap(away_o, "grp", grp_size, 4))
    first = heads_backward(0, p, pq, q, k, v, o, go, ptok)
    plane_a = tie(plane_a, *first)
    (go,) = tie((go,), *plane_a)
    next_i, away_i = [total(part, found) for part, found in zip(halves(next_i), halves(plane_a[0]))]
    next_o, away_o = [total(part, found) for part, found in zip(halves(next_o), halves(plane_a[1]))]
    plane_a = (swap(away_i, "grp", grp_size, 4), swap(away_o, "grp", grp_size, 2))
    second = heads_backward(1, p, pq, q, k, v, o, go, ptok)
    plane_a = tie(plane_a, *second)
    (gr1,) = tie((gr1,), *plane_a)
    both = lambda left, right: jnp.concatenate([left, right], axis=1)
    quarter = next_i.shape[0] // psg_size
    lines_a = [
        both(
            total(next_i[i * quarter : (i + 1) * quarter], plane_a[0][i * quarter : (i + 1) * quarter]),
            total(next_o[i * quarter : (i + 1) * quarter], plane_a[1][i * quarter : (i + 1) * quarter]),
        )
        for i in range(psg_size)
    ]
    line_a = line_send(lines_a[1:], psg_size)
    keep_b, send_b, grad_p, grad_q = weights(
        me,
        gr1,
        o,
        xt,
        first,
        second,
        dproj,
        vec1,
        vec2,
        dbi,
        query_weight,
        key_weight,
        value_weight,
        ptok,
    )
    core_b = swap(send_b, "grp", grp_size, 1)
    line_a = tie(line_a, grad_q)
    piece_a = line_total(lines_a[0], line_a, grp_size)
    spread_a = line_send([piece_a] * (psg_size - 1), psg_size)
    parts_b = core_parts(keep_b, core_b)
    plane_b = plane_send(parts_b[1:], grp_size)
    out_embed, out_grad = roll_back(lengths, pass_embed, grad_p)
    plane_b = tie(plane_b, out_embed, out_grad, *spread_a)
    lines_b = line_parts((parts_b[0], *plane_b), psg_size)
    line_b = line_send(lines_b[1:], psg_size)
    spread_a = tie(spread_a, *plane_b)
    ff = inner_weight.shape[1]
    held_i = jnp.concatenate([part[:, :ff] for part in (piece_a, *spread_a)])
    held_o = jnp.concatenate([part[:, ff:] for part in (piece_a, *spread_a)])
    found_a = (swap(held_i, "grp", grp_size, 4), swap(held_o, "grp", grp_size, 2))
    line_b = tie(line_b, *found_a)
    piece_b = line_total(lines_b[0], line_b, grp_size)
    spread_b = line_send([piece_b] * (psg_size - 1), psg_size)
    found_a = tie(found_a, *line_b)
    held_i = jnp.concatenate([held_i, found_a[0]])
    held_o = jnp.concatenate([held_o, found_a[1]])
    found_a = (swap(held_i, "grp", grp_size, 2), swap(held_o, "grp", grp_size, 4))
    found_a = tie(found_a, *spread_b)
    joined_b = jnp.concatenate([piece_b, *spread_b])
    gathered_b = plane_send([joined_b] * 3, grp_size)
    held_i = jnp.concatenate([held_i, found_a[0]])
    held_o = jnp.concatenate([held_o, found_a[1]])
    other_i, other_o = swap(held_i, "grp", grp_size, 1), swap(held_o, "grp", grp_size, 1)
    dwi, dwo = unpack_ffn(me, held_i, other_i, held_o, other_o)
    gathered_b = tie(gathered_b, dwi, dwo)
    kept_b = jnp.concatenate([joined_b, *gathered_b])
    other_b = swap(kept_b, "grp", grp_size, 1)
    dwq, dwk, dwv, dout, dproj, g2, s2, bo, g1, s1, bout, bi, bq, bv = unpack_attention(
        me, kept_b, other_b, width, project_weight.shape[1], inner_weight.shape[1]
    )
    flat = lambda vector: vector.reshape(-1)
    return (
        out_embed,
        query_embed,
        flat(losses),
        out_grad,
        grad_q,
        dwq,
        flat(bq),
        dwk,
        dwv,
        flat(bv),
        dout,
        flat(bout),
        flat(g1),
        flat(s1),
        dwi,
        flat(bi),
        dwo,
        flat(bo),
        flat(g2),
        flat(s2),
        dproj,
    )


def solution(mesh):
    split = P(("grp", "psg"), None)
    in_specs = (split, split, split, P("grp")) + (P(),) * 16
    out_specs = (split, split, P("grp"), split, split) + (P(),) * 16
    body = functools.partial(local, mesh.shape["grp"], mesh.shape["psg"])
    return jax.shard_map(body, mesh=mesh, in_specs=in_specs, out_specs=out_specs, check_vma=False)
```

```python
import functools

import jax
import jax.numpy as jnp
from jax import lax
from jax.experimental import pallas as pl
from jax.experimental.pallas import tpu as pltpu
from jax.sharding import PartitionSpec as P

HEADS = 8
HEAD = 64
QLEN = 32

SHARPNESS = 10.0
SCORE_SCALE = 0.25
NORM_EPS = 1e-06
EMBED_EPS = 1e-06
NEG_FILL = -1e30

F32 = jnp.float32
BF16 = jnp.bfloat16

INV_SQRT_2PI = 0.3989422804014327

INV_SQRT_2 = 0.7071067811865476

QUAD = 4
QLANES = QUAD * HEAD
RB = 256
LANES = 128
FCHUNK = 512
SLICE = 16
ASLICE = 32
PIECE = 16


def dot(left, right):
    return jnp.dot(left, right, preferred_element_type=F32)


def dot_t(left, right):
    return lax.dot_general(left, right, (((1,), (1,)), ((), ())), preferred_element_type=F32)


def t_dot(left, right):
    return lax.dot_general(left, right, (((0,), (0,)), ((), ())), preferred_element_type=F32)


def two_part_dot(left, right_low):
    high = left.astype(BF16)
    rest = (left - high.astype(F32)).astype(BF16)
    return dot(high, right_low) + dot(rest, right_low)


def norm_stats(x):
    center = x - jnp.mean(x, axis=-1, keepdims=True)
    rate = lax.rsqrt(jnp.mean(center * center, axis=-1, keepdims=True) + NORM_EPS)
    return center * rate, rate


def norm_backward(grad, scaled, rate, gain):
    inner = grad * gain
    mean_in = jnp.mean(inner, axis=-1, keepdims=True)
    mean_dot = jnp.mean(inner * scaled, axis=-1, keepdims=True)
    grad_x = rate * (inner - mean_in - scaled * mean_dot)
    return grad_x, jnp.sum(grad * scaled, axis=0, keepdims=True), jnp.sum(grad, axis=0, keepdims=True)


def unit_backward(grad, projected):
    rate = lax.rsqrt(jnp.sum(projected * projected, axis=-1, keepdims=True) + EMBED_EPS)
    unit = projected * rate
    return rate * (grad - unit * jnp.sum(grad * unit, axis=-1, keepdims=True))


def gelu_pair(f):
    phi = 0.5 + 0.5 * lax.erf(f * INV_SQRT_2)
    density = jnp.exp(-0.5 * (f * f)) * INV_SQRT_2PI
    return f * phi, phi + f * density


def segment_ends(lengths_ref):
    count = lengths_ref.shape[1]
    ends = []
    total = jnp.int32(0)
    for s in range(count):
        total = total + lengths_ref[0, s]
        ends.append(total)
    return ends


def longest_start(lengths_ref, longest):
    found = jnp.int32(0)
    start = jnp.int32(0)
    for s in range(lengths_ref.shape[1]):
        found = jnp.where(lengths_ref[0, s] == longest, start, found)
        start = start + lengths_ref[0, s]
    return found


def fill_bias(bias_ref, lengths_ref, ptok, qtok):
    half = ptok // 2
    ends = segment_ends(lengths_ref)
    first = longest_start(lengths_ref, half)

    def segments(place):
        token = place + half + first
        token = jnp.where(token >= ptok, token - ptok, token)
        seg = jnp.zeros_like(token)
        for end in ends:
            seg = seg + jnp.where(token >= end, 1, 0)
        return seg

    row_seg = segments(lax.broadcasted_iota(jnp.int32, (8, half), 1))[:1]
    for r0 in range(0, half, LANES):
        col = segments(lax.broadcasted_iota(jnp.int32, (LANES, LANES), 0) + r0)
        for c in range(0, half, LANES):
            bias_ref[r0 : r0 + LANES, c : c + LANES] = jnp.where(col == row_seg[:, c : c + LANES], 0.0, NEG_FILL)
    for c in range(0, qtok, LANES):
        for r0 in range(0, qtok, LANES):
            row = (lax.broadcasted_iota(jnp.int32, (LANES, LANES), 0) + r0) // QLEN
            col = (lax.broadcasted_iota(jnp.int32, (LANES, LANES), 1) + c) // QLEN
            bias_ref[half + r0 : half + r0 + LANES, c : c + LANES] = jnp.where(row == col, 0.0, NEG_FILL)


def spans(ptok, qtok):
    half = ptok // 2
    return ((0, half, None), (half, half, 0), (ptok, qtok, half))


def owner_place(me_ref, r, turned=False):
    first, second = (r >> 3) & 1, (r >> 2) & 1
    if turned:
        first, second = second, first
    core, x, y, z = me_ref[0] ^ (r >> 4), me_ref[1] ^ first, me_ref[2] ^ second, me_ref[3] ^ (r & 3)
    return pl.multiple_of((((y * 2 + x) * 2 + core) * 4 + z) * PIECE, PIECE)


def to_relative(me_ref, plain_ref, out_ref, turned=False):
    for r in range(32):
        out_ref[r * PIECE : (r + 1) * PIECE] = plain_ref[pl.ds(owner_place(me_ref, r, turned), PIECE), :]


def attention_forward_kernel(
    ptok,
    lengths_hbm,
    xp_hbm,
    xq_hbm,
    wq_hbm,
    wk_hbm,
    wv_hbm,
    wo_hbm,
    bq_hbm,
    bv_hbm,
    bo_hbm,
    q_ref,
    k_ref,
    v_ref,
    o_ref,
    lse_ref,
    x1_ref,
    rate1_ref,
    xt_ref,
    me_ref,
    x_scr,
    r1_scr,
    bias_scr,
    logs_scr,
    lengths_ref,
    xp_ref,
    wq_ref,
    wk_ref,
    wv_ref,
    wo_ref,
    bq_ref,
    bv_ref,
    bo_ref,
    sems,
):
    step = pl.program_id(0)
    rows = x_scr.shape[0]
    qtok = rows - ptok

    @pl.when(step == 0)
    def _():
        pairs = (
            (lengths_hbm, lengths_ref),
            (xp_hbm, xp_ref),
            (xq_hbm, x_scr.at[pl.ds(ptok, qtok)]),
            (bo_hbm, bo_ref),
            (wq_hbm, wq_ref),
            (bq_hbm, bq_ref),
            (wk_hbm, wk_ref),
            (wv_hbm, wv_ref),
            (bv_hbm, bv_ref),
            (wo_hbm, wo_ref),
        )
        copies = [pltpu.make_async_copy(held, ref, sems.at[i]) for i, (held, ref) in enumerate(pairs)]
        for copy in copies:
            copy.start()
        grp = lax.axis_index("grp")
        me_ref[0] = grp & 1
        me_ref[1] = (grp >> 1) & 1
        me_ref[2] = (grp >> 2) & 1
        me_ref[3] = lax.axis_index("psg")
        for copy in copies:
            copy.wait()
        first = longest_start(lengths_ref, ptok // 2)
        source = xp_ref[...]
        for r0 in range(0, ptok, LANES):
            token = lax.broadcasted_iota(jnp.int32, (LANES, ptok), 0) + (r0 + first)
            token = jnp.where(token >= ptok, token - ptok, token)
            pick = jnp.where(lax.broadcasted_iota(jnp.int32, (LANES, ptok), 1) == token, 1.0, 0.0).astype(BF16)
            x_scr[r0 : r0 + LANES] = dot(pick, source).astype(BF16)
        x = x_scr[...]
        xt_ref[...] = jnp.transpose(x)
        r1_scr[...] = x.astype(F32) + bo_ref[...]
        fill_bias(bias_scr, lengths_ref, ptok, qtok)

    x = x_scr[...]
    quad = pl.ds(pl.multiple_of(step * QLANES, QLANES), QLANES)
    q_ref[:, quad] = (dot(x, wq_ref[:, quad]) + bq_ref[:, quad]).astype(BF16) * BF16(HEAD**-0.5)
    k_ref[:, quad] = dot(x, wk_ref[:, quad]).astype(BF16)
    v_ref[:, quad] = (dot(x, wv_ref[:, quad]) + bv_ref[:, quad]).astype(BF16)
    logs_scr[...] = jnp.zeros_like(logs_scr)

    for pair in range(QUAD // 2):
        lanes = pl.ds(pl.multiple_of(step * QLANES + pair * LANES, LANES), LANES)
        for base, size, bias_row in spans(ptok, qtok):
            block = min(RB, size)
            for r0 in range(base, base + size, block):
                lane = lax.broadcasted_iota(jnp.int32, (block, LANES), 1)
                q = q_ref[r0 : r0 + block, lanes]
                keys = k_ref[base : base + size, lanes]
                values = v_ref[base : base + size, lanes]
                mixed = []
                for side in range(2):
                    inside = (lane < HEAD) if side == 0 else (lane >= HEAD)
                    s = dot_t(jnp.where(inside, q, BF16(0)), keys)
                    parts = []
                    totals = []
                    peaks = []
                    for i in range(0, block, ASLICE):
                        part = s[i : i + ASLICE]
                        if bias_row is not None:
                            at = bias_row + r0 - base + i
                            part = part + bias_scr[at : at + ASLICE, :size]
                        peak = jnp.max(part, axis=-1, keepdims=True)
                        e = jnp.exp(part - peak)
                        totals.append(jnp.sum(e, axis=-1, keepdims=True))
                        peaks.append(peak)
                        parts.append(e.astype(BF16))
                    total = jnp.concatenate(totals, axis=0)
                    mixed.append(dot(jnp.concatenate(parts, axis=0), values) * (1.0 / total))
                    log = jnp.concatenate(peaks, axis=0) + jnp.log(total)
                    logs_scr[r0 : r0 + block] = jnp.where(
                        lane == 2 * pair + side, log, logs_scr[r0 : r0 + block]
                    )
                o_ref[r0 : r0 + block, lanes] = jnp.where(lane < HEAD, mixed[0], mixed[1]).astype(BF16)
    lse_ref[step] = jnp.transpose(logs_scr[...])[:8]
    r1_scr[...] += dot(o_ref[:, quad], wo_ref[quad, :])

    @pl.when(step == pl.num_programs(0) - 1)
    def _():
        scaled, rate = norm_stats(r1_scr[...])
        x1_ref[...] = scaled
        rate1_ref[...] = jnp.broadcast_to(rate, rate1_ref.shape)


def spec(shape, index):
    return pl.BlockSpec(shape, index)


def whole(array):
    return pl.BlockSpec(memory_space=pltpu.VMEM)


def in_hbm(array):
    return pltpu.with_memory_space_constraint(array, pltpu.HBM)


def const(array):
    nd = len(array.shape)
    return pl.BlockSpec(array.shape, lambda *_: (0,) * nd)


def smem():
    return pl.BlockSpec(memory_space=pltpu.SMEM)


def cost(micros):
    return pl.CostEstimate(flops=int(micros * 1e9), bytes_accessed=int(micros * 1e6), transcendentals=0)


def shaped(shape, dtype):
    return jax.ShapeDtypeStruct(shape, dtype)


def params(grid_rank, mebibytes):
    return pltpu.CompilerParams(
        dimension_semantics=("arbitrary",) * grid_rank, vmem_limit_bytes=int(mebibytes * 1024 * 1024)
    )


def attention_forward(lengths, xp, xq, wq, bq, wk, wv, bv, wo, bo):
    ptok, width = xp.shape
    qtok = xq.shape[0]
    rows = ptok + qtok
    quads = HEADS // QUAD
    half = ptok // 2
    return pl.pallas_call(
        functools.partial(attention_forward_kernel, ptok),
        grid=(quads,),
        in_specs=[pl.BlockSpec(memory_space=pltpu.HBM)] * 10,
        out_specs=[whole(None)] * 8 + [smem()],
        out_shape=[shaped((rows, width), BF16)] * 4
        + [
            shaped((quads, 8, rows), F32),
            shaped((rows, width), F32),
            shaped((rows, LANES), F32),
            shaped((width, rows), BF16),
            shaped((4,), jnp.int32),
        ],
        scratch_shapes=[
            pltpu.VMEM((rows, width), BF16),
            pltpu.VMEM((rows, width), F32),
            pltpu.VMEM((half + qtok, half), F32),
            pltpu.VMEM((rows, LANES), F32),
            pltpu.SMEM(lengths.shape, jnp.int32),
            pltpu.VMEM(xp.shape, BF16),
        ]
        + [pltpu.VMEM((width, width), BF16)] * 4
        + [pltpu.VMEM((1, width), F32)] * 3
        + [pltpu.SemaphoreType.DMA((10,))],
        compiler_params=params(1, 26),
        cost_estimate=cost(20),
        name="attention_forward",
    )(*[in_hbm(a) for a in (lengths, xp, xq, wq, wk, wv, wo, bq, bv, bo)])


def ffn_forward_kernel(
    aliased,
    rb,
    offset,
    x1_ref,
    g1_ref,
    s1_ref,
    wi_ref,
    bi_ref,
    wo_ref,
    bo_ref,
    g2_ref,
    s2_ref,
    wp_ref,
    *rest,
):
    rest = rest[aliased:]
    u_ref, d_ref, x2_ref, rate2_ref, e_ref, emb_ref, h1_scr, r2_scr = rest
    step = pl.program_id(0)
    rows = h1_scr.shape[0]
    own = slice(offset, offset + rows)
    chunk = pl.ds(pl.multiple_of(step * FCHUNK, FCHUNK), FCHUNK)

    @pl.when(step == 0)
    def _():
        h1 = x1_ref[own] * g1_ref[...] + s1_ref[...]
        h1_scr[...] = h1.astype(BF16)
        r2_scr[...] = h1 + bo_ref[...]

    for r in range(0, rows, rb):
        f = dot(h1_scr[r : r + rb], wi_ref[...])
        bias = bi_ref[...]
        for i in range(0, rb, SLICE):
            u, d = gelu_pair(f[i : i + SLICE] + bias)
            at = offset + r + i
            u_ref[at : at + SLICE, chunk] = u.astype(BF16)
            d_ref[at : at + SLICE, chunk] = d.astype(BF16)
        r2_scr[r : r + rb] += dot(u_ref[offset + r : offset + r + rb, chunk], wo_ref[...])

    @pl.when(step == pl.num_programs(0) - 1)
    def _():
        scaled, rate = norm_stats(r2_scr[...])
        x2_ref[own] = scaled
        rate2_ref[own] = jnp.broadcast_to(rate, (rows, LANES))
        h2 = (scaled * g2_ref[...] + s2_ref[...]).astype(BF16)
        e = dot(h2, wp_ref[...])
        e_ref[own] = e
        size = jnp.sum(e * e, axis=-1, keepdims=True)
        emb_ref[...] = (e * lax.rsqrt(size + EMBED_EPS)).astype(BF16)


def ffn_forward(count, offset, total, x1, g1, s1, wi, bi, wo, bo, g2, s2, wp, previous):
    width = x1.shape[1]
    ff = wi.shape[1]
    dim = wp.shape[1]
    first = 10
    held = list(previous)
    return pl.pallas_call(
        functools.partial(ffn_forward_kernel, len(held), min(RB, count), offset),
        grid=(ff // FCHUNK,),
        in_specs=[
            whole(x1),
            const(g1),
            const(s1),
            spec((width, FCHUNK), lambda c: (0, c)),
            spec((1, FCHUNK), lambda c: (0, c)),
            spec((FCHUNK, width), lambda c: (c, 0)),
            const(bo),
            const(g2),
            const(s2),
            const(wp),
        ]
        + [whole(None)] * len(held),
        out_specs=[whole(None)] * 6,
        out_shape=[
            shaped((total, ff), BF16),
            shaped((total, ff), BF16),
            shaped((total, width), F32),
            shaped((total, LANES), F32),
            shaped((total, dim), F32),
            shaped((count, dim), BF16),
        ],
        scratch_shapes=[
            pltpu.VMEM((count, width), BF16),
            pltpu.VMEM((count, width), F32),
        ],
        input_output_aliases={first + i: i for i in range(len(held))},
        compiler_params=params(1, 16),
        cost_estimate=cost(12 if count > 256 else 4),
        name="ffn_forward",
    )(x1, g1, s1, in_hbm(wi), bi, in_hbm(wo), bo, g2, s2, wp, *held)


def passage_member(lengths_ref, rows):
    ends = segment_ends(lengths_ref)
    lane = lax.broadcasted_iota(jnp.int32, (8, LANES), 1)
    low = jnp.full((8, LANES), rows, jnp.int32)
    high = jnp.zeros((8, LANES), jnp.int32)
    start = jnp.int32(0)
    for s, end in enumerate(ends):
        low = jnp.where(lane == s, start, low)
        high = jnp.where(lane == s, end, high)
        start = end
    token = lax.broadcasted_iota(jnp.int32, (rows, LANES), 0) + longest_start(lengths_ref, rows // 2)
    token = jnp.where(token >= rows, token - rows, token)
    inside = (token >= low[:1]) & (token < high[:1])
    return jnp.where(inside, 1.0, 0.0).astype(BF16)


def soft_match(group, pass_embed):
    return jnp.exp(SHARPNESS * dot_t(group, pass_embed) - SHARPNESS)


def score_kernel(psg, count, lengths_ref, emb_ref, *rest):
    group_refs = rest[:psg]
    score_ref, pooled_ref = rest[psg:]
    member = passage_member(lengths_ref, emb_ref.shape[0])
    group = jnp.concatenate([ref[...] for ref in group_refs], axis=0)
    matched = soft_match(group, emb_ref[...])
    pooled = two_part_dot(matched, member)
    lane = lax.broadcasted_iota(jnp.int32, pooled.shape, 1)
    pooled = jnp.where(lane < count, pooled, 1.0)
    pooled_ref[...] = pooled
    smooth = 1.0 + jnp.log(pooled) * (1.0 / SHARPNESS)
    queries = pooled.shape[0] // QLEN
    score_ref[...] = SCORE_SCALE * jnp.sum(smooth.reshape(queries, QLEN, LANES), axis=1)


def score(lengths, emb, groups):
    psg = len(groups)
    tokens = sum(g.shape[0] for g in groups)
    return pl.pallas_call(
        functools.partial(score_kernel, psg, lengths.shape[1]),
        in_specs=[smem()] + [pl.BlockSpec(memory_space=pltpu.VMEM)] * (1 + psg),
        out_shape=[shaped((tokens // QLEN, LANES), F32), shaped((tokens, LANES), F32)],
        compiler_params=params(0, 8),
        cost_estimate=cost(3),
        name="score",
    )(lengths, emb, *groups)


def loss_kernel(psg, count, where_ref, lengths_ref, positives_ref, pooled_ref, emb_ref, *rest):
    group_refs = rest[:psg]
    score_refs = rest[psg : 2 * psg]
    loss_ref, own_ref = rest[2 * psg : 2 * psg + 2]
    away_refs = rest[2 * psg + 2 : 3 * psg + 1]
    grad_ref = rest[3 * psg + 1]
    position = where_ref[3]
    queries = score_refs[0].shape[0]
    each = queries // psg
    lane = lax.broadcasted_iota(jnp.int32, (queries, LANES), 1)
    row = lax.broadcasted_iota(jnp.int32, (queries, LANES), 0)
    valid = lane < count
    blocks = []
    for e in range(psg):
        found = score_refs[e][...]
        found = jnp.concatenate(
            [found[((d - e) % psg) * each : ((d - e) % psg + 1) * each] for d in range(psg)], axis=0
        )
        blocks.append(jnp.where(valid, found, -jnp.inf))
    target = jnp.zeros((queries, LANES), jnp.int32)
    for d in range(psg):
        for j in range(each):
            chosen = positives_ref[lax.rem(position + d, psg) * each + j]
            target = jnp.where(row == d * each + j, chosen, target)
    peak = blocks[0]
    for found in blocks[1:]:
        peak = jnp.maximum(peak, found)
    peak = jnp.max(peak, axis=-1, keepdims=True)
    total = jnp.zeros((queries, 1), F32)
    picked = jnp.zeros((queries, 1), F32)
    for e in range(psg):
        owner = lax.rem(position + e, psg)
        hit = (target == owner * count + lane) & valid
        total = total + jnp.sum(jnp.exp(blocks[e] - peak), axis=-1, keepdims=True)
        picked = picked + jnp.sum(jnp.where(hit, blocks[e], 0.0), axis=-1, keepdims=True)
        if e == 0:
            own_hit = jnp.where(hit, 1.0, 0.0)
    log_total = peak + jnp.log(total)
    losses = jnp.broadcast_to(log_total - picked, (queries, LANES))
    place = lax.rem(position + row // each, psg) * each + row % each
    losses = jnp.sum(jnp.where(lane == place, losses, 0.0), axis=0, keepdims=True)
    loss_ref[...] = losses[:, :queries]
    grad = jnp.where(valid, jnp.exp(blocks[0] - log_total) - own_hit, 0.0) * SCORE_SCALE
    tokens = queries * QLEN
    grad = jnp.broadcast_to(grad[:, None, :], (queries, QLEN, LANES)).reshape(tokens, LANES)
    grad = grad / pooled_ref[...]
    member = passage_member(lengths_ref, emb_ref.shape[0])
    high = grad.astype(BF16)
    rest_low = (grad - high.astype(F32)).astype(BF16)
    spread = dot_t(high, member) + dot_t(rest_low, member)
    group = jnp.concatenate([ref[...] for ref in group_refs], axis=0)
    low = (soft_match(group, emb_ref[...]) * spread).astype(BF16)
    group_grad = dot(low, emb_ref[...])
    each_tokens = tokens // psg
    own_ref[...] = group_grad[:each_tokens]
    for d in range(1, psg):
        away_refs[d - 1][...] = group_grad[d * each_tokens : (d + 1) * each_tokens].astype(BF16)
    grad_ref[...] = jnp.transpose(dot(jnp.transpose(group), low))


def loss_and_grads(position, lengths, positives, pooled, emb, groups, scores):
    psg = len(groups)
    queries = scores[0].shape[0]
    tokens, dim = groups[0].shape
    vmem = pl.BlockSpec(memory_space=pltpu.VMEM)
    return pl.pallas_call(
        functools.partial(loss_kernel, psg, lengths.shape[1]),
        in_specs=[smem(), smem(), smem()] + [vmem] * (2 + 2 * psg),
        out_shape=[shaped((1, queries), F32), shaped((tokens, dim), F32)]
        + [shaped((tokens, dim), BF16)] * (psg - 1)
        + [shaped(emb.shape, F32)],
        compiler_params=params(0, 8),
        cost_estimate=cost(3),
        name="loss_and_grads",
    )(position, lengths, positives, pooled, emb, *groups, *scores)


def head_backward(grad_embed, e, x2, rate2, wp, g2, s2):
    low = unit_backward(grad_embed, e).astype(BF16)
    grad_h2 = dot_t(low, wp)
    grad_r2, gain_term, shift_term = norm_backward(grad_h2, x2, rate2[:, :1], g2)
    h2 = (x2 * g2 + s2).astype(BF16)
    return grad_r2, gain_term, shift_term, dot(jnp.transpose(low), h2)


def passage_head_kernel(
    grad_ref, e_ref, x2_ref, rate2_ref, wp_ref, g2_ref, s2_ref, gr2_ref, vec_ref, proj_ref
):
    ptok = grad_ref.shape[0]
    grad_r2, gain_term, shift_term, proj = head_backward(
        grad_ref[...], e_ref[:ptok], x2_ref[:ptok], rate2_ref[:ptok], wp_ref[...], g2_ref[...], s2_ref[...]
    )
    gr2_ref[...] = grad_r2
    vec_ref[...] = jnp.zeros_like(vec_ref)
    vec_ref[0:1] = gain_term
    vec_ref[1:2] = shift_term
    proj_ref[...] = proj


def passage_head(grad, e, x2, rate2, wp, g2, s2):
    ptok, dim = grad.shape
    width = x2.shape[1]
    return pl.pallas_call(
        passage_head_kernel,
        grid=(1,),
        in_specs=[
            whole(grad),
            whole(e),
            whole(x2),
            whole(rate2),
            const(wp),
            const(g2),
            const(s2),
        ],
        out_specs=[whole(None)] * 3,
        out_shape=[shaped((ptok, width), F32), shaped((8, width), F32), shaped((dim, width), F32)],
        compiler_params=params(1, 10),
        cost_estimate=cost(4),
        name="passage_head",
    )(grad, e, x2, rate2, wp, g2, s2)


def fixed(shape):
    return pl.BlockSpec(memory_space=pltpu.VMEM)


def ffn_backward_kernel(
    psg,
    me_ref,
    gr2p_ref,
    vec_ref,
    proj_ref,
    own_ref,
    *rest,
):
    away_refs = rest[: psg - 1]
    (
        e_ref,
        x2_ref,
        rate2_ref,
        wp_ref,
        g2_ref,
        s2_ref,
        x1_ref,
        g1_ref,
        s1_ref,
        wi_ref,
        wo_ref,
        u_ref,
        d_ref,
        dproj_ref,
        dvec_ref,
        dbi_ref,
        gh1_ref,
        keep_i_ref,
        send_i_ref,
        keep_o_ref,
        send_o_ref,
        gz_scr,
        turn_scr,
        gzt_scr,
        h1t_scr,
    ) = rest[psg - 1 :]
    step = pl.program_id(0)
    ptok = gr2p_ref.shape[0]

    @pl.when(step == 0)
    def _():
        grad = own_ref[...]
        for ref in away_refs:
            grad = grad + ref[...].astype(F32)
        grad_r2, gain_term, shift_term, proj = head_backward(
            grad, e_ref[ptok:], x2_ref[ptok:], rate2_ref[ptok:], wp_ref[...], g2_ref[...], s2_ref[...]
        )
        dproj_ref[...] = jnp.transpose(proj_ref[...] + proj).astype(BF16)
        gr2p = gr2p_ref[...]
        gh1_ref[:ptok] = gr2p
        gh1_ref[ptok:] = grad_r2
        low_p = gr2p.astype(BF16)
        low_q = grad_r2.astype(BF16)
        gz_scr[:ptok] = low_p
        gz_scr[ptok:] = low_q
        dvec_ref[...] = jnp.zeros_like(dvec_ref)
        dvec_ref[0:1] = vec_ref[0:1] + gain_term
        dvec_ref[1:2] = vec_ref[1:2] + shift_term
        dvec_ref[2:3] = jnp.sum(low_p.astype(F32), axis=0, keepdims=True) + jnp.sum(
            low_q.astype(F32), axis=0, keepdims=True
        )
        turn_scr[...] = jnp.transpose((x1_ref[...] * g1_ref[...] + s1_ref[...]).astype(BF16))
        to_relative(me_ref, turn_scr, h1t_scr)
        turn_scr[...] = jnp.transpose(gz_scr[...])
        to_relative(me_ref, turn_scr, gzt_scr, turned=True)

    chunk = pl.ds(pl.multiple_of(step * FCHUNK, FCHUNK), FCHUNK)
    gz = gz_scr[...]
    grad_active = dot_t(gz, wo_ref[...])
    grad_inner = (grad_active * d_ref[:, chunk].astype(F32)).astype(BF16)
    dbi_ref[:, chunk] = jnp.sum(grad_inner.astype(F32), axis=0, keepdims=True)
    gh1_ref[...] += dot_t(grad_inner, wi_ref[...])
    half = keep_i_ref.shape[0]
    for ref, start in ((keep_i_ref, 0), (send_i_ref, half)):
        ref[:, chunk] = dot(h1t_scr[start : start + half], grad_inner).astype(BF16)
    for ref, start in ((keep_o_ref, 0), (send_o_ref, half)):
        ref[:, chunk] = dot(gzt_scr[start : start + half], u_ref[:, chunk]).astype(BF16)


def ffn_backward(me, gr2p, vec, proj, own, aways, e, x2, rate2, wp, g2, s2, x1, g1, s1, wi, wo, u, d):
    ptok, width = gr2p.shape
    rows = x1.shape[0]
    dim = wp.shape[1]
    ff = wi.shape[1]
    return pl.pallas_call(
        functools.partial(ffn_backward_kernel, 1 + len(aways)),
        grid=(ff // FCHUNK,),
        in_specs=[smem(), whole(gr2p), whole(vec), whole(proj), whole(own)]
        + [whole(a) for a in aways]
        + [
            whole(e),
            whole(x2),
            whole(rate2),
            const(wp),
            const(g2),
            const(s2),
            whole(x1),
            const(g1),
            const(s1),
            spec((width, FCHUNK), lambda c: (0, c)),
            spec((FCHUNK, width), lambda c: (c, 0)),
            whole(u),
            whole(d),
        ],
        out_specs=[
            fixed((width, dim)),
            fixed((8, width)),
            fixed((1, ff)),
            fixed((rows, width)),
        ]
        + [whole(None)] * 4,
        out_shape=[
            shaped((width, dim), BF16),
            shaped((8, width), F32),
            shaped((1, ff), F32),
            shaped((rows, width), F32),
        ]
        + [shaped((width // 2, ff), BF16)] * 4,
        scratch_shapes=[
            pltpu.VMEM((rows, width), BF16),
            pltpu.VMEM((width, rows), BF16),
            pltpu.VMEM((width, rows), BF16),
            pltpu.VMEM((width, rows), BF16),
        ],
        compiler_params=params(1, 20),
        cost_estimate=cost(15),
        name="ffn_backward",
    )(me, gr2p, vec, proj, own, *aways, e, x2, rate2, wp, g2, s2, x1, g1, s1, in_hbm(wi), in_hbm(wo), u, d)


def put_vector(wave_ref, row, vector):
    for i in range(vector.shape[1] // LANES):
        wave_ref[row + i : row + i + 1] = vector[:, i * LANES : (i + 1) * LANES]
    return row + vector.shape[1] // LANES


def take_vector(wave_ref, row, column, out_ref):
    size = out_ref.shape[1]
    for i in range(size // LANES):
        out_ref[:, i * LANES : (i + 1) * LANES] = wave_ref[row + i : row + i + 1, column : column + LANES].astype(
            F32
        )
    return row + size // LANES


def units(pair, ptok, qtok):
    for index, (base, size, bias_row) in enumerate(spans(ptok, qtok)):
        block = min(RB, size)
        place = 0
        for r0 in range(base, base + size, block):
            for side in range(2):
                yield index, base, size, bias_row, r0, block, side, place
                place += block


def one_head(block, side, rows):
    lane = lax.broadcasted_iota(jnp.int32, (block, LANES), 1)
    return jnp.where((lane < HEAD) if side == 0 else (lane >= HEAD), rows, BF16(0))


def probabilities_kernel(ptok, lengths_ref, q_ref, k_ref, lse_ref, p_ref, pq_ref, bias_scr):
    qtok = q_ref.shape[0] - ptok

    @pl.when(pl.program_id(0) == 0)
    def _():
        fill_bias(bias_scr, lengths_ref, ptok, qtok)

    step = pl.program_id(0)
    for pair in range(QUAD // 2):
        lanes = pl.ds(pl.multiple_of(step * QLANES + pair * LANES, LANES), LANES)
        for index, base, size, bias_row, r0, block, side, place in units(pair, ptok, qtok):
            h = 2 * pair + side
            s = dot_t(k_ref[base : base + size, lanes], one_head(block, side, q_ref[r0 : r0 + block, lanes]))
            lse = lse_ref[step, h : h + 1, r0 : r0 + block]
            for i in range(0, size, ASLICE):
                part = s[i : i + ASLICE]
                if bias_row is not None:
                    part = part + bias_scr[bias_row + i : bias_row + i + ASLICE, r0 - base : r0 - base + block]
                p = jnp.exp(part - lse).astype(BF16)
                if index < 2:
                    p_ref[step, 2 * pair + index, i : i + ASLICE, place : place + block] = p
                else:
                    pq_ref[step, pair, i : i + ASLICE, place : place + block] = p


def probabilities(lengths, q, k, lse, ptok):
    rows, width = q.shape
    quads = HEADS // QUAD
    half, qtok = ptok // 2, rows - ptok
    return pl.pallas_call(
        functools.partial(probabilities_kernel, ptok),
        grid=(quads,),
        in_specs=[smem(), whole(q), whole(k), whole(lse)],
        out_specs=[whole(None), whole(None)],
        out_shape=[
            shaped((quads, QUAD, half, 2 * half), BF16),
            shaped((quads, QUAD // 2, qtok, 2 * qtok), BF16),
        ],
        scratch_shapes=[pltpu.VMEM((half + qtok, half), F32)],
        compiler_params=params(1, 10),
        cost_estimate=cost(8),
        name="probabilities",
    )(lengths, q, k, lse)


def first_norm_kernel(
    me_ref,
    gh1_ref,
    x1_ref,
    rate1_ref,
    o_ref,
    dproj_ref,
    vec2_ref,
    dbi_ref,
    g1_ref,
    wo_ref,
    gr1_ref,
    go_ref,
    keep_ref,
    send_ref,
    turn_scr,
    left_scr,
    right_scr,
    lines_scr,
):
    grad_r1, gain_term, shift_term = norm_backward(gh1_ref[...], x1_ref[...], rate1_ref[:, :1], g1_ref[...])
    gr1_ref[...] = grad_r1
    low = grad_r1.astype(BF16)
    go_ref[...] = dot_t(low, wo_ref[...]).astype(BF16)
    turn_scr[...] = jnp.transpose(o_ref[...])
    to_relative(me_ref, turn_scr, left_scr)
    to_relative(me_ref, turn_scr, right_scr, turned=True)
    half_rows, lanes = keep_ref.shape
    middle = lanes // 2
    part = low.shape[1] // 2
    for ref, start in ((keep_ref, 0), (send_ref, half_rows)):
        ref[:, :part] = dot(left_scr[start : start + half_rows], low[:, :part]).astype(BF16)
        ref[:, middle : middle + part] = dot(right_scr[start : start + half_rows], low[:, part:]).astype(BF16)
    row = 0
    for vector in (
        vec2_ref[0:1],
        vec2_ref[1:2],
        vec2_ref[2:3],
        gain_term,
        shift_term,
        jnp.sum(low.astype(F32), axis=0, keepdims=True),
        dbi_ref[...],
    ):
        row = put_vector(lines_scr, row, vector)
    lines_scr[row:] = jnp.zeros((lines_scr.shape[0] - row, LANES), F32)
    turn_scr[:, :LANES] = lines_scr[...].astype(BF16)
    for r in range(32):
        ref = keep_ref if r < 16 else send_ref
        at = slice((r % 16) * PIECE, (r % 16 + 1) * PIECE)
        ref[at, part:middle] = turn_scr[pl.ds(owner_place(me_ref, r), PIECE), :LANES]
        ref[at, middle + part :] = dproj_ref[pl.ds(owner_place(me_ref, r, turned=True), PIECE), :]


def first_norm(me, gh1, x1, rate1, o, dproj, vec2, dbi, g1, wo):
    rows, width = x1.shape
    low = lambda *shape: pltpu.VMEM(shape, BF16)
    lanes = width + LANES + dproj.shape[1]
    return pl.pallas_call(
        first_norm_kernel,
        grid=(1,),
        in_specs=[smem()] + [whole(None)] * 7 + [const(g1), const(wo)],
        out_specs=[whole(None)] * 4,
        out_shape=[
            shaped((rows, width), F32),
            shaped((rows, width), BF16),
            shaped((width // 2, lanes), BF16),
            shaped((width // 2, lanes), BF16),
        ],
        scratch_shapes=[
            low(width, rows),
            low(width, rows),
            low(width, rows),
            pltpu.VMEM((width, LANES), F32),
        ],
        compiler_params=params(1, 16),
        cost_estimate=cost(4),
        name="first_norm",
    )(me, gh1, x1, rate1, o, dproj, vec2, dbi, g1, wo)


def heads_backward_kernel(
    quad,
    ptok,
    p_ref,
    pq_ref,
    q_ref,
    k_ref,
    v_ref,
    o_ref,
    go_ref,
    gq_ref,
    gk_ref,
    gv_ref,
    dd_scr,
    gqt_scr,
    qm_scr,
    gm_scr,
    gs_scr,
    kt_scr,
):
    qtok = q_ref.shape[0] - ptok

    own = slice(quad * QLANES, (quad + 1) * QLANES)
    product = go_ref[:, own].astype(F32) * o_ref[:, own].astype(F32)
    ones = jnp.where(
        lax.broadcasted_iota(jnp.int32, (16, QLANES), 1) // HEAD
        == lax.broadcasted_iota(jnp.int32, (16, QLANES), 0),
        1.0,
        0.0,
    ).astype(BF16)
    high = product.astype(BF16)
    dd_scr[...] = dot_t(ones, high) + dot_t(ones, (product - high.astype(F32)).astype(BF16))
    kt_scr[...] = jnp.transpose(k_ref[:, own])
    for pair in range(QUAD // 2):
        inner = slice(pair * LANES, (pair + 1) * LANES)
        lanes = slice(quad * QLANES + pair * LANES, quad * QLANES + (pair + 1) * LANES)
        last = None
        for index, base, size, bias_row, r0, block, side, place in units(pair, ptok, qtok):
            buffer = (3 * pair + index) % 2
            h = 2 * pair + side
            qm_scr[buffer, place : place + block] = one_head(block, side, q_ref[r0 : r0 + block, lanes])
            gm = one_head(block, side, go_ref[r0 : r0 + block, lanes])
            gm_scr[buffer, place : place + block] = gm
            grad_prob = dot_t(v_ref[base : base + size, lanes], gm)
            dd = dd_scr[h : h + 1, r0 : r0 + block]
            p_at = p_ref.at[quad, 2 * pair + index] if index < 2 else pq_ref.at[quad, pair]
            for i in range(0, size, ASLICE):
                p = p_at[i : i + ASLICE, place : place + block].astype(F32)
                gs = p * (grad_prob[i : i + ASLICE] - dd)
                gs_scr[buffer, i : i + ASLICE, place : place + block] = gs.astype(BF16)
            gqt_scr[h * HEAD : (h + 1) * HEAD, r0 : r0 + block] = dot(
                kt_scr[h * HEAD : (h + 1) * HEAD, base : base + size],
                gs_scr[buffer, :size, place : place + block],
            )
            end = place + block
            if end == 2 * size:
                gv_ref[base : base + size, inner] = dot(p_at[...], gm_scr[buffer, :end]).astype(BF16)
                gk_ref[base : base + size, inner] = dot(gs_scr[buffer, :size, :end], qm_scr[buffer, :end]).astype(
                    BF16
                )
    gq_ref[...] = (jnp.transpose(gqt_scr[...]) * (HEAD**-0.5)).astype(BF16)


def heads_backward(quad, p, pq, q, k, v, o, go, ptok):
    rows, width = q.shape
    half = ptok // 2
    low = lambda *shape: pltpu.VMEM(shape, BF16)
    return pl.pallas_call(
        functools.partial(heads_backward_kernel, quad, ptok),
        grid=(1,),
        in_specs=[whole(None)] * 7,
        out_specs=[whole(None)] * 3,
        out_shape=[shaped((rows, QLANES), BF16)] * 3,
        scratch_shapes=[
            pltpu.VMEM((16, rows), F32),
            pltpu.VMEM((QLANES, rows), F32),
            low(2, 4 * RB, LANES),
            low(2, 4 * RB, LANES),
            low(2, half, 4 * RB),
            low(QLANES, rows),
        ],
        compiler_params=params(1, 16),
        cost_estimate=cost(10),
        name="heads_backward",
    )(p, pq, q, k, v, o, go)


def weights_kernel(
    ptok,
    me_ref,
    gr1_ref,
    xt_ref,
    gq0_ref,
    gk0_ref,
    gv0_ref,
    gq1_ref,
    gk1_ref,
    gv1_ref,
    wq_ref,
    wk_ref,
    wv_ref,
    keep_ref,
    send_ref,
    gp_ref,
    gq_ref,
    xt_scr,
    lines_scr,
    tail_scr,
):
    half_rows = keep_ref.shape[0]
    width = gr1_ref.shape[1]
    gr1 = gr1_ref[...]
    to_relative(me_ref, xt_ref, xt_scr)
    joined = [
        jnp.concatenate([left[...], right[...]], axis=1)
        for left, right in ((gq0_ref, gq1_ref), (gk0_ref, gk1_ref), (gv0_ref, gv1_ref))
    ]
    for ref, start in ((keep_ref, 0), (send_ref, half_rows)):
        for i, grad in enumerate(joined):
            ref[:, i * width : (i + 1) * width] = dot(xt_scr[start : start + half_rows], grad).astype(BF16)
    gin = gr1 + dot_t(joined[0], wq_ref[...]) + dot_t(joined[1], wk_ref[...]) + dot_t(joined[2], wv_ref[...])
    gp_ref[...] = gin[:ptok].astype(BF16)
    gq_ref[...] = gin[ptok:].astype(BF16)
    row = 0
    for vector in (
        jnp.sum(joined[0].astype(F32), axis=0, keepdims=True),
        jnp.sum(joined[2].astype(F32), axis=0, keepdims=True),
    ):
        row = put_vector(lines_scr, row, vector)
    lines_scr[row:] = jnp.zeros((lines_scr.shape[0] - row, LANES), F32)
    tail_scr[...] = lines_scr[...].astype(BF16)
    for r in range(32):
        ref = keep_ref if r < 16 else send_ref
        at = (r % 16) * PIECE
        ref[at : at + PIECE, 3 * width :] = tail_scr[pl.ds(owner_place(me_ref, r), PIECE), :]


def weights(me, gr1, xt, first, second, wq, wk, wv, ptok):
    rows, width = gr1.shape
    lanes = 3 * width + LANES
    low = lambda *shape: pltpu.VMEM(shape, BF16)
    return pl.pallas_call(
        functools.partial(weights_kernel, ptok),
        grid=(1,),
        in_specs=[smem()] + [whole(None)] * 11,
        out_specs=[whole(None)] * 4,
        out_shape=[
            shaped((width // 2, lanes), BF16),
            shaped((width // 2, lanes), BF16),
            shaped((ptok, width), BF16),
            shaped((rows - ptok, width), BF16),
        ],
        scratch_shapes=[
            low(width, rows),
            pltpu.VMEM((width, LANES), F32),
            low(width, LANES),
        ],
        compiler_params=params(1, 14),
        cost_estimate=cost(6),
        name="weights",
    )(me, gr1, xt, *first, *second, wq, wk, wv)


def from_relative(me_ref, kept_ref, other_ref, wave_ref, turned=False, start=0):
    lanes = slice(start, start + wave_ref.shape[1])
    for r in range(32):
        ref = kept_ref if r < 16 else other_ref
        at = (r % 16) * PIECE
        wave_ref[pl.ds(owner_place(me_ref, r, turned), PIECE), :] = ref[at : at + PIECE, lanes]


def unpack_ffn_kernel(
    me_ref, kept_i_ref, other_i_ref, kept_o_ref, other_o_ref, dwi_ref, dwo_ref, wave_i_scr, wave_o_scr
):
    from_relative(me_ref, kept_i_ref, other_i_ref, wave_i_scr)
    from_relative(me_ref, kept_o_ref, other_o_ref, wave_o_scr, turned=True)
    dwi_ref[...] = wave_i_scr[...].astype(F32)
    dwo_ref[...] = jnp.transpose(wave_o_scr[...].astype(F32))


def unpack_ffn(me, ff, *halves):
    width = 2 * halves[0].shape[0]
    half = width // 2
    return pl.pallas_call(
        unpack_ffn_kernel,
        grid=(ff // FCHUNK,),
        in_specs=[smem()] + [spec((half, FCHUNK), lambda c: (0, c))] * 4,
        out_specs=[
            spec((width, FCHUNK), lambda c: (0, c)),
            spec((FCHUNK, width), lambda c: (c, 0)),
        ],
        out_shape=[shaped((width, ff), F32), shaped((ff, width), F32)],
        scratch_shapes=[pltpu.VMEM((width, FCHUNK), BF16)] * 2,
        compiler_params=params(1, 16),
        cost_estimate=cost(6),
        name="unpack_ffn",
    )(me, *halves)


def unpack_output_kernel(
    me_ref,
    kept_l_ref,
    other_l_ref,
    kept_r_ref,
    other_r_ref,
    dout_ref,
    dproj_ref,
    g2_ref,
    s2_ref,
    bo_ref,
    g1_ref,
    s1_ref,
    bout_ref,
    bi_ref,
    left_scr,
    right_scr,
):
    start = kept_l_ref.shape[1] - left_scr.shape[1]
    from_relative(me_ref, kept_l_ref, other_l_ref, left_scr, start=start)
    from_relative(me_ref, kept_r_ref, other_r_ref, right_scr, turned=True, start=start)
    part = dout_ref.shape[1] // 2
    dout_ref[:, :part] = left_scr[:, :part].astype(F32)
    dout_ref[:, part:] = right_scr[:, :part].astype(F32)
    dproj_ref[...] = right_scr[:, part:].astype(F32)
    row = 0
    for ref in (g2_ref, s2_ref, bo_ref, g1_ref, s1_ref, bout_ref, bi_ref):
        row = take_vector(left_scr, row, part, ref)


def unpack_output(me, width, dim, ff, *halves):
    return pl.pallas_call(
        unpack_output_kernel,
        grid=(1,),
        in_specs=[smem()] + [whole(None)] * 4,
        out_specs=[whole(None)] * 9,
        out_shape=[shaped((width, width), F32), shaped((width, dim), F32)]
        + [shaped((1, width), F32)] * 6
        + [shaped((1, ff), F32)],
        scratch_shapes=[
            pltpu.VMEM((width, width // 2 + LANES), BF16),
            pltpu.VMEM((width, width // 2 + dim), BF16),
        ],
        compiler_params=params(1, 8),
        cost_estimate=cost(2),
        name="unpack_output",
    )(me, *halves)


def unpack_attention_kernel(me_ref, kept_ref, other_ref, dwq_ref, dwk_ref, dwv_ref, bq_ref, bv_ref, wave_scr):
    from_relative(me_ref, kept_ref, other_ref, wave_scr)
    column = 0
    for ref in (dwq_ref, dwk_ref, dwv_ref):
        ref[...] = wave_scr[:, column : column + ref.shape[1]].astype(F32)
        column += ref.shape[1]
    row = 0
    for ref in (bq_ref, bv_ref):
        row = take_vector(wave_scr, row, column, ref)


def unpack_attention(me, kept, other, width):
    return pl.pallas_call(
        unpack_attention_kernel,
        grid=(1,),
        in_specs=[smem()] + [whole(None)] * 2,
        out_specs=[whole(None)] * 5,
        out_shape=[shaped((width, width), F32)] * 3 + [shaped((1, width), F32)] * 2,
        scratch_shapes=[pltpu.VMEM((width, kept.shape[1]), BF16)],
        compiler_params=params(1, 12),
        cost_estimate=cost(3),
        name="unpack_attention",
    )(me, kept, other)


def swap(block, axis_name, size, bit):
    return lax.ppermute(block, axis_name, [(i, i ^ bit) for i in range(size)])


def total(*parts):
    found = parts[0].astype(F32)
    for part in parts[1:]:
        found = found + part.astype(F32)
    return found.astype(BF16)


def core_parts(keep, found):
    size = keep.shape[0] // 4
    return [total(keep[i * size : (i + 1) * size], found[i * size : (i + 1) * size]) for i in range(4)]


def halves(block):
    size = block.shape[0] // 2
    return block[:size], block[size:]


def plane_send(blocks, grp_size):
    return tuple(swap(block, "grp", grp_size, bits) for block, bits in zip(blocks, (4, 2, 6)))


def line_parts(parts, psg_size):
    size = parts[0].shape[0] // psg_size
    return [total(*[part[i * size : (i + 1) * size] for part in parts]) for i in range(psg_size)]


def line_send(blocks, psg_size):
    return tuple(swap(block, "psg", psg_size, d) for d, block in enumerate(blocks, 1))


def line_total(own, founds, grp_size):
    piece = total(own, *founds)
    bit = 8
    while bit < grp_size:
        piece = total(piece, swap(piece, "grp", grp_size, bit))
        bit *= 2
    return piece


def tie(values, *others):
    return lax.optimization_barrier((tuple(values), others))[0]


def roll_back_kernel(lengths_ref, embed_ref, grad_ref, embed_out, grad_out):
    count = embed_ref.shape[0]
    first = longest_start(lengths_ref, count // 2)
    for r0 in range(0, count, LANES):
        token = lax.broadcasted_iota(jnp.int32, (LANES, count), 0) + (r0 - first)
        token = jnp.where(token < 0, token + count, token)
        pick = jnp.where(lax.broadcasted_iota(jnp.int32, (LANES, count), 1) == token, 1.0, 0.0).astype(BF16)
        embed_out[r0 : r0 + LANES] = dot(pick, embed_ref[...]).astype(BF16)
        grad_out[r0 : r0 + LANES] = dot(pick, grad_ref[...]).astype(BF16)


def roll_back(lengths, embed, grad):
    return pl.pallas_call(
        roll_back_kernel,
        grid=(1,),
        in_specs=[smem(), whole(embed), whole(grad)],
        out_specs=[whole(None)] * 2,
        out_shape=[shaped(embed.shape, BF16), shaped(grad.shape, BF16)],
        compiler_params=params(1, 8),
        cost_estimate=cost(4),
        name="roll_back",
    )(lengths, embed, grad)


def shift_gather(block, axis_name, axis_size):
    found = [block]
    for distance in range(1, axis_size):
        ring = [(i, (i - distance) % axis_size) for i in range(axis_size)]
        found.append(lax.ppermute(block, axis_name, ring))
    return found


def local(
    grp_size,
    psg_size,
    passages,
    queries,
    lengths,
    positives,
    query_weight,
    query_bias,
    key_weight,
    value_weight,
    value_bias,
    output_weight,
    output_bias,
    first_gain,
    first_shift,
    inner_weight,
    inner_bias,
    outer_weight,
    outer_bias,
    second_gain,
    second_shift,
    project_weight,
):
    ptok, width = passages.shape
    qtok = queries.shape[0]
    rows = ptok + qtok
    row = lambda vector: vector.reshape(1, -1)
    g1, s1, g2, s2 = row(first_gain), row(first_shift), row(second_gain), row(second_shift)
    q, k, v, o, lse, x1, rate1, xt, me = attention_forward(
        lengths,
        passages,
        queries,
        query_weight,
        row(query_bias),
        key_weight,
        value_weight,
        row(value_bias),
        output_weight,
        row(output_bias),
    )
    layer = (x1, g1, s1, inner_weight, row(inner_bias), outer_weight, row(outer_bias), g2, s2, project_weight)
    *held, query_embed = ffn_forward(qtok, ptok, rows, *layer, ())
    groups = shift_gather(query_embed, "psg", psg_size)
    u, d, x2, rate2, e, pass_embed = ffn_forward(ptok, 0, rows, *layer, held)
    own_scores, pooled = score(lengths, pass_embed, groups)
    scores = shift_gather(own_scores, "psg", psg_size)
    (late_lse,) = tie((lse,), own_scores)
    p, pq = probabilities(lengths, q, k, late_lse, ptok)
    scores[1:] = tie(scores[1:], p, pq)
    losses, own, *rest = loss_and_grads(me, lengths, positives, pooled, pass_embed, groups, scores)
    aways = []
    for distance, part in enumerate(rest[:-1], 1):
        ring = [(i, (i + distance) % psg_size) for i in range(psg_size)]
        aways.append(lax.ppermute(part, "psg", ring))
    gr2p, vec, proj = passage_head(rest[-1], e, x2, rate2, project_weight, g2, s2)
    dproj, vec2, dbi, gh1, keep_i, send_i, keep_o, send_o = ffn_backward(
        me,
        gr2p,
        vec,
        proj,
        own,
        aways,
        e,
        x2,
        rate2,
        project_weight,
        g2,
        s2,
        x1,
        g1,
        s1,
        inner_weight,
        outer_weight,
        u,
        d,
    )
    core_a = (swap(send_i, "grp", grp_size, 1), swap(send_o, "grp", grp_size, 1))
    gr1, go, keep_n, send_n = first_norm(me, gh1, x1, rate1, o, dproj, vec2, dbi, g1, output_weight)
    core_n = swap(send_n, "grp", grp_size, 1)
    *core_a, core_n, go = tie((*core_a, core_n, go))
    both = lambda left, right: jnp.concatenate([left, right], axis=1)
    middle = keep_n.shape[1] // 2
    parts_n = [total(part, found) for part, found in zip(halves(keep_n), halves(core_n))]
    parts_i = [total(part, found) for part, found in zip(halves(keep_i), halves(core_a[0]))]
    parts_o = [total(part, found) for part, found in zip(halves(keep_o), halves(core_a[1]))]
    next_l, away_l = [both(part, extra[:, :middle]) for part, extra in zip(parts_i, parts_n)]
    next_r, away_r = [both(part, extra[:, middle:]) for part, extra in zip(parts_o, parts_n)]
    plane_a = (swap(away_l, "grp", grp_size, 2), swap(away_r, "grp", grp_size, 4))
    first = heads_backward(0, p, pq, q, k, v, o, go, ptok)
    plane_a = tie(plane_a, *first)
    (go,) = tie((go,), *plane_a)
    next_l, away_l = [total(part, found) for part, found in zip(halves(next_l), halves(plane_a[0]))]
    next_r, away_r = [total(part, found) for part, found in zip(halves(next_r), halves(plane_a[1]))]
    plane_a = (swap(away_l, "grp", grp_size, 4), swap(away_r, "grp", grp_size, 2))
    second = heads_backward(1, p, pq, q, k, v, o, go, ptok)
    plane_a = tie(plane_a, *second)
    (gr1,) = tie((gr1,), *plane_a)
    quarter = next_l.shape[0] // psg_size
    lines_a = [
        both(
            total(next_l[i * quarter : (i + 1) * quarter], plane_a[0][i * quarter : (i + 1) * quarter]),
            total(next_r[i * quarter : (i + 1) * quarter], plane_a[1][i * quarter : (i + 1) * quarter]),
        )
        for i in range(psg_size)
    ]
    line_a = line_send(lines_a[1:], psg_size)
    keep_b, send_b, grad_p, grad_q = weights(
        me, gr1, xt, first, second, query_weight, key_weight, value_weight, ptok
    )
    core_b = swap(send_b, "grp", grp_size, 1)
    parts_b = core_parts(keep_b, core_b)
    plane_b = plane_send(parts_b[1:], grp_size)
    (late_grad,) = tie((grad_p,), *parts_b[1:])
    out_embed, out_grad = roll_back(lengths, pass_embed, late_grad)
    line_a = tie(line_a, grad_q)
    piece_a = line_total(lines_a[0], line_a, grp_size)
    spread_a = line_send([piece_a] * (psg_size - 1), psg_size)
    plane_b = tie(plane_b, out_grad, *spread_a)
    lines_b = line_parts((parts_b[0], *plane_b), psg_size)
    line_b = line_send(lines_b[1:], psg_size)
    spread_a = tie(spread_a, *lines_b)
    wide = next_l.shape[1]
    held_l = jnp.concatenate([part[:, :wide] for part in (piece_a, *spread_a)])
    held_r = jnp.concatenate([part[:, wide:] for part in (piece_a, *spread_a)])
    found_a = (swap(held_l, "grp", grp_size, 4), swap(held_r, "grp", grp_size, 2))
    line_b = tie(line_b, held_l, held_r)
    piece_b = line_total(lines_b[0], line_b, grp_size)
    spread_b = line_send([piece_b] * (psg_size - 1), psg_size)
    found_a = tie(found_a, piece_b)
    held_l = jnp.concatenate([held_l, found_a[0]])
    held_r = jnp.concatenate([held_r, found_a[1]])
    found_a = (swap(held_l, "grp", grp_size, 2), swap(held_r, "grp", grp_size, 4))
    spread_b = tie(spread_b, held_l, held_r)
    joined_b = jnp.concatenate([piece_b, *spread_b])
    gathered_b = plane_send([joined_b] * 3, grp_size)
    found_a = tie(found_a, joined_b)
    held_l = jnp.concatenate([held_l, found_a[0]])
    held_r = jnp.concatenate([held_r, found_a[1]])
    other_l, other_r = swap(held_l, "grp", grp_size, 1), swap(held_r, "grp", grp_size, 1)
    ff = inner_weight.shape[1]
    dwi, dwo = unpack_ffn(me, ff, held_l, other_l, held_r, other_r)
    dout, dproj, g2, s2, bo, g1, s1, bout, bi = unpack_output(
        me, width, project_weight.shape[1], ff, held_l, other_l, held_r, other_r
    )
    gathered_b = tie(gathered_b, dwi, dout)
    kept_b = jnp.concatenate([joined_b, *gathered_b])
    other_b = swap(kept_b, "grp", grp_size, 1)
    dwq, dwk, dwv, bq, bv = unpack_attention(me, kept_b, other_b, width)
    flat = lambda vector: vector.reshape(-1)
    return (
        out_embed,
        query_embed,
        flat(losses),
        out_grad,
        grad_q,
        dwq,
        flat(bq),
        dwk,
        dwv,
        flat(bv),
        dout,
        flat(bout),
        flat(g1),
        flat(s1),
        dwi,
        flat(bi),
        dwo,
        flat(bo),
        flat(g2),
        flat(s2),
        dproj,
    )


def solution(mesh):
    split = P(("grp", "psg"), None)
    in_specs = (split, split, split, P("grp")) + (P(),) * 16
    out_specs = (split, split, P("grp"), split, split) + (P(),) * 16
    body = functools.partial(local, mesh.shape["grp"], mesh.shape["psg"])
    return jax.shard_map(body, mesh=mesh, in_specs=in_specs, out_specs=out_specs, check_vma=False)
```

```python
import functools

import jax
import jax.numpy as jnp
from jax import lax
from jax.experimental import pallas as pl
from jax.experimental.pallas import tpu as pltpu
from jax.sharding import PartitionSpec as P

HEADS = 8
HEAD = 64
QLEN = 32

SHARPNESS = 10.0
SCORE_SCALE = 0.25
NORM_EPS = 1e-06
EMBED_EPS = 1e-06
NEG_FILL = -1e30

F32 = jnp.float32
BF16 = jnp.bfloat16

HALF_LOG2_E = -0.7213475204444817
LOG2_INV_SQRT_2PI = -1.3257480647361595

INV_SQRT_2 = 0.7071067811865476

QUAD = 4
QLANES = QUAD * HEAD
RB = 256
LANES = 128
FCHUNK = 512
SLICE = 16
ASLICE = 32
PIECE = 16


def dot(left, right):
    return jnp.dot(left, right, preferred_element_type=F32)


def dot_t(left, right):
    return lax.dot_general(left, right, (((1,), (1,)), ((), ())), preferred_element_type=F32)


def t_dot(left, right):
    return lax.dot_general(left, right, (((0,), (0,)), ((), ())), preferred_element_type=F32)


def two_part_dot(left, right_low):
    high = left.astype(BF16)
    rest = (left - high.astype(F32)).astype(BF16)
    return dot(high, right_low) + dot(rest, right_low)


def norm_stats(x):
    center = x - jnp.mean(x, axis=-1, keepdims=True)
    rate = lax.rsqrt(jnp.mean(center * center, axis=-1, keepdims=True) + NORM_EPS)
    return center * rate, rate


def norm_backward(grad, scaled, rate, gain):
    inner = grad * gain
    mean_in = jnp.mean(inner, axis=-1, keepdims=True)
    mean_dot = jnp.mean(inner * scaled, axis=-1, keepdims=True)
    grad_x = rate * (inner - mean_in - scaled * mean_dot)
    return grad_x, jnp.sum(grad * scaled, axis=0, keepdims=True), jnp.sum(grad, axis=0, keepdims=True)


def unit_backward(grad, projected):
    rate = lax.rsqrt(jnp.sum(projected * projected, axis=-1, keepdims=True) + EMBED_EPS)
    unit = projected * rate
    return rate * (grad - unit * jnp.sum(grad * unit, axis=-1, keepdims=True))


def gelu_pair(f):
    phi = 0.5 + 0.5 * lax.erf(f * INV_SQRT_2)
    density = jnp.exp2((f * f) * HALF_LOG2_E + LOG2_INV_SQRT_2PI)
    return f * phi, phi + f * density


def segment_ends(lengths_ref):
    count = lengths_ref.shape[1]
    ends = []
    total = jnp.int32(0)
    for s in range(count):
        total = total + lengths_ref[0, s]
        ends.append(total)
    return ends


def longest_start(lengths_ref, longest):
    found = jnp.int32(0)
    start = jnp.int32(0)
    for s in range(lengths_ref.shape[1]):
        found = jnp.where(lengths_ref[0, s] == longest, start, found)
        start = start + lengths_ref[0, s]
    return found


def shift_pick(shift):
    shape = (LANES, LANES + PIECE)
    row = lax.broadcasted_iota(jnp.int32, shape, 0) + shift
    return jnp.where(lax.broadcasted_iota(jnp.int32, shape, 1) == row, 1.0, 0.0).astype(BF16)


def fill_bias(bias_ref, lengths_ref, ptok, qtok):
    half = ptok // 2
    ends = segment_ends(lengths_ref)
    first = longest_start(lengths_ref, half)

    def segments(place):
        token = place + half + first
        token = jnp.where(token >= ptok, token - ptok, token)
        seg = jnp.zeros_like(token)
        for end in ends:
            seg = seg + jnp.where(token >= end, 1, 0)
        return seg

    row_seg = segments(lax.broadcasted_iota(jnp.int32, (8, half), 1))[:1]
    for r0 in range(0, half, LANES):
        col = segments(lax.broadcasted_iota(jnp.int32, (LANES, LANES), 0) + r0)
        for c in range(0, half, LANES):
            bias_ref[r0 : r0 + LANES, c : c + LANES] = jnp.where(col == row_seg[:, c : c + LANES], 0.0, NEG_FILL)
    for c in range(0, qtok, LANES):
        for r0 in range(0, qtok, LANES):
            row = (lax.broadcasted_iota(jnp.int32, (LANES, LANES), 0) + r0) // QLEN
            col = (lax.broadcasted_iota(jnp.int32, (LANES, LANES), 1) + c) // QLEN
            bias_ref[half + r0 : half + r0 + LANES, c : c + LANES] = jnp.where(row == col, 0.0, NEG_FILL)


def spans(ptok, qtok):
    half = ptok // 2
    return ((0, half, None), (half, half, 0), (ptok, qtok, half))


def owner_place(me_ref, r, turned=False):
    first, second = (r >> 3) & 1, (r >> 2) & 1
    if turned:
        first, second = second, first
    core, x, y, z = me_ref[0] ^ (r >> 4), me_ref[1] ^ first, me_ref[2] ^ second, me_ref[3] ^ (r & 3)
    return pl.multiple_of((((y * 2 + x) * 2 + core) * 4 + z) * PIECE, PIECE)


def to_relative(me_ref, plain_ref, out_ref, turned=False):
    for r in range(32):
        out_ref[r * PIECE : (r + 1) * PIECE] = plain_ref[pl.ds(owner_place(me_ref, r, turned), PIECE), :]


def attention_forward_kernel(
    ptok,
    lengths_hbm,
    xp_hbm,
    xq_hbm,
    wq_hbm,
    wk_hbm,
    wv_hbm,
    wo_hbm,
    bq_hbm,
    bv_hbm,
    bo_hbm,
    q_ref,
    k_ref,
    v_ref,
    o_ref,
    lse_ref,
    x1_ref,
    rate1_ref,
    xt_ref,
    me_ref,
    x_scr,
    r1_scr,
    bias_scr,
    logs_scr,
    lengths_ref,
    xp_ref,
    wq_ref,
    wk_ref,
    wv_ref,
    wo_ref,
    bq_ref,
    bv_ref,
    bo_ref,
    sems,
):
    step = pl.program_id(0)
    rows = x_scr.shape[0]
    qtok = rows - ptok

    @pl.when(step == 0)
    def _():
        pairs = (
            (lengths_hbm, lengths_ref),
            (xp_hbm, xp_ref.at[pl.ds(0, ptok)]),
            (xp_hbm, xp_ref.at[pl.ds(ptok, ptok)]),
            (xq_hbm, x_scr.at[pl.ds(ptok, qtok)]),
            (bo_hbm, bo_ref),
            (wq_hbm, wq_ref),
            (bq_hbm, bq_ref),
            (wk_hbm, wk_ref),
            (wv_hbm, wv_ref),
            (bv_hbm, bv_ref),
            (wo_hbm, wo_ref),
        )
        copies = [pltpu.make_async_copy(held, ref, sems.at[i]) for i, (held, ref) in enumerate(pairs)]
        for copy in copies:
            copy.start()
        grp = lax.axis_index("grp")
        me_ref[0] = grp & 1
        me_ref[1] = (grp >> 1) & 1
        me_ref[2] = (grp >> 2) & 1
        me_ref[3] = lax.axis_index("psg")
        for copy in copies:
            copy.wait()
        first = longest_start(lengths_ref, ptok // 2)
        aligned = (first // PIECE) * PIECE
        pick = shift_pick(first - aligned)
        for r0 in range(0, ptok, LANES):
            at = pl.multiple_of(aligned + r0, PIECE)
            x_scr[r0 : r0 + LANES] = dot(pick, xp_ref[pl.ds(at, LANES + PIECE), :]).astype(BF16)
        x = x_scr[...]
        xt_ref[...] = jnp.transpose(x)
        r1_scr[...] = x.astype(F32) + bo_ref[...]
        fill_bias(bias_scr, lengths_ref, ptok, qtok)

    x = x_scr[...]
    quad = pl.ds(pl.multiple_of(step * QLANES, QLANES), QLANES)
    q_ref[:, quad] = (dot(x, wq_ref[:, quad]) + bq_ref[:, quad]).astype(BF16) * BF16(HEAD**-0.5)
    k_ref[:, quad] = dot(x, wk_ref[:, quad]).astype(BF16)
    v_ref[:, quad] = (dot(x, wv_ref[:, quad]) + bv_ref[:, quad]).astype(BF16)
    logs_scr[...] = jnp.zeros_like(logs_scr)

    for pair in range(QUAD // 2):
        lanes = pl.ds(pl.multiple_of(step * QLANES + pair * LANES, LANES), LANES)
        for base, size, bias_row in spans(ptok, qtok):
            block = min(RB, size)
            for r0 in range(base, base + size, block):
                lane = lax.broadcasted_iota(jnp.int32, (block, LANES), 1)
                q = q_ref[r0 : r0 + block, lanes]
                keys = k_ref[base : base + size, lanes]
                values = v_ref[base : base + size, lanes]
                key_lane = lax.broadcasted_iota(jnp.int32, (size, LANES), 1)
                sides = (key_lane < HEAD, key_lane >= HEAD)
                mixed = []
                for side in range(2):
                    inside = (lane < HEAD) if side == 0 else (lane >= HEAD)
                    s = dot_t(jnp.where(inside, q, BF16(0)), keys)
                    parts = []
                    peaks = []
                    for i in range(0, block, ASLICE):
                        part = s[i : i + ASLICE]
                        if bias_row is not None:
                            at = bias_row + r0 - base + i
                            part = part + bias_scr[at : at + ASLICE, :size]
                        peak = jnp.max(part, axis=-1, keepdims=True)
                        parts.append(jnp.exp(part - peak).astype(BF16))
                        peaks.append(peak)
                    found = dot(jnp.concatenate(parts, axis=0), jnp.where(sides[side], values, BF16(1)))
                    turned = pltpu.roll(found, HEAD, 1)
                    mixed.append(found * (1.0 / turned))
                    log = jnp.concatenate(peaks, axis=0) + jnp.log(turned if side == 0 else found)
                    logs_scr[r0 : r0 + block] = jnp.where(
                        lane == 2 * pair + side, log, logs_scr[r0 : r0 + block]
                    )
                o_ref[r0 : r0 + block, lanes] = jnp.where(lane < HEAD, mixed[0], mixed[1]).astype(BF16)
    lse_ref[step] = jnp.transpose(logs_scr[...])[:8]
    r1_scr[...] += dot(o_ref[:, quad], wo_ref[quad, :])

    @pl.when(step == pl.num_programs(0) - 1)
    def _():
        scaled, rate = norm_stats(r1_scr[...])
        x1_ref[...] = scaled
        rate1_ref[...] = jnp.broadcast_to(rate, rate1_ref.shape)


def spec(shape, index):
    return pl.BlockSpec(shape, index)


def whole(array):
    return pl.BlockSpec(memory_space=pltpu.VMEM)


def in_hbm(array):
    return pltpu.with_memory_space_constraint(array, pltpu.HBM)


def const(array):
    nd = len(array.shape)
    return pl.BlockSpec(array.shape, lambda *_: (0,) * nd)


def smem():
    return pl.BlockSpec(memory_space=pltpu.SMEM)


def cost(micros):
    return pl.CostEstimate(flops=int(micros * 1e9), bytes_accessed=int(micros * 1e6), transcendentals=0)


def shaped(shape, dtype):
    return jax.ShapeDtypeStruct(shape, dtype)


def params(grid_rank, mebibytes):
    return pltpu.CompilerParams(
        dimension_semantics=("arbitrary",) * grid_rank, vmem_limit_bytes=int(mebibytes * 1024 * 1024)
    )


def attention_forward(lengths, xp, xq, wq, bq, wk, wv, bv, wo, bo):
    ptok, width = xp.shape
    qtok = xq.shape[0]
    rows = ptok + qtok
    quads = HEADS // QUAD
    half = ptok // 2
    return pl.pallas_call(
        functools.partial(attention_forward_kernel, ptok),
        grid=(quads,),
        in_specs=[pl.BlockSpec(memory_space=pltpu.HBM)] * 10,
        out_specs=[whole(None)] * 8 + [smem()],
        out_shape=[shaped((rows, width), BF16)] * 4
        + [
            shaped((quads, 8, rows), F32),
            shaped((rows, width), F32),
            shaped((rows, LANES), F32),
            shaped((width, rows), BF16),
            shaped((4,), jnp.int32),
        ],
        scratch_shapes=[
            pltpu.VMEM((rows, width), BF16),
            pltpu.VMEM((rows, width), F32),
            pltpu.VMEM((half + qtok, half), F32),
            pltpu.VMEM((rows, LANES), F32),
            pltpu.SMEM(lengths.shape, jnp.int32),
            pltpu.VMEM((2 * ptok, width), BF16),
        ]
        + [pltpu.VMEM((width, width), BF16)] * 4
        + [pltpu.VMEM((1, width), F32)] * 3
        + [pltpu.SemaphoreType.DMA((11,))],
        compiler_params=params(1, 28),
        cost_estimate=cost(20),
        name="attention_forward",
    )(*[in_hbm(a) for a in (lengths, xp, xq, wq, wk, wv, wo, bq, bv, bo)])


def ffn_forward_kernel(
    aliased,
    rb,
    offset,
    x1_ref,
    g1_ref,
    s1_ref,
    wi_ref,
    bi_ref,
    wo_ref,
    bo_ref,
    g2_ref,
    s2_ref,
    wp_ref,
    *rest,
):
    rest = rest[aliased:]
    u_ref, d_ref, x2_ref, rate2_ref, e_ref, emb_ref, h1_scr, r2_scr = rest
    step = pl.program_id(0)
    rows = h1_scr.shape[0]
    own = slice(offset, offset + rows)
    chunk = pl.ds(pl.multiple_of(step * FCHUNK, FCHUNK), FCHUNK)

    @pl.when(step == 0)
    def _():
        h1 = x1_ref[own] * g1_ref[...] + s1_ref[...]
        h1_scr[...] = h1.astype(BF16)
        r2_scr[...] = h1 + bo_ref[...]

    for r in range(0, rows, rb):
        f = dot(h1_scr[r : r + rb], wi_ref[...])
        bias = bi_ref[...]
        for i in range(0, rb, SLICE):
            u, d = gelu_pair(f[i : i + SLICE] + bias)
            at = offset + r + i
            u_ref[at : at + SLICE, chunk] = u.astype(BF16)
            d_ref[at : at + SLICE, chunk] = d.astype(BF16)
        r2_scr[r : r + rb] += dot(u_ref[offset + r : offset + r + rb, chunk], wo_ref[...])

    @pl.when(step == pl.num_programs(0) - 1)
    def _():
        scaled, rate = norm_stats(r2_scr[...])
        x2_ref[own] = scaled
        rate2_ref[own] = jnp.broadcast_to(rate, (rows, LANES))
        h2 = (scaled * g2_ref[...] + s2_ref[...]).astype(BF16)
        e = dot(h2, wp_ref[...])
        e_ref[own] = e
        size = jnp.sum(e * e, axis=-1, keepdims=True)
        emb_ref[...] = (e * lax.rsqrt(size + EMBED_EPS)).astype(BF16)


def ffn_forward(count, offset, total, x1, g1, s1, wi, bi, wo, bo, g2, s2, wp, previous):
    width = x1.shape[1]
    ff = wi.shape[1]
    dim = wp.shape[1]
    first = 10
    held = list(previous)
    return pl.pallas_call(
        functools.partial(ffn_forward_kernel, len(held), min(RB, count), offset),
        grid=(ff // FCHUNK,),
        in_specs=[
            whole(x1),
            const(g1),
            const(s1),
            spec((width, FCHUNK), lambda c: (0, c)),
            spec((1, FCHUNK), lambda c: (0, c)),
            spec((FCHUNK, width), lambda c: (c, 0)),
            const(bo),
            const(g2),
            const(s2),
            const(wp),
        ]
        + [whole(None)] * len(held),
        out_specs=[whole(None)] * 6,
        out_shape=[
            shaped((total, ff), BF16),
            shaped((total, ff), BF16),
            shaped((total, width), F32),
            shaped((total, LANES), F32),
            shaped((total, dim), F32),
            shaped((count, dim), BF16),
        ],
        scratch_shapes=[
            pltpu.VMEM((count, width), BF16),
            pltpu.VMEM((count, width), F32),
        ],
        input_output_aliases={first + i: i for i in range(len(held))},
        compiler_params=params(1, 16),
        cost_estimate=cost(12 if count > 256 else 4),
        name="ffn_forward",
    )(x1, g1, s1, in_hbm(wi), bi, in_hbm(wo), bo, g2, s2, wp, *held)


def passage_member(lengths_ref, rows):
    ends = segment_ends(lengths_ref)
    lane = lax.broadcasted_iota(jnp.int32, (8, LANES), 1)
    low = jnp.full((8, LANES), rows, jnp.int32)
    high = jnp.zeros((8, LANES), jnp.int32)
    start = jnp.int32(0)
    for s, end in enumerate(ends):
        low = jnp.where(lane == s, start, low)
        high = jnp.where(lane == s, end, high)
        start = end
    token = lax.broadcasted_iota(jnp.int32, (rows, LANES), 0) + longest_start(lengths_ref, rows // 2)
    token = jnp.where(token >= rows, token - rows, token)
    inside = (token >= low[:1]) & (token < high[:1])
    return jnp.where(inside, 1.0, 0.0).astype(BF16)


def soft_match(group, pass_embed):
    return jnp.exp(SHARPNESS * dot_t(group, pass_embed) - SHARPNESS)


def score_kernel(psg, count, lengths_ref, emb_ref, *rest):
    group_refs = rest[:psg]
    score_ref, pooled_ref = rest[psg:]
    member = passage_member(lengths_ref, emb_ref.shape[0])
    group = jnp.concatenate([ref[...] for ref in group_refs], axis=0)
    matched = soft_match(group, emb_ref[...])
    pooled = two_part_dot(matched, member)
    lane = lax.broadcasted_iota(jnp.int32, pooled.shape, 1)
    pooled = jnp.where(lane < count, pooled, 1.0)
    pooled_ref[...] = pooled
    smooth = 1.0 + jnp.log(pooled) * (1.0 / SHARPNESS)
    queries = pooled.shape[0] // QLEN
    score_ref[...] = SCORE_SCALE * jnp.sum(smooth.reshape(queries, QLEN, LANES), axis=1)


def score(lengths, emb, groups):
    psg = len(groups)
    tokens = sum(g.shape[0] for g in groups)
    return pl.pallas_call(
        functools.partial(score_kernel, psg, lengths.shape[1]),
        in_specs=[smem()] + [pl.BlockSpec(memory_space=pltpu.VMEM)] * (1 + psg),
        out_shape=[shaped((tokens // QLEN, LANES), F32), shaped((tokens, LANES), F32)],
        compiler_params=params(0, 8),
        cost_estimate=cost(3),
        name="score",
    )(lengths, emb, *groups)


def loss_kernel(psg, count, where_ref, lengths_ref, positives_ref, pooled_ref, emb_ref, *rest):
    group_refs = rest[:psg]
    score_refs = rest[psg : 2 * psg]
    loss_ref, own_ref = rest[2 * psg : 2 * psg + 2]
    away_refs = rest[2 * psg + 2 : 3 * psg + 1]
    grad_ref = rest[3 * psg + 1]
    position = where_ref[3]
    queries = score_refs[0].shape[0]
    each = queries // psg
    lane = lax.broadcasted_iota(jnp.int32, (queries, LANES), 1)
    row = lax.broadcasted_iota(jnp.int32, (queries, LANES), 0)
    valid = lane < count
    blocks = []
    for e in range(psg):
        found = score_refs[e][...]
        found = jnp.concatenate(
            [found[((d - e) % psg) * each : ((d - e) % psg + 1) * each] for d in range(psg)], axis=0
        )
        blocks.append(jnp.where(valid, found, -jnp.inf))
    target = jnp.zeros((queries, LANES), jnp.int32)
    for d in range(psg):
        for j in range(each):
            chosen = positives_ref[lax.rem(position + d, psg) * each + j]
            target = jnp.where(row == d * each + j, chosen, target)
    peak = blocks[0]
    for found in blocks[1:]:
        peak = jnp.maximum(peak, found)
    peak = jnp.max(peak, axis=-1, keepdims=True)
    total = jnp.zeros((queries, 1), F32)
    picked = jnp.zeros((queries, 1), F32)
    for e in range(psg):
        owner = lax.rem(position + e, psg)
        hit = (target == owner * count + lane) & valid
        total = total + jnp.sum(jnp.exp(blocks[e] - peak), axis=-1, keepdims=True)
        picked = picked + jnp.sum(jnp.where(hit, blocks[e], 0.0), axis=-1, keepdims=True)
        if e == 0:
            own_hit = jnp.where(hit, 1.0, 0.0)
    log_total = peak + jnp.log(total)
    losses = jnp.broadcast_to(log_total - picked, (queries, LANES))
    place = lax.rem(position + row // each, psg) * each + row % each
    losses = jnp.sum(jnp.where(lane == place, losses, 0.0), axis=0, keepdims=True)
    loss_ref[...] = losses[:, :queries]
    grad = jnp.where(valid, jnp.exp(blocks[0] - log_total) - own_hit, 0.0) * SCORE_SCALE
    tokens = queries * QLEN
    grad = jnp.broadcast_to(grad[:, None, :], (queries, QLEN, LANES)).reshape(tokens, LANES)
    grad = grad / pooled_ref[...]
    member = passage_member(lengths_ref, emb_ref.shape[0])
    high = grad.astype(BF16)
    rest_low = (grad - high.astype(F32)).astype(BF16)
    spread = dot_t(high, member) + dot_t(rest_low, member)
    group = jnp.concatenate([ref[...] for ref in group_refs], axis=0)
    low = (soft_match(group, emb_ref[...]) * spread).astype(BF16)
    group_grad = dot(low, emb_ref[...])
    each_tokens = tokens // psg
    own_ref[...] = group_grad[:each_tokens]
    for d in range(1, psg):
        away_refs[d - 1][...] = group_grad[d * each_tokens : (d + 1) * each_tokens].astype(BF16)
    grad_ref[...] = jnp.transpose(dot(jnp.transpose(group), low))


def loss_and_grads(position, lengths, positives, pooled, emb, groups, scores):
    psg = len(groups)
    queries = scores[0].shape[0]
    tokens, dim = groups[0].shape
    vmem = pl.BlockSpec(memory_space=pltpu.VMEM)
    return pl.pallas_call(
        functools.partial(loss_kernel, psg, lengths.shape[1]),
        in_specs=[smem(), smem(), smem()] + [vmem] * (2 + 2 * psg),
        out_shape=[shaped((1, queries), F32), shaped((tokens, dim), F32)]
        + [shaped((tokens, dim), BF16)] * (psg - 1)
        + [shaped(emb.shape, F32)],
        compiler_params=params(0, 8),
        cost_estimate=cost(3),
        name="loss_and_grads",
    )(position, lengths, positives, pooled, emb, *groups, *scores)


def head_backward(grad_embed, e, x2, rate2, wp, g2, s2):
    low = unit_backward(grad_embed, e).astype(BF16)
    grad_h2 = dot_t(low, wp)
    grad_r2, gain_term, shift_term = norm_backward(grad_h2, x2, rate2[:, :1], g2)
    h2 = (x2 * g2 + s2).astype(BF16)
    return grad_r2, gain_term, shift_term, dot(jnp.transpose(low), h2)


def passage_head_kernel(
    grad_ref, e_ref, x2_ref, rate2_ref, wp_ref, g2_ref, s2_ref, gr2_ref, vec_ref, proj_ref
):
    ptok = grad_ref.shape[0]
    grad_r2, gain_term, shift_term, proj = head_backward(
        grad_ref[...], e_ref[:ptok], x2_ref[:ptok], rate2_ref[:ptok], wp_ref[...], g2_ref[...], s2_ref[...]
    )
    gr2_ref[...] = grad_r2
    vec_ref[...] = jnp.zeros_like(vec_ref)
    vec_ref[0:1] = gain_term
    vec_ref[1:2] = shift_term
    proj_ref[...] = proj


def passage_head(grad, e, x2, rate2, wp, g2, s2):
    ptok, dim = grad.shape
    width = x2.shape[1]
    return pl.pallas_call(
        passage_head_kernel,
        grid=(1,),
        in_specs=[
            whole(grad),
            whole(e),
            whole(x2),
            whole(rate2),
            const(wp),
            const(g2),
            const(s2),
        ],
        out_specs=[whole(None)] * 3,
        out_shape=[shaped((ptok, width), F32), shaped((8, width), F32), shaped((dim, width), F32)],
        compiler_params=params(1, 10),
        cost_estimate=cost(4),
        name="passage_head",
    )(grad, e, x2, rate2, wp, g2, s2)


def fixed(shape):
    return pl.BlockSpec(memory_space=pltpu.VMEM)


def ffn_backward_kernel(
    psg,
    me_ref,
    gr2p_ref,
    vec_ref,
    proj_ref,
    own_ref,
    *rest,
):
    away_refs = rest[: psg - 1]
    (
        e_ref,
        x2_ref,
        rate2_ref,
        wp_ref,
        g2_ref,
        s2_ref,
        x1_ref,
        g1_ref,
        s1_ref,
        wi_ref,
        wo_ref,
        u_ref,
        d_ref,
        dproj_ref,
        dvec_ref,
        dbi_ref,
        gh1_ref,
        keep_i_ref,
        send_i_ref,
        keep_o_ref,
        send_o_ref,
        gz_scr,
        turn_scr,
        gzt_scr,
        h1t_scr,
        gh1_scr,
    ) = rest[psg - 1 :]
    step = pl.program_id(0)
    ptok = gr2p_ref.shape[0]

    @pl.when(step == 0)
    def _():
        grad = own_ref[...]
        for ref in away_refs:
            grad = grad + ref[...].astype(F32)
        grad_r2, gain_term, shift_term, proj = head_backward(
            grad, e_ref[ptok:], x2_ref[ptok:], rate2_ref[ptok:], wp_ref[...], g2_ref[...], s2_ref[...]
        )
        dproj_ref[...] = jnp.transpose(proj_ref[...] + proj).astype(BF16)
        gr2p = gr2p_ref[...]
        gh1_scr[:ptok] = gr2p
        gh1_scr[ptok:] = grad_r2
        low_p = gr2p.astype(BF16)
        low_q = grad_r2.astype(BF16)
        gz_scr[:ptok] = low_p
        gz_scr[ptok:] = low_q
        dvec_ref[...] = jnp.zeros_like(dvec_ref)
        dvec_ref[0:1] = vec_ref[0:1] + gain_term
        dvec_ref[1:2] = vec_ref[1:2] + shift_term
        dvec_ref[2:3] = jnp.sum(low_p.astype(F32), axis=0, keepdims=True) + jnp.sum(
            low_q.astype(F32), axis=0, keepdims=True
        )
        turn_scr[...] = jnp.transpose((x1_ref[...] * g1_ref[...] + s1_ref[...]).astype(BF16))
        to_relative(me_ref, turn_scr, h1t_scr)
        turn_scr[...] = jnp.transpose(gz_scr[...])
        to_relative(me_ref, turn_scr, gzt_scr, turned=True)

    chunk = pl.ds(pl.multiple_of(step * FCHUNK, FCHUNK), FCHUNK)
    gz = gz_scr[...]
    grad_active = dot_t(gz, wo_ref[...])
    grad_inner = (grad_active * d_ref[:, chunk].astype(F32)).astype(BF16)
    dbi_ref[:, chunk] = jnp.sum(grad_inner.astype(F32), axis=0, keepdims=True)
    gh1_scr[...] += dot_t(grad_inner, wi_ref[...])
    half = keep_i_ref.shape[0]
    for term, keep_ref, send_ref in (
        (dot(h1t_scr[...], grad_inner), keep_i_ref, send_i_ref),
        (dot(gzt_scr[...], u_ref[:, chunk]), keep_o_ref, send_o_ref),
    ):
        keep_ref[:, chunk] = term[:half].astype(BF16)
        send_ref[:, chunk] = term[half:].astype(BF16)

    @pl.when(step == pl.num_programs(0) - 1)
    def _():
        gh1_ref[...] = gh1_scr[...]


def ffn_backward(me, gr2p, vec, proj, own, aways, e, x2, rate2, wp, g2, s2, x1, g1, s1, wi, wo, u, d):
    ptok, width = gr2p.shape
    rows = x1.shape[0]
    dim = wp.shape[1]
    ff = wi.shape[1]
    return pl.pallas_call(
        functools.partial(ffn_backward_kernel, 1 + len(aways)),
        grid=(ff // FCHUNK,),
        in_specs=[smem(), whole(gr2p), whole(vec), whole(proj), whole(own)]
        + [whole(a) for a in aways]
        + [
            whole(e),
            whole(x2),
            whole(rate2),
            const(wp),
            const(g2),
            const(s2),
            whole(x1),
            const(g1),
            const(s1),
            spec((width, FCHUNK), lambda c: (0, c)),
            spec((FCHUNK, width), lambda c: (c, 0)),
            whole(u),
            whole(d),
        ],
        out_specs=[
            fixed((width, dim)),
            fixed((8, width)),
            fixed((1, ff)),
            fixed((rows, width)),
        ]
        + [whole(None)] * 4,
        out_shape=[
            shaped((width, dim), BF16),
            shaped((8, width), F32),
            shaped((1, ff), F32),
            shaped((rows, width), F32),
        ]
        + [shaped((width // 2, ff), BF16)] * 4,
        scratch_shapes=[
            pltpu.VMEM((rows, width), BF16),
            pltpu.VMEM((width, rows), BF16),
            pltpu.VMEM((width, rows), BF16),
            pltpu.VMEM((width, rows), BF16),
            pltpu.VMEM((rows, width), F32),
        ],
        compiler_params=params(1, 20),
        cost_estimate=cost(15),
        name="ffn_backward",
    )(me, gr2p, vec, proj, own, *aways, e, x2, rate2, wp, g2, s2, x1, g1, s1, in_hbm(wi), in_hbm(wo), u, d)


def put_vector(wave_ref, row, vector):
    for i in range(vector.shape[1] // LANES):
        wave_ref[row + i : row + i + 1] = vector[:, i * LANES : (i + 1) * LANES]
    return row + vector.shape[1] // LANES


def take_vector(wave_ref, row, column, out_ref):
    size = out_ref.shape[1]
    for i in range(size // LANES):
        out_ref[:, i * LANES : (i + 1) * LANES] = wave_ref[row + i : row + i + 1, column : column + LANES].astype(
            F32
        )
    return row + size // LANES


def units(pair, ptok, qtok):
    for index, (base, size, bias_row) in enumerate(spans(ptok, qtok)):
        block = min(RB, size)
        place = 0
        for r0 in range(base, base + size, block):
            for side in range(2):
                yield index, base, size, bias_row, r0, block, side, place
                place += block


def one_head(block, side, rows):
    lane = lax.broadcasted_iota(jnp.int32, (block, LANES), 1)
    return jnp.where((lane < HEAD) if side == 0 else (lane >= HEAD), rows, BF16(0))


def probabilities_kernel(ptok, lengths_ref, q_ref, k_ref, lse_ref, p_ref, pq_ref, bias_scr):
    qtok = q_ref.shape[0] - ptok

    @pl.when(pl.program_id(0) == 0)
    def _():
        fill_bias(bias_scr, lengths_ref, ptok, qtok)

    step = pl.program_id(0)
    for pair in range(QUAD // 2):
        lanes = pl.ds(pl.multiple_of(step * QLANES + pair * LANES, LANES), LANES)
        for index, base, size, bias_row, r0, block, side, place in units(pair, ptok, qtok):
            h = 2 * pair + side
            s = dot_t(k_ref[base : base + size, lanes], one_head(block, side, q_ref[r0 : r0 + block, lanes]))
            lse = lse_ref[step, h : h + 1, r0 : r0 + block]
            for i in range(0, size, ASLICE):
                part = s[i : i + ASLICE]
                if bias_row is not None:
                    part = part + bias_scr[bias_row + i : bias_row + i + ASLICE, r0 - base : r0 - base + block]
                p = jnp.exp(part - lse).astype(BF16)
                if index < 2:
                    p_ref[step, 2 * pair + index, i : i + ASLICE, place : place + block] = p
                else:
                    pq_ref[step, pair, i : i + ASLICE, place : place + block] = p


def probabilities(lengths, q, k, lse, ptok):
    rows, width = q.shape
    quads = HEADS // QUAD
    half, qtok = ptok // 2, rows - ptok
    return pl.pallas_call(
        functools.partial(probabilities_kernel, ptok),
        grid=(quads,),
        in_specs=[smem(), whole(q), whole(k), whole(lse)],
        out_specs=[whole(None), whole(None)],
        out_shape=[
            shaped((quads, QUAD, half, 2 * half), BF16),
            shaped((quads, QUAD // 2, qtok, 2 * qtok), BF16),
        ],
        scratch_shapes=[pltpu.VMEM((half + qtok, half), F32)],
        compiler_params=params(1, 10),
        cost_estimate=cost(8),
        name="probabilities",
    )(lengths, q, k, lse)


def first_norm_kernel(gh1_ref, x1_ref, rate1_ref, g1_ref, wo_ref, gr1_ref, go_ref, vec_ref):
    grad_r1, gain_term, shift_term = norm_backward(gh1_ref[...], x1_ref[...], rate1_ref[:, :1], g1_ref[...])
    gr1_ref[...] = grad_r1
    low = grad_r1.astype(BF16)
    vec_ref[...] = jnp.zeros_like(vec_ref)
    vec_ref[0:1] = gain_term
    vec_ref[1:2] = shift_term
    vec_ref[2:3] = jnp.sum(low.astype(F32), axis=0, keepdims=True)
    go_ref[...] = dot_t(low, wo_ref[...]).astype(BF16)


def first_norm(gh1, x1, rate1, g1, wo):
    rows, width = x1.shape
    return pl.pallas_call(
        first_norm_kernel,
        grid=(1,),
        in_specs=[whole(gh1), whole(x1), whole(rate1), const(g1), const(wo)],
        out_specs=[whole(None)] * 3,
        out_shape=[shaped((rows, width), F32), shaped((rows, width), BF16), shaped((8, width), F32)],
        compiler_params=params(1, 9),
        cost_estimate=cost(4),
        name="first_norm",
    )(gh1, x1, rate1, g1, wo)


def heads_backward_kernel(
    quad,
    ptok,
    p_ref,
    pq_ref,
    q_ref,
    k_ref,
    v_ref,
    o_ref,
    go_ref,
    gq_ref,
    gk_ref,
    gv_ref,
    dd_scr,
    gqt_scr,
    qm_scr,
    gm_scr,
    gs_scr,
    kt_scr,
):
    qtok = q_ref.shape[0] - ptok

    own = slice(quad * QLANES, (quad + 1) * QLANES)
    product = go_ref[:, own].astype(F32) * o_ref[:, own].astype(F32)
    ones = jnp.where(
        lax.broadcasted_iota(jnp.int32, (16, QLANES), 1) // HEAD
        == lax.broadcasted_iota(jnp.int32, (16, QLANES), 0),
        1.0,
        0.0,
    ).astype(BF16)
    high = product.astype(BF16)
    dd_scr[...] = dot_t(ones, high) + dot_t(ones, (product - high.astype(F32)).astype(BF16))
    kt_scr[...] = jnp.transpose(k_ref[:, own])
    for pair in range(QUAD // 2):
        inner = slice(pair * LANES, (pair + 1) * LANES)
        lanes = slice(quad * QLANES + pair * LANES, quad * QLANES + (pair + 1) * LANES)
        last = None
        for index, base, size, bias_row, r0, block, side, place in units(pair, ptok, qtok):
            buffer = (3 * pair + index) % 2
            h = 2 * pair + side
            qm_scr[buffer, place : place + block] = one_head(block, side, q_ref[r0 : r0 + block, lanes])
            gm = one_head(block, side, go_ref[r0 : r0 + block, lanes])
            gm_scr[buffer, place : place + block] = gm
            grad_prob = dot_t(v_ref[base : base + size, lanes], gm)
            dd = dd_scr[h : h + 1, r0 : r0 + block]
            p_at = p_ref.at[quad, 2 * pair + index] if index < 2 else pq_ref.at[quad, pair]
            for i in range(0, size, ASLICE):
                p = p_at[i : i + ASLICE, place : place + block].astype(F32)
                gs = p * (grad_prob[i : i + ASLICE] - dd)
                gs_scr[buffer, i : i + ASLICE, place : place + block] = gs.astype(BF16)
            gqt_scr[h * HEAD : (h + 1) * HEAD, r0 : r0 + block] = dot(
                kt_scr[h * HEAD : (h + 1) * HEAD, base : base + size],
                gs_scr[buffer, :size, place : place + block],
            )
            end = place + block
            if end == 2 * size:
                gv_ref[base : base + size, inner] = dot(p_at[...], gm_scr[buffer, :end]).astype(BF16)
                gk_ref[base : base + size, inner] = dot(gs_scr[buffer, :size, :end], qm_scr[buffer, :end]).astype(
                    BF16
                )
    gq_ref[...] = (jnp.transpose(gqt_scr[...]) * (HEAD**-0.5)).astype(BF16)


def heads_backward(quad, p, pq, q, k, v, o, go, ptok):
    rows, width = q.shape
    half = ptok // 2
    low = lambda *shape: pltpu.VMEM(shape, BF16)
    return pl.pallas_call(
        functools.partial(heads_backward_kernel, quad, ptok),
        grid=(1,),
        in_specs=[whole(None)] * 7,
        out_specs=[whole(None)] * 3,
        out_shape=[shaped((rows, QLANES), BF16)] * 3,
        scratch_shapes=[
            pltpu.VMEM((16, rows), F32),
            pltpu.VMEM((QLANES, rows), F32),
            low(2, 4 * RB, LANES),
            low(2, 4 * RB, LANES),
            low(2, half, 4 * RB),
            low(QLANES, rows),
        ],
        compiler_params=params(1, 16),
        cost_estimate=cost(10),
        name="heads_backward",
    )(p, pq, q, k, v, o, go)


def output_term_kernel(me_ref, gr1_ref, o_ref, dout_ref, turn_scr, ot_scr):
    turn_scr[...] = jnp.transpose(o_ref[...])
    to_relative(me_ref, turn_scr, ot_scr)
    dout_ref[...] = dot(ot_scr[...], gr1_ref[...].astype(BF16)).astype(BF16)


def output_term(me, gr1, o):
    rows, width = gr1.shape
    return pl.pallas_call(
        output_term_kernel,
        grid=(1,),
        in_specs=[smem(), whole(gr1), whole(o)],
        out_specs=whole(None),
        out_shape=shaped((width, width), BF16),
        scratch_shapes=[pltpu.VMEM((width, rows), BF16)] * 2,
        compiler_params=params(1, 8),
        cost_estimate=cost(2),
        name="output_term",
    )(me, gr1, o)


def weights_kernel(
    ptok,
    me_ref,
    gr1_ref,
    dout_ref,
    xt_ref,
    gq0_ref,
    gk0_ref,
    gv0_ref,
    gq1_ref,
    gk1_ref,
    gv1_ref,
    dproj_ref,
    vec1_ref,
    vec2_ref,
    dbi_ref,
    wq_ref,
    wk_ref,
    wv_ref,
    keep_ref,
    send_ref,
    gp_ref,
    gq_ref,
    xt_scr,
    lines_scr,
    tail_scr,
):
    half_rows = keep_ref.shape[0]
    width = gr1_ref.shape[1]
    gr1 = gr1_ref[...]
    to_relative(me_ref, xt_ref, xt_scr)
    joined = [
        jnp.concatenate([left[...], right[...]], axis=1)
        for left, right in ((gq0_ref, gq1_ref), (gk0_ref, gk1_ref), (gv0_ref, gv1_ref))
    ]
    for i, grad in enumerate(joined):
        term = dot(xt_scr[...], grad)
        keep_ref[:, i * width : (i + 1) * width] = term[:half_rows].astype(BF16)
        send_ref[:, i * width : (i + 1) * width] = term[half_rows:].astype(BF16)
    keep_ref[:, 3 * width : 4 * width] = dout_ref[:half_rows]
    send_ref[:, 3 * width : 4 * width] = dout_ref[half_rows:]
    gin = gr1 + dot_t(joined[0], wq_ref[...]) + dot_t(joined[1], wk_ref[...]) + dot_t(joined[2], wv_ref[...])
    gp_ref[...] = gin[:ptok].astype(BF16)
    gq_ref[...] = gin[ptok:].astype(BF16)
    row = 0
    for vector in (
        vec2_ref[0:1],
        vec2_ref[1:2],
        vec2_ref[2:3],
        vec1_ref[0:1],
        vec1_ref[1:2],
        vec1_ref[2:3],
        dbi_ref[...],
        jnp.sum(joined[0].astype(F32), axis=0, keepdims=True),
        jnp.sum(joined[2].astype(F32), axis=0, keepdims=True),
    ):
        row = put_vector(lines_scr, row, vector)
    lines_scr[row:] = jnp.zeros((lines_scr.shape[0] - row, LANES), F32)
    dim = dproj_ref.shape[1]
    tail_scr[:, :dim] = dproj_ref[...]
    tail_scr[:, dim:] = lines_scr[...].astype(BF16)
    for r in range(32):
        ref = keep_ref if r < 16 else send_ref
        at = (r % 16) * PIECE
        ref[at : at + PIECE, 4 * width :] = tail_scr[pl.ds(owner_place(me_ref, r), PIECE), :]


def weights(me, gr1, dout, xt, first, second, dproj, vec1, vec2, dbi, wq, wk, wv, ptok):
    rows, width = gr1.shape
    lanes = 4 * width + dproj.shape[1] + LANES
    low = lambda *shape: pltpu.VMEM(shape, BF16)
    return pl.pallas_call(
        functools.partial(weights_kernel, ptok),
        grid=(1,),
        in_specs=[smem()] + [whole(None)] * 16,
        out_specs=[whole(None)] * 4,
        out_shape=[
            shaped((width // 2, lanes), BF16),
            shaped((width // 2, lanes), BF16),
            shaped((ptok, width), BF16),
            shaped((rows - ptok, width), BF16),
        ],
        scratch_shapes=[
            low(width, rows),
            pltpu.VMEM((width, LANES), F32),
            low(width, dproj.shape[1] + LANES),
        ],
        compiler_params=params(1, 16),
        cost_estimate=cost(6),
        name="weights",
    )(me, gr1, dout, xt, *first, *second, dproj, vec1, vec2, dbi, wq, wk, wv)


def from_relative(me_ref, kept_ref, other_ref, wave_ref, turned=False):
    for r in range(32):
        ref = kept_ref if r < 16 else other_ref
        at = (r % 16) * PIECE
        wave_ref[pl.ds(owner_place(me_ref, r, turned), PIECE), :] = ref[at : at + PIECE]


def unpack_ffn_kernel(
    me_ref, kept_i_ref, other_i_ref, kept_o_ref, other_o_ref, dwi_ref, dwo_ref, wave_i_scr, wave_o_scr
):
    from_relative(me_ref, kept_i_ref, other_i_ref, wave_i_scr)
    from_relative(me_ref, kept_o_ref, other_o_ref, wave_o_scr, turned=True)
    dwi_ref[...] = wave_i_scr[...].astype(F32)
    dwo_ref[...] = jnp.transpose(wave_o_scr[...].astype(F32))


def unpack_ffn(me, *halves):
    half, ff = halves[0].shape
    width = 2 * half
    return pl.pallas_call(
        unpack_ffn_kernel,
        grid=(ff // FCHUNK,),
        in_specs=[smem()] + [spec((half, FCHUNK), lambda c: (0, c))] * 4,
        out_specs=[
            spec((width, FCHUNK), lambda c: (0, c)),
            spec((FCHUNK, width), lambda c: (c, 0)),
        ],
        out_shape=[shaped((width, ff), F32), shaped((ff, width), F32)],
        scratch_shapes=[pltpu.VMEM((width, FCHUNK), BF16)] * 2,
        compiler_params=params(1, 16),
        cost_estimate=cost(6),
        name="unpack_ffn",
    )(me, *halves)


def unpack_attention_kernel(
    me_ref,
    kept_ref,
    other_ref,
    dwq_ref,
    dwk_ref,
    dwv_ref,
    dout_ref,
    dproj_ref,
    g2_ref,
    s2_ref,
    bo_ref,
    g1_ref,
    s1_ref,
    bout_ref,
    bi_ref,
    bq_ref,
    bv_ref,
    wave_scr,
):
    from_relative(me_ref, kept_ref, other_ref, wave_scr)
    column = 0
    for ref in (dwq_ref, dwk_ref, dwv_ref, dout_ref, dproj_ref):
        ref[...] = wave_scr[:, column : column + ref.shape[1]].astype(F32)
        column += ref.shape[1]
    row = 0
    for ref in (g2_ref, s2_ref, bo_ref, g1_ref, s1_ref, bout_ref, bi_ref, bq_ref, bv_ref):
        row = take_vector(wave_scr, row, column, ref)


def unpack_attention(me, kept, other, width, dim, ff):
    vmem = pl.BlockSpec(memory_space=pltpu.VMEM)
    return pl.pallas_call(
        unpack_attention_kernel,
        in_specs=[smem()] + [vmem] * 2,
        out_shape=[shaped((width, width), F32)] * 4
        + [shaped((width, dim), F32)]
        + [shaped((1, width), F32)] * 6
        + [shaped((1, ff), F32)]
        + [shaped((1, width), F32)] * 2,
        scratch_shapes=[pltpu.VMEM((width, kept.shape[1]), BF16)],
        compiler_params=params(0, 16),
        cost_estimate=cost(3),
        name="unpack_attention",
    )(me, kept, other)


def swap(block, axis_name, size, bit):
    return lax.ppermute(block, axis_name, [(i, i ^ bit) for i in range(size)])


def total(*parts):
    found = parts[0].astype(F32)
    for part in parts[1:]:
        found = found + part.astype(F32)
    return found.astype(BF16)


def core_parts(keep, found):
    size = keep.shape[0] // 4
    return [total(keep[i * size : (i + 1) * size], found[i * size : (i + 1) * size]) for i in range(4)]


def halves(block):
    size = block.shape[0] // 2
    return block[:size], block[size:]


def plane_send(blocks, grp_size):
    return tuple(swap(block, "grp", grp_size, bits) for block, bits in zip(blocks, (4, 2, 6)))


def line_parts(parts, psg_size):
    size = parts[0].shape[0] // psg_size
    return [total(*[part[i * size : (i + 1) * size] for part in parts]) for i in range(psg_size)]


def line_send(blocks, psg_size):
    return tuple(swap(block, "psg", psg_size, d) for d, block in enumerate(blocks, 1))


def line_total(own, founds, grp_size):
    piece = total(own, *founds)
    bit = 8
    while bit < grp_size:
        piece = total(piece, swap(piece, "grp", grp_size, bit))
        bit *= 2
    return piece


def tie(values, *others):
    return lax.optimization_barrier((tuple(values), others))[0]


def roll_back_kernel(lengths_ref, embed_ref, grad_ref, embed_out, grad_out, embed_scr, grad_scr):
    count = embed_ref.shape[0]
    back = count - longest_start(lengths_ref, count // 2)
    back = jnp.where(back == count, 0, back)
    aligned = (back // PIECE) * PIECE
    pick = shift_pick(back - aligned)
    for ref, scr, out in ((embed_ref, embed_scr, embed_out), (grad_ref, grad_scr, grad_out)):
        scr[:count] = ref[...]
        scr[count:] = ref[...]
        for r0 in range(0, count, LANES):
            at = pl.multiple_of(aligned + r0, PIECE)
            out[r0 : r0 + LANES] = dot(pick, scr[pl.ds(at, LANES + PIECE), :]).astype(BF16)


def roll_back(lengths, embed, grad):
    return pl.pallas_call(
        roll_back_kernel,
        grid=(1,),
        in_specs=[smem(), whole(embed), whole(grad)],
        out_specs=[whole(None)] * 2,
        out_shape=[shaped(embed.shape, BF16), shaped(grad.shape, BF16)],
        scratch_shapes=[
            pltpu.VMEM((2 * embed.shape[0], embed.shape[1]), BF16),
            pltpu.VMEM((2 * grad.shape[0], grad.shape[1]), BF16),
        ],
        compiler_params=params(1, 10),
        cost_estimate=cost(4),
        name="roll_back",
    )(lengths, embed, grad)


def shift_gather(block, axis_name, axis_size):
    found = [block]
    for distance in range(1, axis_size):
        ring = [(i, (i - distance) % axis_size) for i in range(axis_size)]
        found.append(lax.ppermute(block, axis_name, ring))
    return found


def local(
    grp_size,
    psg_size,
    passages,
    queries,
    lengths,
    positives,
    query_weight,
    query_bias,
    key_weight,
    value_weight,
    value_bias,
    output_weight,
    output_bias,
    first_gain,
    first_shift,
    inner_weight,
    inner_bias,
    outer_weight,
    outer_bias,
    second_gain,
    second_shift,
    project_weight,
):
    ptok, width = passages.shape
    qtok = queries.shape[0]
    rows = ptok + qtok
    row = lambda vector: vector.reshape(1, -1)
    g1, s1, g2, s2 = row(first_gain), row(first_shift), row(second_gain), row(second_shift)
    q, k, v, o, lse, x1, rate1, xt, me = attention_forward(
        lengths,
        passages,
        queries,
        query_weight,
        row(query_bias),
        key_weight,
        value_weight,
        row(value_bias),
        output_weight,
        row(output_bias),
    )
    layer = (x1, g1, s1, inner_weight, row(inner_bias), outer_weight, row(outer_bias), g2, s2, project_weight)
    *held, query_embed = ffn_forward(qtok, ptok, rows, *layer, ())
    groups = shift_gather(query_embed, "psg", psg_size)
    u, d, x2, rate2, e, pass_embed = ffn_forward(ptok, 0, rows, *layer, held)
    own_scores, pooled = score(lengths, pass_embed, groups)
    scores = shift_gather(own_scores, "psg", psg_size)
    (late_lse,) = tie((lse,), own_scores)
    p, pq = probabilities(lengths, q, k, late_lse, ptok)
    scores[1:] = tie(scores[1:], p, pq)
    losses, own, *rest = loss_and_grads(me, lengths, positives, pooled, pass_embed, groups, scores)
    aways = []
    for distance, part in enumerate(rest[:-1], 1):
        ring = [(i, (i + distance) % psg_size) for i in range(psg_size)]
        aways.append(lax.ppermute(part, "psg", ring))
    gr2p, vec, proj = passage_head(rest[-1], e, x2, rate2, project_weight, g2, s2)
    dproj, vec2, dbi, gh1, keep_i, send_i, keep_o, send_o = ffn_backward(
        me,
        gr2p,
        vec,
        proj,
        own,
        aways,
        e,
        x2,
        rate2,
        project_weight,
        g2,
        s2,
        x1,
        g1,
        s1,
        inner_weight,
        outer_weight,
        u,
        d,
    )
    core_a = (swap(send_i, "grp", grp_size, 1), swap(send_o, "grp", grp_size, 1))
    gr1, go, vec1 = first_norm(gh1, x1, rate1, g1, output_weight)
    *core_a, go = tie((*core_a, go))
    next_i, away_i = [total(part, found) for part, found in zip(halves(keep_i), halves(core_a[0]))]
    next_o, away_o = [total(part, found) for part, found in zip(halves(keep_o), halves(core_a[1]))]
    plane_a = (swap(away_i, "grp", grp_size, 2), swap(away_o, "grp", grp_size, 4))
    first = heads_backward(0, p, pq, q, k, v, o, go, ptok)
    dout = output_term(me, gr1, o)
    plane_a = tie(plane_a, dout, *first)
    (go,) = tie((go,), *plane_a)
    next_i, away_i = [total(part, found) for part, found in zip(halves(next_i), halves(plane_a[0]))]
    next_o, away_o = [total(part, found) for part, found in zip(halves(next_o), halves(plane_a[1]))]
    plane_a = (swap(away_i, "grp", grp_size, 4), swap(away_o, "grp", grp_size, 2))
    second = heads_backward(1, p, pq, q, k, v, o, go, ptok)
    plane_a = tie(plane_a, *second)
    (gr1,) = tie((gr1,), *plane_a)
    both = lambda left, right: jnp.concatenate([left, right], axis=1)
    quarter = next_i.shape[0] // psg_size
    lines_a = [
        both(
            total(next_i[i * quarter : (i + 1) * quarter], plane_a[0][i * quarter : (i + 1) * quarter]),
            total(next_o[i * quarter : (i + 1) * quarter], plane_a[1][i * quarter : (i + 1) * quarter]),
        )
        for i in range(psg_size)
    ]
    line_a = line_send(lines_a[1:], psg_size)
    keep_b, send_b, grad_p, grad_q = weights(
        me,
        gr1,
        dout,
        xt,
        first,
        second,
        dproj,
        vec1,
        vec2,
        dbi,
        query_weight,
        key_weight,
        value_weight,
        ptok,
    )
    core_b = swap(send_b, "grp", grp_size, 1)
    line_a = tie(line_a, grad_q)
    piece_a = line_total(lines_a[0], line_a, grp_size)
    spread_a = line_send([piece_a] * (psg_size - 1), psg_size)
    parts_b = core_parts(keep_b, core_b)
    plane_b = plane_send(parts_b[1:], grp_size)
    (late_grad,) = tie((grad_p,), *parts_b[1:])
    out_embed, out_grad = roll_back(lengths, pass_embed, late_grad)
    plane_b = tie(plane_b, out_grad, *spread_a)
    lines_b = line_parts((parts_b[0], *plane_b), psg_size)
    line_b = line_send(lines_b[1:], psg_size)
    spread_a = tie(spread_a, *lines_b)
    ff = inner_weight.shape[1]
    held_i = jnp.concatenate([part[:, :ff] for part in (piece_a, *spread_a)])
    held_o = jnp.concatenate([part[:, ff:] for part in (piece_a, *spread_a)])
    found_a = (swap(held_i, "grp", grp_size, 4), swap(held_o, "grp", grp_size, 2))
    line_b = tie(line_b, held_i, held_o)
    piece_b = line_total(lines_b[0], line_b, grp_size)
    spread_b = line_send([piece_b] * (psg_size - 1), psg_size)
    found_a = tie(found_a, piece_b)
    held_i = jnp.concatenate([held_i, found_a[0]])
    held_o = jnp.concatenate([held_o, found_a[1]])
    found_a = (swap(held_i, "grp", grp_size, 2), swap(held_o, "grp", grp_size, 4))
    spread_b = tie(spread_b, held_i, held_o)
    joined_b = jnp.concatenate([piece_b, *spread_b])
    gathered_b = plane_send([joined_b] * 3, grp_size)
    found_a = tie(found_a, joined_b)
    held_i = jnp.concatenate([held_i, found_a[0]])
    held_o = jnp.concatenate([held_o, found_a[1]])
    other_i, other_o = swap(held_i, "grp", grp_size, 1), swap(held_o, "grp", grp_size, 1)
    dwi, dwo = unpack_ffn(me, held_i, other_i, held_o, other_o)
    gathered_b = tie(gathered_b, dwi, dwo)
    kept_b = jnp.concatenate([joined_b, *gathered_b])
    other_b = swap(kept_b, "grp", grp_size, 1)
    dwq, dwk, dwv, dout, dproj, g2, s2, bo, g1, s1, bout, bi, bq, bv = unpack_attention(
        me, kept_b, other_b, width, project_weight.shape[1], inner_weight.shape[1]
    )
    flat = lambda vector: vector.reshape(-1)
    return (
        out_embed,
        query_embed,
        flat(losses),
        out_grad,
        grad_q,
        dwq,
        flat(bq),
        dwk,
        dwv,
        flat(bv),
        dout,
        flat(bout),
        flat(g1),
        flat(s1),
        dwi,
        flat(bi),
        dwo,
        flat(bo),
        flat(g2),
        flat(s2),
        dproj,
    )


def solution(mesh):
    split = P(("grp", "psg"), None)
    in_specs = (split, split, split, P("grp")) + (P(),) * 16
    out_specs = (split, split, P("grp"), split, split) + (P(),) * 16
    body = functools.partial(local, mesh.shape["grp"], mesh.shape["psg"])
    return jax.shard_map(body, mesh=mesh, in_specs=in_specs, out_specs=out_specs, check_vma=False)
```

```python
import functools

import jax
import jax.numpy as jnp
from jax import lax
from jax.experimental import pallas as pl
from jax.experimental.pallas import tpu as pltpu
from jax.sharding import PartitionSpec as P

HEADS = 8
HEAD = 64
QLEN = 32

SHARPNESS = 10.0
SCORE_SCALE = 0.25
NORM_EPS = 1e-06
EMBED_EPS = 1e-06
NEG_FILL = -1e30

F32 = jnp.float32
BF16 = jnp.bfloat16

HALF_LOG2_E = -0.7213475204444817
LOG2_INV_SQRT_2PI = -1.3257480647361595

INV_SQRT_2 = 0.7071067811865476

QUAD = 4
QLANES = QUAD * HEAD
RB = 256
LANES = 128
FCHUNK = 512
SLICE = 16
ASLICE = 32
PIECE = 16


def dot(left, right):
    return jnp.dot(left, right, preferred_element_type=F32)


def dot_t(left, right):
    return lax.dot_general(left, right, (((1,), (1,)), ((), ())), preferred_element_type=F32)


def t_dot(left, right):
    return lax.dot_general(left, right, (((0,), (0,)), ((), ())), preferred_element_type=F32)


def two_part_dot(left, right_low):
    high = left.astype(BF16)
    rest = (left - high.astype(F32)).astype(BF16)
    return dot(high, right_low) + dot(rest, right_low)


def norm_stats(x):
    center = x - jnp.mean(x, axis=-1, keepdims=True)
    rate = lax.rsqrt(jnp.mean(center * center, axis=-1, keepdims=True) + NORM_EPS)
    return center * rate, rate


def norm_backward(grad, scaled, rate, gain):
    inner = grad * gain
    mean_in = jnp.mean(inner, axis=-1, keepdims=True)
    mean_dot = jnp.mean(inner * scaled, axis=-1, keepdims=True)
    grad_x = rate * (inner - mean_in - scaled * mean_dot)
    return grad_x, jnp.sum(grad * scaled, axis=0, keepdims=True), jnp.sum(grad, axis=0, keepdims=True)


def unit_backward(grad, projected):
    rate = lax.rsqrt(jnp.sum(projected * projected, axis=-1, keepdims=True) + EMBED_EPS)
    unit = projected * rate
    return rate * (grad - unit * jnp.sum(grad * unit, axis=-1, keepdims=True))


def gelu_pair(f):
    phi = 0.5 + 0.5 * lax.erf(f * INV_SQRT_2)
    density = jnp.exp2((f * f) * HALF_LOG2_E + LOG2_INV_SQRT_2PI)
    return f * phi, phi + f * density


def segment_ends(lengths_ref):
    count = lengths_ref.shape[1]
    ends = []
    total = jnp.int32(0)
    for s in range(count):
        total = total + lengths_ref[0, s]
        ends.append(total)
    return ends


def longest_start(lengths_ref, longest):
    found = jnp.int32(0)
    start = jnp.int32(0)
    for s in range(lengths_ref.shape[1]):
        found = jnp.where(lengths_ref[0, s] == longest, start, found)
        start = start + lengths_ref[0, s]
    return found


def shift_pick(shift):
    shape = (LANES, LANES + PIECE)
    row = lax.broadcasted_iota(jnp.int32, shape, 0) + shift
    return jnp.where(lax.broadcasted_iota(jnp.int32, shape, 1) == row, 1.0, 0.0).astype(BF16)


def fill_bias(bias_ref, lengths_ref, ptok, qtok):
    half = ptok // 2
    ends = segment_ends(lengths_ref)
    first = longest_start(lengths_ref, half)

    def segments(place):
        token = place + half + first
        token = jnp.where(token >= ptok, token - ptok, token)
        seg = jnp.zeros_like(token)
        for end in ends:
            seg = seg + jnp.where(token >= end, 1, 0)
        return seg

    row_seg = segments(lax.broadcasted_iota(jnp.int32, (8, half), 1))[:1]
    for r0 in range(0, half, LANES):
        col = segments(lax.broadcasted_iota(jnp.int32, (LANES, LANES), 0) + r0)
        for c in range(0, half, LANES):
            bias_ref[r0 : r0 + LANES, c : c + LANES] = jnp.where(col == row_seg[:, c : c + LANES], 0.0, NEG_FILL)
    for c in range(0, qtok, LANES):
        for r0 in range(0, qtok, LANES):
            row = (lax.broadcasted_iota(jnp.int32, (LANES, LANES), 0) + r0) // QLEN
            col = (lax.broadcasted_iota(jnp.int32, (LANES, LANES), 1) + c) // QLEN
            bias_ref[half + r0 : half + r0 + LANES, c : c + LANES] = jnp.where(row == col, 0.0, NEG_FILL)


def spans(ptok, qtok):
    half = ptok // 2
    return ((0, half, None), (half, half, 0), (ptok, qtok, half))


def owner_place(me_ref, r, turned=False):
    first, second = (r >> 3) & 1, (r >> 2) & 1
    if turned:
        first, second = second, first
    core, x, y, z = me_ref[0] ^ (r >> 4), me_ref[1] ^ first, me_ref[2] ^ second, me_ref[3] ^ (r & 3)
    return pl.multiple_of((((y * 2 + x) * 2 + core) * 4 + z) * PIECE, PIECE)


def to_relative(me_ref, plain_ref, out_ref, turned=False):
    for r in range(32):
        out_ref[r * PIECE : (r + 1) * PIECE] = plain_ref[pl.ds(owner_place(me_ref, r, turned), PIECE), :]


def units(pair, ptok, qtok):
    for index, (base, size, bias_row) in enumerate(spans(ptok, qtok)):
        block = min(RB, size)
        place = 0
        for r0 in range(base, base + size, block):
            for side in range(2):
                yield index, base, size, bias_row, r0, block, side, place
                place += block


def one_head(block, side, rows):
    lane = lax.broadcasted_iota(jnp.int32, (block, LANES), 1)
    return jnp.where((lane < HEAD) if side == 0 else (lane >= HEAD), rows, BF16(0))


def attention_forward_kernel(
    ptok,
    lengths_hbm,
    xp_hbm,
    xq_hbm,
    wq_hbm,
    wk_hbm,
    wv_hbm,
    wo_hbm,
    bq_hbm,
    bv_hbm,
    bo_hbm,
    q_ref,
    k_ref,
    v_ref,
    o_ref,
    lse_ref,
    x1_ref,
    rate1_ref,
    xt_ref,
    me_ref,
    x_scr,
    r1_scr,
    bias_scr,
    vt_scr,
    ot_scr,
    lengths_ref,
    xp_ref,
    wq_ref,
    wk_ref,
    wv_ref,
    wo_ref,
    bq_ref,
    bv_ref,
    bo_ref,
    sems,
):
    step = pl.program_id(0)
    rows = x_scr.shape[0]
    qtok = rows - ptok

    @pl.when(step == 0)
    def _():
        pairs = (
            (lengths_hbm, lengths_ref),
            (xp_hbm, xp_ref.at[pl.ds(0, ptok)]),
            (xp_hbm, xp_ref.at[pl.ds(ptok, ptok)]),
            (xq_hbm, x_scr.at[pl.ds(ptok, qtok)]),
            (bo_hbm, bo_ref),
            (wq_hbm, wq_ref),
            (bq_hbm, bq_ref),
            (wk_hbm, wk_ref),
            (wv_hbm, wv_ref),
            (bv_hbm, bv_ref),
            (wo_hbm, wo_ref),
        )
        copies = [pltpu.make_async_copy(held, ref, sems.at[i]) for i, (held, ref) in enumerate(pairs)]
        for copy in copies:
            copy.start()
        grp = lax.axis_index("grp")
        me_ref[0] = grp & 1
        me_ref[1] = (grp >> 1) & 1
        me_ref[2] = (grp >> 2) & 1
        me_ref[3] = lax.axis_index("psg")
        for copy in copies:
            copy.wait()
        first = longest_start(lengths_ref, ptok // 2)
        aligned = (first // PIECE) * PIECE
        pick = shift_pick(first - aligned)
        for r0 in range(0, ptok, LANES):
            at = pl.multiple_of(aligned + r0, PIECE)
            x_scr[r0 : r0 + LANES] = dot(pick, xp_ref[pl.ds(at, LANES + PIECE), :]).astype(BF16)
        x = x_scr[...]
        xt_ref[...] = jnp.transpose(x)
        r1_scr[...] = x.astype(F32) + bo_ref[...]
        fill_bias(bias_scr, lengths_ref, ptok, qtok)

    x = x_scr[...]
    quad = pl.ds(pl.multiple_of(step * QLANES, QLANES), QLANES)
    q_ref[:, quad] = (dot(x, wq_ref[:, quad]) + bq_ref[:, quad]).astype(BF16) * BF16(HEAD**-0.5)
    k_ref[:, quad] = dot(x, wk_ref[:, quad]).astype(BF16)
    v_ref[:, quad] = (dot(x, wv_ref[:, quad]) + bv_ref[:, quad]).astype(BF16)
    turned = jnp.transpose(v_ref[:, quad])
    for h in range(QUAD):
        vt_scr[h, :HEAD] = turned[h * HEAD : (h + 1) * HEAD]
        vt_scr[h, HEAD:] = jnp.ones((vt_scr.shape[1] - HEAD, rows), BF16)
    todo = [(pair, *unit) for pair in range(QUAD // 2) for unit in units(pair, ptok, qtok)]

    def logits(pair, index, base, size, bias_row, r0, block, side, place):
        lanes = pl.ds(pl.multiple_of(step * QLANES + pair * LANES, LANES), LANES)
        return dot_t(k_ref[base : base + size, lanes], one_head(block, side, q_ref[r0 : r0 + block, lanes]))

    ahead = logits(*todo[0])
    for i, (pair, index, base, size, bias_row, r0, block, side, place) in enumerate(todo):
        s = ahead
        if i + 1 < len(todo):
            ahead = logits(*todo[i + 1])
        h = 2 * pair + side
        parts = []
        high = None
        for j in range(0, size, ASLICE):
            part = s[j : j + ASLICE]
            if bias_row is not None:
                part = part + bias_scr[bias_row + j : bias_row + j + ASLICE, r0 - base : r0 - base + block]
            parts.append(part)
            for m in range(0, ASLICE, 8):
                high = part[m : m + 8] if high is None else jnp.maximum(high, part[m : m + 8])
        peak = jnp.max(high, axis=0, keepdims=True)
        e = jnp.concatenate([jnp.exp(part - peak).astype(BF16) for part in parts], axis=0)
        found = dot(vt_scr[h, :, base : base + size], e)
        sums = found[HEAD : HEAD + 1]
        ot_scr[h * HEAD : (h + 1) * HEAD, r0 : r0 + block] = (found[:HEAD] * (1.0 / sums)).astype(BF16)
        lse_ref[step, h : h + 1, r0 : r0 + block] = peak + jnp.log(sums)
    o_ref[:, quad] = jnp.transpose(ot_scr[...])
    r1_scr[...] += dot(o_ref[:, quad], wo_ref[quad, :])

    @pl.when(step == pl.num_programs(0) - 1)
    def _():
        scaled, rate = norm_stats(r1_scr[...])
        x1_ref[...] = scaled
        rate1_ref[...] = jnp.broadcast_to(rate, rate1_ref.shape)


def spec(shape, index):
    return pl.BlockSpec(shape, index)


def whole(array):
    return pl.BlockSpec(memory_space=pltpu.VMEM)


def in_hbm(array):
    return pltpu.with_memory_space_constraint(array, pltpu.HBM)


def const(array):
    nd = len(array.shape)
    return pl.BlockSpec(array.shape, lambda *_: (0,) * nd)


def smem():
    return pl.BlockSpec(memory_space=pltpu.SMEM)


def cost(micros):
    return pl.CostEstimate(flops=int(micros * 1e9), bytes_accessed=int(micros * 1e6), transcendentals=0)


def shaped(shape, dtype):
    return jax.ShapeDtypeStruct(shape, dtype)


def params(grid_rank, mebibytes):
    return pltpu.CompilerParams(
        dimension_semantics=("arbitrary",) * grid_rank, vmem_limit_bytes=int(mebibytes * 1024 * 1024)
    )


def attention_forward(lengths, xp, xq, wq, bq, wk, wv, bv, wo, bo):
    ptok, width = xp.shape
    qtok = xq.shape[0]
    rows = ptok + qtok
    quads = HEADS // QUAD
    half = ptok // 2
    return pl.pallas_call(
        functools.partial(attention_forward_kernel, ptok),
        grid=(quads,),
        in_specs=[pl.BlockSpec(memory_space=pltpu.HBM)] * 10,
        out_specs=[whole(None)] * 8 + [smem()],
        out_shape=[shaped((rows, width), BF16)] * 4
        + [
            shaped((quads, 8, rows), F32),
            shaped((rows, width), F32),
            shaped((rows, LANES), F32),
            shaped((width, rows), BF16),
            shaped((4,), jnp.int32),
        ],
        scratch_shapes=[
            pltpu.VMEM((rows, width), BF16),
            pltpu.VMEM((rows, width), F32),
            pltpu.VMEM((half + qtok, half), F32),
            pltpu.VMEM((QUAD, HEAD + 16, rows), BF16),
            pltpu.VMEM((QLANES, rows), BF16),
            pltpu.SMEM(lengths.shape, jnp.int32),
            pltpu.VMEM((2 * ptok, width), BF16),
        ]
        + [pltpu.VMEM((width, width), BF16)] * 4
        + [pltpu.VMEM((1, width), F32)] * 3
        + [pltpu.SemaphoreType.DMA((11,))],
        compiler_params=params(1, 23),
        cost_estimate=cost(20),
        name="attention_forward",
    )(*[in_hbm(a) for a in (lengths, xp, xq, wq, wk, wv, wo, bq, bv, bo)])


def ffn_forward_kernel(
    aliased,
    rb,
    offset,
    x1_ref,
    g1_ref,
    s1_ref,
    wi_ref,
    bi_ref,
    wo_ref,
    bo_ref,
    g2_ref,
    s2_ref,
    wp_ref,
    *rest,
):
    rest = rest[aliased:]
    u_ref, d_ref, x2_ref, rate2_ref, e_ref, emb_ref, h1_scr, r2_scr = rest
    step = pl.program_id(0)
    rows = h1_scr.shape[0]
    own = slice(offset, offset + rows)
    chunk = pl.ds(pl.multiple_of(step * FCHUNK, FCHUNK), FCHUNK)

    @pl.when(step == 0)
    def _():
        h1 = x1_ref[own] * g1_ref[...] + s1_ref[...]
        h1_scr[...] = h1.astype(BF16)
        r2_scr[...] = h1 + bo_ref[...]

    ahead = dot(h1_scr[:rb], wi_ref[...])
    for r in range(0, rows, rb):
        f = ahead
        if r + rb < rows:
            ahead = dot(h1_scr[r + rb : r + 2 * rb], wi_ref[...])
        bias = bi_ref[...]
        for i in range(0, rb, SLICE):
            u, d = gelu_pair(f[i : i + SLICE] + bias)
            at = offset + r + i
            u_ref[at : at + SLICE, chunk] = u.astype(BF16)
            d_ref[at : at + SLICE, chunk] = d.astype(BF16)
        r2_scr[r : r + rb] += dot(u_ref[offset + r : offset + r + rb, chunk], wo_ref[...])

    @pl.when(step == pl.num_programs(0) - 1)
    def _():
        scaled, rate = norm_stats(r2_scr[...])
        x2_ref[own] = scaled
        rate2_ref[own] = jnp.broadcast_to(rate, (rows, LANES))
        h2 = (scaled * g2_ref[...] + s2_ref[...]).astype(BF16)
        e = dot(h2, wp_ref[...])
        e_ref[own] = e
        size = jnp.sum(e * e, axis=-1, keepdims=True)
        emb_ref[...] = (e * lax.rsqrt(size + EMBED_EPS)).astype(BF16)


def ffn_forward(count, offset, total, x1, g1, s1, wi, bi, wo, bo, g2, s2, wp, previous):
    width = x1.shape[1]
    ff = wi.shape[1]
    dim = wp.shape[1]
    first = 10
    held = list(previous)
    return pl.pallas_call(
        functools.partial(ffn_forward_kernel, len(held), min(RB, count), offset),
        grid=(ff // FCHUNK,),
        in_specs=[
            whole(x1),
            const(g1),
            const(s1),
            spec((width, FCHUNK), lambda c: (0, c)),
            spec((1, FCHUNK), lambda c: (0, c)),
            spec((FCHUNK, width), lambda c: (c, 0)),
            const(bo),
            const(g2),
            const(s2),
            const(wp),
        ]
        + [whole(None)] * len(held),
        out_specs=[whole(None)] * 6,
        out_shape=[
            shaped((total, ff), BF16),
            shaped((total, ff), BF16),
            shaped((total, width), F32),
            shaped((total, LANES), F32),
            shaped((total, dim), F32),
            shaped((count, dim), BF16),
        ],
        scratch_shapes=[
            pltpu.VMEM((count, width), BF16),
            pltpu.VMEM((count, width), F32),
        ],
        input_output_aliases={first + i: i for i in range(len(held))},
        compiler_params=params(1, 15),
        cost_estimate=cost(12 if count > 256 else 4),
        name="ffn_forward",
    )(x1, g1, s1, in_hbm(wi), bi, in_hbm(wo), bo, g2, s2, wp, *held)


def passage_member(lengths_ref, rows):
    ends = segment_ends(lengths_ref)
    lane = lax.broadcasted_iota(jnp.int32, (8, LANES), 1)
    low = jnp.full((8, LANES), rows, jnp.int32)
    high = jnp.zeros((8, LANES), jnp.int32)
    start = jnp.int32(0)
    for s, end in enumerate(ends):
        low = jnp.where(lane == s, start, low)
        high = jnp.where(lane == s, end, high)
        start = end
    token = lax.broadcasted_iota(jnp.int32, (rows, LANES), 0) + longest_start(lengths_ref, rows // 2)
    token = jnp.where(token >= rows, token - rows, token)
    inside = (token >= low[:1]) & (token < high[:1])
    return jnp.where(inside, 1.0, 0.0).astype(BF16)


def soft_match(group, pass_embed):
    return jnp.exp(SHARPNESS * dot_t(group, pass_embed) - SHARPNESS)


def score_kernel(psg, count, lengths_ref, emb_ref, *rest):
    group_refs = rest[:psg]
    score_ref, pooled_ref = rest[psg:]
    member = passage_member(lengths_ref, emb_ref.shape[0])
    group = jnp.concatenate([ref[...] for ref in group_refs], axis=0)
    matched = soft_match(group, emb_ref[...])
    pooled = two_part_dot(matched, member)
    lane = lax.broadcasted_iota(jnp.int32, pooled.shape, 1)
    pooled = jnp.where(lane < count, pooled, 1.0)
    pooled_ref[...] = pooled
    smooth = 1.0 + jnp.log(pooled) * (1.0 / SHARPNESS)
    queries = pooled.shape[0] // QLEN
    score_ref[...] = SCORE_SCALE * jnp.sum(smooth.reshape(queries, QLEN, LANES), axis=1)


def score(lengths, emb, groups):
    psg = len(groups)
    tokens = sum(g.shape[0] for g in groups)
    return pl.pallas_call(
        functools.partial(score_kernel, psg, lengths.shape[1]),
        in_specs=[smem()] + [pl.BlockSpec(memory_space=pltpu.VMEM)] * (1 + psg),
        out_shape=[shaped((tokens // QLEN, LANES), F32), shaped((tokens, LANES), F32)],
        compiler_params=params(0, 8),
        cost_estimate=cost(3),
        name="score",
    )(lengths, emb, *groups)


def loss_kernel(psg, count, where_ref, lengths_ref, positives_ref, pooled_ref, emb_ref, *rest):
    group_refs = rest[:psg]
    score_refs = rest[psg : 2 * psg]
    loss_ref, own_ref = rest[2 * psg : 2 * psg + 2]
    away_refs = rest[2 * psg + 2 : 3 * psg + 1]
    grad_ref = rest[3 * psg + 1]
    position = where_ref[3]
    queries = score_refs[0].shape[0]
    each = queries // psg
    lane = lax.broadcasted_iota(jnp.int32, (queries, LANES), 1)
    row = lax.broadcasted_iota(jnp.int32, (queries, LANES), 0)
    valid = lane < count
    blocks = []
    for e in range(psg):
        found = score_refs[e][...]
        found = jnp.concatenate(
            [found[((d - e) % psg) * each : ((d - e) % psg + 1) * each] for d in range(psg)], axis=0
        )
        blocks.append(jnp.where(valid, found, -jnp.inf))
    target = jnp.zeros((queries, LANES), jnp.int32)
    for d in range(psg):
        for j in range(each):
            chosen = positives_ref[lax.rem(position + d, psg) * each + j]
            target = jnp.where(row == d * each + j, chosen, target)
    peak = blocks[0]
    for found in blocks[1:]:
        peak = jnp.maximum(peak, found)
    peak = jnp.max(peak, axis=-1, keepdims=True)
    total = jnp.zeros((queries, 1), F32)
    picked = jnp.zeros((queries, 1), F32)
    for e in range(psg):
        owner = lax.rem(position + e, psg)
        hit = (target == owner * count + lane) & valid
        total = total + jnp.sum(jnp.exp(blocks[e] - peak), axis=-1, keepdims=True)
        picked = picked + jnp.sum(jnp.where(hit, blocks[e], 0.0), axis=-1, keepdims=True)
        if e == 0:
            own_hit = jnp.where(hit, 1.0, 0.0)
    log_total = peak + jnp.log(total)
    losses = jnp.broadcast_to(log_total - picked, (queries, LANES))
    place = lax.rem(position + row // each, psg) * each + row % each
    losses = jnp.sum(jnp.where(lane == place, losses, 0.0), axis=0, keepdims=True)
    loss_ref[...] = losses[:, :queries]
    grad = jnp.where(valid, jnp.exp(blocks[0] - log_total) - own_hit, 0.0) * SCORE_SCALE
    tokens = queries * QLEN
    grad = jnp.broadcast_to(grad[:, None, :], (queries, QLEN, LANES)).reshape(tokens, LANES)
    grad = grad / pooled_ref[...]
    member = passage_member(lengths_ref, emb_ref.shape[0])
    high = grad.astype(BF16)
    rest_low = (grad - high.astype(F32)).astype(BF16)
    spread = dot_t(high, member) + dot_t(rest_low, member)
    group = jnp.concatenate([ref[...] for ref in group_refs], axis=0)
    low = (soft_match(group, emb_ref[...]) * spread).astype(BF16)
    group_grad = dot(low, emb_ref[...])
    each_tokens = tokens // psg
    own_ref[...] = group_grad[:each_tokens]
    for d in range(1, psg):
        away_refs[d - 1][...] = group_grad[d * each_tokens : (d + 1) * each_tokens].astype(BF16)
    grad_ref[...] = jnp.transpose(dot(jnp.transpose(group), low))


def loss_and_grads(position, lengths, positives, pooled, emb, groups, scores):
    psg = len(groups)
    queries = scores[0].shape[0]
    tokens, dim = groups[0].shape
    vmem = pl.BlockSpec(memory_space=pltpu.VMEM)
    return pl.pallas_call(
        functools.partial(loss_kernel, psg, lengths.shape[1]),
        in_specs=[smem(), smem(), smem()] + [vmem] * (2 + 2 * psg),
        out_shape=[shaped((1, queries), F32), shaped((tokens, dim), F32)]
        + [shaped((tokens, dim), BF16)] * (psg - 1)
        + [shaped(emb.shape, F32)],
        compiler_params=params(0, 8),
        cost_estimate=cost(3),
        name="loss_and_grads",
    )(position, lengths, positives, pooled, emb, *groups, *scores)


def head_backward(grad_embed, e, x2, rate2, wp, g2, s2):
    low = unit_backward(grad_embed, e).astype(BF16)
    grad_h2 = dot_t(low, wp)
    grad_r2, gain_term, shift_term = norm_backward(grad_h2, x2, rate2[:, :1], g2)
    h2 = (x2 * g2 + s2).astype(BF16)
    return grad_r2, gain_term, shift_term, dot(jnp.transpose(low), h2)


def passage_head_kernel(
    grad_ref, e_ref, x2_ref, rate2_ref, wp_ref, g2_ref, s2_ref, gr2_ref, vec_ref, proj_ref
):
    ptok = grad_ref.shape[0]
    grad_r2, gain_term, shift_term, proj = head_backward(
        grad_ref[...], e_ref[:ptok], x2_ref[:ptok], rate2_ref[:ptok], wp_ref[...], g2_ref[...], s2_ref[...]
    )
    gr2_ref[...] = grad_r2
    vec_ref[...] = jnp.zeros_like(vec_ref)
    vec_ref[0:1] = gain_term
    vec_ref[1:2] = shift_term
    proj_ref[...] = proj


def passage_head(grad, e, x2, rate2, wp, g2, s2):
    ptok, dim = grad.shape
    width = x2.shape[1]
    return pl.pallas_call(
        passage_head_kernel,
        grid=(1,),
        in_specs=[
            whole(grad),
            whole(e),
            whole(x2),
            whole(rate2),
            const(wp),
            const(g2),
            const(s2),
        ],
        out_specs=[whole(None)] * 3,
        out_shape=[shaped((ptok, width), F32), shaped((8, width), F32), shaped((dim, width), F32)],
        compiler_params=params(1, 10),
        cost_estimate=cost(4),
        name="passage_head",
    )(grad, e, x2, rate2, wp, g2, s2)


def fixed(shape):
    return pl.BlockSpec(memory_space=pltpu.VMEM)


def ffn_backward_kernel(
    psg,
    me_ref,
    gr2p_ref,
    vec_ref,
    proj_ref,
    own_ref,
    *rest,
):
    away_refs = rest[: psg - 1]
    (
        e_ref,
        x2_ref,
        rate2_ref,
        wp_ref,
        g2_ref,
        s2_ref,
        x1_ref,
        g1_ref,
        s1_ref,
        wi_ref,
        wo_ref,
        u_ref,
        d_ref,
        dproj_ref,
        dvec_ref,
        dbi_ref,
        gh1_ref,
        keep_i_ref,
        send_i_ref,
        keep_o_ref,
        send_o_ref,
        gz_scr,
        turn_scr,
        gzt_scr,
        h1t_scr,
        gh1_scr,
        gi_scr,
    ) = rest[psg - 1 :]
    step = pl.program_id(0)
    ptok = gr2p_ref.shape[0]
    rows = gz_scr.shape[0]

    @pl.when(step == 0)
    def _():
        grad = own_ref[...]
        for ref in away_refs:
            grad = grad + ref[...].astype(F32)
        grad_r2, gain_term, shift_term, proj = head_backward(
            grad, e_ref[ptok:], x2_ref[ptok:], rate2_ref[ptok:], wp_ref[...], g2_ref[...], s2_ref[...]
        )
        dproj_ref[...] = jnp.transpose(proj_ref[...] + proj).astype(BF16)
        gr2p = gr2p_ref[...]
        gh1_scr[:ptok] = gr2p
        gh1_scr[ptok:] = grad_r2
        low_p = gr2p.astype(BF16)
        low_q = grad_r2.astype(BF16)
        gz_scr[:ptok] = low_p
        gz_scr[ptok:] = low_q
        dvec_ref[...] = jnp.zeros_like(dvec_ref)
        dvec_ref[0:1] = vec_ref[0:1] + gain_term
        dvec_ref[1:2] = vec_ref[1:2] + shift_term
        dvec_ref[2:3] = jnp.sum(low_p.astype(F32), axis=0, keepdims=True) + jnp.sum(
            low_q.astype(F32), axis=0, keepdims=True
        )
        turn_scr[...] = jnp.transpose((x1_ref[...] * g1_ref[...] + s1_ref[...]).astype(BF16))
        to_relative(me_ref, turn_scr, h1t_scr)
        turn_scr[...] = jnp.transpose(gz_scr[...])
        to_relative(me_ref, turn_scr, gzt_scr, turned=True)

    chunk = pl.ds(pl.multiple_of(step * FCHUNK, FCHUNK), FCHUNK)
    third = rows // 3
    outer = dot(gzt_scr[...], u_ref[:, chunk])
    ahead = dot_t(gz_scr[:third], wo_ref[...])
    sums = jnp.zeros((8, FCHUNK), F32)
    for r in range(0, rows, third):
        grad_active = ahead
        if r + third < rows:
            ahead = dot_t(gz_scr[r + third : r + 2 * third], wo_ref[...])
        for i in range(0, third, SLICE):
            at = r + i
            low = (grad_active[i : i + SLICE] * d_ref[at : at + SLICE, chunk].astype(F32)).astype(BF16)
            gi_scr[at : at + SLICE] = low
            kept = low.astype(F32)
            for m in range(0, SLICE, 8):
                sums = sums + kept[m : m + 8]
        gh1_scr[r : r + third] += dot_t(gi_scr[r : r + third], wi_ref[...])
    dbi_ref[:, chunk] = jnp.sum(sums, axis=0, keepdims=True)
    half = keep_i_ref.shape[0]
    for term, keep_ref, send_ref in (
        (outer, keep_o_ref, send_o_ref),
        (dot(h1t_scr[...], gi_scr[...]), keep_i_ref, send_i_ref),
    ):
        keep_ref[:, chunk] = term[:half].astype(BF16)
        send_ref[:, chunk] = term[half:].astype(BF16)

    @pl.when(step == pl.num_programs(0) - 1)
    def _():
        gh1_ref[...] = gh1_scr[...]


def ffn_backward(me, gr2p, vec, proj, own, aways, e, x2, rate2, wp, g2, s2, x1, g1, s1, wi, wo, u, d):
    ptok, width = gr2p.shape
    rows = x1.shape[0]
    dim = wp.shape[1]
    ff = wi.shape[1]
    return pl.pallas_call(
        functools.partial(ffn_backward_kernel, 1 + len(aways)),
        grid=(ff // FCHUNK,),
        in_specs=[smem(), whole(gr2p), whole(vec), whole(proj), whole(own)]
        + [whole(a) for a in aways]
        + [
            whole(e),
            whole(x2),
            whole(rate2),
            const(wp),
            const(g2),
            const(s2),
            whole(x1),
            const(g1),
            const(s1),
            spec((width, FCHUNK), lambda c: (0, c)),
            spec((FCHUNK, width), lambda c: (c, 0)),
            whole(u),
            whole(d),
        ],
        out_specs=[
            fixed((width, dim)),
            fixed((8, width)),
            fixed((1, ff)),
            fixed((rows, width)),
        ]
        + [whole(None)] * 4,
        out_shape=[
            shaped((width, dim), BF16),
            shaped((8, width), F32),
            shaped((1, ff), F32),
            shaped((rows, width), F32),
        ]
        + [shaped((width // 2, ff), BF16)] * 4,
        scratch_shapes=[
            pltpu.VMEM((rows, width), BF16),
            pltpu.VMEM((width, rows), BF16),
            pltpu.VMEM((width, rows), BF16),
            pltpu.VMEM((width, rows), BF16),
            pltpu.VMEM((rows, width), F32),
            pltpu.VMEM((rows, FCHUNK), BF16),
        ],
        compiler_params=params(1, 17),
        cost_estimate=cost(15),
        name="ffn_backward",
    )(me, gr2p, vec, proj, own, *aways, e, x2, rate2, wp, g2, s2, x1, g1, s1, in_hbm(wi), in_hbm(wo), u, d)


def put_vector(wave_ref, row, vector):
    for i in range(vector.shape[1] // LANES):
        wave_ref[row + i : row + i + 1] = vector[:, i * LANES : (i + 1) * LANES]
    return row + vector.shape[1] // LANES


def take_vector(wave_ref, row, column, out_ref):
    size = out_ref.shape[1]
    for i in range(size // LANES):
        out_ref[:, i * LANES : (i + 1) * LANES] = wave_ref[row + i : row + i + 1, column : column + LANES].astype(
            F32
        )
    return row + size // LANES


def probabilities_kernel(ptok, lengths_ref, q_ref, k_ref, lse_ref, p_ref, pq_ref, bias_scr):
    qtok = q_ref.shape[0] - ptok

    @pl.when(pl.program_id(0) == 0)
    def _():
        fill_bias(bias_scr, lengths_ref, ptok, qtok)

    step = pl.program_id(0)
    todo = [(pair, *unit) for pair in range(QUAD // 2) for unit in units(pair, ptok, qtok)]

    def logits(pair, index, base, size, bias_row, r0, block, side, place):
        lanes = pl.ds(pl.multiple_of(step * QLANES + pair * LANES, LANES), LANES)
        return dot_t(k_ref[base : base + size, lanes], one_head(block, side, q_ref[r0 : r0 + block, lanes]))

    ahead = logits(*todo[0])
    for i, (pair, index, base, size, bias_row, r0, block, side, place) in enumerate(todo):
        s = ahead
        if i + 1 < len(todo):
            ahead = logits(*todo[i + 1])
        h = 2 * pair + side
        lse = lse_ref[step, h : h + 1, r0 : r0 + block]
        for j in range(0, size, ASLICE):
            part = s[j : j + ASLICE]
            if bias_row is not None:
                part = part + bias_scr[bias_row + j : bias_row + j + ASLICE, r0 - base : r0 - base + block]
            p = jnp.exp(part - lse).astype(BF16)
            if index < 2:
                p_ref[step, 2 * pair + index, j : j + ASLICE, place : place + block] = p
            else:
                pq_ref[step, pair, j : j + ASLICE, place : place + block] = p


def probabilities(lengths, q, k, lse, ptok):
    rows, width = q.shape
    quads = HEADS // QUAD
    half, qtok = ptok // 2, rows - ptok
    return pl.pallas_call(
        functools.partial(probabilities_kernel, ptok),
        grid=(quads,),
        in_specs=[smem(), whole(q), whole(k), whole(lse)],
        out_specs=[whole(None), whole(None)],
        out_shape=[
            shaped((quads, QUAD, half, 2 * half), BF16),
            shaped((quads, QUAD // 2, qtok, 2 * qtok), BF16),
        ],
        scratch_shapes=[pltpu.VMEM((half + qtok, half), F32)],
        compiler_params=params(1, 10),
        cost_estimate=cost(8),
        name="probabilities",
    )(lengths, q, k, lse)


def first_norm_kernel(gh1_ref, x1_ref, rate1_ref, g1_ref, wo_ref, gr1_ref, go_ref, vec_ref):
    grad_r1, gain_term, shift_term = norm_backward(gh1_ref[...], x1_ref[...], rate1_ref[:, :1], g1_ref[...])
    gr1_ref[...] = grad_r1
    low = grad_r1.astype(BF16)
    vec_ref[...] = jnp.zeros_like(vec_ref)
    vec_ref[0:1] = gain_term
    vec_ref[1:2] = shift_term
    vec_ref[2:3] = jnp.sum(low.astype(F32), axis=0, keepdims=True)
    go_ref[...] = dot_t(low, wo_ref[...]).astype(BF16)


def first_norm(gh1, x1, rate1, g1, wo):
    rows, width = x1.shape
    return pl.pallas_call(
        first_norm_kernel,
        grid=(1,),
        in_specs=[whole(gh1), whole(x1), whole(rate1), const(g1), const(wo)],
        out_specs=[whole(None)] * 3,
        out_shape=[shaped((rows, width), F32), shaped((rows, width), BF16), shaped((8, width), F32)],
        compiler_params=params(1, 9),
        cost_estimate=cost(4),
        name="first_norm",
    )(gh1, x1, rate1, g1, wo)


def heads_backward_kernel(
    quad,
    ptok,
    p_ref,
    pq_ref,
    q_ref,
    k_ref,
    v_ref,
    o_ref,
    go_ref,
    gq_ref,
    gk_ref,
    gv_ref,
    dd_scr,
    gqt_scr,
    qm_scr,
    gm_scr,
    gs_scr,
    kt_scr,
):
    qtok = q_ref.shape[0] - ptok

    own = slice(quad * QLANES, (quad + 1) * QLANES)
    product = go_ref[:, own].astype(F32) * o_ref[:, own].astype(F32)
    ones = jnp.where(
        lax.broadcasted_iota(jnp.int32, (16, QLANES), 1) // HEAD
        == lax.broadcasted_iota(jnp.int32, (16, QLANES), 0),
        1.0,
        0.0,
    ).astype(BF16)
    high = product.astype(BF16)
    dd_scr[...] = dot_t(ones, high) + dot_t(ones, (product - high.astype(F32)).astype(BF16))
    kt_scr[...] = jnp.transpose(k_ref[:, own])
    todo = [(pair, *unit) for pair in range(QUAD // 2) for unit in units(pair, ptok, qtok)]

    def begin(pair, index, base, size, bias_row, r0, block, side, place):
        lanes = slice(quad * QLANES + pair * LANES, quad * QLANES + (pair + 1) * LANES)
        buffer = (3 * pair + index) % 2
        qm_scr[buffer, place : place + block] = one_head(block, side, q_ref[r0 : r0 + block, lanes])
        gm = one_head(block, side, go_ref[r0 : r0 + block, lanes])
        gm_scr[buffer, place : place + block] = gm
        return dot_t(v_ref[base : base + size, lanes], gm)

    ahead = begin(*todo[0])
    for t, (pair, index, base, size, bias_row, r0, block, side, place) in enumerate(todo):
        grad_prob = ahead
        if t + 1 < len(todo):
            ahead = begin(*todo[t + 1])
        inner = slice(pair * LANES, (pair + 1) * LANES)
        buffer = (3 * pair + index) % 2
        h = 2 * pair + side
        dd = dd_scr[h : h + 1, r0 : r0 + block]
        p_at = p_ref.at[quad, 2 * pair + index] if index < 2 else pq_ref.at[quad, pair]
        for i in range(0, size, ASLICE):
            p = p_at[i : i + ASLICE, place : place + block].astype(F32)
            gs = p * (grad_prob[i : i + ASLICE] - dd)
            gs_scr[buffer, i : i + ASLICE, place : place + block] = gs.astype(BF16)
        gqt_scr[h * HEAD : (h + 1) * HEAD, r0 : r0 + block] = dot(
            kt_scr[h * HEAD : (h + 1) * HEAD, base : base + size],
            gs_scr[buffer, :size, place : place + block],
        )
        end = place + block
        if end == 2 * size:
            gv_ref[base : base + size, inner] = dot(p_at[...], gm_scr[buffer, :end]).astype(BF16)
            gk_ref[base : base + size, inner] = dot(gs_scr[buffer, :size, :end], qm_scr[buffer, :end]).astype(BF16)
    gq_ref[...] = (jnp.transpose(gqt_scr[...]) * (HEAD**-0.5)).astype(BF16)


def heads_backward(quad, p, pq, q, k, v, o, go, ptok):
    rows, width = q.shape
    half = ptok // 2
    low = lambda *shape: pltpu.VMEM(shape, BF16)
    return pl.pallas_call(
        functools.partial(heads_backward_kernel, quad, ptok),
        grid=(1,),
        in_specs=[whole(None)] * 7,
        out_specs=[whole(None)] * 3,
        out_shape=[shaped((rows, QLANES), BF16)] * 3,
        scratch_shapes=[
            pltpu.VMEM((16, rows), F32),
            pltpu.VMEM((QLANES, rows), F32),
            low(2, 4 * RB, LANES),
            low(2, 4 * RB, LANES),
            low(2, half, 4 * RB),
            low(QLANES, rows),
        ],
        compiler_params=params(1, 16),
        cost_estimate=cost(10),
        name="heads_backward",
    )(p, pq, q, k, v, o, go)


def output_term_kernel(me_ref, gr1_ref, o_ref, dout_ref, turn_scr, ot_scr):
    turn_scr[...] = jnp.transpose(o_ref[...])
    to_relative(me_ref, turn_scr, ot_scr)
    dout_ref[...] = dot(ot_scr[...], gr1_ref[...].astype(BF16)).astype(BF16)


def output_term(me, gr1, o):
    rows, width = gr1.shape
    return pl.pallas_call(
        output_term_kernel,
        grid=(1,),
        in_specs=[smem(), whole(gr1), whole(o)],
        out_specs=whole(None),
        out_shape=shaped((width, width), BF16),
        scratch_shapes=[pltpu.VMEM((width, rows), BF16)] * 2,
        compiler_params=params(1, 8),
        cost_estimate=cost(2),
        name="output_term",
    )(me, gr1, o)


def weights_kernel(
    ptok,
    me_ref,
    gr1_ref,
    dout_ref,
    xt_ref,
    gq0_ref,
    gk0_ref,
    gv0_ref,
    gq1_ref,
    gk1_ref,
    gv1_ref,
    dproj_ref,
    vec1_ref,
    vec2_ref,
    dbi_ref,
    wq_ref,
    wk_ref,
    wv_ref,
    keep_ref,
    send_ref,
    gp_ref,
    gq_ref,
    xt_scr,
    lines_scr,
    tail_scr,
):
    half_rows = keep_ref.shape[0]
    width = gr1_ref.shape[1]
    gr1 = gr1_ref[...]
    to_relative(me_ref, xt_ref, xt_scr)
    joined = [
        jnp.concatenate([left[...], right[...]], axis=1)
        for left, right in ((gq0_ref, gq1_ref), (gk0_ref, gk1_ref), (gv0_ref, gv1_ref))
    ]
    for i, grad in enumerate(joined):
        term = dot(xt_scr[...], grad)
        keep_ref[:, i * width : (i + 1) * width] = term[:half_rows].astype(BF16)
        send_ref[:, i * width : (i + 1) * width] = term[half_rows:].astype(BF16)
    keep_ref[:, 3 * width : 4 * width] = dout_ref[:half_rows]
    send_ref[:, 3 * width : 4 * width] = dout_ref[half_rows:]
    gin = gr1 + dot_t(joined[0], wq_ref[...]) + dot_t(joined[1], wk_ref[...]) + dot_t(joined[2], wv_ref[...])
    gp_ref[...] = gin[:ptok].astype(BF16)
    gq_ref[...] = gin[ptok:].astype(BF16)
    row = 0
    for vector in (
        vec2_ref[0:1],
        vec2_ref[1:2],
        vec2_ref[2:3],
        vec1_ref[0:1],
        vec1_ref[1:2],
        vec1_ref[2:3],
        dbi_ref[...],
        jnp.sum(joined[0].astype(F32), axis=0, keepdims=True),
        jnp.sum(joined[2].astype(F32), axis=0, keepdims=True),
    ):
        row = put_vector(lines_scr, row, vector)
    lines_scr[row:] = jnp.zeros((lines_scr.shape[0] - row, LANES), F32)
    dim = dproj_ref.shape[1]
    tail_scr[:, :dim] = dproj_ref[...]
    tail_scr[:, dim:] = lines_scr[...].astype(BF16)
    for r in range(32):
        ref = keep_ref if r < 16 else send_ref
        at = (r % 16) * PIECE
        ref[at : at + PIECE, 4 * width :] = tail_scr[pl.ds(owner_place(me_ref, r), PIECE), :]


def weights(me, gr1, dout, xt, first, second, dproj, vec1, vec2, dbi, wq, wk, wv, ptok):
    rows, width = gr1.shape
    lanes = 4 * width + dproj.shape[1] + LANES
    low = lambda *shape: pltpu.VMEM(shape, BF16)
    return pl.pallas_call(
        functools.partial(weights_kernel, ptok),
        grid=(1,),
        in_specs=[smem()] + [whole(None)] * 16,
        out_specs=[whole(None)] * 4,
        out_shape=[
            shaped((width // 2, lanes), BF16),
            shaped((width // 2, lanes), BF16),
            shaped((ptok, width), BF16),
            shaped((rows - ptok, width), BF16),
        ],
        scratch_shapes=[
            low(width, rows),
            pltpu.VMEM((width, LANES), F32),
            low(width, dproj.shape[1] + LANES),
        ],
        compiler_params=params(1, 16),
        cost_estimate=cost(6),
        name="weights",
    )(me, gr1, dout, xt, *first, *second, dproj, vec1, vec2, dbi, wq, wk, wv)


def from_relative(me_ref, kept_ref, other_ref, wave_ref, turned=False):
    for r in range(32):
        ref = kept_ref if r < 16 else other_ref
        at = (r % 16) * PIECE
        wave_ref[pl.ds(owner_place(me_ref, r, turned), PIECE), :] = ref[at : at + PIECE]


def unpack_ffn_kernel(
    me_ref, kept_i_ref, other_i_ref, kept_o_ref, other_o_ref, dwi_ref, dwo_ref, wave_i_scr, wave_o_scr
):
    from_relative(me_ref, kept_i_ref, other_i_ref, wave_i_scr)
    from_relative(me_ref, kept_o_ref, other_o_ref, wave_o_scr, turned=True)
    dwi_ref[...] = wave_i_scr[...].astype(F32)
    dwo_ref[...] = jnp.transpose(wave_o_scr[...].astype(F32))


def unpack_ffn(me, *halves):
    half, ff = halves[0].shape
    width = 2 * half
    return pl.pallas_call(
        unpack_ffn_kernel,
        grid=(ff // FCHUNK,),
        in_specs=[smem()] + [spec((half, FCHUNK), lambda c: (0, c))] * 4,
        out_specs=[
            spec((width, FCHUNK), lambda c: (0, c)),
            spec((FCHUNK, width), lambda c: (c, 0)),
        ],
        out_shape=[shaped((width, ff), F32), shaped((ff, width), F32)],
        scratch_shapes=[pltpu.VMEM((width, FCHUNK), BF16)] * 2,
        compiler_params=params(1, 16),
        cost_estimate=cost(6),
        name="unpack_ffn",
    )(me, *halves)


def unpack_attention_kernel(
    me_ref,
    kept_ref,
    other_ref,
    dwq_ref,
    dwk_ref,
    dwv_ref,
    dout_ref,
    dproj_ref,
    g2_ref,
    s2_ref,
    bo_ref,
    g1_ref,
    s1_ref,
    bout_ref,
    bi_ref,
    bq_ref,
    bv_ref,
    wave_scr,
):
    from_relative(me_ref, kept_ref, other_ref, wave_scr)
    column = 0
    for ref in (dwq_ref, dwk_ref, dwv_ref, dout_ref, dproj_ref):
        ref[...] = wave_scr[:, column : column + ref.shape[1]].astype(F32)
        column += ref.shape[1]
    row = 0
    for ref in (g2_ref, s2_ref, bo_ref, g1_ref, s1_ref, bout_ref, bi_ref, bq_ref, bv_ref):
        row = take_vector(wave_scr, row, column, ref)


def unpack_attention(me, kept, other, width, dim, ff):
    vmem = pl.BlockSpec(memory_space=pltpu.VMEM)
    return pl.pallas_call(
        unpack_attention_kernel,
        in_specs=[smem()] + [vmem] * 2,
        out_shape=[shaped((width, width), F32)] * 4
        + [shaped((width, dim), F32)]
        + [shaped((1, width), F32)] * 6
        + [shaped((1, ff), F32)]
        + [shaped((1, width), F32)] * 2,
        scratch_shapes=[pltpu.VMEM((width, kept.shape[1]), BF16)],
        compiler_params=params(0, 16),
        cost_estimate=cost(3),
        name="unpack_attention",
    )(me, kept, other)


def swap(block, axis_name, size, bit):
    return lax.ppermute(block, axis_name, [(i, i ^ bit) for i in range(size)])


def total(*parts):
    found = parts[0].astype(F32)
    for part in parts[1:]:
        found = found + part.astype(F32)
    return found.astype(BF16)


def core_parts(keep, found):
    size = keep.shape[0] // 4
    return [total(keep[i * size : (i + 1) * size], found[i * size : (i + 1) * size]) for i in range(4)]


def halves(block):
    size = block.shape[0] // 2
    return block[:size], block[size:]


def plane_send(blocks, grp_size):
    return tuple(swap(block, "grp", grp_size, bits) for block, bits in zip(blocks, (4, 2, 6)))


def line_parts(parts, psg_size):
    size = parts[0].shape[0] // psg_size
    return [total(*[part[i * size : (i + 1) * size] for part in parts]) for i in range(psg_size)]


def line_send(blocks, psg_size):
    return tuple(swap(block, "psg", psg_size, d) for d, block in enumerate(blocks, 1))


def line_total(own, founds, grp_size):
    piece = total(own, *founds)
    bit = 8
    while bit < grp_size:
        piece = total(piece, swap(piece, "grp", grp_size, bit))
        bit *= 2
    return piece


def tie(values, *others):
    return lax.optimization_barrier((tuple(values), others))[0]


def roll_back_kernel(lengths_ref, embed_ref, grad_ref, embed_out, grad_out, embed_scr, grad_scr):
    count = embed_ref.shape[0]
    back = count - longest_start(lengths_ref, count // 2)
    back = jnp.where(back == count, 0, back)
    aligned = (back // PIECE) * PIECE
    pick = shift_pick(back - aligned)
    for ref, scr, out in ((embed_ref, embed_scr, embed_out), (grad_ref, grad_scr, grad_out)):
        scr[:count] = ref[...]
        scr[count:] = ref[...]
        for r0 in range(0, count, LANES):
            at = pl.multiple_of(aligned + r0, PIECE)
            out[r0 : r0 + LANES] = dot(pick, scr[pl.ds(at, LANES + PIECE), :]).astype(BF16)


def roll_back(lengths, embed, grad):
    return pl.pallas_call(
        roll_back_kernel,
        grid=(1,),
        in_specs=[smem(), whole(embed), whole(grad)],
        out_specs=[whole(None)] * 2,
        out_shape=[shaped(embed.shape, BF16), shaped(grad.shape, BF16)],
        scratch_shapes=[
            pltpu.VMEM((2 * embed.shape[0], embed.shape[1]), BF16),
            pltpu.VMEM((2 * grad.shape[0], grad.shape[1]), BF16),
        ],
        compiler_params=params(1, 10),
        cost_estimate=cost(4),
        name="roll_back",
    )(lengths, embed, grad)


def shift_gather(block, axis_name, axis_size):
    found = [block]
    for distance in range(1, axis_size):
        ring = [(i, (i - distance) % axis_size) for i in range(axis_size)]
        found.append(lax.ppermute(block, axis_name, ring))
    return found


def local(
    grp_size,
    psg_size,
    passages,
    queries,
    lengths,
    positives,
    query_weight,
    query_bias,
    key_weight,
    value_weight,
    value_bias,
    output_weight,
    output_bias,
    first_gain,
    first_shift,
    inner_weight,
    inner_bias,
    outer_weight,
    outer_bias,
    second_gain,
    second_shift,
    project_weight,
):
    ptok, width = passages.shape
    qtok = queries.shape[0]
    rows = ptok + qtok
    row = lambda vector: vector.reshape(1, -1)
    g1, s1, g2, s2 = row(first_gain), row(first_shift), row(second_gain), row(second_shift)
    q, k, v, o, lse, x1, rate1, xt, me = attention_forward(
        lengths,
        passages,
        queries,
        query_weight,
        row(query_bias),
        key_weight,
        value_weight,
        row(value_bias),
        output_weight,
        row(output_bias),
    )
    layer = (x1, g1, s1, inner_weight, row(inner_bias), outer_weight, row(outer_bias), g2, s2, project_weight)
    *held, query_embed = ffn_forward(qtok, ptok, rows, *layer, ())
    groups = shift_gather(query_embed, "psg", psg_size)
    u, d, x2, rate2, e, pass_embed = ffn_forward(ptok, 0, rows, *layer, held)
    own_scores, pooled = score(lengths, pass_embed, groups)
    scores = shift_gather(own_scores, "psg", psg_size)
    (late_lse,) = tie((lse,), own_scores)
    p, pq = probabilities(lengths, q, k, late_lse, ptok)
    scores[1:] = tie(scores[1:], p, pq)
    losses, own, *rest = loss_and_grads(me, lengths, positives, pooled, pass_embed, groups, scores)
    aways = []
    for distance, part in enumerate(rest[:-1], 1):
        ring = [(i, (i + distance) % psg_size) for i in range(psg_size)]
        aways.append(lax.ppermute(part, "psg", ring))
    gr2p, vec, proj = passage_head(rest[-1], e, x2, rate2, project_weight, g2, s2)
    dproj, vec2, dbi, gh1, keep_i, send_i, keep_o, send_o = ffn_backward(
        me,
        gr2p,
        vec,
        proj,
        own,
        aways,
        e,
        x2,
        rate2,
        project_weight,
        g2,
        s2,
        x1,
        g1,
        s1,
        inner_weight,
        outer_weight,
        u,
        d,
    )
    core_a = (swap(send_i, "grp", grp_size, 1), swap(send_o, "grp", grp_size, 1))
    gr1, go, vec1 = first_norm(gh1, x1, rate1, g1, output_weight)
    *core_a, go = tie((*core_a, go))
    next_i, away_i = [total(part, found) for part, found in zip(halves(keep_i), halves(core_a[0]))]
    next_o, away_o = [total(part, found) for part, found in zip(halves(keep_o), halves(core_a[1]))]
    plane_a = (swap(away_i, "grp", grp_size, 2), swap(away_o, "grp", grp_size, 4))
    first = heads_backward(0, p, pq, q, k, v, o, go, ptok)
    dout = output_term(me, gr1, o)
    plane_a = tie(plane_a, dout, *first)
    (go,) = tie((go,), *plane_a)
    next_i, away_i = [total(part, found) for part, found in zip(halves(next_i), halves(plane_a[0]))]
    next_o, away_o = [total(part, found) for part, found in zip(halves(next_o), halves(plane_a[1]))]
    plane_a = (swap(away_i, "grp", grp_size, 4), swap(away_o, "grp", grp_size, 2))
    second = heads_backward(1, p, pq, q, k, v, o, go, ptok)
    plane_a = tie(plane_a, *second)
    (gr1,) = tie((gr1,), *plane_a)
    both = lambda left, right: jnp.concatenate([left, right], axis=1)
    quarter = next_i.shape[0] // psg_size
    lines_a = [
        both(
            total(next_i[i * quarter : (i + 1) * quarter], plane_a[0][i * quarter : (i + 1) * quarter]),
            total(next_o[i * quarter : (i + 1) * quarter], plane_a[1][i * quarter : (i + 1) * quarter]),
        )
        for i in range(psg_size)
    ]
    line_a = line_send(lines_a[1:], psg_size)
    keep_b, send_b, grad_p, grad_q = weights(
        me,
        gr1,
        dout,
        xt,
        first,
        second,
        dproj,
        vec1,
        vec2,
        dbi,
        query_weight,
        key_weight,
        value_weight,
        ptok,
    )
    core_b = swap(send_b, "grp", grp_size, 1)
    line_a = tie(line_a, grad_q)
    piece_a = line_total(lines_a[0], line_a, grp_size)
    spread_a = line_send([piece_a] * (psg_size - 1), psg_size)
    parts_b = core_parts(keep_b, core_b)
    plane_b = plane_send(parts_b[1:], grp_size)
    (late_grad,) = tie((grad_p,), *parts_b[1:])
    out_embed, out_grad = roll_back(lengths, pass_embed, late_grad)
    plane_b = tie(plane_b, out_grad, *spread_a)
    lines_b = line_parts((parts_b[0], *plane_b), psg_size)
    line_b = line_send(lines_b[1:], psg_size)
    spread_a = tie(spread_a, *lines_b)
    ff = inner_weight.shape[1]
    held_i = jnp.concatenate([part[:, :ff] for part in (piece_a, *spread_a)])
    held_o = jnp.concatenate([part[:, ff:] for part in (piece_a, *spread_a)])
    found_a = (swap(held_i, "grp", grp_size, 4), swap(held_o, "grp", grp_size, 2))
    line_b = tie(line_b, held_i, held_o)
    piece_b = line_total(lines_b[0], line_b, grp_size)
    spread_b = line_send([piece_b] * (psg_size - 1), psg_size)
    found_a = tie(found_a, piece_b)
    held_i = jnp.concatenate([held_i, found_a[0]])
    held_o = jnp.concatenate([held_o, found_a[1]])
    found_a = (swap(held_i, "grp", grp_size, 2), swap(held_o, "grp", grp_size, 4))
    spread_b = tie(spread_b, held_i, held_o)
    joined_b = jnp.concatenate([piece_b, *spread_b])
    gathered_b = plane_send([joined_b] * 3, grp_size)
    found_a = tie(found_a, joined_b)
    held_i = jnp.concatenate([held_i, found_a[0]])
    held_o = jnp.concatenate([held_o, found_a[1]])
    other_i, other_o = swap(held_i, "grp", grp_size, 1), swap(held_o, "grp", grp_size, 1)
    dwi, dwo = unpack_ffn(me, held_i, other_i, held_o, other_o)
    gathered_b = tie(gathered_b, dwi, dwo)
    kept_b = jnp.concatenate([joined_b, *gathered_b])
    other_b = swap(kept_b, "grp", grp_size, 1)
    dwq, dwk, dwv, dout, dproj, g2, s2, bo, g1, s1, bout, bi, bq, bv = unpack_attention(
        me, kept_b, other_b, width, project_weight.shape[1], inner_weight.shape[1]
    )
    flat = lambda vector: vector.reshape(-1)
    return (
        out_embed,
        query_embed,
        flat(losses),
        out_grad,
        grad_q,
        dwq,
        flat(bq),
        dwk,
        dwv,
        flat(bv),
        dout,
        flat(bout),
        flat(g1),
        flat(s1),
        dwi,
        flat(bi),
        dwo,
        flat(bo),
        flat(g2),
        flat(s2),
        dproj,
    )


def solution(mesh):
    split = P(("grp", "psg"), None)
    in_specs = (split, split, split, P("grp")) + (P(),) * 16
    out_specs = (split, split, P("grp"), split, split) + (P(),) * 16
    body = functools.partial(local, mesh.shape["grp"], mesh.shape["psg"])
    return jax.shard_map(body, mesh=mesh, in_specs=in_specs, out_specs=out_specs, check_vma=False)
```

```python
import functools

import jax
import jax.numpy as jnp
from jax import lax
from jax.experimental import pallas as pl
from jax.experimental.pallas import tpu as pltpu
from jax.sharding import PartitionSpec as P

HEADS = 8
HEAD = 64
QLEN = 32

SHARPNESS = 10.0
SCORE_SCALE = 0.25
NORM_EPS = 1e-06
EMBED_EPS = 1e-06
NEG_FILL = -1e30

F32 = jnp.float32
BF16 = jnp.bfloat16

HALF_LOG2_E = -0.7213475204444817
LOG2_INV_SQRT_2PI = -1.3257480647361595

INV_SQRT_2 = 0.7071067811865476

QUAD = 4
QLANES = QUAD * HEAD
RB = 256
LANES = 128
FCHUNK = 512
SLICE = 16
ASLICE = 32
PIECE = 16


def dot(left, right):
    return jnp.dot(left, right, preferred_element_type=F32)


def dot_t(left, right):
    return lax.dot_general(left, right, (((1,), (1,)), ((), ())), preferred_element_type=F32)


def t_dot(left, right):
    return lax.dot_general(left, right, (((0,), (0,)), ((), ())), preferred_element_type=F32)


def two_part_dot(left, right_low):
    high = left.astype(BF16)
    rest = (left - high.astype(F32)).astype(BF16)
    return dot(high, right_low) + dot(rest, right_low)


def norm_stats(x):
    center = x - jnp.mean(x, axis=-1, keepdims=True)
    rate = lax.rsqrt(jnp.mean(center * center, axis=-1, keepdims=True) + NORM_EPS)
    return center * rate, rate


def norm_backward(grad, scaled, rate, gain):
    inner = grad * gain
    mean_in = jnp.mean(inner, axis=-1, keepdims=True)
    mean_dot = jnp.mean(inner * scaled, axis=-1, keepdims=True)
    grad_x = rate * (inner - mean_in - scaled * mean_dot)
    return grad_x, jnp.sum(grad * scaled, axis=0, keepdims=True), jnp.sum(grad, axis=0, keepdims=True)


def unit_backward(grad, projected):
    rate = lax.rsqrt(jnp.sum(projected * projected, axis=-1, keepdims=True) + EMBED_EPS)
    unit = projected * rate
    return rate * (grad - unit * jnp.sum(grad * unit, axis=-1, keepdims=True))


def gelu_pair(f):
    phi = 0.5 + 0.5 * lax.erf(f * INV_SQRT_2)
    density = jnp.exp2((f * f) * HALF_LOG2_E + LOG2_INV_SQRT_2PI)
    return f * phi, phi + f * density


def segment_ends(lengths_ref):
    count = lengths_ref.shape[1]
    ends = []
    total = jnp.int32(0)
    for s in range(count):
        total = total + lengths_ref[0, s]
        ends.append(total)
    return ends


def longest_start(lengths_ref, longest):
    found = jnp.int32(0)
    start = jnp.int32(0)
    for s in range(lengths_ref.shape[1]):
        found = jnp.where(lengths_ref[0, s] == longest, start, found)
        start = start + lengths_ref[0, s]
    return found


def shift_pick(shift):
    shape = (LANES, LANES + PIECE)
    row = lax.broadcasted_iota(jnp.int32, shape, 0) + shift
    return jnp.where(lax.broadcasted_iota(jnp.int32, shape, 1) == row, 1.0, 0.0).astype(BF16)


def fill_bias(bias_ref, lengths_ref, ptok, qtok):
    half = ptok // 2
    ends = segment_ends(lengths_ref)
    first = longest_start(lengths_ref, half)

    def segments(place):
        token = place + half + first
        token = jnp.where(token >= ptok, token - ptok, token)
        seg = jnp.zeros_like(token)
        for end in ends:
            seg = seg + jnp.where(token >= end, 1, 0)
        return seg

    row_seg = segments(lax.broadcasted_iota(jnp.int32, (8, half), 1))[:1]
    for r0 in range(0, half, LANES):
        col = segments(lax.broadcasted_iota(jnp.int32, (LANES, LANES), 0) + r0)
        for c in range(0, half, LANES):
            bias_ref[r0 : r0 + LANES, c : c + LANES] = jnp.where(col == row_seg[:, c : c + LANES], 0.0, NEG_FILL)
    for c in range(0, qtok, LANES):
        for r0 in range(0, qtok, LANES):
            row = (lax.broadcasted_iota(jnp.int32, (LANES, LANES), 0) + r0) // QLEN
            col = (lax.broadcasted_iota(jnp.int32, (LANES, LANES), 1) + c) // QLEN
            bias_ref[half + r0 : half + r0 + LANES, c : c + LANES] = jnp.where(row == col, 0.0, NEG_FILL)


def spans(ptok, qtok):
    half = ptok // 2
    return ((0, half, None), (half, half, 0), (ptok, qtok, half))


def owner_place(me_ref, r, turned=False):
    first, second = (r >> 3) & 1, (r >> 2) & 1
    if turned:
        first, second = second, first
    core, x, y, z = me_ref[0] ^ (r >> 4), me_ref[1] ^ first, me_ref[2] ^ second, me_ref[3] ^ (r & 3)
    return pl.multiple_of((((y * 2 + x) * 2 + core) * 4 + z) * PIECE, PIECE)


def to_relative(me_ref, plain_ref, out_ref, turned=False):
    for r in range(32):
        out_ref[r * PIECE : (r + 1) * PIECE] = plain_ref[pl.ds(owner_place(me_ref, r, turned), PIECE), :]


def units(pair, ptok, qtok):
    for index, (base, size, bias_row) in enumerate(spans(ptok, qtok)):
        block = min(RB, size)
        place = 0
        for r0 in range(base, base + size, block):
            for side in range(2):
                yield index, base, size, bias_row, r0, block, side, place
                place += block


def one_head(block, side, rows):
    lane = lax.broadcasted_iota(jnp.int32, (block, LANES), 1)
    return jnp.where((lane < HEAD) if side == 0 else (lane >= HEAD), rows, BF16(0))


def attention_forward_kernel(
    ptok,
    lengths_hbm,
    xp_hbm,
    xq_hbm,
    wq_hbm,
    wk_hbm,
    wv_hbm,
    wo_hbm,
    bq_hbm,
    bv_hbm,
    bo_hbm,
    q_ref,
    k_ref,
    v_ref,
    o_ref,
    lse_ref,
    x1_ref,
    rate1_ref,
    xt_ref,
    me_ref,
    x_scr,
    r1_scr,
    bias_scr,
    vt_scr,
    ot_scr,
    lengths_ref,
    xp_ref,
    wq_ref,
    wk_ref,
    wv_ref,
    wo_ref,
    bq_ref,
    bv_ref,
    bo_ref,
    sems,
):
    step = pl.program_id(0)
    rows = x_scr.shape[0]
    qtok = rows - ptok

    @pl.when(step == 0)
    def _():
        pairs = (
            (lengths_hbm, lengths_ref),
            (xp_hbm, xp_ref.at[pl.ds(0, ptok)]),
            (xp_hbm, xp_ref.at[pl.ds(ptok, ptok)]),
            (xq_hbm, x_scr.at[pl.ds(ptok, qtok)]),
            (bo_hbm, bo_ref),
            (wq_hbm, wq_ref),
            (bq_hbm, bq_ref),
            (wk_hbm, wk_ref),
            (wv_hbm, wv_ref),
            (bv_hbm, bv_ref),
            (wo_hbm, wo_ref),
        )
        copies = [pltpu.make_async_copy(held, ref, sems.at[i]) for i, (held, ref) in enumerate(pairs)]
        for copy in copies:
            copy.start()
        grp = lax.axis_index("grp")
        me_ref[0] = grp & 1
        me_ref[1] = (grp >> 1) & 1
        me_ref[2] = (grp >> 2) & 1
        me_ref[3] = lax.axis_index("psg")
        for copy in copies:
            copy.wait()
        first = longest_start(lengths_ref, ptok // 2)
        aligned = (first // PIECE) * PIECE
        pick = shift_pick(first - aligned)
        for r0 in range(0, ptok, LANES):
            at = pl.multiple_of(aligned + r0, PIECE)
            x_scr[r0 : r0 + LANES] = dot(pick, xp_ref[pl.ds(at, LANES + PIECE), :]).astype(BF16)
        x = x_scr[...]
        xt_ref[...] = jnp.transpose(x)
        r1_scr[...] = x.astype(F32) + bo_ref[...]
        fill_bias(bias_scr, lengths_ref, ptok, qtok)

    x = x_scr[...]
    quad = pl.ds(pl.multiple_of(step * QLANES, QLANES), QLANES)
    q_ref[:, quad] = (dot(x, wq_ref[:, quad]) + bq_ref[:, quad]).astype(BF16) * BF16(HEAD**-0.5)
    k_ref[:, quad] = dot(x, wk_ref[:, quad]).astype(BF16)
    v_ref[:, quad] = (dot(x, wv_ref[:, quad]) + bv_ref[:, quad]).astype(BF16)
    turned = jnp.transpose(v_ref[:, quad])
    for h in range(QUAD):
        vt_scr[h, :HEAD] = turned[h * HEAD : (h + 1) * HEAD]
        vt_scr[h, HEAD:] = jnp.ones((vt_scr.shape[1] - HEAD, rows), BF16)
    todo = [(pair, *unit) for pair in range(QUAD // 2) for unit in units(pair, ptok, qtok)]

    def logits(pair, index, base, size, bias_row, r0, block, side, place):
        lanes = pl.ds(pl.multiple_of(step * QLANES + pair * LANES, LANES), LANES)
        return dot_t(k_ref[base : base + size, lanes], one_head(block, side, q_ref[r0 : r0 + block, lanes]))

    ahead = logits(*todo[0])
    for i, (pair, index, base, size, bias_row, r0, block, side, place) in enumerate(todo):
        s = ahead
        if i + 1 < len(todo):
            ahead = logits(*todo[i + 1])
        h = 2 * pair + side
        parts = []
        high = None
        for j in range(0, size, ASLICE):
            part = s[j : j + ASLICE]
            if bias_row is not None:
                part = part + bias_scr[bias_row + j : bias_row + j + ASLICE, r0 - base : r0 - base + block]
            parts.append(part)
            for m in range(0, ASLICE, 8):
                high = part[m : m + 8] if high is None else jnp.maximum(high, part[m : m + 8])
        peak = jnp.max(high, axis=0, keepdims=True)
        e = jnp.concatenate([jnp.exp(part - peak).astype(BF16) for part in parts], axis=0)
        found = dot(vt_scr[h, :, base : base + size], e)
        sums = found[HEAD : HEAD + 1]
        ot_scr[h * HEAD : (h + 1) * HEAD, r0 : r0 + block] = (found[:HEAD] * (1.0 / sums)).astype(BF16)
        lse_ref[step, h : h + 1, r0 : r0 + block] = peak + jnp.log(sums)
    o_ref[:, quad] = jnp.transpose(ot_scr[...])
    r1_scr[...] += dot(o_ref[:, quad], wo_ref[quad, :])

    @pl.when(step == pl.num_programs(0) - 1)
    def _():
        scaled, rate = norm_stats(r1_scr[...])
        x1_ref[...] = scaled
        rate1_ref[...] = jnp.broadcast_to(rate, rate1_ref.shape)


def spec(shape, index):
    return pl.BlockSpec(shape, index)


def whole(array):
    return pl.BlockSpec(memory_space=pltpu.VMEM)


def in_hbm(array):
    return pltpu.with_memory_space_constraint(array, pltpu.HBM)


def const(array):
    nd = len(array.shape)
    return pl.BlockSpec(array.shape, lambda *_: (0,) * nd)


def smem():
    return pl.BlockSpec(memory_space=pltpu.SMEM)


def cost(micros):
    return pl.CostEstimate(flops=int(micros * 1e9), bytes_accessed=int(micros * 1e6), transcendentals=0)


def shaped(shape, dtype):
    return jax.ShapeDtypeStruct(shape, dtype)


def params(grid_rank, mebibytes):
    return pltpu.CompilerParams(
        dimension_semantics=("arbitrary",) * grid_rank, vmem_limit_bytes=int(mebibytes * 1024 * 1024)
    )


def attention_forward(lengths, xp, xq, wq, bq, wk, wv, bv, wo, bo):
    ptok, width = xp.shape
    qtok = xq.shape[0]
    rows = ptok + qtok
    quads = HEADS // QUAD
    half = ptok // 2
    return pl.pallas_call(
        functools.partial(attention_forward_kernel, ptok),
        grid=(quads,),
        in_specs=[pl.BlockSpec(memory_space=pltpu.HBM)] * 10,
        out_specs=[whole(None)] * 8 + [smem()],
        out_shape=[shaped((rows, width), BF16)] * 4
        + [
            shaped((quads, 8, rows), F32),
            shaped((rows, width), F32),
            shaped((rows, LANES), F32),
            shaped((width, rows), BF16),
            shaped((4,), jnp.int32),
        ],
        scratch_shapes=[
            pltpu.VMEM((rows, width), BF16),
            pltpu.VMEM((rows, width), F32),
            pltpu.VMEM((half + qtok, half), F32),
            pltpu.VMEM((QUAD, HEAD + 16, rows), BF16),
            pltpu.VMEM((QLANES, rows), BF16),
            pltpu.SMEM(lengths.shape, jnp.int32),
            pltpu.VMEM((2 * ptok, width), BF16),
        ]
        + [pltpu.VMEM((width, width), BF16)] * 4
        + [pltpu.VMEM((1, width), F32)] * 3
        + [pltpu.SemaphoreType.DMA((11,))],
        compiler_params=params(1, 23),
        cost_estimate=cost(20),
        name="attention_forward",
    )(*[in_hbm(a) for a in (lengths, xp, xq, wq, wk, wv, wo, bq, bv, bo)])


def ffn_forward_kernel(
    aliased,
    rb,
    offset,
    x1_ref,
    g1_ref,
    s1_ref,
    wi_ref,
    bi_ref,
    wo_ref,
    bo_ref,
    g2_ref,
    s2_ref,
    wp_ref,
    *rest,
):
    rest = rest[aliased:]
    u_ref, d_ref, x2_ref, rate2_ref, e_ref, emb_ref, h1_scr, r2_scr = rest
    step = pl.program_id(0)
    rows = h1_scr.shape[0]
    own = slice(offset, offset + rows)
    chunk = pl.ds(pl.multiple_of(step * FCHUNK, FCHUNK), FCHUNK)

    @pl.when(step == 0)
    def _():
        h1 = x1_ref[own] * g1_ref[...] + s1_ref[...]
        h1_scr[...] = h1.astype(BF16)
        r2_scr[...] = h1 + bo_ref[...]

    ahead = dot(h1_scr[:rb], wi_ref[...])
    for r in range(0, rows, rb):
        f = ahead
        if r + rb < rows:
            ahead = dot(h1_scr[r + rb : r + 2 * rb], wi_ref[...])
        bias = bi_ref[...]
        for i in range(0, rb, SLICE):
            u, d = gelu_pair(f[i : i + SLICE] + bias)
            at = offset + r + i
            u_ref[at : at + SLICE, chunk] = u.astype(BF16)
            d_ref[at : at + SLICE, chunk] = d.astype(BF16)
        r2_scr[r : r + rb] += dot(u_ref[offset + r : offset + r + rb, chunk], wo_ref[...])

    @pl.when(step == pl.num_programs(0) - 1)
    def _():
        scaled, rate = norm_stats(r2_scr[...])
        x2_ref[own] = scaled
        rate2_ref[own] = jnp.broadcast_to(rate, (rows, LANES))
        h2 = (scaled * g2_ref[...] + s2_ref[...]).astype(BF16)
        e = dot(h2, wp_ref[...])
        e_ref[own] = e
        size = jnp.sum(e * e, axis=-1, keepdims=True)
        emb_ref[...] = (e * lax.rsqrt(size + EMBED_EPS)).astype(BF16)


def held_first(previous):
    return len(previous) > 0


def ffn_forward(count, offset, total, x1, g1, s1, wi, bi, wo, bo, g2, s2, wp, previous):
    width = x1.shape[1]
    ff = wi.shape[1]
    dim = wp.shape[1]
    first = 10
    pin = in_hbm if held_first(previous) else (lambda array: array)
    held = list(previous)
    return pl.pallas_call(
        functools.partial(ffn_forward_kernel, len(held), min(RB, count), offset),
        grid=(ff // FCHUNK,),
        in_specs=[
            whole(x1),
            const(g1),
            const(s1),
            spec((width, FCHUNK), lambda c: (0, c)),
            spec((1, FCHUNK), lambda c: (0, c)),
            spec((FCHUNK, width), lambda c: (c, 0)),
            const(bo),
            const(g2),
            const(s2),
            const(wp),
        ]
        + [whole(None)] * len(held),
        out_specs=[whole(None)] * 6,
        out_shape=[
            shaped((total, ff), BF16),
            shaped((total, ff), BF16),
            shaped((total, width), F32),
            shaped((total, LANES), F32),
            shaped((total, dim), F32),
            shaped((count, dim), BF16),
        ],
        scratch_shapes=[
            pltpu.VMEM((count, width), BF16),
            pltpu.VMEM((count, width), F32),
        ],
        input_output_aliases={first + i: i for i in range(len(held))},
        compiler_params=params(1, 15),
        cost_estimate=cost(12 if count > 256 else 4),
        name="ffn_forward",
    )(x1, g1, s1, pin(wi), bi, pin(wo), bo, g2, s2, wp, *held)


def passage_member(lengths_ref, rows):
    ends = segment_ends(lengths_ref)
    lane = lax.broadcasted_iota(jnp.int32, (8, LANES), 1)
    low = jnp.full((8, LANES), rows, jnp.int32)
    high = jnp.zeros((8, LANES), jnp.int32)
    start = jnp.int32(0)
    for s, end in enumerate(ends):
        low = jnp.where(lane == s, start, low)
        high = jnp.where(lane == s, end, high)
        start = end
    token = lax.broadcasted_iota(jnp.int32, (rows, LANES), 0) + longest_start(lengths_ref, rows // 2)
    token = jnp.where(token >= rows, token - rows, token)
    inside = (token >= low[:1]) & (token < high[:1])
    return jnp.where(inside, 1.0, 0.0).astype(BF16)


def soft_match(group, pass_embed):
    return jnp.exp(SHARPNESS * dot_t(group, pass_embed) - SHARPNESS)


def score_kernel(psg, count, lengths_ref, emb_ref, *rest):
    group_refs = rest[:psg]
    score_ref, pooled_ref = rest[psg:]
    member = passage_member(lengths_ref, emb_ref.shape[0])
    group = jnp.concatenate([ref[...] for ref in group_refs], axis=0)
    matched = soft_match(group, emb_ref[...])
    pooled = two_part_dot(matched, member)
    lane = lax.broadcasted_iota(jnp.int32, pooled.shape, 1)
    pooled = jnp.where(lane < count, pooled, 1.0)
    pooled_ref[...] = pooled
    smooth = 1.0 + jnp.log(pooled) * (1.0 / SHARPNESS)
    queries = pooled.shape[0] // QLEN
    score_ref[...] = SCORE_SCALE * jnp.sum(smooth.reshape(queries, QLEN, LANES), axis=1)


def score(lengths, emb, groups):
    psg = len(groups)
    tokens = sum(g.shape[0] for g in groups)
    return pl.pallas_call(
        functools.partial(score_kernel, psg, lengths.shape[1]),
        in_specs=[smem()] + [pl.BlockSpec(memory_space=pltpu.VMEM)] * (1 + psg),
        out_shape=[shaped((tokens // QLEN, LANES), F32), shaped((tokens, LANES), F32)],
        compiler_params=params(0, 8),
        cost_estimate=cost(3),
        name="score",
    )(lengths, emb, *groups)


def loss_kernel(psg, count, where_ref, lengths_ref, positives_ref, pooled_ref, emb_ref, *rest):
    group_refs = rest[:psg]
    score_refs = rest[psg : 2 * psg]
    loss_ref, own_ref = rest[2 * psg : 2 * psg + 2]
    away_refs = rest[2 * psg + 2 : 3 * psg + 1]
    grad_ref = rest[3 * psg + 1]
    position = where_ref[3]
    queries = score_refs[0].shape[0]
    each = queries // psg
    lane = lax.broadcasted_iota(jnp.int32, (queries, LANES), 1)
    row = lax.broadcasted_iota(jnp.int32, (queries, LANES), 0)
    valid = lane < count
    blocks = []
    for e in range(psg):
        found = score_refs[e][...]
        found = jnp.concatenate(
            [found[((d - e) % psg) * each : ((d - e) % psg + 1) * each] for d in range(psg)], axis=0
        )
        blocks.append(jnp.where(valid, found, -jnp.inf))
    target = jnp.zeros((queries, LANES), jnp.int32)
    for d in range(psg):
        for j in range(each):
            chosen = positives_ref[lax.rem(position + d, psg) * each + j]
            target = jnp.where(row == d * each + j, chosen, target)
    peak = blocks[0]
    for found in blocks[1:]:
        peak = jnp.maximum(peak, found)
    peak = jnp.max(peak, axis=-1, keepdims=True)
    total = jnp.zeros((queries, 1), F32)
    picked = jnp.zeros((queries, 1), F32)
    for e in range(psg):
        owner = lax.rem(position + e, psg)
        hit = (target == owner * count + lane) & valid
        total = total + jnp.sum(jnp.exp(blocks[e] - peak), axis=-1, keepdims=True)
        picked = picked + jnp.sum(jnp.where(hit, blocks[e], 0.0), axis=-1, keepdims=True)
        if e == 0:
            own_hit = jnp.where(hit, 1.0, 0.0)
    log_total = peak + jnp.log(total)
    losses = jnp.broadcast_to(log_total - picked, (queries, LANES))
    place = lax.rem(position + row // each, psg) * each + row % each
    losses = jnp.sum(jnp.where(lane == place, losses, 0.0), axis=0, keepdims=True)
    loss_ref[...] = losses[:, :queries]
    grad = jnp.where(valid, jnp.exp(blocks[0] - log_total) - own_hit, 0.0) * SCORE_SCALE
    tokens = queries * QLEN
    grad = jnp.broadcast_to(grad[:, None, :], (queries, QLEN, LANES)).reshape(tokens, LANES)
    grad = grad / pooled_ref[...]
    member = passage_member(lengths_ref, emb_ref.shape[0])
    high = grad.astype(BF16)
    rest_low = (grad - high.astype(F32)).astype(BF16)
    spread = dot_t(high, member) + dot_t(rest_low, member)
    group = jnp.concatenate([ref[...] for ref in group_refs], axis=0)
    low = (soft_match(group, emb_ref[...]) * spread).astype(BF16)
    group_grad = dot(low, emb_ref[...])
    each_tokens = tokens // psg
    own_ref[...] = group_grad[:each_tokens]
    for d in range(1, psg):
        away_refs[d - 1][...] = group_grad[d * each_tokens : (d + 1) * each_tokens].astype(BF16)
    grad_ref[...] = jnp.transpose(dot(jnp.transpose(group), low))


def loss_and_grads(position, lengths, positives, pooled, emb, groups, scores):
    psg = len(groups)
    queries = scores[0].shape[0]
    tokens, dim = groups[0].shape
    vmem = pl.BlockSpec(memory_space=pltpu.VMEM)
    return pl.pallas_call(
        functools.partial(loss_kernel, psg, lengths.shape[1]),
        in_specs=[smem(), smem(), smem()] + [vmem] * (2 + 2 * psg),
        out_shape=[shaped((1, queries), F32), shaped((tokens, dim), F32)]
        + [shaped((tokens, dim), BF16)] * (psg - 1)
        + [shaped(emb.shape, F32)],
        compiler_params=params(0, 8),
        cost_estimate=cost(3),
        name="loss_and_grads",
    )(position, lengths, positives, pooled, emb, *groups, *scores)


def head_backward(grad_embed, e, x2, rate2, wp, g2, s2):
    low = unit_backward(grad_embed, e).astype(BF16)
    grad_h2 = dot_t(low, wp)
    grad_r2, gain_term, shift_term = norm_backward(grad_h2, x2, rate2[:, :1], g2)
    h2 = (x2 * g2 + s2).astype(BF16)
    return grad_r2, gain_term, shift_term, dot(jnp.transpose(low), h2)


def passage_head_kernel(
    grad_ref, e_ref, x2_ref, rate2_ref, wp_ref, g2_ref, s2_ref, gr2_ref, vec_ref, proj_ref
):
    ptok = grad_ref.shape[0]
    grad_r2, gain_term, shift_term, proj = head_backward(
        grad_ref[...], e_ref[:ptok], x2_ref[:ptok], rate2_ref[:ptok], wp_ref[...], g2_ref[...], s2_ref[...]
    )
    gr2_ref[...] = grad_r2
    vec_ref[...] = jnp.zeros_like(vec_ref)
    vec_ref[0:1] = gain_term
    vec_ref[1:2] = shift_term
    proj_ref[...] = proj


def passage_head(grad, e, x2, rate2, wp, g2, s2):
    ptok, dim = grad.shape
    width = x2.shape[1]
    return pl.pallas_call(
        passage_head_kernel,
        grid=(1,),
        in_specs=[
            whole(grad),
            whole(e),
            whole(x2),
            whole(rate2),
            const(wp),
            const(g2),
            const(s2),
        ],
        out_specs=[whole(None)] * 3,
        out_shape=[shaped((ptok, width), F32), shaped((8, width), F32), shaped((dim, width), F32)],
        compiler_params=params(1, 10),
        cost_estimate=cost(4),
        name="passage_head",
    )(grad, e, x2, rate2, wp, g2, s2)


def fixed(shape):
    return pl.BlockSpec(memory_space=pltpu.VMEM)


def ffn_backward_kernel(
    psg,
    me_ref,
    gr2p_ref,
    vec_ref,
    proj_ref,
    own_ref,
    *rest,
):
    away_refs = rest[: psg - 1]
    (
        e_ref,
        x2_ref,
        rate2_ref,
        wp_ref,
        g2_ref,
        s2_ref,
        x1_ref,
        g1_ref,
        s1_ref,
        wi_ref,
        wo_ref,
        u_ref,
        d_ref,
        dproj_ref,
        dvec_ref,
        dbi_ref,
        gh1_ref,
        keep_i_ref,
        send_i_ref,
        keep_o_ref,
        send_o_ref,
        gz_scr,
        turn_scr,
        gzt_scr,
        h1t_scr,
        gh1_scr,
        gi_scr,
    ) = rest[psg - 1 :]
    step = pl.program_id(0)
    ptok = gr2p_ref.shape[0]
    rows = gz_scr.shape[0]

    @pl.when(step == 0)
    def _():
        grad = own_ref[...]
        for ref in away_refs:
            grad = grad + ref[...].astype(F32)
        grad_r2, gain_term, shift_term, proj = head_backward(
            grad, e_ref[ptok:], x2_ref[ptok:], rate2_ref[ptok:], wp_ref[...], g2_ref[...], s2_ref[...]
        )
        dproj_ref[...] = jnp.transpose(proj_ref[...] + proj).astype(BF16)
        gr2p = gr2p_ref[...]
        gh1_scr[:ptok] = gr2p
        gh1_scr[ptok:] = grad_r2
        low_p = gr2p.astype(BF16)
        low_q = grad_r2.astype(BF16)
        gz_scr[:ptok] = low_p
        gz_scr[ptok:] = low_q
        dvec_ref[...] = jnp.zeros_like(dvec_ref)
        dvec_ref[0:1] = vec_ref[0:1] + gain_term
        dvec_ref[1:2] = vec_ref[1:2] + shift_term
        dvec_ref[2:3] = jnp.sum(low_p.astype(F32), axis=0, keepdims=True) + jnp.sum(
            low_q.astype(F32), axis=0, keepdims=True
        )
        turn_scr[...] = jnp.transpose((x1_ref[...] * g1_ref[...] + s1_ref[...]).astype(BF16))
        to_relative(me_ref, turn_scr, h1t_scr)
        turn_scr[...] = jnp.transpose(gz_scr[...])
        to_relative(me_ref, turn_scr, gzt_scr, turned=True)

    chunk = pl.ds(pl.multiple_of(step * FCHUNK, FCHUNK), FCHUNK)
    third = rows // 3
    outer = dot(gzt_scr[...], u_ref[:, chunk])
    ahead = dot_t(gz_scr[:third], wo_ref[...])
    sums = jnp.zeros((8, FCHUNK), F32)
    for r in range(0, rows, third):
        grad_active = ahead
        if r + third < rows:
            ahead = dot_t(gz_scr[r + third : r + 2 * third], wo_ref[...])
        for i in range(0, third, SLICE):
            at = r + i
            low = (grad_active[i : i + SLICE] * d_ref[at : at + SLICE, chunk].astype(F32)).astype(BF16)
            gi_scr[at : at + SLICE] = low
            kept = low.astype(F32)
            for m in range(0, SLICE, 8):
                sums = sums + kept[m : m + 8]
        gh1_scr[r : r + third] += dot_t(gi_scr[r : r + third], wi_ref[...])
    dbi_ref[:, chunk] = jnp.sum(sums, axis=0, keepdims=True)
    half = keep_i_ref.shape[0]
    for term, keep_ref, send_ref in (
        (outer, keep_o_ref, send_o_ref),
        (dot(h1t_scr[...], gi_scr[...]), keep_i_ref, send_i_ref),
    ):
        keep_ref[:, chunk] = term[:half].astype(BF16)
        send_ref[:, chunk] = term[half:].astype(BF16)

    @pl.when(step == pl.num_programs(0) - 1)
    def _():
        gh1_ref[...] = gh1_scr[...]


def ffn_backward(me, gr2p, vec, proj, own, aways, e, x2, rate2, wp, g2, s2, x1, g1, s1, wi, wo, u, d):
    ptok, width = gr2p.shape
    rows = x1.shape[0]
    dim = wp.shape[1]
    ff = wi.shape[1]
    return pl.pallas_call(
        functools.partial(ffn_backward_kernel, 1 + len(aways)),
        grid=(ff // FCHUNK,),
        in_specs=[smem(), whole(gr2p), whole(vec), whole(proj), whole(own)]
        + [whole(a) for a in aways]
        + [
            whole(e),
            whole(x2),
            whole(rate2),
            const(wp),
            const(g2),
            const(s2),
            whole(x1),
            const(g1),
            const(s1),
            spec((width, FCHUNK), lambda c: (0, c)),
            spec((FCHUNK, width), lambda c: (c, 0)),
            whole(u),
            whole(d),
        ],
        out_specs=[
            fixed((width, dim)),
            fixed((8, width)),
            fixed((1, ff)),
            fixed((rows, width)),
        ]
        + [whole(None)] * 4,
        out_shape=[
            shaped((width, dim), BF16),
            shaped((8, width), F32),
            shaped((1, ff), F32),
            shaped((rows, width), F32),
        ]
        + [shaped((width // 2, ff), BF16)] * 4,
        scratch_shapes=[
            pltpu.VMEM((rows, width), BF16),
            pltpu.VMEM((width, rows), BF16),
            pltpu.VMEM((width, rows), BF16),
            pltpu.VMEM((width, rows), BF16),
            pltpu.VMEM((rows, width), F32),
            pltpu.VMEM((rows, FCHUNK), BF16),
        ],
        compiler_params=params(1, 17),
        cost_estimate=cost(15),
        name="ffn_backward",
    )(me, gr2p, vec, proj, own, *aways, e, x2, rate2, wp, g2, s2, x1, g1, s1, in_hbm(wi), in_hbm(wo), u, d)


def put_vector(wave_ref, row, vector):
    for i in range(vector.shape[1] // LANES):
        wave_ref[row + i : row + i + 1] = vector[:, i * LANES : (i + 1) * LANES]
    return row + vector.shape[1] // LANES


def take_vector(wave_ref, row, column, out_ref):
    size = out_ref.shape[1]
    for i in range(size // LANES):
        out_ref[:, i * LANES : (i + 1) * LANES] = wave_ref[row + i : row + i + 1, column : column + LANES].astype(
            F32
        )
    return row + size // LANES


def probabilities_kernel(ptok, lengths_ref, q_ref, k_ref, lse_ref, p_ref, pq_ref, bias_scr):
    qtok = q_ref.shape[0] - ptok

    @pl.when(pl.program_id(0) == 0)
    def _():
        fill_bias(bias_scr, lengths_ref, ptok, qtok)

    step = pl.program_id(0)
    todo = [(pair, *unit) for pair in range(QUAD // 2) for unit in units(pair, ptok, qtok)]

    def logits(pair, index, base, size, bias_row, r0, block, side, place):
        lanes = pl.ds(pl.multiple_of(step * QLANES + pair * LANES, LANES), LANES)
        return dot_t(k_ref[base : base + size, lanes], one_head(block, side, q_ref[r0 : r0 + block, lanes]))

    ahead = logits(*todo[0])
    for i, (pair, index, base, size, bias_row, r0, block, side, place) in enumerate(todo):
        s = ahead
        if i + 1 < len(todo):
            ahead = logits(*todo[i + 1])
        h = 2 * pair + side
        lse = lse_ref[step, h : h + 1, r0 : r0 + block]
        for j in range(0, size, ASLICE):
            part = s[j : j + ASLICE]
            if bias_row is not None:
                part = part + bias_scr[bias_row + j : bias_row + j + ASLICE, r0 - base : r0 - base + block]
            p = jnp.exp(part - lse).astype(BF16)
            if index < 2:
                p_ref[step, 2 * pair + index, j : j + ASLICE, place : place + block] = p
            else:
                pq_ref[step, pair, j : j + ASLICE, place : place + block] = p


def probabilities(lengths, q, k, lse, ptok):
    rows, width = q.shape
    quads = HEADS // QUAD
    half, qtok = ptok // 2, rows - ptok
    return pl.pallas_call(
        functools.partial(probabilities_kernel, ptok),
        grid=(quads,),
        in_specs=[smem(), whole(q), whole(k), whole(lse)],
        out_specs=[whole(None), whole(None)],
        out_shape=[
            shaped((quads, QUAD, half, 2 * half), BF16),
            shaped((quads, QUAD // 2, qtok, 2 * qtok), BF16),
        ],
        scratch_shapes=[pltpu.VMEM((half + qtok, half), F32)],
        compiler_params=params(1, 10),
        cost_estimate=cost(8),
        name="probabilities",
    )(lengths, q, k, lse)


def first_norm_kernel(gh1_ref, x1_ref, rate1_ref, g1_ref, wo_ref, gr1_ref, go_ref, vec_ref):
    grad_r1, gain_term, shift_term = norm_backward(gh1_ref[...], x1_ref[...], rate1_ref[:, :1], g1_ref[...])
    gr1_ref[...] = grad_r1
    low = grad_r1.astype(BF16)
    vec_ref[...] = jnp.zeros_like(vec_ref)
    vec_ref[0:1] = gain_term
    vec_ref[1:2] = shift_term
    vec_ref[2:3] = jnp.sum(low.astype(F32), axis=0, keepdims=True)
    go_ref[...] = dot_t(low, wo_ref[...]).astype(BF16)


def first_norm(gh1, x1, rate1, g1, wo):
    rows, width = x1.shape
    return pl.pallas_call(
        first_norm_kernel,
        grid=(1,),
        in_specs=[whole(gh1), whole(x1), whole(rate1), const(g1), const(wo)],
        out_specs=[whole(None)] * 3,
        out_shape=[shaped((rows, width), F32), shaped((rows, width), BF16), shaped((8, width), F32)],
        compiler_params=params(1, 9),
        cost_estimate=cost(4),
        name="first_norm",
    )(gh1, x1, rate1, g1, wo)


def heads_backward_kernel(
    quad,
    ptok,
    p_ref,
    pq_ref,
    q_ref,
    k_ref,
    v_ref,
    o_ref,
    go_ref,
    gq_ref,
    gk_ref,
    gv_ref,
    dd_scr,
    gqt_scr,
    qm_scr,
    gm_scr,
    gs_scr,
    kt_scr,
):
    qtok = q_ref.shape[0] - ptok

    own = slice(quad * QLANES, (quad + 1) * QLANES)
    product = go_ref[:, own].astype(F32) * o_ref[:, own].astype(F32)
    ones = jnp.where(
        lax.broadcasted_iota(jnp.int32, (16, QLANES), 1) // HEAD
        == lax.broadcasted_iota(jnp.int32, (16, QLANES), 0),
        1.0,
        0.0,
    ).astype(BF16)
    high = product.astype(BF16)
    dd_scr[...] = dot_t(ones, high) + dot_t(ones, (product - high.astype(F32)).astype(BF16))
    kt_scr[...] = jnp.transpose(k_ref[:, own])
    todo = [(pair, *unit) for pair in range(QUAD // 2) for unit in units(pair, ptok, qtok)]

    def begin(pair, index, base, size, bias_row, r0, block, side, place):
        lanes = slice(quad * QLANES + pair * LANES, quad * QLANES + (pair + 1) * LANES)
        buffer = (3 * pair + index) % 2
        qm_scr[buffer, place : place + block] = one_head(block, side, q_ref[r0 : r0 + block, lanes])
        gm = one_head(block, side, go_ref[r0 : r0 + block, lanes])
        gm_scr[buffer, place : place + block] = gm
        return dot_t(v_ref[base : base + size, lanes], gm)

    ahead = begin(*todo[0])
    for t, (pair, index, base, size, bias_row, r0, block, side, place) in enumerate(todo):
        grad_prob = ahead
        if t + 1 < len(todo):
            ahead = begin(*todo[t + 1])
        inner = slice(pair * LANES, (pair + 1) * LANES)
        buffer = (3 * pair + index) % 2
        h = 2 * pair + side
        dd = dd_scr[h : h + 1, r0 : r0 + block]
        p_at = p_ref.at[quad, 2 * pair + index] if index < 2 else pq_ref.at[quad, pair]
        for i in range(0, size, ASLICE):
            p = p_at[i : i + ASLICE, place : place + block].astype(F32)
            gs = p * (grad_prob[i : i + ASLICE] - dd)
            gs_scr[buffer, i : i + ASLICE, place : place + block] = gs.astype(BF16)
        gqt_scr[h * HEAD : (h + 1) * HEAD, r0 : r0 + block] = dot(
            kt_scr[h * HEAD : (h + 1) * HEAD, base : base + size],
            gs_scr[buffer, :size, place : place + block],
        )
        end = place + block
        if end == 2 * size:
            gv_ref[base : base + size, inner] = dot(p_at[...], gm_scr[buffer, :end]).astype(BF16)
            gk_ref[base : base + size, inner] = dot(gs_scr[buffer, :size, :end], qm_scr[buffer, :end]).astype(BF16)
    gq_ref[...] = (jnp.transpose(gqt_scr[...]) * (HEAD**-0.5)).astype(BF16)


def heads_backward(quad, p, pq, q, k, v, o, go, ptok):
    rows, width = q.shape
    half = ptok // 2
    low = lambda *shape: pltpu.VMEM(shape, BF16)
    return pl.pallas_call(
        functools.partial(heads_backward_kernel, quad, ptok),
        grid=(1,),
        in_specs=[whole(None)] * 7,
        out_specs=[whole(None)] * 3,
        out_shape=[shaped((rows, QLANES), BF16)] * 3,
        scratch_shapes=[
            pltpu.VMEM((16, rows), F32),
            pltpu.VMEM((QLANES, rows), F32),
            low(2, 4 * RB, LANES),
            low(2, 4 * RB, LANES),
            low(2, half, 4 * RB),
            low(QLANES, rows),
        ],
        compiler_params=params(1, 16),
        cost_estimate=cost(10),
        name="heads_backward",
    )(p, pq, q, k, v, o, go)


def output_term_kernel(me_ref, gr1_ref, o_ref, dout_ref, turn_scr, ot_scr):
    turn_scr[...] = jnp.transpose(o_ref[...])
    to_relative(me_ref, turn_scr, ot_scr)
    dout_ref[...] = dot(ot_scr[...], gr1_ref[...].astype(BF16)).astype(BF16)


def output_term(me, gr1, o):
    rows, width = gr1.shape
    return pl.pallas_call(
        output_term_kernel,
        grid=(1,),
        in_specs=[smem(), whole(gr1), whole(o)],
        out_specs=whole(None),
        out_shape=shaped((width, width), BF16),
        scratch_shapes=[pltpu.VMEM((width, rows), BF16)] * 2,
        compiler_params=params(1, 8),
        cost_estimate=cost(2),
        name="output_term",
    )(me, gr1, o)


def weights_kernel(
    ptok,
    me_ref,
    gr1_ref,
    dout_ref,
    xt_ref,
    gq0_ref,
    gk0_ref,
    gv0_ref,
    gq1_ref,
    gk1_ref,
    gv1_ref,
    dproj_ref,
    vec1_ref,
    vec2_ref,
    dbi_ref,
    wq_ref,
    wk_ref,
    wv_ref,
    keep_ref,
    send_ref,
    gp_ref,
    gq_ref,
    xt_scr,
    lines_scr,
    tail_scr,
):
    half_rows = keep_ref.shape[0]
    width = gr1_ref.shape[1]
    gr1 = gr1_ref[...]
    to_relative(me_ref, xt_ref, xt_scr)
    joined = [
        jnp.concatenate([left[...], right[...]], axis=1)
        for left, right in ((gq0_ref, gq1_ref), (gk0_ref, gk1_ref), (gv0_ref, gv1_ref))
    ]
    for i, grad in enumerate(joined):
        term = dot(xt_scr[...], grad)
        keep_ref[:, i * width : (i + 1) * width] = term[:half_rows].astype(BF16)
        send_ref[:, i * width : (i + 1) * width] = term[half_rows:].astype(BF16)
    keep_ref[:, 3 * width : 4 * width] = dout_ref[:half_rows]
    send_ref[:, 3 * width : 4 * width] = dout_ref[half_rows:]
    gin = gr1 + dot_t(joined[0], wq_ref[...]) + dot_t(joined[1], wk_ref[...]) + dot_t(joined[2], wv_ref[...])
    gp_ref[...] = gin[:ptok].astype(BF16)
    gq_ref[...] = gin[ptok:].astype(BF16)
    row = 0
    for vector in (
        vec2_ref[0:1],
        vec2_ref[1:2],
        vec2_ref[2:3],
        vec1_ref[0:1],
        vec1_ref[1:2],
        vec1_ref[2:3],
        dbi_ref[...],
        jnp.sum(joined[0].astype(F32), axis=0, keepdims=True),
        jnp.sum(joined[2].astype(F32), axis=0, keepdims=True),
    ):
        row = put_vector(lines_scr, row, vector)
    lines_scr[row:] = jnp.zeros((lines_scr.shape[0] - row, LANES), F32)
    dim = dproj_ref.shape[1]
    tail_scr[:, :dim] = dproj_ref[...]
    tail_scr[:, dim:] = lines_scr[...].astype(BF16)
    for r in range(32):
        ref = keep_ref if r < 16 else send_ref
        at = (r % 16) * PIECE
        ref[at : at + PIECE, 4 * width :] = tail_scr[pl.ds(owner_place(me_ref, r), PIECE), :]


def weights(me, gr1, dout, xt, first, second, dproj, vec1, vec2, dbi, wq, wk, wv, ptok):
    rows, width = gr1.shape
    lanes = 4 * width + dproj.shape[1] + LANES
    low = lambda *shape: pltpu.VMEM(shape, BF16)
    return pl.pallas_call(
        functools.partial(weights_kernel, ptok),
        grid=(1,),
        in_specs=[smem()] + [whole(None)] * 16,
        out_specs=[whole(None)] * 4,
        out_shape=[
            shaped((width // 2, lanes), BF16),
            shaped((width // 2, lanes), BF16),
            shaped((ptok, width), BF16),
            shaped((rows - ptok, width), BF16),
        ],
        scratch_shapes=[
            low(width, rows),
            pltpu.VMEM((width, LANES), F32),
            low(width, dproj.shape[1] + LANES),
        ],
        compiler_params=params(1, 16),
        cost_estimate=cost(6),
        name="weights",
    )(me, gr1, dout, xt, *first, *second, dproj, vec1, vec2, dbi, wq, wk, wv)


def from_relative(me_ref, kept_ref, other_ref, wave_ref, turned=False):
    for r in range(32):
        ref = kept_ref if r < 16 else other_ref
        at = (r % 16) * PIECE
        wave_ref[pl.ds(owner_place(me_ref, r, turned), PIECE), :] = ref[at : at + PIECE]


def unpack_ffn_kernel(
    me_ref, kept_i_ref, other_i_ref, kept_o_ref, other_o_ref, dwi_ref, dwo_ref, wave_i_scr, wave_o_scr
):
    from_relative(me_ref, kept_i_ref, other_i_ref, wave_i_scr)
    from_relative(me_ref, kept_o_ref, other_o_ref, wave_o_scr, turned=True)
    dwi_ref[...] = wave_i_scr[...].astype(F32)
    dwo_ref[...] = jnp.transpose(wave_o_scr[...].astype(F32))


def unpack_ffn(me, *halves):
    half, ff = halves[0].shape
    width = 2 * half
    return pl.pallas_call(
        unpack_ffn_kernel,
        grid=(ff // FCHUNK,),
        in_specs=[smem()] + [spec((half, FCHUNK), lambda c: (0, c))] * 4,
        out_specs=[
            spec((width, FCHUNK), lambda c: (0, c)),
            spec((FCHUNK, width), lambda c: (c, 0)),
        ],
        out_shape=[shaped((width, ff), F32), shaped((ff, width), F32)],
        scratch_shapes=[pltpu.VMEM((width, FCHUNK), BF16)] * 2,
        compiler_params=params(1, 16),
        cost_estimate=cost(6),
        name="unpack_ffn",
    )(me, *halves)


def unpack_attention_kernel(
    me_ref,
    kept_ref,
    other_ref,
    dwq_ref,
    dwk_ref,
    dwv_ref,
    dout_ref,
    dproj_ref,
    g2_ref,
    s2_ref,
    bo_ref,
    g1_ref,
    s1_ref,
    bout_ref,
    bi_ref,
    bq_ref,
    bv_ref,
    wave_scr,
):
    step = pl.program_id(0)
    width, columns = dwq_ref.shape
    for i, out_ref in enumerate((dwq_ref, dwk_ref, dwv_ref, dout_ref)):
        lanes = pl.ds(pl.multiple_of(i * width + step * columns, columns), columns)
        for r in range(32):
            ref = kept_ref if r < 16 else other_ref
            at = (r % 16) * PIECE
            out_ref[pl.ds(owner_place(me_ref, r), PIECE), :] = ref[at : at + PIECE, lanes].astype(F32)

    @pl.when(step == 0)
    def _():
        first = 4 * width
        dim = dproj_ref.shape[1]
        for r in range(32):
            ref = kept_ref if r < 16 else other_ref
            at = (r % 16) * PIECE
            wave_scr[pl.ds(owner_place(me_ref, r), PIECE), :] = ref[at : at + PIECE, first:].astype(F32)
        dproj_ref[...] = wave_scr[:, :dim]
        row = 0
        for ref in (g2_ref, s2_ref, bo_ref, g1_ref, s1_ref, bout_ref, bi_ref, bq_ref, bv_ref):
            row = take_vector(wave_scr, row, dim, ref)


def unpack_attention(me, kept, other, width, dim, ff):
    fixed_block = lambda shape: spec(shape, lambda i: (0, 0))
    columns = LANES
    return pl.pallas_call(
        unpack_attention_kernel,
        grid=(width // columns,),
        in_specs=[smem()] + [whole(None)] * 2,
        out_specs=[spec((width, columns), lambda i: (0, i))] * 4
        + [fixed_block((width, dim))]
        + [fixed_block((1, width))] * 6
        + [fixed_block((1, ff))]
        + [fixed_block((1, width))] * 2,
        out_shape=[shaped((width, width), F32)] * 4
        + [shaped((width, dim), F32)]
        + [shaped((1, width), F32)] * 6
        + [shaped((1, ff), F32)]
        + [shaped((1, width), F32)] * 2,
        scratch_shapes=[pltpu.VMEM((width, kept.shape[1] - 4 * width), F32)],
        compiler_params=params(1, 16),
        cost_estimate=cost(3),
        name="unpack_attention",
    )(me, kept, other)


def swap(block, axis_name, size, bit):
    return lax.ppermute(block, axis_name, [(i, i ^ bit) for i in range(size)])


def total(*parts):
    found = parts[0].astype(F32)
    for part in parts[1:]:
        found = found + part.astype(F32)
    return found.astype(BF16)


def core_parts(keep, found):
    size = keep.shape[0] // 4
    return [total(keep[i * size : (i + 1) * size], found[i * size : (i + 1) * size]) for i in range(4)]


def halves(block):
    size = block.shape[0] // 2
    return block[:size], block[size:]


def plane_send(blocks, grp_size):
    return tuple(swap(block, "grp", grp_size, bits) for block, bits in zip(blocks, (4, 2, 6)))


def line_parts(parts, psg_size):
    size = parts[0].shape[0] // psg_size
    return [total(*[part[i * size : (i + 1) * size] for part in parts]) for i in range(psg_size)]


def line_send(blocks, psg_size):
    return tuple(swap(block, "psg", psg_size, d) for d, block in enumerate(blocks, 1))


def line_total(own, founds, grp_size):
    piece = total(own, *founds)
    bit = 8
    while bit < grp_size:
        piece = total(piece, swap(piece, "grp", grp_size, bit))
        bit *= 2
    return piece


def tie(values, *others):
    return lax.optimization_barrier((tuple(values), others))[0]


def roll_back_kernel(lengths_ref, embed_ref, grad_ref, embed_out, grad_out, embed_scr, grad_scr):
    count = embed_ref.shape[0]
    back = count - longest_start(lengths_ref, count // 2)
    back = jnp.where(back == count, 0, back)
    aligned = (back // PIECE) * PIECE
    pick = shift_pick(back - aligned)
    for ref, scr, out in ((embed_ref, embed_scr, embed_out), (grad_ref, grad_scr, grad_out)):
        scr[:count] = ref[...]
        scr[count:] = ref[...]
        for r0 in range(0, count, LANES):
            at = pl.multiple_of(aligned + r0, PIECE)
            out[r0 : r0 + LANES] = dot(pick, scr[pl.ds(at, LANES + PIECE), :]).astype(BF16)


def roll_back(lengths, embed, grad):
    return pl.pallas_call(
        roll_back_kernel,
        grid=(1,),
        in_specs=[smem(), whole(embed), whole(grad)],
        out_specs=[whole(None)] * 2,
        out_shape=[shaped(embed.shape, BF16), shaped(grad.shape, BF16)],
        scratch_shapes=[
            pltpu.VMEM((2 * embed.shape[0], embed.shape[1]), BF16),
            pltpu.VMEM((2 * grad.shape[0], grad.shape[1]), BF16),
        ],
        compiler_params=params(1, 10),
        cost_estimate=cost(4),
        name="roll_back",
    )(lengths, embed, grad)


def shift_gather(block, axis_name, axis_size):
    found = [block]
    for distance in range(1, axis_size):
        ring = [(i, (i - distance) % axis_size) for i in range(axis_size)]
        found.append(lax.ppermute(block, axis_name, ring))
    return found


def local(
    grp_size,
    psg_size,
    passages,
    queries,
    lengths,
    positives,
    query_weight,
    query_bias,
    key_weight,
    value_weight,
    value_bias,
    output_weight,
    output_bias,
    first_gain,
    first_shift,
    inner_weight,
    inner_bias,
    outer_weight,
    outer_bias,
    second_gain,
    second_shift,
    project_weight,
):
    ptok, width = passages.shape
    qtok = queries.shape[0]
    rows = ptok + qtok
    row = lambda vector: vector.reshape(1, -1)
    g1, s1, g2, s2 = row(first_gain), row(first_shift), row(second_gain), row(second_shift)
    q, k, v, o, lse, x1, rate1, xt, me = attention_forward(
        lengths,
        passages,
        queries,
        query_weight,
        row(query_bias),
        key_weight,
        value_weight,
        row(value_bias),
        output_weight,
        row(output_bias),
    )
    layer = (x1, g1, s1, inner_weight, row(inner_bias), outer_weight, row(outer_bias), g2, s2, project_weight)
    *held, query_embed = ffn_forward(qtok, ptok, rows, *layer, ())
    groups = shift_gather(query_embed, "psg", psg_size)
    u, d, x2, rate2, e, pass_embed = ffn_forward(ptok, 0, rows, *layer, held)
    own_scores, pooled = score(lengths, pass_embed, groups)
    scores = shift_gather(own_scores, "psg", psg_size)
    (late_lse,) = tie((lse,), own_scores)
    p, pq = probabilities(lengths, q, k, late_lse, ptok)
    scores[1:] = tie(scores[1:], p, pq)
    losses, own, *rest = loss_and_grads(me, lengths, positives, pooled, pass_embed, groups, scores)
    aways = []
    for distance, part in enumerate(rest[:-1], 1):
        ring = [(i, (i + distance) % psg_size) for i in range(psg_size)]
        aways.append(lax.ppermute(part, "psg", ring))
    gr2p, vec, proj = passage_head(rest[-1], e, x2, rate2, project_weight, g2, s2)
    dproj, vec2, dbi, gh1, keep_i, send_i, keep_o, send_o = ffn_backward(
        me,
        gr2p,
        vec,
        proj,
        own,
        aways,
        e,
        x2,
        rate2,
        project_weight,
        g2,
        s2,
        x1,
        g1,
        s1,
        inner_weight,
        outer_weight,
        u,
        d,
    )
    core_a = (swap(send_i, "grp", grp_size, 1), swap(send_o, "grp", grp_size, 1))
    gr1, go, vec1 = first_norm(gh1, x1, rate1, g1, output_weight)
    *core_a, go = tie((*core_a, go))
    next_i, away_i = [total(part, found) for part, found in zip(halves(keep_i), halves(core_a[0]))]
    next_o, away_o = [total(part, found) for part, found in zip(halves(keep_o), halves(core_a[1]))]
    plane_a = (swap(away_i, "grp", grp_size, 2), swap(away_o, "grp", grp_size, 4))
    first = heads_backward(0, p, pq, q, k, v, o, go, ptok)
    dout = output_term(me, gr1, o)
    plane_a = tie(plane_a, dout, *first)
    (go,) = tie((go,), *plane_a)
    next_i, away_i = [total(part, found) for part, found in zip(halves(next_i), halves(plane_a[0]))]
    next_o, away_o = [total(part, found) for part, found in zip(halves(next_o), halves(plane_a[1]))]
    plane_a = (swap(away_i, "grp", grp_size, 4), swap(away_o, "grp", grp_size, 2))
    second = heads_backward(1, p, pq, q, k, v, o, go, ptok)
    plane_a = tie(plane_a, *second)
    (gr1,) = tie((gr1,), *plane_a)
    both = lambda left, right: jnp.concatenate([left, right], axis=1)
    quarter = next_i.shape[0] // psg_size
    lines_a = [
        both(
            total(next_i[i * quarter : (i + 1) * quarter], plane_a[0][i * quarter : (i + 1) * quarter]),
            total(next_o[i * quarter : (i + 1) * quarter], plane_a[1][i * quarter : (i + 1) * quarter]),
        )
        for i in range(psg_size)
    ]
    line_a = line_send(lines_a[1:], psg_size)
    keep_b, send_b, grad_p, grad_q = weights(
        me,
        gr1,
        dout,
        xt,
        first,
        second,
        dproj,
        vec1,
        vec2,
        dbi,
        query_weight,
        key_weight,
        value_weight,
        ptok,
    )
    core_b = swap(send_b, "grp", grp_size, 1)
    line_a = tie(line_a, grad_q)
    piece_a = line_total(lines_a[0], line_a, grp_size)
    spread_a = line_send([piece_a] * (psg_size - 1), psg_size)
    parts_b = core_parts(keep_b, core_b)
    plane_b = plane_send(parts_b[1:], grp_size)
    (late_grad,) = tie((grad_p,), *parts_b[1:])
    out_embed, out_grad = roll_back(lengths, pass_embed, late_grad)
    plane_b = tie(plane_b, out_grad, *spread_a)
    lines_b = line_parts((parts_b[0], *plane_b), psg_size)
    line_b = line_send(lines_b[1:], psg_size)
    spread_a = tie(spread_a, *lines_b)
    ff = inner_weight.shape[1]
    held_i = jnp.concatenate([part[:, :ff] for part in (piece_a, *spread_a)])
    held_o = jnp.concatenate([part[:, ff:] for part in (piece_a, *spread_a)])
    found_a = (swap(held_i, "grp", grp_size, 4), swap(held_o, "grp", grp_size, 2))
    line_b = tie(line_b, held_i, held_o)
    piece_b = line_total(lines_b[0], line_b, grp_size)
    spread_b = line_send([piece_b] * (psg_size - 1), psg_size)
    found_a = tie(found_a, piece_b)
    held_i = jnp.concatenate([held_i, found_a[0]])
    held_o = jnp.concatenate([held_o, found_a[1]])
    found_a = (swap(held_i, "grp", grp_size, 2), swap(held_o, "grp", grp_size, 4))
    spread_b = tie(spread_b, held_i, held_o)
    joined_b = jnp.concatenate([piece_b, *spread_b])
    gathered_b = plane_send([joined_b] * 3, grp_size)
    found_a = tie(found_a, joined_b)
    held_i = jnp.concatenate([held_i, found_a[0]])
    held_o = jnp.concatenate([held_o, found_a[1]])
    other_i, other_o = swap(held_i, "grp", grp_size, 1), swap(held_o, "grp", grp_size, 1)
    dwi, dwo = unpack_ffn(me, held_i, other_i, held_o, other_o)
    gathered_b = tie(gathered_b, dwi, dwo)
    kept_b = jnp.concatenate([joined_b, *gathered_b])
    other_b = swap(kept_b, "grp", grp_size, 1)
    dwq, dwk, dwv, dout, dproj, g2, s2, bo, g1, s1, bout, bi, bq, bv = unpack_attention(
        me, kept_b, other_b, width, project_weight.shape[1], inner_weight.shape[1]
    )
    flat = lambda vector: vector.reshape(-1)
    return (
        out_embed,
        query_embed,
        flat(losses),
        out_grad,
        grad_q,
        dwq,
        flat(bq),
        dwk,
        dwv,
        flat(bv),
        dout,
        flat(bout),
        flat(g1),
        flat(s1),
        dwi,
        flat(bi),
        dwo,
        flat(bo),
        flat(g2),
        flat(s2),
        dproj,
    )


def solution(mesh):
    split = P(("grp", "psg"), None)
    in_specs = (split, split, split, P("grp")) + (P(),) * 16
    out_specs = (split, split, P("grp"), split, split) + (P(),) * 16
    body = functools.partial(local, mesh.shape["grp"], mesh.shape["psg"])
    return jax.shard_map(body, mesh=mesh, in_specs=in_specs, out_specs=out_specs, check_vma=False)
```
